128 devices in a mesh: seq: 4 (over y), ep: 32 (over z, x, core).
Axes of the slice: x: 4, y: 4, z: 4, core: 2. Of those that a mesh axis runs over, the one named last changes fastest.
Arguments:
- queries: bfloat16 [4, 256, 4, 4096], P('seq', 'ep'), may hold values from -160 to 160
- fresh_key_values: bfloat16 [4, 256, 4, 1024], P('seq', 'ep'), may hold values from -6 to 6
- key_value_pages: bfloat16 [4, 768, 16, 1024], P('seq', 'ep'), may hold values from -6 to 6
- page_owner: int32 [4, 4096, 2], P('seq'), may hold values from 0 to 31, all different within a row; in each aligned block of 128 rows (0 to 127, 128 to 255, ..., all dimensions but the last counted through in order) at most 16 rows name the same one
- page_slot: int32 [4, 4096, 2], P('seq'), may hold values from 0 to 23
- page_count: int32 [4, 256], P(None, 'ep'), may hold values from 1 to 1024
- sinks: float32 [64], replicated, may hold values from 1 to 5
- hidden: bfloat16 [4, 256, 4, 2880], P('seq', 'ep'), may hold values from -6 to 6
- norm_gain: float32 [2880], replicated, may hold values from 0.1 to 1.9
- expert_ids: int32 [4, 256, 4, 4], P('seq', 'ep'), may hold values from 0 to 127, all different within a row; in each aligned block of 32 rows (0 to 31, 32 to 63, ..., all dimensions but the last counted through in order) at most 2 rows name the same one
- gate_prob: float32 [4, 256, 4, 4], P('seq', 'ep'), may hold values from 0.05 to 0.6
- gate_up: bfloat16 [128, 2880, 2880], P(('seq', 'ep')), may hold values from -0.109375 to 0.109375
- down_proj: bfloat16 [128, 1440, 2880], P(('seq', 'ep')), may hold values from -0.15625 to 0.15625
Outputs:
- attention: bfloat16 [4, 256, 4, 4096], P('seq', 'ep')
- mixture: bfloat16 [4, 256, 4, 2880], P('seq', 'ep')
The draws below stay inside these ranges and needn't reach their ends.
Inputs may be any that keep to these rules, and one draw needn't show every extreme that they name: `page_owner`: each pair of pages names 2 different owners; in one segment the 256 pages of one ep index's prefix name one owner at most 16 times. `expert_ids`: each token names 4 different experts; the tokens of one device name one expert at most 2 times.
All inputs are finite; a program needn't handle non-finite values.
Results may differ from the reference program's by a relative error of at most 0.0068.
Values may be sent and summed in bfloat16 or wider, within the bound.
A program may use at most 192 MiB of HBM per device.

```python
import math
import jax
import jax.numpy as jnp
import numpy as np
from jax import lax

D = 2880
QUERY_HEADS = 64
KEY_VALUE_HEADS = 8
HEAD_WIDTH = 64
TOPK = 4
HID = 1440
SCORED_STEPS = 4
PAGE_TOKENS = 16
NPS = 256
PAGES_PER_UNIT = 24
PROMPTS_PER_UNIT = 8
EXPERTS = 128
TOK_DEV = 32
CAP = 16
ECAP = 2
N_SEQ = 4
N_EP = 32


def draw_queries(key, part):
    key = jax.random.fold_in(key, 11)
    shape = (N_SEQ, N_EP * PROMPTS_PER_UNIT, SCORED_STEPS, QUERY_HEADS * HEAD_WIDTH)
    base = jax.random.normal(key, shape, jnp.float32)
    return jnp.clip(base, -6.0, 6.0).astype(jnp.bfloat16)


def with_ends(values, key, smallest, top_value):
    index_at = [jax.random.randint(jax.random.fold_in(key, axis), (), 0, length) for axis, length in enumerate(values.shape)]
    longest = values.shape.index(max(values.shape))
    neighbour = index_at[:longest] + [(index_at[longest] + 1) % values.shape[longest]] + index_at[longest + 1:]
    return values.at[tuple(index_at)].set(smallest).at[tuple(neighbour)].set(top_value)


def levels(rng, dims, split, least, top_value):
    loudness, own = 1.0, jax.random.fold_in(rng, 6)
    for axis_at, blocks in split:
        draws = jnp.exp(jax.random.uniform(jax.random.fold_in(own, axis_at), (blocks,), jnp.float32, least / len(split), top_value / len(split)))
        loudness = loudness * jnp.repeat(draws, dims[axis_at] // blocks).reshape([-1 if axis == axis_at else 1 for axis in range(len(dims))])
    return loudness


def routed_block(key, own, number, rows, amount, top, most, slope):
    ranking = jax.random.permutation(key, amount)
    packed, usual = portions_of(amount, rows * top, most, slope, True), portions_of(amount, rows * top, most, slope, False)
    places = jnp.arange(amount)

    def named(sizes, turn):
        used = int((sizes > 0).sum())
        fixed = max(1, used // 4)
        moved = fixed + (places - fixed + turn * (used - fixed)) % max(1, amount - fixed)
        return jnp.zeros((amount,), jnp.int32).at[ranking[jnp.where(places < fixed, places, moved)]].set(jnp.asarray(sizes, jnp.int32))

    sizes = jnp.where(number % 4 == 0, named(packed, number // 4), named(usual, number - number // 4 - 1))
    mixed = jax.random.permutation(jax.random.fold_in(own, 3), amount)
    donor, receiver = mixed[0:amount // 2 * 2:2], mixed[1:amount // 2 * 2:2]
    slack = jnp.minimum(sizes[donor] - 1, most - sizes[receiver]) // 2
    slack = jnp.where((donor == ranking[0]) | (receiver == ranking[0]) | (sizes[receiver] == 0), 0, jnp.maximum(slack, 0))
    moved = jax.random.randint(jax.random.fold_in(own, 4), (amount // 2,), 0, 1 << 20) % (slack + 1)
    sizes = sizes.at[donor].add(-moved).at[receiver].add(moved)
    labels = jnp.searchsorted(jnp.cumsum(sizes), jnp.arange(rows * top), side="right").astype(jnp.int32)
    listing = labels.reshape(top, rows).T
    listing = listing[jax.random.permutation(jax.random.fold_in(own, 1), rows)]
    turn = jax.random.randint(jax.random.fold_in(own, 2), (rows, 1), 0, top)
    return jnp.take_along_axis(listing, (jnp.arange(top)[None, :] + turn) % top, axis=1)


def portions_of(amount, total, limit, slope, full):
    loads = [(1 << 20) // math.isqrt(rank ** slope) + 1 for rank in range(1, amount + 1)]
    largest = limit if full else min(limit, max(-(-total // amount), total * loads[0] // sum(loads)))
    least = 1 if total - largest >= amount - 1 else 0
    holding, surplus = [largest] + [least] * (amount - 1), total - largest - least * (amount - 1)
    while surplus > 0:
        free = [i for i in range(1, amount) if holding[i] < largest] or [i for i in range(1, amount) if holding[i] < limit]
        mass, budget = sum([loads[i] for i in free]), surplus
        for i in free:
            more = min(limit - holding[i], max(1, budget * loads[i] // mass), surplus)
            holding[i] = holding[i] + more
            surplus = surplus - more
    return np.array(holding)


def gaussian(stream_key, extent, width, reach, split=(), held_as=jnp.bfloat16):
    loudness = levels(stream_key, extent, split, -0.22, 0.18) if split else 1.0
    values = jax.random.normal(stream_key, extent, jnp.float32) * width * loudness
    return jnp.minimum(jnp.maximum(values, -reach), reach).astype(held_as)


def setup_inputs(seed: int = 0) -> dict:
    splits = jax.random.split(jax.random.key(seed), 14)
    queries = draw_queries(jax.random.fold_in(splits[13], 71), 0)
    fresh_key_values = gaussian(splits[1], (N_SEQ, N_EP * PROMPTS_PER_UNIT, SCORED_STEPS, 2 * KEY_VALUE_HEADS * HEAD_WIDTH), 1.0, 6.0, ((0, 4), (1, 32)))
    key_value_pages = gaussian(splits[2], (N_SEQ, N_EP * PAGES_PER_UNIT, PAGE_TOKENS, 2 * KEY_VALUE_HEADS * HEAD_WIDTH), 1.0, 6.0, ((0, 4), (1, 32)))
    page_owner_keys = jax.random.split(jax.random.fold_in(splits[3], 1), N_SEQ * (N_EP * NPS // 2) // (NPS // 2))
    page_owner_turns = jax.random.permutation(jax.random.fold_in(splits[3], 3), N_SEQ * (N_EP * NPS // 2) // (NPS // 2))
    page_owner = jax.vmap(lambda own, number: routed_block(jax.random.fold_in(splits[3], 2), own, number, NPS // 2, N_EP, 2, CAP, 2))(page_owner_keys, page_owner_turns).reshape((N_SEQ, N_EP * NPS // 2, 2))
    page_slot = with_ends(jax.random.randint(splits[4], (N_SEQ, N_EP * NPS // 2, 2), 0, PAGES_PER_UNIT), jax.random.fold_in(splits[4], 1), 0, PAGES_PER_UNIT - 1).astype(jnp.int32)
    page_count = with_ends(jax.random.randint(splits[5], (N_SEQ, N_EP * PROMPTS_PER_UNIT), 1, N_SEQ * NPS + 1), jax.random.fold_in(splits[5], 1), 1, N_SEQ * NPS).astype(jnp.int32)
    sinks = jnp.clip(jax.random.uniform(splits[6], (QUERY_HEADS,), jnp.float32, 1.0, 5.0), 1.0, 5.0)
    hidden = gaussian(splits[7], (N_SEQ, N_EP * PROMPTS_PER_UNIT, SCORED_STEPS, D), 1.0, 6.0, ((0, 4), (1, 32)))
    norm_gain = jnp.clip(1.0 + 0.18 * jax.random.normal(splits[8], (D,), jnp.float32), 0.1, 1.9)
    expert_ids_keys = jax.random.split(jax.random.fold_in(splits[9], 1), N_SEQ * (N_EP * PROMPTS_PER_UNIT) * SCORED_STEPS // TOK_DEV)
    expert_ids_turns = jax.random.permutation(jax.random.fold_in(splits[9], 3), N_SEQ * (N_EP * PROMPTS_PER_UNIT) * SCORED_STEPS // TOK_DEV)
    expert_ids = jax.vmap(lambda own, number: routed_block(jax.random.fold_in(splits[9], 2), own, number, TOK_DEV, EXPERTS, TOPK, ECAP, 1))(expert_ids_keys, expert_ids_turns).reshape((N_SEQ, N_EP * PROMPTS_PER_UNIT, SCORED_STEPS, TOPK))
    gate_prob = jnp.clip(jnp.exp(math.log(0.6) - 2.4849067 * jax.random.uniform(splits[10], (N_SEQ, N_EP * PROMPTS_PER_UNIT, SCORED_STEPS, TOPK), jnp.float32) ** levels(splits[10], (N_SEQ, N_EP * PROMPTS_PER_UNIT, SCORED_STEPS, TOPK), ((0, 4), (1, 32)), -0.2, 0.2)), 0.05, 0.6)
    gate_up = gaussian(splits[11], (EXPERTS, D, 2 * HID), D ** -0.5, 0.109375, ((0, 128),))
    down_proj = gaussian(splits[12], (EXPERTS, HID, D), HID ** -0.5, 0.15625, ((0, 128),))
    return dict(queries=queries, fresh_key_values=fresh_key_values, key_value_pages=key_value_pages, page_owner=page_owner, page_slot=page_slot, page_count=page_count, sinks=sinks, hidden=hidden, norm_gain=norm_gain, expert_ids=expert_ids, gate_prob=gate_prob, gate_up=gate_up, down_proj=down_proj)


SCALE = 0.125
NEGATIVE = -1e+30
EPSILON = 1e-05

def softmax_parts(scores, shown):
    scores = jnp.where(shown, scores, NEGATIVE)
    maxima = lax.optimization_barrier(jnp.max(scores, axis=-1))
    weights_full = jnp.where(shown, jnp.exp(scores - maxima[..., None]), 0.0)
    totals = lax.optimization_barrier(jnp.sum(weights_full, axis=-1))
    return (maxima, totals, weights_full)

def shared_scores(query_matrix, key_value_table, visible):
    prompt_batch, position_index, _ = query_matrix.shape
    prompt_length = key_value_table.shape[0]
    split_point = KEY_VALUE_HEADS * HEAD_WIDTH
    query_head_rows = query_matrix.reshape(prompt_batch, position_index, KEY_VALUE_HEADS, QUERY_HEADS // KEY_VALUE_HEADS, HEAD_WIDTH).astype(jnp.float32)
    key_head_rows = key_value_table[:, :split_point].reshape(prompt_length, KEY_VALUE_HEADS, HEAD_WIDTH).astype(jnp.float32)
    value_head_rows = key_value_table[:, split_point:].reshape(prompt_length, KEY_VALUE_HEADS, HEAD_WIDTH).astype(jnp.float32)
    scores = jnp.einsum('psvgd,kvd->psvgk', query_head_rows, key_head_rows) * SCALE
    maxima, totals, weights_full = softmax_parts(scores, visible[:, None, None, None, :])
    rounded = lax.optimization_barrier(weights_full.astype(jnp.bfloat16))
    outputs = jnp.einsum('psvgk,kvd->psvgd', rounded.astype(jnp.float32), value_head_rows)
    return (maxima.reshape(prompt_batch, position_index, QUERY_HEADS), totals.reshape(prompt_batch, position_index, QUERY_HEADS), outputs.reshape(prompt_batch, position_index, QUERY_HEADS * HEAD_WIDTH))

def own_scores(query_matrix, key_value_table, visible):
    prompt_batch, position_index, _ = query_matrix.shape
    prompt_length = key_value_table.shape[1]
    split_point = KEY_VALUE_HEADS * HEAD_WIDTH
    query_head_rows = query_matrix.reshape(prompt_batch, position_index, KEY_VALUE_HEADS, QUERY_HEADS // KEY_VALUE_HEADS, HEAD_WIDTH).astype(jnp.float32)
    key_head_rows = key_value_table[:, :, :split_point].reshape(prompt_batch, prompt_length, KEY_VALUE_HEADS, HEAD_WIDTH).astype(jnp.float32)
    value_head_rows = key_value_table[:, :, split_point:].reshape(prompt_batch, prompt_length, KEY_VALUE_HEADS, HEAD_WIDTH).astype(jnp.float32)
    scores = jnp.einsum('psvgd,pkvd->psvgk', query_head_rows, key_head_rows) * SCALE
    maxima, totals, weights_full = softmax_parts(scores, visible[:, :, None, None, :])
    rounded = lax.optimization_barrier(weights_full.astype(jnp.bfloat16))
    outputs = jnp.einsum('psvgk,pkvd->psvgd', rounded.astype(jnp.float32), value_head_rows)
    return (maxima.reshape(prompt_batch, position_index, QUERY_HEADS), totals.reshape(prompt_batch, position_index, QUERY_HEADS), outputs.reshape(prompt_batch, position_index, QUERY_HEADS * HEAD_WIDTH))

def grouped(array):
    rest = array.shape[2:]
    shaped = jnp.moveaxis(array.reshape((N_SEQ, N_EP, PROMPTS_PER_UNIT) + rest), 1, 0)
    return shaped.reshape((N_EP, N_SEQ * PROMPTS_PER_UNIT) + rest)

def reference(queries, fresh_key_values, key_value_pages, page_owner, page_slot, page_count, sinks, hidden, norm_gain, expert_ids, gate_prob, gate_up, down_proj):
    group_rows = N_SEQ * PROMPTS_PER_UNIT
    feature_columns = 2 * KEY_VALUE_HEADS * HEAD_WIDTH
    group_queries = grouped(queries)
    group_new = grouped(fresh_key_values)
    counts = grouped(page_count)
    index_rows = (page_owner * PAGES_PER_UNIT + page_slot).reshape(N_SEQ, N_EP, NPS)

    def one_block(number):
        segment = number // N_EP
        member = number % N_EP
        keys = key_value_pages[segment][index_rows[segment, member]].reshape(NPS * PAGE_TOKENS, feature_columns)
        live = (segment * NPS + jnp.arange(NPS, dtype=jnp.int32))[None, :] < counts[member][:, None]
        visible = jnp.repeat(live, PAGE_TOKENS, axis=1)
        return shared_scores(group_queries[member], keys, visible)
    seg_max, seg_total, seg_out = lax.map(one_block, jnp.arange(N_SEQ * N_EP, dtype=jnp.int32))
    seg_max = seg_max.reshape(N_SEQ, N_EP, group_rows, SCORED_STEPS, QUERY_HEADS)
    seg_total = seg_total.reshape(N_SEQ, N_EP, group_rows, SCORED_STEPS, QUERY_HEADS)
    seg_out = seg_out.reshape(N_SEQ, N_EP, group_rows, SCORED_STEPS, QUERY_HEADS * HEAD_WIDTH)
    causal = jnp.arange(SCORED_STEPS)[:, None] >= jnp.arange(SCORED_STEPS)[None, :]
    own_visible = jnp.broadcast_to(causal[None], (N_EP * group_rows, SCORED_STEPS, SCORED_STEPS))
    own_max, own_total, own_out = own_scores(group_queries.reshape(N_EP * group_rows, SCORED_STEPS, QUERY_HEADS * HEAD_WIDTH), group_new.reshape(N_EP * group_rows, SCORED_STEPS, feature_columns), own_visible)
    own_max = own_max.reshape(N_EP, group_rows, SCORED_STEPS, QUERY_HEADS)
    own_total = own_total.reshape(N_EP, group_rows, SCORED_STEPS, QUERY_HEADS)
    own_out = own_out.reshape(N_EP, group_rows, SCORED_STEPS, QUERY_HEADS * HEAD_WIDTH)
    highest = jnp.maximum(lax.optimization_barrier(jnp.max(seg_max, axis=0)), own_max)
    highest = jnp.maximum(highest, sinks)
    factor = jnp.exp(seg_max - highest[None])
    own_factor = jnp.exp(own_max - highest)
    denominator = lax.optimization_barrier(jnp.sum(seg_total * factor, axis=0)) + own_total * own_factor + jnp.exp(sinks - highest)
    numerator = lax.optimization_barrier(jnp.sum(seg_out * jnp.repeat(factor, HEAD_WIDTH, axis=-1), axis=0)) + own_out * jnp.repeat(own_factor, HEAD_WIDTH, axis=-1)
    result = (numerator / jnp.repeat(denominator, HEAD_WIDTH, axis=-1)).astype(jnp.bfloat16)
    result = jnp.moveaxis(result.reshape(N_EP, N_SEQ, PROMPTS_PER_UNIT, SCORED_STEPS, QUERY_HEADS * HEAD_WIDTH), 0, 1)
    attention = result.reshape(queries.shape)
    devices = N_SEQ * N_EP
    flat_hidden = hidden.reshape(devices * TOK_DEV, D).astype(jnp.float32)
    meansq = lax.optimization_barrier(jnp.mean(flat_hidden * flat_hidden, axis=-1, keepdims=True))
    normed = (flat_hidden * lax.rsqrt(meansq + EPSILON) * norm_gain).astype(jnp.bfloat16)
    chosen = expert_ids.reshape(devices, TOK_DEV * TOPK)
    onehot = (chosen[:, :, None] == jnp.arange(EXPERTS, dtype=jnp.int32)[None, None, :]).astype(jnp.int32)
    ranks = lax.optimization_barrier(jnp.sum((jnp.cumsum(onehot, axis=1) - 1) * onehot, axis=-1))
    slot_index = jnp.arange(devices, dtype=jnp.int32)[:, None] * ECAP + ranks
    token_index = jnp.arange(devices, dtype=jnp.int32)[:, None] * TOK_DEV + jnp.arange(TOK_DEV * TOPK, dtype=jnp.int32)[None, :] // TOPK
    table = jnp.zeros((EXPERTS, devices * ECAP), jnp.int32).at[chosen, slot_index].set(token_index)

    def one_expert(expert):
        token_rows = normed[table[expert]]
        projected = jnp.dot(token_rows, gate_up[expert], preferred_element_type=jnp.float32)
        gate = projected[:, :HID]
        upper = projected[:, HID:]
        active = ((upper + 1.0) * gate * jax.nn.sigmoid(1.702 * gate)).astype(jnp.bfloat16)
        return jnp.dot(active, down_proj[expert], preferred_element_type=jnp.float32).astype(jnp.bfloat16)
    expert_rows = lax.map(one_expert, jnp.arange(EXPERTS, dtype=jnp.int32))
    picked = expert_rows[chosen, slot_index].astype(jnp.float32)
    weighted = picked * gate_prob.reshape(devices, TOK_DEV * TOPK, 1)
    mixture = lax.optimization_barrier(jnp.sum(weighted.reshape(devices, TOK_DEV, TOPK, D), axis=2)).astype(jnp.bfloat16).reshape(hidden.shape)
    return (attention, mixture)
```

```python
import functools

import jax
import jax.numpy as jnp
from jax import lax
from jax.experimental import pallas as pl
from jax.experimental.pallas import tpu as pltpu
from jax.sharding import PartitionSpec as P

D = 2880
QUERY_HEADS = 64
KEY_VALUE_HEADS = 8
GROUP = QUERY_HEADS // KEY_VALUE_HEADS
HEAD_WIDTH = 64
TOPK = 4
HID = 1440
SCORED_STEPS = 4
PAGE_TOKENS = 16
NPS = 256
PAGES = 24
PROMPTS = 8
N_SEQ = 4
N_EP = 32
ROWS = PROMPTS * SCORED_STEPS
HEAD_COLUMNS = GROUP * HEAD_WIDTH
NEGATIVE = -1e30
FLOOR = -1e29
EPSILON = 1e-05
MESH = pl.DeviceIdType.MESH
F32 = jnp.float32
BF16 = jnp.bfloat16
HIGHEST = lax.Precision.HIGHEST


def place():
    y = lax.axis_index("seq")
    ep = lax.axis_index("ep")
    return y, lax.div(ep, 8), lax.rem(lax.div(ep, 2), 4), lax.rem(ep, 2)


def device(y, z, x, c):
    return (y, z * 8 + x * 2 + c)


def head_of(y, x):
    return lax.div(y, 2) * 4 + x


def nt(a, b, precision=None):
    return lax.dot_general(
        a, b, (((1,), (1,)), ((), ())), preferred_element_type=F32, precision=precision
    )


def nn(a, b, precision=None):
    return lax.dot_general(
        a, b, (((1,), (0,)), ((), ())), preferred_element_type=F32, precision=precision
    )


def iota(shape, axis):
    return lax.broadcasted_iota(jnp.int32, shape, axis)


def exchange_kernel(
    q_ref, f_ref, page_ref, table_ref, count_ref,
    q_all, f_all, pool, tables, counts,
    relay, f_relay,
    q_send, q_recv, f_send, f_recv, a_send, a_recv, z_send, z_recv, c_send, c_recv,
    i_send, i_recv, local,
):
    y, z, x, c = place()
    mate = 3 - y

    def at(dy, dx):
        return device(lax.rem(y + dy, 4), z, lax.rem(x + dx, 4), c)

    plane = [(dy, dx) for dy in range(4) for dx in range(4) if (dy, dx) != (0, 0)]
    up = device(y, lax.rem(z + 1, 4), x, c)
    down = device(y, lax.rem(z + 3, 4), x, c)
    twin = device(y, z, x, 1 - c)

    barrier = pltpu.get_barrier_semaphore()
    for peer in [at(dy, dx) for dy, dx in plane] + [up, down, twin]:
        pl.semaphore_signal(barrier, inc=1, device_id=peer, device_id_type=MESH)

    for h in range(KEY_VALUE_HEADS):
        low, high = h * HEAD_WIDTH, (h + 1) * HEAD_WIDTH
        split = KEY_VALUE_HEADS * HEAD_WIDTH
        rows = jnp.concatenate(
            [page_ref[:, low:high], page_ref[:, split + low : split + high]], axis=1
        )
        relay[h] = rows.reshape(PAGES, PAGE_TOKENS, 2 * HEAD_WIDTH)
        f_relay[h] = jnp.concatenate(
            [f_ref[:, low:high], f_ref[:, split + low : split + high]], axis=1
        )
    pl.semaphore_wait(barrier, len(plane) + 3)

    def spot(segment_slot, zz, xx, cc):
        return pool.at[segment_slot, pl.ds((zz * 8 + xx * 2 + cc) * PAGES, PAGES)]

    order = [(0, 0), (0, 1), (0, 3), (1, 0), (1, 1), (1, 3), (0, 2), (1, 2)]
    first = []
    for n, (p, dx) in enumerate(order):
        yy = y if p == 0 else mate
        xx = lax.rem(x + dx, 4)
        target = spot(lax.div(y, 2), z, x, c)
        source = relay.at[head_of(yy, xx)]
        if (p, dx) == (0, 0):
            copy = pltpu.make_async_copy(source, target, local.at[0])
        else:
            copy = pltpu.make_async_remote_copy(
                source, target, a_send.at[n], a_recv.at[n],
                device_id=device(yy, z, xx, c), device_id_type=MESH,
            )
        copy.start()
        first.append(copy)

    small = []
    mine = pltpu.make_async_copy(table_ref, tables.at[lax.div(y, 2)], local.at[1])
    mine.start()
    small.append(mine)
    mine = pltpu.make_async_copy(count_ref, counts.at[x], local.at[2])
    mine.start()
    small.append(mine)
    other = pltpu.make_async_remote_copy(
        table_ref, tables.at[lax.div(y, 2)], i_send.at[0], i_recv.at[0],
        device_id=device(mate, z, x, c), device_id_type=MESH,
    )
    other.start()
    small.append(other)
    for dx in range(1, 4):
        other = pltpu.make_async_remote_copy(
            count_ref, counts.at[x], i_send.at[dx], i_recv.at[dx],
            device_id=at(0, dx), device_id_type=MESH,
        )
        other.start()
        small.append(other)

    for dy in range(4):
        for dx in range(4):
            n = dy * 4 + dx
            h = head_of(lax.rem(y + dy, 4), lax.rem(x + dx, 4))
            q_source = q_ref.at[:, pl.ds(pl.multiple_of(h * HEAD_COLUMNS, HEAD_COLUMNS), HEAD_COLUMNS)]
            f_source = f_relay.at[h]
            slot = x * 4 + y
            if n == 0:
                copies = [
                    pltpu.make_async_copy(q_source, q_all.at[slot], local.at[3]),
                    pltpu.make_async_copy(f_source, f_all.at[slot], local.at[4]),
                ]
            else:
                copies = [
                    pltpu.make_async_remote_copy(
                        q_source, q_all.at[slot], q_send.at[n], q_recv.at[n],
                        device_id=at(dy, dx), device_id_type=MESH,
                    ),
                    pltpu.make_async_remote_copy(
                        f_source, f_all.at[slot], f_send.at[n], f_recv.at[n],
                        device_id=at(dy, dx), device_id_type=MESH,
                    ),
                ]
            for copy in copies:
                copy.start()
            small.extend(copies)

    def chunk(n):
        p, dx = order[n]
        yy = y if p == 0 else mate
        return lax.div(yy, 2), lax.rem(x - dx + 4, 4)

    def pass_on(n, zz, way, peer):
        segment_slot, xx = chunk(n)
        block = spot(segment_slot, zz, xx, c)
        sends, recvs = (c_send, c_recv) if way >= 3 else (z_send, z_recv)
        number = (way - 3 if way >= 3 else way) * 8 + n
        copy = pltpu.make_async_remote_copy(
            block, block, sends.at[number], recvs.at[number],
            device_id=peer, device_id_type=MESH,
        )
        copy.start()
        return copy

    upward, downward, further, across = [], [], [], []
    for n in range(8):
        if n == 0:
            first[n].wait()
        else:
            first[n].wait_recv()
        upward.append(pass_on(n, z, 0, up))
        downward.append(pass_on(n, z, 1, down))
        across.append(pass_on(n, z, 3, twin))
    for n in range(8):
        upward[n].wait_recv()
        if n % 2 == 0:
            further.append(pass_on(n, lax.rem(z + 3, 4), 2, up))
        across.append(pass_on(n, lax.rem(z + 3, 4), 4, twin))
        downward[n].wait_recv()
        if n % 2 == 1:
            further.append(pass_on(n, lax.rem(z + 1, 4), 2, down))
        across.append(pass_on(n, lax.rem(z + 1, 4), 5, twin))
    for n in range(8):
        further[n].wait_recv()
        across.append(pass_on(n, lax.rem(z + 2, 4), 6, twin))
    for copy in across:
        copy.wait()
    for copy in first[1:] + upward + downward + further:
        copy.wait_send()
    for copy in small:
        copy.wait()


def exchange(queries, fresh, pages, table, count):
    vmem = pl.BlockSpec(memory_space=pltpu.VMEM)
    anywhere = pl.BlockSpec(memory_space=pl.ANY)
    dma = pltpu.SemaphoreType.DMA
    return pl.pallas_call(
        exchange_kernel,
        out_shape=(
            jax.ShapeDtypeStruct((16, ROWS, HEAD_COLUMNS), BF16),
            jax.ShapeDtypeStruct((16, ROWS, 2 * HEAD_WIDTH), BF16),
            jax.ShapeDtypeStruct((2, N_EP * PAGES, PAGE_TOKENS, 2 * HEAD_WIDTH), BF16),
            jax.ShapeDtypeStruct((2, 8, 128), jnp.int32),
            jax.ShapeDtypeStruct((4, 8, 128), jnp.int32),
        ),
        in_specs=[vmem] * 5,
        out_specs=(anywhere,) * 5,
        scratch_shapes=[
            pltpu.VMEM((KEY_VALUE_HEADS, PAGES, PAGE_TOKENS, 2 * HEAD_WIDTH), BF16),
            pltpu.VMEM((KEY_VALUE_HEADS, ROWS, 2 * HEAD_WIDTH), BF16),
            dma((16,)), dma((16,)), dma((16,)), dma((16,)), dma((8,)), dma((8,)),
            dma((24,)), dma((24,)), dma((32,)), dma((32,)), dma((4,)), dma((4,)), dma((5,)),
        ],
        compiler_params=pltpu.CompilerParams(
            collective_id=1, has_side_effects=True, vmem_limit_bytes=16 << 20
        ),
        name="exchange",
    )(queries, fresh, pages, table, count)


BK = 1024
HALF = BK // 2
GK = 512
KEYS = 2 * NPS * PAGE_TOKENS
CHUNKS = 4
COLS = 256
VROWS = 80


def score_kernel(
    tables, counts, sinks, q_all, f_all, pool, o_ref, lse_ref,
    kv, vt, qs, f_sorted, limit_ref, m_ref, acc, sorted_out, s0, s1,
):
    y = lax.axis_index("seq")
    outer_pair = jnp.logical_or(y == 0, y == 3)
    pick = (iota((VROWS, 128), 0) + HEAD_WIDTH == iota((VROWS, 128), 1)).astype(BF16)
    sink_row = sinks[0:1, :]

    def values_of(rows):
        moved = nt(pick, rows)
        return jnp.where(iota(moved.shape, 0) >= HEAD_WIDTH, 1.0, moved).astype(BF16)

    def unit(e, carry):
        c = counts[e][0:1, :].astype(F32)
        n_row = jnp.where(
            outer_pair,
            jnp.minimum(c, 256.0) + jnp.maximum(c - 768.0, 0.0),
            jnp.clip(c - 256.0, 0.0, 512.0),
        )
        i0 = iota((128, 128), 0)
        i1 = iota((128, 128), 1)
        n_col = jnp.sum(jnp.where(i0 == i1, n_row, 0.0), axis=1, keepdims=True)
        ahead = jnp.logical_or(n_col > n_row, jnp.logical_and(n_col == n_row, i0 < i1))
        pos_row = jnp.sum(jnp.where(ahead, 1.0, 0.0), axis=0, keepdims=True)
        behind = jnp.logical_or(n_row > n_col, jnp.logical_and(n_col == n_row, i1 < i0))
        pos_col = jnp.sum(jnp.where(behind, 1.0, 0.0), axis=1, keepdims=True)
        perm = (pos_row == i0.astype(F32)).astype(BF16)
        perm_t = (pos_col == i1.astype(F32)).astype(BF16)
        q_sorted = (nn(perm, q_all[pl.ds(e * 4, 4)].reshape(128, HEAD_COLUMNS)) * 0.125).astype(BF16)
        f_sorted[...] = nn(perm, f_all[pl.ds(e * 4, 4)].reshape(128, 128)).astype(BF16)
        none = jnp.zeros((ROWS, HEAD_WIDTH), BF16)
        lane_row = lax.rem(iota((128, COLS), 1), ROWS).astype(F32)
        longest = []
        for ch in range(CHUNKS):
            for g in range(GROUP):
                piece = q_sorted[ch * ROWS : (ch + 1) * ROWS, g * HEAD_WIDTH : (g + 1) * HEAD_WIDTH]
                qs[ch, g * ROWS : (g + 1) * ROWS, :] = jnp.concatenate([piece, none], axis=1)
            member = pos_col == lane_row + float(ch * ROWS)
            limit = jnp.sum(jnp.where(member, n_col, 0.0), axis=0, keepdims=True) * PAGE_TOKENS
            limit_ref[ch] = jnp.broadcast_to(limit, (8, COLS))
            longest.append(jnp.max(limit).astype(jnp.int32))
            rows = f_sorted[ch * ROWS : (ch + 1) * ROWS, :]
            s = nt(rows, qs[ch])
            ki = iota((ROWS, COLS), 0)
            ri = lax.rem(iota((ROWS, COLS), 1), ROWS)
            seen = jnp.logical_and(
                lax.div(ki, SCORED_STEPS) == lax.div(ri, SCORED_STEPS), ki <= ri
            )
            s = jnp.where(seen, s, NEGATIVE)
            m0 = jnp.maximum(jnp.max(s, axis=0, keepdims=True), sink_row)
            p = jnp.exp(s - m0).astype(BF16)
            start = nn(values_of(rows), p)
            start = start + jnp.where(
                iota((VROWS, COLS), 0) >= HEAD_WIDTH, jnp.exp(sink_row - m0), 0.0
            )
            m_ref[ch] = jnp.broadcast_to(jnp.where(outer_pair, m0, FLOOR), (8, COLS))
            acc[ch] = jnp.where(outer_pair, start, 0.0)

        def gather(kb, carry):
            p0 = kb * (GK // PAGE_TOKENS)
            ss = lax.div(p0, NPS)
            within = lax.rem(p0, NPS)
            row = e * 2 + lax.div(within, 128)
            lane = lax.rem(within, 128)
            base = pl.multiple_of(kb * GK, GK)
            rows = [
                pool[tables[ss, row, lane + i] + ss * (N_EP * PAGES)]
                for i in range(GK // PAGE_TOKENS)
            ]
            found = jnp.concatenate(rows, axis=0)
            kv[pl.ds(base, GK), :] = found
            vt[kb] = values_of(found)
            return carry

        lax.fori_loop(0, lax.div(longest[0] + (BK - 1), BK) * (BK // GK), gather, 0)

        key = iota((HALF, COLS), 0).astype(F32)
        for ch in range(CHUNKS):
            q = qs[ch]
            limit = limit_ref[ch][0:1, :]

            def scores(start):
                return nt(kv[pl.ds(pl.multiple_of(start, HALF), HALF), :], q)

            def absorb(s, start, state):
                before, total = state
                s = jnp.where(key < limit - start.astype(F32), s, NEGATIVE)
                after = jnp.maximum(before, jnp.max(s, axis=0, keepdims=True))
                p = jnp.exp(s - after).astype(BF16)
                values = vt[lax.div(start, GK)]
                return after, total * jnp.exp(before - after) + nn(values, p)

            def block(kb, state):
                start = kb * BK
                s1[...] = scores(start + HALF)
                state = absorb(s0[...], start, state)
                s0[...] = scores(jnp.minimum(start + BK, KEYS - HALF))
                return absorb(s1[...], start + HALF, state)

            s0[...] = scores(0)
            state = (m_ref[ch][0:1, :], acc[ch])
            state = lax.fori_loop(0, lax.div(longest[ch] + (BK - 1), BK), block, state)
            m_ref[ch] = jnp.broadcast_to(state[0], (8, COLS))
            acc[ch] = state[1]

        lse = jnp.zeros((8, 128), F32)
        for ch in range(CHUNKS):
            total = jnp.maximum(acc[ch][HEAD_WIDTH : HEAD_WIDTH + 1, :], 1e-30)
            out = acc[ch][0:HEAD_WIDTH, :] / total
            padded = jnp.concatenate([out, jnp.zeros_like(out)], axis=0)
            turned = padded.T.astype(BF16)
            for g in range(GROUP):
                sorted_out[ch * ROWS : (ch + 1) * ROWS, g * HEAD_WIDTH : (g + 1) * HEAD_WIDTH] = (
                    turned[g * ROWS : (g + 1) * ROWS, 0:HEAD_WIDTH]
                )
            row = m_ref[ch][0:1, :] + jnp.log(total)
            mine = lax.div(iota((8, COLS), 1), ROWS) == iota((8, COLS), 0)
            member = (pos_col == lane_row + float(ch * ROWS)).astype(F32)
            lse = lse + nt(jnp.where(mine, row, 0.0), member, HIGHEST)
        lse_ref[e] = lse
        o_ref[e] = nn(perm_t, sorted_out[...]).astype(BF16)
        return carry

    lax.fori_loop(0, 4, unit, 0)


def score(tables, counts, sinks, q_all, f_all, pool):
    vmem = pl.BlockSpec(memory_space=pltpu.VMEM)
    return pl.pallas_call(
        score_kernel,
        out_shape=(
            jax.ShapeDtypeStruct((4, 128, HEAD_COLUMNS), BF16),
            jax.ShapeDtypeStruct((4, 8, 128), F32),
        ),
        in_specs=[pl.BlockSpec(memory_space=pltpu.SMEM)] + [vmem] * 5,
        out_specs=(vmem, vmem),
        scratch_shapes=[
            pltpu.VMEM((KEYS, 128), BF16),
            pltpu.VMEM((KEYS // GK, VROWS, GK), BF16),
            pltpu.VMEM((CHUNKS, COLS, 128), BF16),
            pltpu.VMEM((128, 128), BF16),
            pltpu.VMEM((CHUNKS, 8, COLS), F32),
            pltpu.VMEM((CHUNKS, 8, COLS), F32),
            pltpu.VMEM((CHUNKS, VROWS, COLS), F32),
            pltpu.VMEM((128, HEAD_COLUMNS), BF16),
            pltpu.VMEM((HALF, COLS), F32),
            pltpu.VMEM((HALF, COLS), F32),
        ],
        compiler_params=pltpu.CompilerParams(vmem_limit_bytes=40 << 20),
        cost_estimate=pl.CostEstimate(
            flops=25_000_000_000, bytes_accessed=8_000_000, transcendentals=20_000_000
        ),
        name="score",
    )(tables, counts, sinks, q_all, f_all, pool)


def merge_kernel(o_ref, lse_ref, out_ref, o_all, lse_all, o_send, o_recv, l_send, l_recv, local):
    y, z, x, c = place()

    def at(dy, dx):
        return device(lax.rem(y + dy, 4), z, lax.rem(x + dx, 4), c)

    plane = [(dy, dx) for dy in range(4) for dx in range(4) if (dy, dx) != (0, 0)]
    barrier = pltpu.get_barrier_semaphore()
    for dy, dx in plane:
        pl.semaphore_signal(barrier, inc=1, device_id=at(dy, dx), device_id_type=MESH)
    pl.semaphore_wait(barrier, len(plane))
    inner_pair = jnp.logical_or(y == 1, y == 2).astype(jnp.int32)
    slot = inner_pair * 8 + head_of(y, x)
    copies = []
    for dy in range(4):
        for dx in range(4):
            n = dy * 4 + dx
            q = lax.rem(y + dy, 4)
            e = lax.rem(x + dx, 4)
            o_source = o_ref.at[e, pl.ds(pl.multiple_of(q * ROWS, ROWS), ROWS)]
            if n == 0:
                pair = [
                    pltpu.make_async_copy(o_source, o_all.at[slot], local.at[0]),
                    pltpu.make_async_copy(lse_ref.at[e], lse_all.at[slot], local.at[1]),
                ]
            else:
                pair = [
                    pltpu.make_async_remote_copy(
                        o_source, o_all.at[slot], o_send.at[n], o_recv.at[n],
                        device_id=at(dy, dx), device_id_type=MESH,
                    ),
                    pltpu.make_async_remote_copy(
                        lse_ref.at[e], lse_all.at[slot], l_send.at[n], l_recv.at[n],
                        device_id=at(dy, dx), device_id_type=MESH,
                    ),
                ]
            for copy in pair:
                copy.start()
            copies.extend(pair)
    for copy in copies:
        copy.wait()
    mine = (iota((ROWS, 128), 1) == iota((ROWS, 128), 0) + y * ROWS).astype(F32)
    logs = nt(mine, lse_all[...].reshape(128, 128), HIGHEST)
    log0, log1 = logs[:, :64], logs[:, 64:]
    top = jnp.maximum(log0, log1)
    w0, w1 = jnp.exp(log0 - top), jnp.exp(log1 - top)
    share0, share1 = w0 / (w0 + w1), w1 / (w0 + w1)
    parts = []
    for share in (share0, share1):
        high = share.astype(BF16)
        parts.append((high, (share - high.astype(F32)).astype(BF16)))
    for h in range(KEY_VALUE_HEADS):
        shape = (64, HEAD_COLUMNS)
        spread = (iota(shape, 0) == lax.div(iota(shape, 1), HEAD_WIDTH) + h * GROUP).astype(BF16)
        wide = [nn(high, spread) + nn(low, spread) for high, low in parts]
        result = wide[0] * o_all[h].astype(F32) + wide[1] * o_all[8 + h].astype(F32)
        out_ref[:, h * HEAD_COLUMNS : (h + 1) * HEAD_COLUMNS] = result.astype(BF16)


def merge(o, lse):
    vmem = pl.BlockSpec(memory_space=pltpu.VMEM)
    dma = pltpu.SemaphoreType.DMA
    return pl.pallas_call(
        merge_kernel,
        out_shape=jax.ShapeDtypeStruct((ROWS, QUERY_HEADS * HEAD_WIDTH), BF16),
        in_specs=[vmem, vmem],
        out_specs=vmem,
        scratch_shapes=[
            pltpu.VMEM((16, ROWS, HEAD_COLUMNS), BF16),
            pltpu.VMEM((16, 8, 128), F32),
            dma((16,)), dma((16,)), dma((16,)), dma((16,)), dma((2,)),
        ],
        compiler_params=pltpu.CompilerParams(
            collective_id=2, has_side_effects=True, vmem_limit_bytes=16 << 20
        ),
        name="merge",
    )(o, lse)


def per_device(
    queries, fresh_key_values, key_value_pages, page_owner, page_slot, page_count, sinks,
    hidden, norm_gain, expert_ids, gate_prob, gate_up, down_proj,
):
    y, z, x, c = place()

    flat_hidden = hidden.reshape(ROWS, D).astype(F32)
    meansq = jnp.mean(flat_hidden * flat_hidden, axis=-1, keepdims=True)
    normed = (flat_hidden * lax.rsqrt(meansq + EPSILON) * norm_gain).astype(BF16)
    chosen = expert_ids.reshape(ROWS * TOPK)
    number = jnp.arange(ROWS * TOPK, dtype=jnp.int32)
    same = jnp.logical_and(chosen[:, None] == chosen[None, :], number[None, :] < number[:, None])
    rank = jnp.sum(same.astype(jnp.int32), axis=1)
    slots = (chosen * 2 + rank).reshape(ROWS, TOPK)
    hit = slots[None, :, :] == jnp.arange(256, dtype=jnp.int32)[:, None, None]
    spread = jnp.any(hit, axis=-1).astype(BF16)
    buffer = jnp.dot(spread, normed, preferred_element_type=F32).astype(BF16)
    weights = jnp.sum(
        jnp.where(
            slots[:, :, None] == jnp.arange(256, dtype=jnp.int32)[None, None, :],
            gate_prob.reshape(ROWS, TOPK, 1),
            0.0,
        ),
        axis=1,
    )
    arrived = lax.all_to_all(buffer, ("seq", "ep"), split_axis=0, concat_axis=0, tiled=True)

    index = (page_owner * PAGES + page_slot).reshape(4, 4, 2, NPS)
    index = lax.dynamic_index_in_dim(index, z, 0, keepdims=False)
    index = lax.dynamic_index_in_dim(index, c, 1, keepdims=False)
    table = index.reshape(8, 128)
    count = jnp.broadcast_to(jnp.repeat(page_count.reshape(32), 4)[None, :], (8, 128))
    q_all, f_all, pool, tables, counts = exchange(
        queries.reshape(ROWS, QUERY_HEADS * HEAD_WIDTH),
        fresh_key_values.reshape(ROWS, 2 * KEY_VALUE_HEADS * HEAD_WIDTH),
        key_value_pages.reshape(PAGES * PAGE_TOKENS, 2 * KEY_VALUE_HEADS * HEAD_WIDTH),
        table,
        count,
    )
    head_sinks = lax.dynamic_slice_in_dim(sinks, head_of(y, x) * GROUP, GROUP)
    sink_rows = jnp.broadcast_to(jnp.repeat(head_sinks, ROWS)[None, :], (8, COLS))
    o, lse = score(
        tables, counts, sink_rows, q_all, f_all,
        pool.reshape(2 * N_EP * PAGES, PAGE_TOKENS, 2 * HEAD_WIDTH),
    )
    attention = merge(o, lse).reshape(queries.shape)

    projected = jnp.dot(arrived, gate_up[0], preferred_element_type=F32)
    gate, upper = projected[:, :HID], projected[:, HID:]
    active = ((upper + 1.0) * gate * jax.nn.sigmoid(1.702 * gate)).astype(BF16)
    result = jnp.dot(active, down_proj[0], preferred_element_type=F32).astype(BF16)
    returned = lax.all_to_all(result, ("seq", "ep"), split_axis=0, concat_axis=0, tiled=True)
    high = weights.astype(BF16)
    low = (weights - high.astype(F32)).astype(BF16)
    mixture = (
        jnp.dot(high, returned, preferred_element_type=F32)
        + jnp.dot(low, returned, preferred_element_type=F32)
    ).astype(BF16).reshape(hidden.shape)
    return (attention, mixture)


def solution(mesh):
    return jax.shard_map(
        per_device,
        mesh=mesh,
        in_specs=(
            P("seq", "ep", None, None),
            P("seq", "ep", None, None),
            P("seq", "ep", None, None),
            P("seq", None, None),
            P("seq", None, None),
            P(None, "ep"),
            P(),
            P("seq", "ep", None, None),
            P(),
            P("seq", "ep", None, None),
            P("seq", "ep", None, None),
            P(("seq", "ep"), None, None),
            P(("seq", "ep"), None, None),
        ),
        out_specs=(P("seq", "ep", None, None), P("seq", "ep", None, None)),
        check_vma=False,
    )
```

```python
import functools

import jax
import jax.numpy as jnp
from jax import lax
from jax.experimental import pallas as pl
from jax.experimental.pallas import tpu as pltpu
from jax.sharding import PartitionSpec as P

D = 2880
QUERY_HEADS = 64
KEY_VALUE_HEADS = 8
GROUP = QUERY_HEADS // KEY_VALUE_HEADS
HEAD_WIDTH = 64
TOPK = 4
HID = 1440
SCORED_STEPS = 4
PAGE_TOKENS = 16
NPS = 256
PAGES = 24
PROMPTS = 8
N_SEQ = 4
N_EP = 32
ROWS = PROMPTS * SCORED_STEPS
HEAD_COLUMNS = GROUP * HEAD_WIDTH
NEGATIVE = -1e30
FLOOR = -1e29
EPSILON = 1e-05
MESH = pl.DeviceIdType.MESH
F32 = jnp.float32
BF16 = jnp.bfloat16
HIGHEST = lax.Precision.HIGHEST


def place():
    y = lax.axis_index("seq")
    ep = lax.axis_index("ep")
    return y, lax.div(ep, 8), lax.rem(lax.div(ep, 2), 4), lax.rem(ep, 2)


def device(y, z, x, c):
    return (y, z * 8 + x * 2 + c)


def head_of(y, x):
    return lax.div(y, 2) * 4 + x


def nt(a, b, precision=None):
    return lax.dot_general(
        a, b, (((1,), (1,)), ((), ())), preferred_element_type=F32, precision=precision
    )


def nn(a, b, precision=None):
    return lax.dot_general(
        a, b, (((1,), (0,)), ((), ())), preferred_element_type=F32, precision=precision
    )


def iota(shape, axis):
    return lax.broadcasted_iota(jnp.int32, shape, axis)


def exchange_kernel(
    q_ref, f_ref, page_ref, table_ref, count_ref,
    q_all, f_all, pool, tables, counts,
    relay, f_relay,
    q_send, q_recv, f_send, f_recv, a_send, a_recv, z_send, z_recv, c_send, c_recv,
    i_send, i_recv, local,
):
    y, z, x, c = place()
    mate = 3 - y

    def at(dy, dx):
        return device(lax.rem(y + dy, 4), z, lax.rem(x + dx, 4), c)

    plane = [(dy, dx) for dy in range(4) for dx in range(4) if (dy, dx) != (0, 0)]
    up = device(y, lax.rem(z + 1, 4), x, c)
    down = device(y, lax.rem(z + 3, 4), x, c)
    twin = device(y, z, x, 1 - c)

    barrier = pltpu.get_barrier_semaphore()
    for peer in [at(dy, dx) for dy, dx in plane] + [up, down, twin]:
        pl.semaphore_signal(barrier, inc=1, device_id=peer, device_id_type=MESH)

    for h in range(KEY_VALUE_HEADS):
        low, high = h * HEAD_WIDTH, (h + 1) * HEAD_WIDTH
        split = KEY_VALUE_HEADS * HEAD_WIDTH
        rows = jnp.concatenate(
            [page_ref[:, low:high], page_ref[:, split + low : split + high]], axis=1
        )
        relay[h] = rows.reshape(PAGES, PAGE_TOKENS, 2 * HEAD_WIDTH)
        f_relay[h] = jnp.concatenate(
            [f_ref[:, low:high], f_ref[:, split + low : split + high]], axis=1
        )
    pl.semaphore_wait(barrier, len(plane) + 3)

    def spot(segment_slot, zz, xx, cc):
        return pool.at[segment_slot, pl.ds((zz * 8 + xx * 2 + cc) * PAGES, PAGES)]

    order = [(0, 0), (0, 1), (0, 3), (1, 0), (1, 1), (1, 3), (0, 2), (1, 2)]
    first = []
    for n, (p, dx) in enumerate(order):
        yy = y if p == 0 else mate
        xx = lax.rem(x + dx, 4)
        target = spot(lax.div(y, 2), z, x, c)
        source = relay.at[head_of(yy, xx)]
        if (p, dx) == (0, 0):
            copy = pltpu.make_async_copy(source, target, local.at[0])
        else:
            copy = pltpu.make_async_remote_copy(
                source, target, a_send.at[n], a_recv.at[n],
                device_id=device(yy, z, xx, c), device_id_type=MESH,
            )
        copy.start()
        first.append(copy)

    small = []
    mine = pltpu.make_async_copy(table_ref, tables.at[lax.div(y, 2)], local.at[1])
    mine.start()
    small.append(mine)
    mine = pltpu.make_async_copy(count_ref, counts.at[x], local.at[2])
    mine.start()
    small.append(mine)
    other = pltpu.make_async_remote_copy(
        table_ref, tables.at[lax.div(y, 2)], i_send.at[0], i_recv.at[0],
        device_id=device(mate, z, x, c), device_id_type=MESH,
    )
    other.start()
    small.append(other)
    for dx in range(1, 4):
        other = pltpu.make_async_remote_copy(
            count_ref, counts.at[x], i_send.at[dx], i_recv.at[dx],
            device_id=at(0, dx), device_id_type=MESH,
        )
        other.start()
        small.append(other)

    for dy in range(4):
        for dx in range(4):
            n = dy * 4 + dx
            h = head_of(lax.rem(y + dy, 4), lax.rem(x + dx, 4))
            q_source = q_ref.at[:, pl.ds(pl.multiple_of(h * HEAD_COLUMNS, HEAD_COLUMNS), HEAD_COLUMNS)]
            f_source = f_relay.at[h]
            slot = x * 4 + y
            if n == 0:
                copies = [
                    pltpu.make_async_copy(q_source, q_all.at[slot], local.at[3]),
                    pltpu.make_async_copy(f_source, f_all.at[slot], local.at[4]),
                ]
            else:
                copies = [
                    pltpu.make_async_remote_copy(
                        q_source, q_all.at[slot], q_send.at[n], q_recv.at[n],
                        device_id=at(dy, dx), device_id_type=MESH,
                    ),
                    pltpu.make_async_remote_copy(
                        f_source, f_all.at[slot], f_send.at[n], f_recv.at[n],
                        device_id=at(dy, dx), device_id_type=MESH,
                    ),
                ]
            for copy in copies:
                copy.start()
            small.extend(copies)

    def chunk(n):
        p, dx = order[n]
        yy = y if p == 0 else mate
        return lax.div(yy, 2), lax.rem(x - dx + 4, 4)

    def pass_on(n, zz, way, peer):
        segment_slot, xx = chunk(n)
        block = spot(segment_slot, zz, xx, c)
        sends, recvs = (c_send, c_recv) if way >= 3 else (z_send, z_recv)
        number = (way - 3 if way >= 3 else way) * 8 + n
        copy = pltpu.make_async_remote_copy(
            block, block, sends.at[number], recvs.at[number],
            device_id=peer, device_id_type=MESH,
        )
        copy.start()
        return copy

    upward, downward, further, across = [], [], [], []
    for n in range(8):
        if n == 0:
            first[n].wait()
        else:
            first[n].wait_recv()
        upward.append(pass_on(n, z, 0, up))
        downward.append(pass_on(n, z, 1, down))
        across.append(pass_on(n, z, 3, twin))
    for n in range(8):
        upward[n].wait_recv()
        if n % 2 == 0:
            further.append(pass_on(n, lax.rem(z + 3, 4), 2, up))
        across.append(pass_on(n, lax.rem(z + 3, 4), 4, twin))
        downward[n].wait_recv()
        if n % 2 == 1:
            further.append(pass_on(n, lax.rem(z + 1, 4), 2, down))
        across.append(pass_on(n, lax.rem(z + 1, 4), 5, twin))
    for n in range(8):
        further[n].wait_recv()
        across.append(pass_on(n, lax.rem(z + 2, 4), 6, twin))
    for copy in across:
        copy.wait()
    for copy in first[1:] + upward + downward + further:
        copy.wait_send()
    for copy in small:
        copy.wait()


def exchange(queries, fresh, pages, table, count):
    vmem = pl.BlockSpec(memory_space=pltpu.VMEM)
    anywhere = pl.BlockSpec(memory_space=pl.ANY)
    dma = pltpu.SemaphoreType.DMA
    return pl.pallas_call(
        exchange_kernel,
        out_shape=(
            jax.ShapeDtypeStruct((16, ROWS, HEAD_COLUMNS), BF16),
            jax.ShapeDtypeStruct((16, ROWS, 2 * HEAD_WIDTH), BF16),
            jax.ShapeDtypeStruct((2, N_EP * PAGES, PAGE_TOKENS, 2 * HEAD_WIDTH), BF16),
            jax.ShapeDtypeStruct((2, 8, 128), jnp.int32),
            jax.ShapeDtypeStruct((4, 8, 128), jnp.int32),
        ),
        in_specs=[vmem] * 5,
        out_specs=(anywhere,) * 5,
        scratch_shapes=[
            pltpu.VMEM((KEY_VALUE_HEADS, PAGES, PAGE_TOKENS, 2 * HEAD_WIDTH), BF16),
            pltpu.VMEM((KEY_VALUE_HEADS, ROWS, 2 * HEAD_WIDTH), BF16),
            dma((16,)), dma((16,)), dma((16,)), dma((16,)), dma((8,)), dma((8,)),
            dma((24,)), dma((24,)), dma((32,)), dma((32,)), dma((4,)), dma((4,)), dma((5,)),
        ],
        compiler_params=pltpu.CompilerParams(
            collective_id=1, has_side_effects=True, vmem_limit_bytes=16 << 20
        ),
        name="exchange",
    )(queries, fresh, pages, table, count)


BK = 1024
GK = 2048
KEYS = 2 * NPS * PAGE_TOKENS
UNITS = 4
CHUNKS = 4
COLS = 256
VROWS = 80


def values_of(rows):
    pick = (iota((VROWS, 128), 0) + HEAD_WIDTH == iota((VROWS, 128), 1)).astype(BF16)
    moved = nt(pick, rows)
    return jnp.where(iota(moved.shape, 0) >= HEAD_WIDTH, 1.0, moved).astype(BF16)


def score_kernel(
    tables, counts, sinks, q_all, f_all, pool, o_ref, lse_ref,
    kv, vt, qs, limit_ref, m_ref, acc, sorted_out, s0, s1, lengths,
):
    y = lax.axis_index("seq")
    outer_pair = jnp.logical_or(y == 0, y == 3)
    sink_row = sinks[0:1, :]
    i0 = iota((128, 128), 0)
    i1 = iota((128, 128), 1)
    lane_row = lax.rem(iota((128, COLS), 1), ROWS).astype(F32)

    def ordering(e):
        c = counts[e][0:1, :].astype(F32)
        n_row = jnp.where(
            outer_pair,
            jnp.minimum(c, 256.0) + jnp.maximum(c - 768.0, 0.0),
            jnp.clip(c - 256.0, 0.0, 512.0),
        )
        n_col = jnp.sum(jnp.where(i0 == i1, n_row, 0.0), axis=1, keepdims=True)
        behind = jnp.logical_or(n_row > n_col, jnp.logical_and(n_col == n_row, i1 < i0))
        pos_col = jnp.sum(jnp.where(behind, 1.0, 0.0), axis=1, keepdims=True)
        return n_row, n_col, pos_col

    for e in range(UNITS):
        n_row, n_col, pos_col = ordering(e)
        ahead = jnp.logical_or(n_col > n_row, jnp.logical_and(n_col == n_row, i0 < i1))
        pos_row = jnp.sum(jnp.where(ahead, 1.0, 0.0), axis=0, keepdims=True)
        perm = (pos_row == i0.astype(F32)).astype(BF16)
        q_sorted = nn(perm, q_all[e * 4 : e * 4 + 4].reshape(128, HEAD_COLUMNS)) * 0.125
        q_sorted = q_sorted.astype(BF16)
        f_sorted = nn(perm, f_all[e * 4 : e * 4 + 4].reshape(128, 128)).astype(BF16)
        none = jnp.zeros((ROWS, HEAD_WIDTH), BF16)
        for ch in range(CHUNKS):
            u = e * CHUNKS + ch
            for g in range(GROUP):
                piece = q_sorted[ch * ROWS : (ch + 1) * ROWS, g * HEAD_WIDTH : (g + 1) * HEAD_WIDTH]
                qs[u, g * ROWS : (g + 1) * ROWS, :] = jnp.concatenate([piece, none], axis=1)
            member = pos_col == lane_row + float(ch * ROWS)
            limit = jnp.sum(jnp.where(member, n_col, 0.0), axis=0, keepdims=True) * PAGE_TOKENS
            limit_ref[u] = jnp.broadcast_to(limit, (8, COLS))
            lengths[u] = jnp.max(limit).astype(jnp.int32)
            rows = f_sorted[ch * ROWS : (ch + 1) * ROWS, :]
            s = nt(rows, qs[u])
            ki = iota((ROWS, COLS), 0)
            ri = lax.rem(iota((ROWS, COLS), 1), ROWS)
            seen = jnp.logical_and(
                lax.div(ki, SCORED_STEPS) == lax.div(ri, SCORED_STEPS), ki <= ri
            )
            s = jnp.where(seen, s, NEGATIVE)
            m0 = jnp.maximum(jnp.max(s, axis=0, keepdims=True), sink_row)
            p = jnp.exp(s - m0).astype(BF16)
            start = nn(values_of(rows), p)
            start = start + jnp.where(
                iota((VROWS, COLS), 0) >= HEAD_WIDTH, jnp.exp(sink_row - m0), 0.0
            )
            m_ref[u] = jnp.broadcast_to(jnp.where(outer_pair, m0, FLOOR), (8, COLS))
            acc[u] = jnp.where(outer_pair, start, 0.0)

    def unit(e, carry):
        def gather(kb, carry):
            p0 = kb * (GK // PAGE_TOKENS)
            ss = lax.div(p0, NPS)
            row = e * 2 + lax.div(lax.rem(p0, NPS), 128)
            rows = [
                pool[tables[ss, row, i] + ss * (N_EP * PAGES)] for i in range(GK // PAGE_TOKENS)
            ]
            for i in range(GK // BK):
                part = rows[i * (BK // PAGE_TOKENS) : (i + 1) * (BK // PAGE_TOKENS)]
                found = jnp.concatenate(part, axis=0)
                kv[pl.ds(pl.multiple_of(kb * GK + i * BK, BK), BK), :] = found
                vt[kb * (GK // BK) + i] = values_of(found)
            return carry

        lax.fori_loop(0, lax.div(lengths[e * CHUNKS] + (GK - 1), GK), gather, 0)

        key = iota((BK, COLS), 0).astype(F32)

        def produce(store, u, kb):
            keys = kv[pl.ds(pl.multiple_of(kb * BK, BK), BK), :]
            s = nt(keys, qs[u])
            limit = limit_ref[u][0:1, :] - (kb * BK).astype(F32)
            s = jnp.where(key < limit, s, NEGATIVE)
            store[...] = s
            return jnp.max(s, axis=0, keepdims=True)

        def absorb(store, u, kb, top):
            before = m_ref[u][0:1, :]
            after = jnp.maximum(before, top)
            p = jnp.exp(store[...] - after).astype(BF16)
            acc[u] = acc[u] * jnp.exp(before - after) + nn(vt[kb], p)
            m_ref[u] = jnp.broadcast_to(after, (8, COLS))

        def chunk(ch, top):
            u = e * CHUNKS + ch
            count = lax.div(lengths[u] + (BK - 1), BK)
            after_u = e * CHUNKS + jnp.minimum(ch + 1, CHUNKS - 1)

            def pair(i, top):
                last = 2 * i + 2 >= count
                next_top = produce(s1, u, 2 * i + 1)
                absorb(s0, u, 2 * i, top)
                top = produce(s0, jnp.where(last, after_u, u), jnp.where(last, 0, 2 * i + 2))
                absorb(s1, u, 2 * i + 1, next_top)
                return top

            top = lax.fori_loop(0, lax.div(count, 2), pair, top)

            def odd(top):
                absorb(s0, u, count - 1, top)
                return produce(s0, after_u, jnp.int32(0))

            return lax.cond(lax.rem(count, 2) == 1, odd, lambda top: top, top)

        used = sum([(lengths[e * CHUNKS + ch] > 0).astype(jnp.int32) for ch in range(CHUNKS)])

        @pl.when(used > 0)
        def _():
            top = produce(s0, e * CHUNKS, jnp.int32(0))
            lax.fori_loop(0, used, chunk, top)

        return carry

    lax.fori_loop(0, UNITS, unit, 0)

    for e in range(UNITS):
        _, _, pos_col = ordering(e)
        perm_t = (pos_col == i1.astype(F32)).astype(BF16)
        lse = jnp.zeros((8, 128), F32)
        for ch in range(CHUNKS):
            u = e * CHUNKS + ch
            total = jnp.maximum(acc[u][HEAD_WIDTH : HEAD_WIDTH + 1, :], 1e-30)
            out = acc[u][0:HEAD_WIDTH, :] / total
            padded = jnp.concatenate([out, jnp.zeros_like(out)], axis=0)
            turned = padded.T.astype(BF16)
            for g in range(GROUP):
                sorted_out[e, ch * ROWS : (ch + 1) * ROWS, g * HEAD_WIDTH : (g + 1) * HEAD_WIDTH] = (
                    turned[g * ROWS : (g + 1) * ROWS, 0:HEAD_WIDTH]
                )
            row = m_ref[u][0:1, :] + jnp.log(total)
            mine = lax.div(iota((8, COLS), 1), ROWS) == iota((8, COLS), 0)
            member = (pos_col == lane_row + float(ch * ROWS)).astype(F32)
            lse = lse + nt(jnp.where(mine, row, 0.0), member, HIGHEST)
        lse_ref[e] = lse
        o_ref[e] = nn(perm_t, sorted_out[e]).astype(BF16)


def score(tables, counts, sinks, q_all, f_all, pool):
    vmem = pl.BlockSpec(memory_space=pltpu.VMEM)
    return pl.pallas_call(
        score_kernel,
        out_shape=(
            jax.ShapeDtypeStruct((UNITS, 128, HEAD_COLUMNS), BF16),
            jax.ShapeDtypeStruct((UNITS, 8, 128), F32),
        ),
        in_specs=[pl.BlockSpec(memory_space=pltpu.SMEM)] + [vmem] * 5,
        out_specs=(vmem, vmem),
        scratch_shapes=[
            pltpu.VMEM((KEYS, 128), BF16),
            pltpu.VMEM((KEYS // BK, VROWS, BK), BF16),
            pltpu.VMEM((UNITS * CHUNKS, COLS, 128), BF16),
            pltpu.VMEM((UNITS * CHUNKS, 8, COLS), F32),
            pltpu.VMEM((UNITS * CHUNKS, 8, COLS), F32),
            pltpu.VMEM((UNITS * CHUNKS, VROWS, COLS), F32),
            pltpu.VMEM((UNITS, 128, HEAD_COLUMNS), BF16),
            pltpu.VMEM((BK, COLS), F32),
            pltpu.VMEM((BK, COLS), F32),
            pltpu.SMEM((UNITS * CHUNKS,), jnp.int32),
        ],
        compiler_params=pltpu.CompilerParams(vmem_limit_bytes=40 << 20),
        cost_estimate=pl.CostEstimate(
            flops=25_000_000_000, bytes_accessed=8_000_000, transcendentals=20_000_000
        ),
        name="score",
    )(tables, counts, sinks, q_all, f_all, pool)


def merge_kernel(o_ref, lse_ref, out_ref, o_all, lse_all, o_send, o_recv, l_send, l_recv, local):
    y, z, x, c = place()

    def at(dy, dx):
        return device(lax.rem(y + dy, 4), z, lax.rem(x + dx, 4), c)

    plane = [(dy, dx) for dy in range(4) for dx in range(4) if (dy, dx) != (0, 0)]
    barrier = pltpu.get_barrier_semaphore()
    for dy, dx in plane:
        pl.semaphore_signal(barrier, inc=1, device_id=at(dy, dx), device_id_type=MESH)
    pl.semaphore_wait(barrier, len(plane))
    inner_pair = jnp.logical_or(y == 1, y == 2).astype(jnp.int32)
    slot = inner_pair * 8 + head_of(y, x)
    copies = []
    for dy in range(4):
        for dx in range(4):
            n = dy * 4 + dx
            q = lax.rem(y + dy, 4)
            e = lax.rem(x + dx, 4)
            o_source = o_ref.at[e, pl.ds(pl.multiple_of(q * ROWS, ROWS), ROWS)]
            if n == 0:
                pair = [
                    pltpu.make_async_copy(o_source, o_all.at[slot], local.at[0]),
                    pltpu.make_async_copy(lse_ref.at[e], lse_all.at[slot], local.at[1]),
                ]
            else:
                pair = [
                    pltpu.make_async_remote_copy(
                        o_source, o_all.at[slot], o_send.at[n], o_recv.at[n],
                        device_id=at(dy, dx), device_id_type=MESH,
                    ),
                    pltpu.make_async_remote_copy(
                        lse_ref.at[e], lse_all.at[slot], l_send.at[n], l_recv.at[n],
                        device_id=at(dy, dx), device_id_type=MESH,
                    ),
                ]
            for copy in pair:
                copy.start()
            copies.extend(pair)
    for copy in copies:
        copy.wait()
    mine = (iota((ROWS, 128), 1) == iota((ROWS, 128), 0) + y * ROWS).astype(F32)
    logs = nt(mine, lse_all[...].reshape(128, 128), HIGHEST)
    log0, log1 = logs[:, :64], logs[:, 64:]
    top = jnp.maximum(log0, log1)
    w0, w1 = jnp.exp(log0 - top), jnp.exp(log1 - top)
    share0, share1 = w0 / (w0 + w1), w1 / (w0 + w1)
    parts = []
    for share in (share0, share1):
        high = share.astype(BF16)
        parts.append((high, (share - high.astype(F32)).astype(BF16)))
    for h in range(KEY_VALUE_HEADS):
        shape = (64, HEAD_COLUMNS)
        spread = (iota(shape, 0) == lax.div(iota(shape, 1), HEAD_WIDTH) + h * GROUP).astype(BF16)
        wide = [nn(high, spread) + nn(low, spread) for high, low in parts]
        result = wide[0] * o_all[h].astype(F32) + wide[1] * o_all[8 + h].astype(F32)
        out_ref[:, h * HEAD_COLUMNS : (h + 1) * HEAD_COLUMNS] = result.astype(BF16)


def merge(o, lse):
    vmem = pl.BlockSpec(memory_space=pltpu.VMEM)
    dma = pltpu.SemaphoreType.DMA
    return pl.pallas_call(
        merge_kernel,
        out_shape=jax.ShapeDtypeStruct((ROWS, QUERY_HEADS * HEAD_WIDTH), BF16),
        in_specs=[vmem, vmem],
        out_specs=vmem,
        scratch_shapes=[
            pltpu.VMEM((16, ROWS, HEAD_COLUMNS), BF16),
            pltpu.VMEM((16, 8, 128), F32),
            dma((16,)), dma((16,)), dma((16,)), dma((16,)), dma((2,)),
        ],
        compiler_params=pltpu.CompilerParams(
            collective_id=2, has_side_effects=True, vmem_limit_bytes=16 << 20
        ),
        name="merge",
    )(o, lse)


def per_device(
    queries, fresh_key_values, key_value_pages, page_owner, page_slot, page_count, sinks,
    hidden, norm_gain, expert_ids, gate_prob, gate_up, down_proj,
):
    y, z, x, c = place()

    flat_hidden = hidden.reshape(ROWS, D).astype(F32)
    meansq = jnp.mean(flat_hidden * flat_hidden, axis=-1, keepdims=True)
    normed = (flat_hidden * lax.rsqrt(meansq + EPSILON) * norm_gain).astype(BF16)
    chosen = expert_ids.reshape(ROWS * TOPK)
    number = jnp.arange(ROWS * TOPK, dtype=jnp.int32)
    same = jnp.logical_and(chosen[:, None] == chosen[None, :], number[None, :] < number[:, None])
    rank = jnp.sum(same.astype(jnp.int32), axis=1)
    slots = (chosen * 2 + rank).reshape(ROWS, TOPK)
    hit = slots[None, :, :] == jnp.arange(256, dtype=jnp.int32)[:, None, None]
    spread = jnp.any(hit, axis=-1).astype(BF16)
    buffer = jnp.dot(spread, normed, preferred_element_type=F32).astype(BF16)
    weights = jnp.sum(
        jnp.where(
            slots[:, :, None] == jnp.arange(256, dtype=jnp.int32)[None, None, :],
            gate_prob.reshape(ROWS, TOPK, 1),
            0.0,
        ),
        axis=1,
    )
    arrived = lax.all_to_all(buffer, ("seq", "ep"), split_axis=0, concat_axis=0, tiled=True)

    index = (page_owner * PAGES + page_slot).reshape(4, 4, 2, NPS)
    index = lax.dynamic_index_in_dim(index, z, 0, keepdims=False)
    index = lax.dynamic_index_in_dim(index, c, 1, keepdims=False)
    table = index.reshape(8, 128)
    count = jnp.broadcast_to(jnp.repeat(page_count.reshape(32), 4)[None, :], (8, 128))
    q_all, f_all, pool, tables, counts = exchange(
        queries.reshape(ROWS, QUERY_HEADS * HEAD_WIDTH),
        fresh_key_values.reshape(ROWS, 2 * KEY_VALUE_HEADS * HEAD_WIDTH),
        key_value_pages.reshape(PAGES * PAGE_TOKENS, 2 * KEY_VALUE_HEADS * HEAD_WIDTH),
        table,
        count,
    )
    head_sinks = lax.dynamic_slice_in_dim(sinks, head_of(y, x) * GROUP, GROUP)
    sink_rows = jnp.broadcast_to(jnp.repeat(head_sinks, ROWS)[None, :], (8, COLS))
    o, lse = score(
        tables, counts, sink_rows, q_all, f_all,
        pool.reshape(2 * N_EP * PAGES, PAGE_TOKENS, 2 * HEAD_WIDTH),
    )
    attention = merge(o, lse).reshape(queries.shape)

    projected = jnp.dot(arrived, gate_up[0], preferred_element_type=F32)
    gate, upper = projected[:, :HID], projected[:, HID:]
    active = ((upper + 1.0) * gate * jax.nn.sigmoid(1.702 * gate)).astype(BF16)
    result = jnp.dot(active, down_proj[0], preferred_element_type=F32).astype(BF16)
    returned = lax.all_to_all(result, ("seq", "ep"), split_axis=0, concat_axis=0, tiled=True)
    high = weights.astype(BF16)
    low = (weights - high.astype(F32)).astype(BF16)
    mixture = (
        jnp.dot(high, returned, preferred_element_type=F32)
        + jnp.dot(low, returned, preferred_element_type=F32)
    ).astype(BF16).reshape(hidden.shape)
    return (attention, mixture)


def solution(mesh):
    return jax.shard_map(
        per_device,
        mesh=mesh,
        in_specs=(
            P("seq", "ep", None, None),
            P("seq", "ep", None, None),
            P("seq", "ep", None, None),
            P("seq", None, None),
            P("seq", None, None),
            P(None, "ep"),
            P(),
            P("seq", "ep", None, None),
            P(),
            P("seq", "ep", None, None),
            P("seq", "ep", None, None),
            P(("seq", "ep"), None, None),
            P(("seq", "ep"), None, None),
        ),
        out_specs=(P("seq", "ep", None, None), P("seq", "ep", None, None)),
        check_vma=False,
    )
```

```python
import functools

import jax
import jax.numpy as jnp
from jax import lax
from jax.experimental import pallas as pl
from jax.experimental.pallas import tpu as pltpu
from jax.sharding import PartitionSpec as P

D = 2880
QUERY_HEADS = 64
KEY_VALUE_HEADS = 8
GROUP = QUERY_HEADS // KEY_VALUE_HEADS
HEAD_WIDTH = 64
TOPK = 4
HID = 1440
SCORED_STEPS = 4
PAGE_TOKENS = 16
NPS = 256
PAGES = 24
PROMPTS = 8
N_SEQ = 4
N_EP = 32
ROWS = PROMPTS * SCORED_STEPS
HEAD_COLUMNS = GROUP * HEAD_WIDTH
NEGATIVE = -1e30
FLOOR = -1e29
EPSILON = 1e-05
MESH = pl.DeviceIdType.MESH
F32 = jnp.float32
BF16 = jnp.bfloat16
HIGHEST = lax.Precision.HIGHEST


def place():
    y = lax.axis_index("seq")
    ep = lax.axis_index("ep")
    return y, lax.div(ep, 8), lax.rem(lax.div(ep, 2), 4), lax.rem(ep, 2)


def device(y, z, x, c):
    return (y, z * 8 + x * 2 + c)


def head_of(y, x):
    return lax.div(y, 2) * 4 + x


def nt(a, b, precision=None):
    return lax.dot_general(
        a, b, (((1,), (1,)), ((), ())), preferred_element_type=F32, precision=precision
    )


def nn(a, b, precision=None):
    return lax.dot_general(
        a, b, (((1,), (0,)), ((), ())), preferred_element_type=F32, precision=precision
    )


def iota(shape, axis):
    return lax.broadcasted_iota(jnp.int32, shape, axis)


def exchange_kernel(
    q_ref, f_ref, page_ref, table_ref, count_ref, hidden_ref, gain_ref, spread_ref, up_ref, down_ref,
    q_all, f_all, pool, tables, counts, expert_out,
    relay, f_relay, rows_out, rows_mid, rows_sorted, rows_in, up_w, down_w, projected, active,
    q_send, q_recv, f_send, f_recv, a_send, a_recv, z_send, z_recv, c_send, c_recv,
    i_send, i_recv, d_send, d_recv, e_send, e_recv, local, w_sem,
):
    y, z, x, c = place()
    mate = 3 - y

    def at(dy, dx):
        return device(lax.rem(y + dy, 4), z, lax.rem(x + dx, 4), c)

    plane = [(dy, dx) for dy in range(4) for dx in range(4) if (dy, dx) != (0, 0)]
    up = device(y, lax.rem(z + 1, 4), x, c)
    down = device(y, lax.rem(z + 3, 4), x, c)
    twin = device(y, z, x, 1 - c)

    def beside(dy, dz):
        return device(lax.rem(y + dy, 4), lax.rem(z + dz, 4), x, c)

    def around(dx, dc):
        return device(y, z, lax.rem(x + dx, 4), lax.rem(c + dc, 2))

    peers = [at(dy, dx) for dy, dx in plane]
    peers += [beside(dy, dz) for dy in range(4) for dz in range(1, 4)]
    peers += [around(dx, 1) for dx in range(4)]
    barrier = pltpu.get_barrier_semaphore()
    for peer in peers:
        pl.semaphore_signal(barrier, inc=1, device_id=peer, device_id_type=MESH)

    weights = []
    for n in range(4):
        part = pl.ds(n * (D // 4), D // 4)
        weights.append(pltpu.make_async_copy(up_ref.at[0, part], up_w.at[part], w_sem.at[n]))
    for n in range(2):
        part = pl.ds(n * (HID // 2), HID // 2)
        weights.append(pltpu.make_async_copy(down_ref.at[0, part], down_w.at[part], w_sem.at[4 + n]))
    for copy in weights:
        copy.start()

    for h in range(KEY_VALUE_HEADS):
        low, high = h * HEAD_WIDTH, (h + 1) * HEAD_WIDTH
        split = KEY_VALUE_HEADS * HEAD_WIDTH
        rows = jnp.concatenate(
            [page_ref[:, low:high], page_ref[:, split + low : split + high]], axis=1
        )
        relay[h] = rows.reshape(PAGES, PAGE_TOKENS, 2 * HEAD_WIDTH)
        f_relay[h] = jnp.concatenate(
            [f_ref[:, low:high], f_ref[:, split + low : split + high]], axis=1
        )
    pl.semaphore_wait(barrier, len(peers))

    def spot(segment_slot, zz, xx, cc):
        return pool.at[segment_slot, pl.ds((zz * 8 + xx * 2 + cc) * PAGES, PAGES)]

    order = [(0, 0), (0, 1), (0, 3), (1, 0), (1, 1), (1, 3), (0, 2), (1, 2)]
    first = []
    for n, (p, dx) in enumerate(order):
        yy = y if p == 0 else mate
        xx = lax.rem(x + dx, 4)
        target = spot(lax.div(y, 2), z, x, c)
        source = relay.at[head_of(yy, xx)]
        if (p, dx) == (0, 0):
            copy = pltpu.make_async_copy(source, target, local.at[0])
        else:
            copy = pltpu.make_async_remote_copy(
                source, target, a_send.at[n], a_recv.at[n],
                device_id=device(yy, z, xx, c), device_id_type=MESH,
            )
        copy.start()
        first.append(copy)

    small = []
    mine = pltpu.make_async_copy(table_ref, tables.at[lax.div(y, 2)], local.at[1])
    mine.start()
    small.append(mine)
    mine = pltpu.make_async_copy(count_ref, counts.at[x], local.at[2])
    mine.start()
    small.append(mine)
    other = pltpu.make_async_remote_copy(
        table_ref, tables.at[lax.div(y, 2)], i_send.at[0], i_recv.at[0],
        device_id=device(mate, z, x, c), device_id_type=MESH,
    )
    other.start()
    small.append(other)
    for dx in range(1, 4):
        other = pltpu.make_async_remote_copy(
            count_ref, counts.at[x], i_send.at[dx], i_recv.at[dx],
            device_id=at(0, dx), device_id_type=MESH,
        )
        other.start()
        small.append(other)

    h32 = hidden_ref[...].astype(F32)
    scale = lax.rsqrt(jnp.mean(h32 * h32, axis=-1, keepdims=True) + EPSILON)
    normed = (h32 * scale * gain_ref[...]).astype(BF16)
    rows_out[...] = nn(spread_ref[...], normed).astype(BF16).reshape(16, 16, D)
    routed = []
    for dy in range(4):
        for dz in range(4):
            n = dy * 4 + dz
            source = rows_out.at[lax.rem(y + dy, 4) * 4 + lax.rem(z + dz, 4)]
            target = rows_mid.at[y * 4 + z]
            if n == 0:
                copy = pltpu.make_async_copy(source, target, local.at[5])
            else:
                copy = pltpu.make_async_remote_copy(
                    source, target, d_send.at[n], d_recv.at[n],
                    device_id=beside(dy, dz), device_id_type=MESH,
                )
            copy.start()
            routed.append(copy)

    for dy in range(4):
        for dx in range(4):
            n = dy * 4 + dx
            h = head_of(lax.rem(y + dy, 4), lax.rem(x + dx, 4))
            q_source = q_ref.at[:, pl.ds(pl.multiple_of(h * HEAD_COLUMNS, HEAD_COLUMNS), HEAD_COLUMNS)]
            f_source = f_relay.at[h]
            slot = x * 4 + y
            if n == 0:
                copies = [
                    pltpu.make_async_copy(q_source, q_all.at[slot], local.at[3]),
                    pltpu.make_async_copy(f_source, f_all.at[slot], local.at[4]),
                ]
            else:
                copies = [
                    pltpu.make_async_remote_copy(
                        q_source, q_all.at[slot], q_send.at[n], q_recv.at[n],
                        device_id=at(dy, dx), device_id_type=MESH,
                    ),
                    pltpu.make_async_remote_copy(
                        f_source, f_all.at[slot], f_send.at[n], f_recv.at[n],
                        device_id=at(dy, dx), device_id_type=MESH,
                    ),
                ]
            for copy in copies:
                copy.start()
            small.extend(copies)

    def chunk(n):
        p, dx = order[n]
        yy = y if p == 0 else mate
        return lax.div(yy, 2), lax.rem(x - dx + 4, 4)

    def pass_on(n, zz, way, peer):
        segment_slot, xx = chunk(n)
        block = spot(segment_slot, zz, xx, c)
        sends, recvs = (c_send, c_recv) if way >= 3 else (z_send, z_recv)
        number = (way - 3 if way >= 3 else way) * 8 + n
        copy = pltpu.make_async_remote_copy(
            block, block, sends.at[number], recvs.at[number],
            device_id=peer, device_id_type=MESH,
        )
        copy.start()
        return copy

    upward, downward, further, across = [], [], [], []
    for n in range(8):
        if n == 0:
            first[n].wait()
        else:
            first[n].wait_recv()
        upward.append(pass_on(n, z, 0, up))
        downward.append(pass_on(n, z, 1, down))
        across.append(pass_on(n, z, 3, twin))

    for copy in routed:
        copy.wait()
    ri = iota((256, 256), 0)
    ci = iota((256, 256), 1)

    def slot_of(i):
        return lax.div(lax.rem(i, 32), 2) * 16 + lax.div(i, 32) * 2 + lax.rem(i, 2)

    regroup = (slot_of(ri) == ci).astype(BF16)
    rows_sorted[...] = nn(regroup, rows_mid[...].reshape(256, D)).astype(BF16).reshape(8, 32, D)
    delivered = []
    for dx in range(4):
        for dc in range(2):
            n = dx * 2 + dc
            source = rows_sorted.at[lax.rem(x + dx, 4) * 2 + lax.rem(c + dc, 2)]
            target = rows_in.at[x * 2 + c]
            if n == 0:
                copy = pltpu.make_async_copy(source, target, local.at[6])
            else:
                copy = pltpu.make_async_remote_copy(
                    source, target, e_send.at[n], e_recv.at[n],
                    device_id=around(dx, dc), device_id_type=MESH,
                )
            copy.start()
            delivered.append(copy)

    for n in range(8):
        upward[n].wait_recv()
        if n % 2 == 0:
            further.append(pass_on(n, lax.rem(z + 3, 4), 2, up))
        across.append(pass_on(n, lax.rem(z + 3, 4), 4, twin))
        downward[n].wait_recv()
        if n % 2 == 1:
            further.append(pass_on(n, lax.rem(z + 1, 4), 2, down))
        across.append(pass_on(n, lax.rem(z + 1, 4), 5, twin))
    for n in range(8):
        further[n].wait_recv()
        across.append(pass_on(n, lax.rem(z + 2, 4), 6, twin))

    for copy in weights + delivered:
        copy.wait()

    def tiles(work):
        @pl.loop(0, D // TILE)
        def _(j):
            work(pl.ds(pl.multiple_of(j * TILE, TILE), TILE))

        work(pl.ds(D // TILE * TILE, D % TILE))

    def project(part):
        projected[:, part] = nn(rows_in[...].reshape(256, D), up_w[:, part])

    tiles(project)

    @pl.loop(0, 8)
    def _(j):
        part = pl.ds(pl.multiple_of(j * 32, 32), 32)
        wide = projected[part, :]
        gate, upper = wide[:, :HID], wide[:, HID:]
        active[part, :] = ((upper + 1.0) * gate * jax.nn.sigmoid(1.702 * gate)).astype(BF16)

    back = (slot_of(ci) == ri).astype(BF16)
    active[...] = nn(back, active[...]).astype(BF16)

    def finish(part):
        expert_out[:, part] = nn(active[...], down_w[:, part]).astype(BF16)

    tiles(finish)

    for copy in across:
        copy.wait()
    for copy in first[1:] + upward + downward + further:
        copy.wait_send()
    for copy in small:
        copy.wait()


TILE = 384


def exchange(queries, fresh, pages, table, count, hidden, gain, spread, gate_up, down_proj):
    vmem = pl.BlockSpec(memory_space=pltpu.VMEM)
    anywhere = pl.BlockSpec(memory_space=pl.ANY)
    dma = pltpu.SemaphoreType.DMA
    return pl.pallas_call(
        exchange_kernel,
        out_shape=(
            jax.ShapeDtypeStruct((16, ROWS, HEAD_COLUMNS), BF16),
            jax.ShapeDtypeStruct((16, ROWS, 2 * HEAD_WIDTH), BF16),
            jax.ShapeDtypeStruct((2, N_EP * PAGES, PAGE_TOKENS, 2 * HEAD_WIDTH), BF16),
            jax.ShapeDtypeStruct((2, 8, 128), jnp.int32),
            jax.ShapeDtypeStruct((4, 8, 128), jnp.int32),
            jax.ShapeDtypeStruct((256, D), BF16),
        ),
        in_specs=[vmem] * 8 + [anywhere] * 2,
        out_specs=(anywhere,) * 5 + (vmem,),
        scratch_shapes=[
            pltpu.VMEM((KEY_VALUE_HEADS, PAGES, PAGE_TOKENS, 2 * HEAD_WIDTH), BF16),
            pltpu.VMEM((KEY_VALUE_HEADS, ROWS, 2 * HEAD_WIDTH), BF16),
            pltpu.VMEM((16, 16, D), BF16),
            pltpu.VMEM((16, 16, D), BF16),
            pltpu.VMEM((8, 32, D), BF16),
            pltpu.VMEM((8, 32, D), BF16),
            pltpu.VMEM((D, 2 * HID), BF16),
            pltpu.VMEM((HID, D), BF16),
            pltpu.VMEM((256, 2 * HID), F32),
            pltpu.VMEM((256, HID), BF16),
            dma((16,)), dma((16,)), dma((16,)), dma((16,)), dma((8,)), dma((8,)),
            dma((24,)), dma((24,)), dma((32,)), dma((32,)), dma((4,)), dma((4,)),
            dma((16,)), dma((16,)), dma((8,)), dma((8,)), dma((7,)), dma((6,)),
        ],
        compiler_params=pltpu.CompilerParams(
            collective_id=1, has_side_effects=True, vmem_limit_bytes=56 << 20
        ),
        name="exchange",
    )(queries, fresh, pages, table, count, hidden, gain, spread, gate_up, down_proj)


BK = 1024
GK = 2048
KEYS = 2 * NPS * PAGE_TOKENS
UNITS = 4
CHUNKS = 4
COLS = 256
VROWS = 80


def values_of(rows):
    pick = (iota((VROWS, 128), 0) + HEAD_WIDTH == iota((VROWS, 128), 1)).astype(BF16)
    moved = nt(pick, rows)
    return jnp.where(iota(moved.shape, 0) >= HEAD_WIDTH, 1.0, moved).astype(BF16)


def score_kernel(
    tables, counts, sinks, q_all, f_all, pool, o_ref, lse_ref,
    kv, vt, qs, limit_ref, m_ref, acc, sorted_out, s0, s1, lengths,
):
    y = lax.axis_index("seq")
    outer_pair = jnp.logical_or(y == 0, y == 3)
    sink_row = sinks[0:1, :]
    i0 = iota((128, 128), 0)
    i1 = iota((128, 128), 1)
    lane_row = lax.rem(iota((128, COLS), 1), ROWS).astype(F32)

    def ordering(e):
        c = counts[e][0:1, :].astype(F32)
        n_row = jnp.where(
            outer_pair,
            jnp.minimum(c, 256.0) + jnp.maximum(c - 768.0, 0.0),
            jnp.clip(c - 256.0, 0.0, 512.0),
        )
        n_col = jnp.sum(jnp.where(i0 == i1, n_row, 0.0), axis=1, keepdims=True)
        behind = jnp.logical_or(n_row > n_col, jnp.logical_and(n_col == n_row, i1 < i0))
        pos_col = jnp.sum(jnp.where(behind, 1.0, 0.0), axis=1, keepdims=True)
        return n_row, n_col, pos_col

    for e in range(UNITS):
        n_row, n_col, pos_col = ordering(e)
        ahead = jnp.logical_or(n_col > n_row, jnp.logical_and(n_col == n_row, i0 < i1))
        pos_row = jnp.sum(jnp.where(ahead, 1.0, 0.0), axis=0, keepdims=True)
        perm = (pos_row == i0.astype(F32)).astype(BF16)
        q_sorted = nn(perm, q_all[e * 4 : e * 4 + 4].reshape(128, HEAD_COLUMNS)) * 0.125
        q_sorted = q_sorted.astype(BF16)
        f_sorted = nn(perm, f_all[e * 4 : e * 4 + 4].reshape(128, 128)).astype(BF16)
        none = jnp.zeros((ROWS, HEAD_WIDTH), BF16)
        for ch in range(CHUNKS):
            u = e * CHUNKS + ch
            for g in range(GROUP):
                piece = q_sorted[ch * ROWS : (ch + 1) * ROWS, g * HEAD_WIDTH : (g + 1) * HEAD_WIDTH]
                qs[u, g * ROWS : (g + 1) * ROWS, :] = jnp.concatenate([piece, none], axis=1)
            member = pos_col == lane_row + float(ch * ROWS)
            limit = jnp.sum(jnp.where(member, n_col, 0.0), axis=0, keepdims=True) * PAGE_TOKENS
            limit_ref[u] = jnp.broadcast_to(limit, (8, COLS))
            lengths[u] = jnp.max(limit).astype(jnp.int32)
            rows = f_sorted[ch * ROWS : (ch + 1) * ROWS, :]
            s = nt(rows, qs[u])
            ki = iota((ROWS, COLS), 0)
            ri = lax.rem(iota((ROWS, COLS), 1), ROWS)
            seen = jnp.logical_and(
                lax.div(ki, SCORED_STEPS) == lax.div(ri, SCORED_STEPS), ki <= ri
            )
            s = jnp.where(seen, s, NEGATIVE)
            m0 = jnp.maximum(jnp.max(s, axis=0, keepdims=True), sink_row)
            p = jnp.exp(s - m0).astype(BF16)
            start = nn(values_of(rows), p)
            start = start + jnp.where(
                iota((VROWS, COLS), 0) >= HEAD_WIDTH, jnp.exp(sink_row - m0), 0.0
            )
            m_ref[u] = jnp.broadcast_to(jnp.where(outer_pair, m0, FLOOR), (8, COLS))
            acc[u] = jnp.where(outer_pair, start, 0.0)

    def unit(e, carry):
        def gather(kb, carry):
            p0 = kb * (GK // PAGE_TOKENS)
            ss = lax.div(p0, NPS)
            row = e * 2 + lax.div(lax.rem(p0, NPS), 128)
            rows = [
                pool[tables[ss, row, i] + ss * (N_EP * PAGES)] for i in range(GK // PAGE_TOKENS)
            ]
            for i in range(GK // BK):
                part = rows[i * (BK // PAGE_TOKENS) : (i + 1) * (BK // PAGE_TOKENS)]
                found = jnp.concatenate(part, axis=0)
                kv[pl.ds(pl.multiple_of(kb * GK + i * BK, BK), BK), :] = found
                vt[kb * (GK // BK) + i] = values_of(found)
            return carry

        lax.fori_loop(0, lax.div(lengths[e * CHUNKS] + (GK - 1), GK), gather, 0)

        key = iota((BK, COLS), 0).astype(F32)

        def produce(store, u, kb):
            keys = kv[pl.ds(pl.multiple_of(kb * BK, BK), BK), :]
            s = nt(keys, qs[u])
            limit = limit_ref[u][0:1, :] - (kb * BK).astype(F32)
            s = jnp.where(key < limit, s, NEGATIVE)
            store[...] = s
            return jnp.max(s, axis=0, keepdims=True)

        def absorb(store, u, kb, top):
            before = m_ref[u][0:1, :]
            after = jnp.maximum(before, top)
            p = jnp.exp(store[...] - after).astype(BF16)
            acc[u] = acc[u] * jnp.exp(before - after) + nn(vt[kb], p)
            m_ref[u] = jnp.broadcast_to(after, (8, COLS))

        def chunk(ch, top):
            u = e * CHUNKS + ch
            count = lax.div(lengths[u] + (BK - 1), BK)
            after_u = e * CHUNKS + jnp.minimum(ch + 1, CHUNKS - 1)

            def pair(i, top):
                last = 2 * i + 2 >= count
                next_top = produce(s1, u, 2 * i + 1)
                absorb(s0, u, 2 * i, top)
                top = produce(s0, jnp.where(last, after_u, u), jnp.where(last, 0, 2 * i + 2))
                absorb(s1, u, 2 * i + 1, next_top)
                return top

            top = lax.fori_loop(0, lax.div(count, 2), pair, top)

            def odd(top):
                absorb(s0, u, count - 1, top)
                return produce(s0, after_u, jnp.int32(0))

            return lax.cond(lax.rem(count, 2) == 1, odd, lambda top: top, top)

        used = sum([(lengths[e * CHUNKS + ch] > 0).astype(jnp.int32) for ch in range(CHUNKS)])

        @pl.when(used > 0)
        def _():
            top = produce(s0, e * CHUNKS, jnp.int32(0))
            lax.fori_loop(0, used, chunk, top)

        return carry

    lax.fori_loop(0, UNITS, unit, 0)

    for e in range(UNITS):
        _, _, pos_col = ordering(e)
        perm_t = (pos_col == i1.astype(F32)).astype(BF16)
        lse = jnp.zeros((8, 128), F32)
        for ch in range(CHUNKS):
            u = e * CHUNKS + ch
            total = jnp.maximum(acc[u][HEAD_WIDTH : HEAD_WIDTH + 1, :], 1e-30)
            out = acc[u][0:HEAD_WIDTH, :] / total
            padded = jnp.concatenate([out, jnp.zeros_like(out)], axis=0)
            turned = padded.T.astype(BF16)
            for g in range(GROUP):
                sorted_out[e, ch * ROWS : (ch + 1) * ROWS, g * HEAD_WIDTH : (g + 1) * HEAD_WIDTH] = (
                    turned[g * ROWS : (g + 1) * ROWS, 0:HEAD_WIDTH]
                )
            row = m_ref[u][0:1, :] + jnp.log(total)
            mine = lax.div(iota((8, COLS), 1), ROWS) == iota((8, COLS), 0)
            member = (pos_col == lane_row + float(ch * ROWS)).astype(F32)
            lse = lse + nt(jnp.where(mine, row, 0.0), member, HIGHEST)
        lse_ref[e] = lse
        o_ref[e] = nn(perm_t, sorted_out[e]).astype(BF16)


def score(tables, counts, sinks, q_all, f_all, pool):
    vmem = pl.BlockSpec(memory_space=pltpu.VMEM)
    return pl.pallas_call(
        score_kernel,
        out_shape=(
            jax.ShapeDtypeStruct((UNITS, 128, HEAD_COLUMNS), BF16),
            jax.ShapeDtypeStruct((UNITS, 8, 128), F32),
        ),
        in_specs=[pl.BlockSpec(memory_space=pltpu.SMEM)] + [vmem] * 5,
        out_specs=(vmem, vmem),
        scratch_shapes=[
            pltpu.VMEM((KEYS, 128), BF16),
            pltpu.VMEM((KEYS // BK, VROWS, BK), BF16),
            pltpu.VMEM((UNITS * CHUNKS, COLS, 128), BF16),
            pltpu.VMEM((UNITS * CHUNKS, 8, COLS), F32),
            pltpu.VMEM((UNITS * CHUNKS, 8, COLS), F32),
            pltpu.VMEM((UNITS * CHUNKS, VROWS, COLS), F32),
            pltpu.VMEM((UNITS, 128, HEAD_COLUMNS), BF16),
            pltpu.VMEM((BK, COLS), F32),
            pltpu.VMEM((BK, COLS), F32),
            pltpu.SMEM((UNITS * CHUNKS,), jnp.int32),
        ],
        compiler_params=pltpu.CompilerParams(vmem_limit_bytes=40 << 20),
        cost_estimate=pl.CostEstimate(
            flops=25_000_000_000, bytes_accessed=8_000_000, transcendentals=20_000_000
        ),
        name="score",
    )(tables, counts, sinks, q_all, f_all, pool)


def merge_kernel(o_ref, lse_ref, out_ref, o_all, lse_all, o_send, o_recv, l_send, l_recv, local):
    y, z, x, c = place()

    def at(dy, dx):
        return device(lax.rem(y + dy, 4), z, lax.rem(x + dx, 4), c)

    plane = [(dy, dx) for dy in range(4) for dx in range(4) if (dy, dx) != (0, 0)]
    barrier = pltpu.get_barrier_semaphore()
    for dy, dx in plane:
        pl.semaphore_signal(barrier, inc=1, device_id=at(dy, dx), device_id_type=MESH)
    pl.semaphore_wait(barrier, len(plane))
    inner_pair = jnp.logical_or(y == 1, y == 2).astype(jnp.int32)
    slot = inner_pair * 8 + head_of(y, x)
    copies = []
    for dy in range(4):
        for dx in range(4):
            n = dy * 4 + dx
            q = lax.rem(y + dy, 4)
            e = lax.rem(x + dx, 4)
            o_source = o_ref.at[e, pl.ds(pl.multiple_of(q * ROWS, ROWS), ROWS)]
            if n == 0:
                pair = [
                    pltpu.make_async_copy(o_source, o_all.at[slot], local.at[0]),
                    pltpu.make_async_copy(lse_ref.at[e], lse_all.at[slot], local.at[1]),
                ]
            else:
                pair = [
                    pltpu.make_async_remote_copy(
                        o_source, o_all.at[slot], o_send.at[n], o_recv.at[n],
                        device_id=at(dy, dx), device_id_type=MESH,
                    ),
                    pltpu.make_async_remote_copy(
                        lse_ref.at[e], lse_all.at[slot], l_send.at[n], l_recv.at[n],
                        device_id=at(dy, dx), device_id_type=MESH,
                    ),
                ]
            for copy in pair:
                copy.start()
            copies.extend(pair)
    for copy in copies:
        copy.wait()
    mine = (iota((ROWS, 128), 1) == iota((ROWS, 128), 0) + y * ROWS).astype(F32)
    logs = nt(mine, lse_all[...].reshape(128, 128), HIGHEST)
    log0, log1 = logs[:, :64], logs[:, 64:]
    top = jnp.maximum(log0, log1)
    w0, w1 = jnp.exp(log0 - top), jnp.exp(log1 - top)
    share0, share1 = w0 / (w0 + w1), w1 / (w0 + w1)
    parts = []
    for share in (share0, share1):
        high = share.astype(BF16)
        parts.append((high, (share - high.astype(F32)).astype(BF16)))
    for h in range(KEY_VALUE_HEADS):
        shape = (64, HEAD_COLUMNS)
        spread = (iota(shape, 0) == lax.div(iota(shape, 1), HEAD_WIDTH) + h * GROUP).astype(BF16)
        wide = [nn(high, spread) + nn(low, spread) for high, low in parts]
        result = wide[0] * o_all[h].astype(F32) + wide[1] * o_all[8 + h].astype(F32)
        out_ref[:, h * HEAD_COLUMNS : (h + 1) * HEAD_COLUMNS] = result.astype(BF16)


def merge(o, lse):
    vmem = pl.BlockSpec(memory_space=pltpu.VMEM)
    dma = pltpu.SemaphoreType.DMA
    return pl.pallas_call(
        merge_kernel,
        out_shape=jax.ShapeDtypeStruct((ROWS, QUERY_HEADS * HEAD_WIDTH), BF16),
        in_specs=[vmem, vmem],
        out_specs=vmem,
        scratch_shapes=[
            pltpu.VMEM((16, ROWS, HEAD_COLUMNS), BF16),
            pltpu.VMEM((16, 8, 128), F32),
            dma((16,)), dma((16,)), dma((16,)), dma((16,)), dma((2,)),
        ],
        compiler_params=pltpu.CompilerParams(
            collective_id=2, has_side_effects=True, vmem_limit_bytes=16 << 20
        ),
        name="merge",
    )(o, lse)


def per_device(
    queries, fresh_key_values, key_value_pages, page_owner, page_slot, page_count, sinks,
    hidden, norm_gain, expert_ids, gate_prob, gate_up, down_proj,
):
    y, z, x, c = place()

    chosen = expert_ids.reshape(ROWS * TOPK)
    number = jnp.arange(ROWS * TOPK, dtype=jnp.int32)
    same = jnp.logical_and(chosen[:, None] == chosen[None, :], number[None, :] < number[:, None])
    rank = jnp.sum(same.astype(jnp.int32), axis=1)
    slots = (chosen * 2 + rank).reshape(ROWS, TOPK)
    hit = slots[None, :, :] == jnp.arange(256, dtype=jnp.int32)[:, None, None]
    spread = jnp.any(hit, axis=-1).astype(BF16)
    weights = jnp.sum(
        jnp.where(
            slots[:, :, None] == jnp.arange(256, dtype=jnp.int32)[None, None, :],
            gate_prob.reshape(ROWS, TOPK, 1),
            0.0,
        ),
        axis=1,
    )

    index = (page_owner * PAGES + page_slot).reshape(4, 4, 2, NPS)
    index = lax.dynamic_index_in_dim(index, z, 0, keepdims=False)
    index = lax.dynamic_index_in_dim(index, c, 1, keepdims=False)
    table = index.reshape(8, 128)
    count = jnp.broadcast_to(jnp.repeat(page_count.reshape(32), 4)[None, :], (8, 128))
    q_all, f_all, pool, tables, counts, result = exchange(
        queries.reshape(ROWS, QUERY_HEADS * HEAD_WIDTH),
        fresh_key_values.reshape(ROWS, 2 * KEY_VALUE_HEADS * HEAD_WIDTH),
        key_value_pages.reshape(PAGES * PAGE_TOKENS, 2 * KEY_VALUE_HEADS * HEAD_WIDTH),
        table,
        count,
        hidden.reshape(ROWS, D),
        norm_gain.reshape(1, D),
        spread,
        gate_up,
        down_proj,
    )
    head_sinks = lax.dynamic_slice_in_dim(sinks, head_of(y, x) * GROUP, GROUP)
    sink_rows = jnp.broadcast_to(jnp.repeat(head_sinks, ROWS)[None, :], (8, COLS))
    o, lse = score(
        tables, counts, sink_rows, q_all, f_all,
        pool.reshape(2 * N_EP * PAGES, PAGE_TOKENS, 2 * HEAD_WIDTH),
    )
    attention = merge(o, lse).reshape(queries.shape)

    returned = lax.all_to_all(result, ("seq", "ep"), split_axis=0, concat_axis=0, tiled=True)
    high = weights.astype(BF16)
    low = (weights - high.astype(F32)).astype(BF16)
    mixture = (
        jnp.dot(high, returned, preferred_element_type=F32)
        + jnp.dot(low, returned, preferred_element_type=F32)
    ).astype(BF16).reshape(hidden.shape)
    return (attention, mixture)


def solution(mesh):
    return jax.shard_map(
        per_device,
        mesh=mesh,
        in_specs=(
            P("seq", "ep", None, None),
            P("seq", "ep", None, None),
            P("seq", "ep", None, None),
            P("seq", None, None),
            P("seq", None, None),
            P(None, "ep"),
            P(),
            P("seq", "ep", None, None),
            P(),
            P("seq", "ep", None, None),
            P("seq", "ep", None, None),
            P(("seq", "ep"), None, None),
            P(("seq", "ep"), None, None),
        ),
        out_specs=(P("seq", "ep", None, None), P("seq", "ep", None, None)),
        check_vma=False,
    )
```

```python
import jax
import jax.numpy as jnp
from jax import lax
from jax.experimental import pallas as pl
from jax.experimental.pallas import tpu as pltpu
from jax.sharding import PartitionSpec as P

D = 2880
QUERY_HEADS = 64
KEY_VALUE_HEADS = 8
GROUP = QUERY_HEADS // KEY_VALUE_HEADS
HEAD_WIDTH = 64
TOPK = 4
HID = 1440
SCORED_STEPS = 4
PAGE_TOKENS = 16
NPS = 256
PAGES = 24
PROMPTS = 8
N_SEQ = 4
N_EP = 32
ROWS = PROMPTS * SCORED_STEPS
HEAD_COLUMNS = GROUP * HEAD_WIDTH
NEGATIVE = -1e30
FLOOR = -1e29
EPSILON = 1e-05
MESH = pl.DeviceIdType.MESH
F32 = jnp.float32
BF16 = jnp.bfloat16
HIGHEST = lax.Precision.HIGHEST


def place():
    y = lax.axis_index("seq")
    ep = lax.axis_index("ep")
    return y, lax.div(ep, 8), lax.rem(lax.div(ep, 2), 4), lax.rem(ep, 2)


def device(y, z, x, c):
    return (y, z * 8 + x * 2 + c)


def head_of(y, x):
    return lax.div(y, 2) * 4 + x


def nt(a, b, precision=None):
    return lax.dot_general(
        a, b, (((1,), (1,)), ((), ())), preferred_element_type=F32, precision=precision
    )


def nn(a, b, precision=None):
    return lax.dot_general(
        a, b, (((1,), (0,)), ((), ())), preferred_element_type=F32, precision=precision
    )


def iota(shape, axis):
    return lax.broadcasted_iota(jnp.int32, shape, axis)


def route(id_ref, prob_ref):
    i0 = iota((128, 128), 0)
    i1 = iota((128, 128), 1)
    copies = (iota((8, 128), 0) == lax.rem(iota((8, 128), 1), 8)).astype(F32)
    group = lax.div(iota((TOPK, 128), 1), 8)

    def as_row(ref):
        row = jnp.zeros((1, 128), F32)
        for t in range(SCORED_STEPS):
            wide = nn(ref[t].astype(F32), copies, HIGHEST)
            mine = group == iota((TOPK, 128), 0) + t * TOPK
            row = row + jnp.sum(jnp.where(mine, wide, 0.0), axis=0, keepdims=True)
        return row

    ids = as_row(id_ref)
    column = jnp.sum(jnp.where(i0 == i1, ids, 0.0), axis=1, keepdims=True)
    earlier = jnp.logical_and(column == ids, i0 < i1)
    rank = jnp.sum(jnp.where(earlier, 1.0, 0.0), axis=0, keepdims=True)
    slots = iota((256, 128), 0).astype(F32) == 2.0 * ids + rank

    def token(a):
        return lax.rem(a, 8) * SCORED_STEPS + lax.div(a, 32)

    owner_token = (token(iota((128, ROWS), 0)) == iota((128, ROWS), 1)).astype(BF16)
    mine = token(iota((ROWS, 128), 1)) == iota((ROWS, 128), 0)
    share = nt(jnp.where(mine, as_row(prob_ref), 0.0), slots.astype(F32), HIGHEST)
    return slots.astype(BF16), owner_token, share


def exchange_kernel(
    q_ref, f_ref, page_ref, owner_ref, slot_ref, count_ref, hidden_ref, gain_ref, id_ref, prob_ref,
    up_ref, down_ref,
    q_all, f_all, pool, tables, counts, expert_out, share_ref,
    relay, f_relay, table_ref, rows_out, rows_mid, rows_sorted, rows_in, up_w, down_w, projected, active,
    q_send, q_recv, f_send, f_recv, a_send, a_recv, z_send, z_recv, c_send, c_recv,
    i_send, i_recv, d_send, d_recv, e_send, e_recv, local, w_sem,
):
    y, z, x, c = place()
    mate = 3 - y

    def at(dy, dx):
        return device(lax.rem(y + dy, 4), z, lax.rem(x + dx, 4), c)

    plane = [(dy, dx) for dy in range(4) for dx in range(4) if (dy, dx) != (0, 0)]
    up = device(y, lax.rem(z + 1, 4), x, c)
    down = device(y, lax.rem(z + 3, 4), x, c)
    twin = device(y, z, x, 1 - c)

    def beside(dy, dz):
        return device(lax.rem(y + dy, 4), lax.rem(z + dz, 4), x, c)

    def around(dx, dc):
        return device(y, z, lax.rem(x + dx, 4), lax.rem(c + dc, 2))

    peers = [at(dy, dx) for dy, dx in plane]
    peers += [beside(dy, dz) for dy in range(4) for dz in range(1, 4)]
    peers += [around(dx, 1) for dx in range(4)]
    barrier = pltpu.get_barrier_semaphore()
    for peer in peers:
        pl.semaphore_signal(barrier, inc=1, device_id=peer, device_id_type=MESH)

    weights = []
    for n in range(4):
        part = pl.ds(n * (D // 4), D // 4)
        weights.append(pltpu.make_async_copy(up_ref.at[0, part], up_w.at[part], w_sem.at[n]))
    for n in range(2):
        part = pl.ds(n * (HID // 2), HID // 2)
        weights.append(pltpu.make_async_copy(down_ref.at[0, part], down_w.at[part], w_sem.at[4 + n]))
    for copy in weights:
        copy.start()

    h32 = hidden_ref[...].astype(F32)
    scale = lax.rsqrt(jnp.mean(h32 * h32, axis=-1, keepdims=True) + EPSILON)
    normed = (h32 * scale * gain_ref[...]).astype(BF16)
    slots, owner_token, share = route(id_ref, prob_ref)
    share_ref[...] = share
    spread = nn(slots, owner_token).astype(BF16)
    rows_out[...] = nn(spread, normed).astype(BF16).reshape(16, 16, D)
    pl.semaphore_wait(barrier, len(peers))

    routed = []
    for dy in range(4):
        for dz in range(4):
            n = dy * 4 + dz
            source = rows_out.at[lax.rem(y + dy, 4) * 4 + lax.rem(z + dz, 4)]
            target = rows_mid.at[y * 4 + z]
            if n == 0:
                copy = pltpu.make_async_copy(source, target, local.at[5])
            else:
                copy = pltpu.make_async_remote_copy(
                    source, target, d_send.at[n], d_recv.at[n],
                    device_id=beside(dy, dz), device_id_type=MESH,
                )
            copy.start()
            routed.append(copy)

    for h in range(KEY_VALUE_HEADS):
        low, high = h * HEAD_WIDTH, (h + 1) * HEAD_WIDTH
        split = KEY_VALUE_HEADS * HEAD_WIDTH
        rows = jnp.concatenate(
            [page_ref[:, low:high], page_ref[:, split + low : split + high]], axis=1
        )
        relay[h] = rows.reshape(PAGES, PAGE_TOKENS, 2 * HEAD_WIDTH)
        f_relay[h] = jnp.concatenate(
            [f_ref[:, low:high], f_ref[:, split + low : split + high]], axis=1
        )
    for xx in range(4):
        e = z * 8 + xx * 2 + c
        table_ref[xx] = owner_ref[e] * PAGES + slot_ref[e]

    def spot(segment_slot, zz, xx, cc):
        return pool.at[segment_slot, pl.ds((zz * 8 + xx * 2 + cc) * PAGES, PAGES)]

    order = [(0, 0), (0, 1), (0, 3), (1, 0), (1, 1), (1, 3), (0, 2), (1, 2)]
    first = []
    for n, (p, dx) in enumerate(order):
        yy = y if p == 0 else mate
        xx = lax.rem(x + dx, 4)
        target = spot(lax.div(y, 2), z, x, c)
        source = relay.at[head_of(yy, xx)]
        if (p, dx) == (0, 0):
            copy = pltpu.make_async_copy(source, target, local.at[0])
        else:
            copy = pltpu.make_async_remote_copy(
                source, target, a_send.at[n], a_recv.at[n],
                device_id=device(yy, z, xx, c), device_id_type=MESH,
            )
        copy.start()
        first.append(copy)

    small = []
    mine = pltpu.make_async_copy(table_ref, tables.at[lax.div(y, 2)], local.at[1])
    mine.start()
    small.append(mine)
    mine = pltpu.make_async_copy(count_ref, counts.at[x], local.at[2])
    mine.start()
    small.append(mine)
    other = pltpu.make_async_remote_copy(
        table_ref, tables.at[lax.div(y, 2)], i_send.at[0], i_recv.at[0],
        device_id=device(mate, z, x, c), device_id_type=MESH,
    )
    other.start()
    small.append(other)
    for dx in range(1, 4):
        other = pltpu.make_async_remote_copy(
            count_ref, counts.at[x], i_send.at[dx], i_recv.at[dx],
            device_id=at(0, dx), device_id_type=MESH,
        )
        other.start()
        small.append(other)

    for dy in range(4):
        for dx in range(4):
            n = dy * 4 + dx
            h = head_of(lax.rem(y + dy, 4), lax.rem(x + dx, 4))
            q_source = q_ref.at[:, pl.ds(pl.multiple_of(h * HEAD_COLUMNS, HEAD_COLUMNS), HEAD_COLUMNS)]
            f_source = f_relay.at[h]
            slot = x * 4 + y
            if n == 0:
                copies = [
                    pltpu.make_async_copy(q_source, q_all.at[slot], local.at[3]),
                    pltpu.make_async_copy(f_source, f_all.at[slot], local.at[4]),
                ]
            else:
                copies = [
                    pltpu.make_async_remote_copy(
                        q_source, q_all.at[slot], q_send.at[n], q_recv.at[n],
                        device_id=at(dy, dx), device_id_type=MESH,
                    ),
                    pltpu.make_async_remote_copy(
                        f_source, f_all.at[slot], f_send.at[n], f_recv.at[n],
                        device_id=at(dy, dx), device_id_type=MESH,
                    ),
                ]
            for copy in copies:
                copy.start()
            small.extend(copies)

    def chunk(n):
        p, dx = order[n]
        yy = y if p == 0 else mate
        return lax.div(yy, 2), lax.rem(x - dx + 4, 4)

    def pass_on(n, zz, way, peer):
        segment_slot, xx = chunk(n)
        block = spot(segment_slot, zz, xx, c)
        sends, recvs = (c_send, c_recv) if way >= 3 else (z_send, z_recv)
        number = (way - 3 if way >= 3 else way) * 8 + n
        copy = pltpu.make_async_remote_copy(
            block, block, sends.at[number], recvs.at[number],
            device_id=peer, device_id_type=MESH,
        )
        copy.start()
        return copy

    for copy in routed:
        copy.wait()
    ri = iota((256, 256), 0)
    ci = iota((256, 256), 1)

    def slot_of(i):
        return lax.div(lax.rem(i, 32), 2) * 16 + lax.div(i, 32) * 2 + lax.rem(i, 2)

    regroup = (slot_of(ri) == ci).astype(BF16)
    rows_sorted[...] = nn(regroup, rows_mid[...].reshape(256, D)).astype(BF16).reshape(8, 32, D)
    delivered = []
    for dx in range(4):
        for dc in range(2):
            n = dx * 2 + dc
            source = rows_sorted.at[lax.rem(x + dx, 4) * 2 + lax.rem(c + dc, 2)]
            target = rows_in.at[x * 2 + c]
            if n == 0:
                copy = pltpu.make_async_copy(source, target, local.at[6])
            else:
                copy = pltpu.make_async_remote_copy(
                    source, target, e_send.at[n], e_recv.at[n],
                    device_id=around(dx, dc), device_id_type=MESH,
                )
            copy.start()
            delivered.append(copy)

    upward, downward, further, across = [], [], [], []
    for n in range(8):
        if n == 0:
            first[n].wait()
        else:
            first[n].wait_recv()
        upward.append(pass_on(n, z, 0, up))
        downward.append(pass_on(n, z, 1, down))
        across.append(pass_on(n, z, 3, twin))
    for n in range(8):
        upward[n].wait_recv()
        if n % 2 == 0:
            further.append(pass_on(n, lax.rem(z + 3, 4), 2, up))
        across.append(pass_on(n, lax.rem(z + 3, 4), 4, twin))
        downward[n].wait_recv()
        if n % 2 == 1:
            further.append(pass_on(n, lax.rem(z + 1, 4), 2, down))
        across.append(pass_on(n, lax.rem(z + 1, 4), 5, twin))
    for copy in weights + delivered:
        copy.wait()

    def tiles(work):
        @pl.loop(0, D // TILE)
        def _(j):
            work(pl.ds(pl.multiple_of(j * TILE, TILE), TILE))

        work(pl.ds(D // TILE * TILE, D % TILE))

    def project(part):
        projected[:, part] = nn(rows_in[...].reshape(256, D), up_w[:, part])

    tiles(project)

    @pl.loop(0, 8)
    def _(j):
        part = pl.ds(pl.multiple_of(j * 32, 32), 32)
        wide = projected[part, :]
        gate, upper = wide[:, :HID], wide[:, HID:]
        active[part, :] = ((upper + 1.0) * gate * jax.nn.sigmoid(1.702 * gate)).astype(BF16)

    for n in range(8):
        further[n].wait_recv()
        across.append(pass_on(n, lax.rem(z + 2, 4), 6, twin))

    back = (slot_of(ci) == ri).astype(BF16)
    active[...] = nn(back, active[...]).astype(BF16)

    def finish(part):
        expert_out[:, part] = nn(active[...], down_w[:, part]).astype(BF16)

    tiles(finish)

    for copy in across:
        copy.wait()
    for copy in first[1:] + upward + downward + further:
        copy.wait_send()
    for copy in small:
        copy.wait()


TILE = 384


def exchange(
    queries, fresh, pages, owner, slot, count, hidden, gain, ids, prob, gate_up, down_proj
):
    vmem = pl.BlockSpec(memory_space=pltpu.VMEM)
    anywhere = pl.BlockSpec(memory_space=pl.ANY)
    dma = pltpu.SemaphoreType.DMA
    return pl.pallas_call(
        exchange_kernel,
        out_shape=(
            jax.ShapeDtypeStruct((16, ROWS, HEAD_COLUMNS), BF16),
            jax.ShapeDtypeStruct((16, ROWS, 2 * HEAD_WIDTH), BF16),
            jax.ShapeDtypeStruct((2, N_EP * PAGES, PAGE_TOKENS, 2 * HEAD_WIDTH), BF16),
            jax.ShapeDtypeStruct((2, 4, 2, 128), jnp.int32),
            jax.ShapeDtypeStruct((4, N_SEQ, PROMPTS), jnp.int32),
            jax.ShapeDtypeStruct((256, D), BF16),
            jax.ShapeDtypeStruct((ROWS, 256), F32),
        ),
        in_specs=[vmem] * 10 + [anywhere] * 2,
        out_specs=(anywhere,) * 5 + (vmem, vmem),
        scratch_shapes=[
            pltpu.VMEM((KEY_VALUE_HEADS, PAGES, PAGE_TOKENS, 2 * HEAD_WIDTH), BF16),
            pltpu.VMEM((KEY_VALUE_HEADS, ROWS, 2 * HEAD_WIDTH), BF16),
            pltpu.VMEM((4, 2, 128), jnp.int32),
            pltpu.VMEM((16, 16, D), BF16),
            pltpu.VMEM((16, 16, D), BF16),
            pltpu.VMEM((8, 32, D), BF16),
            pltpu.VMEM((8, 32, D), BF16),
            pltpu.VMEM((D, 2 * HID), BF16),
            pltpu.VMEM((HID, D), BF16),
            pltpu.VMEM((256, 2 * HID), F32),
            pltpu.VMEM((256, HID), BF16),
            dma((16,)), dma((16,)), dma((16,)), dma((16,)), dma((8,)), dma((8,)),
            dma((24,)), dma((24,)), dma((32,)), dma((32,)), dma((4,)), dma((4,)),
            dma((16,)), dma((16,)), dma((8,)), dma((8,)), dma((7,)), dma((6,)),
        ],
        compiler_params=pltpu.CompilerParams(
            collective_id=1, has_side_effects=True, vmem_limit_bytes=56 << 20
        ),
        name="exchange",
    )(queries, fresh, pages, owner, slot, count, hidden, gain, ids, prob, gate_up, down_proj)


BK = 1024
GK = 2048
KEYS = 2 * NPS * PAGE_TOKENS
UNITS = 4
CHUNKS = 4
COLS = 256
VROWS = 80


def values_of(rows):
    pick = (iota((VROWS, 128), 0) + HEAD_WIDTH == iota((VROWS, 128), 1)).astype(BF16)
    moved = nt(pick, rows)
    return jnp.where(iota(moved.shape, 0) >= HEAD_WIDTH, 1.0, moved).astype(BF16)


def score_kernel(
    tables, counts, sinks, q_all, f_all, pool_ref, o_ref, lse_ref,
    pool, kv, vt, qs, limit_ref, m_ref, acc, sorted_out, s0, s1, lengths, pool_sem,
):
    y = lax.axis_index("seq")
    outer_pair = jnp.logical_or(y == 0, y == 3)
    sink_row = sinks[0:1, :]
    load = pltpu.make_async_copy(pool_ref, pool, pool_sem)
    load.start()
    i0 = iota((128, 128), 0)
    i1 = iota((128, 128), 1)
    lane_row = lax.rem(iota((128, COLS), 1), ROWS).astype(F32)

    def ordering(e):
        lane = iota((PROMPTS, 128), 1)
        copies = (iota((PROMPTS, 128), 0) == lax.div(lax.rem(lane, ROWS), SCORED_STEPS)).astype(F32)
        wide = nn(counts[e].astype(F32), copies, HIGHEST)
        mine = lax.div(iota((N_SEQ, 128), 1), ROWS) == iota((N_SEQ, 128), 0)
        c = jnp.sum(jnp.where(mine, wide, 0.0), axis=0, keepdims=True)
        n_row = jnp.where(
            outer_pair,
            jnp.minimum(c, 256.0) + jnp.maximum(c - 768.0, 0.0),
            jnp.clip(c - 256.0, 0.0, 512.0),
        )
        n_col = jnp.sum(jnp.where(i0 == i1, n_row, 0.0), axis=1, keepdims=True)
        behind = jnp.logical_or(n_row > n_col, jnp.logical_and(n_col == n_row, i1 < i0))
        pos_col = jnp.sum(jnp.where(behind, 1.0, 0.0), axis=1, keepdims=True)
        return n_row, n_col, pos_col

    for e in range(UNITS):
        n_row, n_col, pos_col = ordering(e)
        ahead = jnp.logical_or(n_col > n_row, jnp.logical_and(n_col == n_row, i0 < i1))
        pos_row = jnp.sum(jnp.where(ahead, 1.0, 0.0), axis=0, keepdims=True)
        perm = (pos_row == i0.astype(F32)).astype(BF16)
        q_sorted = nn(perm, q_all[e * 4 : e * 4 + 4].reshape(128, HEAD_COLUMNS)) * 0.125
        q_sorted = q_sorted.astype(BF16)
        f_sorted = nn(perm, f_all[e * 4 : e * 4 + 4].reshape(128, 128)).astype(BF16)
        none = jnp.zeros((ROWS, HEAD_WIDTH), BF16)
        for ch in range(CHUNKS):
            u = e * CHUNKS + ch
            for g in range(GROUP):
                piece = q_sorted[ch * ROWS : (ch + 1) * ROWS, g * HEAD_WIDTH : (g + 1) * HEAD_WIDTH]
                qs[u, g * ROWS : (g + 1) * ROWS, :] = jnp.concatenate([piece, none], axis=1)
            member = pos_col == lane_row + float(ch * ROWS)
            limit = jnp.sum(jnp.where(member, n_col, 0.0), axis=0, keepdims=True) * PAGE_TOKENS
            limit_ref[u] = jnp.broadcast_to(limit, (8, COLS))
            lengths[u] = jnp.max(limit).astype(jnp.int32)
            rows = f_sorted[ch * ROWS : (ch + 1) * ROWS, :]
            s = nt(rows, qs[u])
            ki = iota((ROWS, COLS), 0)
            ri = lax.rem(iota((ROWS, COLS), 1), ROWS)
            seen = jnp.logical_and(
                lax.div(ki, SCORED_STEPS) == lax.div(ri, SCORED_STEPS), ki <= ri
            )
            s = jnp.where(seen, s, NEGATIVE)
            m0 = jnp.maximum(jnp.max(s, axis=0, keepdims=True), sink_row)
            p = jnp.exp(s - m0).astype(BF16)
            start = nn(values_of(rows), p)
            start = start + jnp.where(
                iota((VROWS, COLS), 0) >= HEAD_WIDTH, jnp.exp(sink_row - m0), 0.0
            )
            m_ref[u] = jnp.broadcast_to(jnp.where(outer_pair, m0, FLOOR), (8, COLS))
            acc[u] = jnp.where(outer_pair, start, 0.0)

    def unit(e, carry):
        def gather(kb, carry):
            p0 = kb * (GK // PAGE_TOKENS)
            ss = lax.div(p0, NPS)
            lane = lax.div(lax.rem(p0, NPS), 2)
            rows = [
                pool[tables[ss, e, i % 2, lane + i // 2] + ss * (N_EP * PAGES)]
                for i in range(GK // PAGE_TOKENS)
            ]
            for i in range(GK // BK):
                part = rows[i * (BK // PAGE_TOKENS) : (i + 1) * (BK // PAGE_TOKENS)]
                found = jnp.concatenate(part, axis=0)
                kv[pl.ds(pl.multiple_of(kb * GK + i * BK, BK), BK), :] = found
                vt[kb * (GK // BK) + i] = values_of(found)
            return carry

        lax.fori_loop(0, lax.div(lengths[e * CHUNKS] + (GK - 1), GK), gather, 0)

        key = iota((BK, COLS), 0).astype(F32)

        def produce(store, u, kb):
            keys = kv[pl.ds(pl.multiple_of(kb * BK, BK), BK), :]
            s = nt(keys, qs[u])
            limit = limit_ref[u][0:1, :] - (kb * BK).astype(F32)
            s = jnp.where(key < limit, s, NEGATIVE)
            store[...] = s
            return jnp.max(s, axis=0, keepdims=True)

        def absorb(store, u, kb, top):
            before = m_ref[u][0:1, :]
            after = jnp.maximum(before, top)
            p = jnp.exp(store[...] - after).astype(BF16)
            acc[u] = acc[u] * jnp.exp(before - after) + nn(vt[kb], p)
            m_ref[u] = jnp.broadcast_to(after, (8, COLS))

        def chunk(ch, top):
            u = e * CHUNKS + ch
            count = lax.div(lengths[u] + (BK - 1), BK)
            after_u = e * CHUNKS + jnp.minimum(ch + 1, CHUNKS - 1)

            def pair(i, top):
                last = 2 * i + 2 >= count
                next_top = produce(s1, u, 2 * i + 1)
                absorb(s0, u, 2 * i, top)
                top = produce(s0, jnp.where(last, after_u, u), jnp.where(last, 0, 2 * i + 2))
                absorb(s1, u, 2 * i + 1, next_top)
                return top

            top = lax.fori_loop(0, lax.div(count, 2), pair, top)

            def odd(top):
                absorb(s0, u, count - 1, top)
                return produce(s0, after_u, jnp.int32(0))

            return lax.cond(lax.rem(count, 2) == 1, odd, lambda top: top, top)

        used = sum([(lengths[e * CHUNKS + ch] > 0).astype(jnp.int32) for ch in range(CHUNKS)])

        @pl.when(used > 0)
        def _():
            top = produce(s0, e * CHUNKS, jnp.int32(0))
            lax.fori_loop(0, used, chunk, top)

        return carry

    load.wait()
    lax.fori_loop(0, UNITS, unit, 0)

    for e in range(UNITS):
        _, _, pos_col = ordering(e)
        perm_t = (pos_col == i1.astype(F32)).astype(BF16)
        lse = jnp.zeros((8, 128), F32)
        for ch in range(CHUNKS):
            u = e * CHUNKS + ch
            total = jnp.maximum(acc[u][HEAD_WIDTH : HEAD_WIDTH + 1, :], 1e-30)
            out = acc[u][0:HEAD_WIDTH, :] / total
            padded = jnp.concatenate([out, jnp.zeros_like(out)], axis=0)
            turned = padded.T.astype(BF16)
            for g in range(GROUP):
                sorted_out[e, ch * ROWS : (ch + 1) * ROWS, g * HEAD_WIDTH : (g + 1) * HEAD_WIDTH] = (
                    turned[g * ROWS : (g + 1) * ROWS, 0:HEAD_WIDTH]
                )
            row = m_ref[u][0:1, :] + jnp.log(total)
            mine = lax.div(iota((8, COLS), 1), ROWS) == iota((8, COLS), 0)
            member = (pos_col == lane_row + float(ch * ROWS)).astype(F32)
            lse = lse + nt(jnp.where(mine, row, 0.0), member, HIGHEST)
        lse_ref[e] = lse
        o_ref[e] = nn(perm_t, sorted_out[e]).astype(BF16)


def score(tables, counts, sinks, q_all, f_all, pool):
    vmem = pl.BlockSpec(memory_space=pltpu.VMEM)
    return pl.pallas_call(
        score_kernel,
        out_shape=(
            jax.ShapeDtypeStruct((UNITS, 128, HEAD_COLUMNS), BF16),
            jax.ShapeDtypeStruct((UNITS, 8, 128), F32),
        ),
        in_specs=[pl.BlockSpec(memory_space=pltpu.SMEM)] + [vmem] * 4
        + [pl.BlockSpec(memory_space=pl.ANY)],
        out_specs=(vmem, vmem),
        scratch_shapes=[
            pltpu.VMEM((2 * N_EP * PAGES, PAGE_TOKENS, 128), BF16),
            pltpu.VMEM((KEYS, 128), BF16),
            pltpu.VMEM((KEYS // BK, VROWS, BK), BF16),
            pltpu.VMEM((UNITS * CHUNKS, COLS, 128), BF16),
            pltpu.VMEM((UNITS * CHUNKS, 8, COLS), F32),
            pltpu.VMEM((UNITS * CHUNKS, 8, COLS), F32),
            pltpu.VMEM((UNITS * CHUNKS, VROWS, COLS), F32),
            pltpu.VMEM((UNITS, 128, HEAD_COLUMNS), BF16),
            pltpu.VMEM((BK, COLS), F32),
            pltpu.VMEM((BK, COLS), F32),
            pltpu.SMEM((UNITS * CHUNKS,), jnp.int32),
            pltpu.SemaphoreType.DMA,
        ],
        compiler_params=pltpu.CompilerParams(vmem_limit_bytes=60 << 20),
        cost_estimate=pl.CostEstimate(
            flops=25_000_000_000, bytes_accessed=8_000_000, transcendentals=20_000_000
        ),
        name="score",
    )(tables, counts, sinks, q_all, f_all, pool)


def merge_kernel(
    o_ref, lse_ref, share_ref, rows_ref, out_ref, mix_ref, o_all, lse_all, o_send, o_recv, l_send, l_recv, local,
):
    y, z, x, c = place()

    def at(dy, dx):
        return device(lax.rem(y + dy, 4), z, lax.rem(x + dx, 4), c)

    plane = [(dy, dx) for dy in range(4) for dx in range(4) if (dy, dx) != (0, 0)]
    barrier = pltpu.get_barrier_semaphore()
    for dy, dx in plane:
        pl.semaphore_signal(barrier, inc=1, device_id=at(dy, dx), device_id_type=MESH)
    pl.semaphore_wait(barrier, len(plane))
    inner_pair = jnp.logical_or(y == 1, y == 2).astype(jnp.int32)
    slot = inner_pair * 8 + head_of(y, x)
    copies = []
    for dy in range(4):
        for dx in range(4):
            n = dy * 4 + dx
            q = lax.rem(y + dy, 4)
            e = lax.rem(x + dx, 4)
            o_source = o_ref.at[e, pl.ds(pl.multiple_of(q * ROWS, ROWS), ROWS)]
            if n == 0:
                pair = [
                    pltpu.make_async_copy(o_source, o_all.at[slot], local.at[0]),
                    pltpu.make_async_copy(lse_ref.at[e], lse_all.at[slot], local.at[1]),
                ]
            else:
                pair = [
                    pltpu.make_async_remote_copy(
                        o_source, o_all.at[slot], o_send.at[n], o_recv.at[n],
                        device_id=at(dy, dx), device_id_type=MESH,
                    ),
                    pltpu.make_async_remote_copy(
                        lse_ref.at[e], lse_all.at[slot], l_send.at[n], l_recv.at[n],
                        device_id=at(dy, dx), device_id_type=MESH,
                    ),
                ]
            for copy in pair:
                copy.start()
            copies.extend(pair)

    share = share_ref[...]
    high = share.astype(BF16)
    low = (share - high.astype(F32)).astype(BF16)
    rows = rows_ref[...]
    mix_ref[...] = (nn(high, rows) + nn(low, rows)).astype(BF16)

    for copy in copies:
        copy.wait()
    mine = (iota((ROWS, 128), 1) == iota((ROWS, 128), 0) + y * ROWS).astype(F32)
    logs = nt(mine, lse_all[...].reshape(128, 128), HIGHEST)
    log0, log1 = logs[:, :64], logs[:, 64:]
    top = jnp.maximum(log0, log1)
    w0, w1 = jnp.exp(log0 - top), jnp.exp(log1 - top)
    share0, share1 = w0 / (w0 + w1), w1 / (w0 + w1)
    parts = []
    for share in (share0, share1):
        high = share.astype(BF16)
        parts.append((high, (share - high.astype(F32)).astype(BF16)))
    for h in range(KEY_VALUE_HEADS):
        shape = (64, HEAD_COLUMNS)
        spread = (iota(shape, 0) == lax.div(iota(shape, 1), HEAD_WIDTH) + h * GROUP).astype(BF16)
        wide = [nn(high, spread) + nn(low, spread) for high, low in parts]
        result = wide[0] * o_all[h].astype(F32) + wide[1] * o_all[8 + h].astype(F32)
        out_ref[:, h * HEAD_COLUMNS : (h + 1) * HEAD_COLUMNS] = result.astype(BF16)


def merge(o, lse, share, rows):
    vmem = pl.BlockSpec(memory_space=pltpu.VMEM)
    dma = pltpu.SemaphoreType.DMA
    return pl.pallas_call(
        merge_kernel,
        out_shape=(
            jax.ShapeDtypeStruct((ROWS, QUERY_HEADS * HEAD_WIDTH), BF16),
            jax.ShapeDtypeStruct((ROWS, D), BF16),
        ),
        in_specs=[vmem] * 4,
        out_specs=(vmem, vmem),
        scratch_shapes=[
            pltpu.VMEM((16, ROWS, HEAD_COLUMNS), BF16),
            pltpu.VMEM((16, 8, 128), F32),
            dma((16,)), dma((16,)), dma((16,)), dma((16,)), dma((2,)),
        ],
        compiler_params=pltpu.CompilerParams(
            collective_id=2, has_side_effects=True, vmem_limit_bytes=16 << 20
        ),
        name="merge",
    )(o, lse, share, rows)


def by_prefix(table):
    return table[0].T.reshape(2, N_EP, NPS // 2).transpose(1, 0, 2)


def per_device(
    queries, fresh_key_values, key_value_pages, page_owner, page_slot, page_count, sinks,
    hidden, norm_gain, expert_ids, gate_prob, gate_up, down_proj,
):
    y, z, x, c = place()

    q_all, f_all, pool, tables, counts, result, share = exchange(
        queries.reshape(ROWS, QUERY_HEADS * HEAD_WIDTH),
        fresh_key_values.reshape(ROWS, 2 * KEY_VALUE_HEADS * HEAD_WIDTH),
        key_value_pages.reshape(PAGES * PAGE_TOKENS, 2 * KEY_VALUE_HEADS * HEAD_WIDTH),
        by_prefix(page_owner),
        by_prefix(page_slot),
        page_count,
        hidden.reshape(ROWS, D),
        norm_gain.reshape(1, D),
        expert_ids[0].transpose(1, 2, 0),
        gate_prob[0].transpose(1, 2, 0),
        gate_up,
        down_proj,
    )
    returned = lax.all_to_all(result, ("seq", "ep"), split_axis=0, concat_axis=0, tiled=True)
    head_sinks = lax.dynamic_slice_in_dim(sinks, head_of(y, x) * GROUP, GROUP)
    sink_rows = jnp.broadcast_to(jnp.repeat(head_sinks, ROWS)[None, :], (8, COLS))
    o, lse = score(
        tables, counts, sink_rows, q_all, f_all,
        pool.reshape(2 * N_EP * PAGES, PAGE_TOKENS, 2 * HEAD_WIDTH),
    )
    attention, mixture = merge(o, lse, share, returned)
    return (attention.reshape(queries.shape), mixture.reshape(hidden.shape))


def solution(mesh):
    return jax.shard_map(
        per_device,
        mesh=mesh,
        in_specs=(
            P("seq", "ep", None, None),
            P("seq", "ep", None, None),
            P("seq", "ep", None, None),
            P("seq", None, None),
            P("seq", None, None),
            P(None, "ep"),
            P(),
            P("seq", "ep", None, None),
            P(),
            P("seq", "ep", None, None),
            P("seq", "ep", None, None),
            P(("seq", "ep"), None, None),
            P(("seq", "ep"), None, None),
        ),
        out_specs=(P("seq", "ep", None, None), P("seq", "ep", None, None)),
        check_vma=False,
    )
```

```python
import jax
import jax.numpy as jnp
from jax import lax
from jax.experimental import pallas as pl
from jax.experimental.pallas import tpu as pltpu
from jax.sharding import PartitionSpec as P

D = 2880
QUERY_HEADS = 64
KEY_VALUE_HEADS = 8
GROUP = QUERY_HEADS // KEY_VALUE_HEADS
HEAD_WIDTH = 64
TOPK = 4
HID = 1440
SCORED_STEPS = 4
PAGE_TOKENS = 16
NPS = 256
PAGES = 24
PROMPTS = 8
N_SEQ = 4
N_EP = 32
ROWS = PROMPTS * SCORED_STEPS
HEAD_COLUMNS = GROUP * HEAD_WIDTH
NEGATIVE = -1e30
FLOOR = -1e29
EPSILON = 1e-05
MESH = pl.DeviceIdType.MESH
F32 = jnp.float32
BF16 = jnp.bfloat16
HIGHEST = lax.Precision.HIGHEST


def place():
    y = lax.axis_index("seq")
    ep = lax.axis_index("ep")
    return y, lax.div(ep, 8), lax.rem(lax.div(ep, 2), 4), lax.rem(ep, 2)


def device(y, z, x, c):
    return (y, z * 8 + x * 2 + c)


def head_of(y, x):
    return lax.div(y, 2) * 4 + x


def nt(a, b, precision=None):
    return lax.dot_general(
        a, b, (((1,), (1,)), ((), ())), preferred_element_type=F32, precision=precision
    )


def nn(a, b, precision=None):
    return lax.dot_general(
        a, b, (((1,), (0,)), ((), ())), preferred_element_type=F32, precision=precision
    )


def iota(shape, axis):
    return lax.broadcasted_iota(jnp.int32, shape, axis)


PARTS = ((0, 1024), (1024, 1024), (2048, D - 2048))


def route(id_ref, prob_ref):
    i0 = iota((128, 128), 0)
    i1 = iota((128, 128), 1)
    copies = (iota((8, 128), 0) == lax.rem(iota((8, 128), 1), 8)).astype(F32)
    group = lax.div(iota((TOPK, 128), 1), 8)

    def as_row(ref):
        row = jnp.zeros((1, 128), F32)
        for t in range(SCORED_STEPS):
            wide = nn(ref[t].astype(F32), copies, HIGHEST)
            mine = group == iota((TOPK, 128), 0) + t * TOPK
            row = row + jnp.sum(jnp.where(mine, wide, 0.0), axis=0, keepdims=True)
        return row

    ids = as_row(id_ref)
    column = jnp.sum(jnp.where(i0 == i1, ids, 0.0), axis=1, keepdims=True)
    earlier = jnp.logical_and(column == ids, i0 < i1)
    rank = jnp.sum(jnp.where(earlier, 1.0, 0.0), axis=0, keepdims=True)
    slots = iota((256, 128), 0).astype(F32) == 2.0 * ids + rank

    def token(a):
        return lax.rem(a, 8) * SCORED_STEPS + lax.div(a, 32)

    owner_token = (token(iota((128, ROWS), 0)) == iota((128, ROWS), 1)).astype(BF16)
    mine = token(iota((ROWS, 128), 1)) == iota((ROWS, 128), 0)
    share = nt(jnp.where(mine, as_row(prob_ref), 0.0), slots.astype(F32), HIGHEST)
    return slots.astype(BF16), owner_token, share


def exchange_kernel(
    q_ref, f_ref, page_ref, owner_ref, slot_ref, count_ref, hidden_ref, gain_ref, id_ref, prob_ref,
    up_ref, down_ref,
    q_all, f_all, pool, tables, counts, expert_out, share_ref,
    relay, f_relay, table_ref, out0, out1, out2, mid0, mid1, mid2, sorted0, sorted1, sorted2,
    in0, in1, in2, up_w, down_w, projected, active,
    q_send, q_recv, f_send, f_recv, a_send, a_recv, z_send, z_recv, c_send, c_recv,
    i_send, i_recv, d_send, d_recv, e_send, e_recv, local, w_sem,
):
    y, z, x, c = place()
    mate = 3 - y
    rows_out, rows_mid = (out0, out1, out2), (mid0, mid1, mid2)
    rows_sorted, rows_in = (sorted0, sorted1, sorted2), (in0, in1, in2)

    def at(dy, dx):
        return device(lax.rem(y + dy, 4), z, lax.rem(x + dx, 4), c)

    plane = [(dy, dx) for dy in range(4) for dx in range(4) if (dy, dx) != (0, 0)]
    up = device(y, lax.rem(z + 1, 4), x, c)
    down = device(y, lax.rem(z + 3, 4), x, c)
    twin = device(y, z, x, 1 - c)

    def beside(dy, dz):
        return device(lax.rem(y + dy, 4), lax.rem(z + dz, 4), x, c)

    def around(dx, dc):
        return device(y, z, lax.rem(x + dx, 4), lax.rem(c + dc, 2))

    peers = [at(dy, dx) for dy, dx in plane]
    peers += [beside(dy, dz) for dy in range(4) for dz in range(1, 4)]
    peers += [around(dx, 1) for dx in range(4)]
    barrier = pltpu.get_barrier_semaphore()
    for peer in peers:
        pl.semaphore_signal(barrier, inc=1, device_id=peer, device_id_type=MESH)

    weights = []
    for n in range(4):
        part = pl.ds(n * (D // 4), D // 4)
        weights.append(pltpu.make_async_copy(up_ref.at[0, part], up_w.at[part], w_sem.at[n]))
    for n in range(2):
        part = pl.ds(n * (HID // 2), HID // 2)
        weights.append(pltpu.make_async_copy(down_ref.at[0, part], down_w.at[part], w_sem.at[4 + n]))
    for copy in weights:
        copy.start()

    h32 = hidden_ref[...].astype(F32)
    scale = lax.rsqrt(jnp.mean(h32 * h32, axis=-1, keepdims=True) + EPSILON)
    normed = (h32 * scale * gain_ref[...]).astype(BF16)
    slots, owner_token, share = route(id_ref, prob_ref)
    share_ref[...] = share
    spread = nn(slots, owner_token).astype(BF16)
    for k, (first_column, columns) in enumerate(PARTS):
        piece = normed[:, first_column : first_column + columns]
        rows_out[k][...] = nn(spread, piece).astype(BF16).reshape(16, 16, columns)
    pl.semaphore_wait(barrier, len(peers))

    routed = []
    for k in range(len(PARTS)):
        for dy in range(4):
            for dz in range(4):
                n = dy * 4 + dz
                source = rows_out[k].at[lax.rem(y + dy, 4) * 4 + lax.rem(z + dz, 4)]
                target = rows_mid[k].at[y * 4 + z]
                if n == 0:
                    copy = pltpu.make_async_copy(source, target, local.at[5 + 2 * k])
                else:
                    copy = pltpu.make_async_remote_copy(
                        source, target, d_send.at[k * 16 + n], d_recv.at[k * 16 + n],
                        device_id=beside(dy, dz), device_id_type=MESH,
                    )
                copy.start()
                routed.append(copy)

    for h in range(KEY_VALUE_HEADS):
        low, high = h * HEAD_WIDTH, (h + 1) * HEAD_WIDTH
        split = KEY_VALUE_HEADS * HEAD_WIDTH
        rows = jnp.concatenate(
            [page_ref[:, low:high], page_ref[:, split + low : split + high]], axis=1
        )
        relay[h] = rows.reshape(PAGES, PAGE_TOKENS, 2 * HEAD_WIDTH)
        f_relay[h] = jnp.concatenate(
            [f_ref[:, low:high], f_ref[:, split + low : split + high]], axis=1
        )
    for xx in range(4):
        e = z * 8 + xx * 2 + c
        table_ref[xx] = owner_ref[e] * PAGES + slot_ref[e]

    def spot(segment_slot, zz, xx, cc):
        return pool.at[segment_slot, pl.ds((zz * 8 + xx * 2 + cc) * PAGES, PAGES)]

    order = [(0, 0), (0, 1), (0, 3), (1, 0), (1, 1), (1, 3), (0, 2), (1, 2)]
    first = []
    for n, (p, dx) in enumerate(order):
        yy = y if p == 0 else mate
        xx = lax.rem(x + dx, 4)
        target = spot(lax.div(y, 2), z, x, c)
        source = relay.at[head_of(yy, xx)]
        if (p, dx) == (0, 0):
            copy = pltpu.make_async_copy(source, target, local.at[0])
        else:
            copy = pltpu.make_async_remote_copy(
                source, target, a_send.at[n], a_recv.at[n],
                device_id=device(yy, z, xx, c), device_id_type=MESH,
            )
        copy.start()
        first.append(copy)

    small = []
    mine = pltpu.make_async_copy(table_ref, tables.at[lax.div(y, 2)], local.at[1])
    mine.start()
    small.append(mine)
    mine = pltpu.make_async_copy(count_ref, counts.at[x], local.at[2])
    mine.start()
    small.append(mine)
    other = pltpu.make_async_remote_copy(
        table_ref, tables.at[lax.div(y, 2)], i_send.at[0], i_recv.at[0],
        device_id=device(mate, z, x, c), device_id_type=MESH,
    )
    other.start()
    small.append(other)
    for dx in range(1, 4):
        other = pltpu.make_async_remote_copy(
            count_ref, counts.at[x], i_send.at[dx], i_recv.at[dx],
            device_id=at(0, dx), device_id_type=MESH,
        )
        other.start()
        small.append(other)

    for dy in range(4):
        for dx in range(4):
            n = dy * 4 + dx
            h = head_of(lax.rem(y + dy, 4), lax.rem(x + dx, 4))
            q_source = q_ref.at[:, pl.ds(pl.multiple_of(h * HEAD_COLUMNS, HEAD_COLUMNS), HEAD_COLUMNS)]
            f_source = f_relay.at[h]
            slot = x * 4 + y
            if n == 0:
                copies = [
                    pltpu.make_async_copy(q_source, q_all.at[slot], local.at[3]),
                    pltpu.make_async_copy(f_source, f_all.at[slot], local.at[4]),
                ]
            else:
                copies = [
                    pltpu.make_async_remote_copy(
                        q_source, q_all.at[slot], q_send.at[n], q_recv.at[n],
                        device_id=at(dy, dx), device_id_type=MESH,
                    ),
                    pltpu.make_async_remote_copy(
                        f_source, f_all.at[slot], f_send.at[n], f_recv.at[n],
                        device_id=at(dy, dx), device_id_type=MESH,
                    ),
                ]
            for copy in copies:
                copy.start()
            small.extend(copies)

    def chunk(n):
        p, dx = order[n]
        yy = y if p == 0 else mate
        return lax.div(yy, 2), lax.rem(x - dx + 4, 4)

    def pass_on(n, zz, way, peer):
        segment_slot, xx = chunk(n)
        block = spot(segment_slot, zz, xx, c)
        sends, recvs = (c_send, c_recv) if way >= 3 else (z_send, z_recv)
        number = (way - 3 if way >= 3 else way) * 8 + n
        copy = pltpu.make_async_remote_copy(
            block, block, sends.at[number], recvs.at[number],
            device_id=peer, device_id_type=MESH,
        )
        copy.start()
        return copy

    ri = iota((256, 256), 0)
    ci = iota((256, 256), 1)

    def slot_of(i):
        return lax.div(lax.rem(i, 32), 2) * 16 + lax.div(i, 32) * 2 + lax.rem(i, 2)

    regroup = (slot_of(ri) == ci).astype(BF16)
    delivered = [[], [], []]
    for k, (_, columns) in enumerate(PARTS):
        for copy in routed[k * 16 : (k + 1) * 16]:
            copy.wait()
        moved = nn(regroup, rows_mid[k][...].reshape(256, columns)).astype(BF16)
        rows_sorted[k][...] = moved.reshape(8, 32, columns)
        for dx in range(4):
            for dc in range(2):
                n = dx * 2 + dc
                source = rows_sorted[k].at[lax.rem(x + dx, 4) * 2 + lax.rem(c + dc, 2)]
                target = rows_in[k].at[x * 2 + c]
                if n == 0:
                    copy = pltpu.make_async_copy(source, target, local.at[6 + 2 * k])
                else:
                    copy = pltpu.make_async_remote_copy(
                        source, target, e_send.at[k * 8 + n], e_recv.at[k * 8 + n],
                        device_id=around(dx, dc), device_id_type=MESH,
                    )
                copy.start()
                delivered[k].append(copy)

    upward, downward, further, across = [], [], [], []
    for n in range(8):
        if n == 0:
            first[n].wait()
        else:
            first[n].wait_recv()
        upward.append(pass_on(n, z, 0, up))
        downward.append(pass_on(n, z, 1, down))
        across.append(pass_on(n, z, 3, twin))

    def forward(n):
        upward[n].wait_recv()
        if n % 2 == 0:
            further.append(pass_on(n, lax.rem(z + 3, 4), 2, up))
        across.append(pass_on(n, lax.rem(z + 3, 4), 4, twin))
        downward[n].wait_recv()
        if n % 2 == 1:
            further.append(pass_on(n, lax.rem(z + 1, 4), 2, down))
        across.append(pass_on(n, lax.rem(z + 1, 4), 5, twin))

    for copy in weights:
        copy.wait()

    def tiles(work):
        @pl.loop(0, D // TILE)
        def _(j):
            work(pl.ds(pl.multiple_of(j * TILE, TILE), TILE))

        work(pl.ds(D // TILE * TILE, D % TILE))

    def project(k):
        first_column, columns = PARTS[k]
        for copy in delivered[k]:
            copy.wait()

        def work(part):
            rows = rows_in[k][...].reshape(256, columns)
            term = nn(rows, up_w[first_column : first_column + columns, part])
            projected[:, part] = term if k == 0 else projected[:, part] + term

        tiles(work)

    project(0)
    project(1)
    for n in range(4):
        forward(n)
    project(2)
    for n in range(4, 8):
        forward(n)

    @pl.loop(0, 8)
    def _(j):
        part = pl.ds(pl.multiple_of(j * 32, 32), 32)
        wide = projected[part, :]
        gate, upper = wide[:, :HID], wide[:, HID:]
        active[part, :] = ((upper + 1.0) * gate * jax.nn.sigmoid(1.702 * gate)).astype(BF16)

    back = (slot_of(ci) == ri).astype(BF16)
    active[...] = nn(back, active[...]).astype(BF16)

    def finish(part):
        rows = nn(active[...], down_w[:, part]).astype(BF16)
        expert_out[:, :, part] = rows.reshape(128, 2, rows.shape[1])

    tiles(finish)

    for n in range(8):
        further[n].wait_recv()
        across.append(pass_on(n, lax.rem(z + 2, 4), 6, twin))
    for copy in across:
        copy.wait()
    for copy in first[1:] + upward + downward + further:
        copy.wait_send()
    for copy in small:
        copy.wait()


TILE = 512


def exchange(
    queries, fresh, pages, owner, slot, count, hidden, gain, ids, prob, gate_up, down_proj
):
    vmem = pl.BlockSpec(memory_space=pltpu.VMEM)
    anywhere = pl.BlockSpec(memory_space=pl.ANY)
    dma = pltpu.SemaphoreType.DMA
    return pl.pallas_call(
        exchange_kernel,
        out_shape=(
            jax.ShapeDtypeStruct((16, ROWS, HEAD_COLUMNS), BF16),
            jax.ShapeDtypeStruct((16, ROWS, 2 * HEAD_WIDTH), BF16),
            jax.ShapeDtypeStruct((2, N_EP * PAGES, PAGE_TOKENS, 2 * HEAD_WIDTH), BF16),
            jax.ShapeDtypeStruct((2, 4, 2, 128), jnp.int32),
            jax.ShapeDtypeStruct((4, N_SEQ, PROMPTS), jnp.int32),
            jax.ShapeDtypeStruct((128, 2, D), BF16),
            jax.ShapeDtypeStruct((ROWS, 256), F32),
        ),
        in_specs=[vmem] * 10 + [anywhere] * 2,
        out_specs=(anywhere,) * 5 + (vmem, vmem),
        scratch_shapes=[
            pltpu.VMEM((KEY_VALUE_HEADS, PAGES, PAGE_TOKENS, 2 * HEAD_WIDTH), BF16),
            pltpu.VMEM((KEY_VALUE_HEADS, ROWS, 2 * HEAD_WIDTH), BF16),
            pltpu.VMEM((4, 2, 128), jnp.int32),
            *[pltpu.VMEM((16, 16, columns), BF16) for _, columns in PARTS * 2],
            *[pltpu.VMEM((8, 32, columns), BF16) for _, columns in PARTS * 2],
            pltpu.VMEM((D, 2 * HID), BF16),
            pltpu.VMEM((HID, D), BF16),
            pltpu.VMEM((256, 2 * HID), F32),
            pltpu.VMEM((256, HID), BF16),
            dma((16,)), dma((16,)), dma((16,)), dma((16,)), dma((8,)), dma((8,)),
            dma((24,)), dma((24,)), dma((32,)), dma((32,)), dma((4,)), dma((4,)),
            dma((48,)), dma((48,)), dma((24,)), dma((24,)), dma((11,)), dma((6,)),
        ],
        compiler_params=pltpu.CompilerParams(
            collective_id=1, has_side_effects=True, vmem_limit_bytes=56 << 20
        ),
        name="exchange",
    )(queries, fresh, pages, owner, slot, count, hidden, gain, ids, prob, gate_up, down_proj)


BK = 1024
GK = 2048
KEYS = 2 * NPS * PAGE_TOKENS
UNITS = 4
CHUNKS = 4
COLS = 256
VROWS = 80


def values_of(rows):
    pick = (iota((VROWS, 128), 0) + HEAD_WIDTH == iota((VROWS, 128), 1)).astype(BF16)
    moved = nt(pick, rows)
    return jnp.where(iota(moved.shape, 0) >= HEAD_WIDTH, 1.0, moved).astype(BF16)


def score_kernel(
    tables, counts, sinks, q_all, f_all, pool, o_ref, lse_ref,
    kv, vt, qs, limit_ref, m_ref, acc, sorted_out, s0, s1, places, lengths,
):
    y = lax.axis_index("seq")
    outer_pair = jnp.logical_or(y == 0, y == 3)
    sink_row = sinks[0:1, :]
    i0 = iota((128, 128), 0)
    i1 = iota((128, 128), 1)
    lane_row = lax.rem(iota((128, COLS), 1), ROWS).astype(F32)

    def ordering(e):
        lane = iota((PROMPTS, 128), 1)
        copies = (iota((PROMPTS, 128), 0) == lax.div(lax.rem(lane, ROWS), SCORED_STEPS)).astype(F32)
        wide = nn(counts[e].astype(F32), copies, HIGHEST)
        mine = lax.div(iota((N_SEQ, 128), 1), ROWS) == iota((N_SEQ, 128), 0)
        c = jnp.sum(jnp.where(mine, wide, 0.0), axis=0, keepdims=True)
        n_row = jnp.where(
            outer_pair,
            jnp.minimum(c, 256.0) + jnp.maximum(c - 768.0, 0.0),
            jnp.clip(c - 256.0, 0.0, 512.0),
        )
        n_col = jnp.sum(jnp.where(i0 == i1, n_row, 0.0), axis=1, keepdims=True)
        behind = jnp.logical_or(n_row > n_col, jnp.logical_and(n_col == n_row, i1 < i0))
        pos_col = jnp.sum(jnp.where(behind, 1.0, 0.0), axis=1, keepdims=True)
        return n_row, n_col, pos_col

    for e in range(UNITS):
        n_row, n_col, pos_col = ordering(e)
        places[e] = pos_col
        ahead = jnp.logical_or(n_col > n_row, jnp.logical_and(n_col == n_row, i0 < i1))
        pos_row = jnp.sum(jnp.where(ahead, 1.0, 0.0), axis=0, keepdims=True)
        perm = (pos_row == i0.astype(F32)).astype(BF16)
        q_sorted = nn(perm, q_all[e * 4 : e * 4 + 4].reshape(128, HEAD_COLUMNS)) * 0.125
        q_sorted = q_sorted.astype(BF16)
        f_sorted = nn(perm, f_all[e * 4 : e * 4 + 4].reshape(128, 128)).astype(BF16)
        none = jnp.zeros((ROWS, HEAD_WIDTH), BF16)
        for ch in range(CHUNKS):
            u = e * CHUNKS + ch
            for g in range(GROUP):
                piece = q_sorted[ch * ROWS : (ch + 1) * ROWS, g * HEAD_WIDTH : (g + 1) * HEAD_WIDTH]
                qs[u, g * ROWS : (g + 1) * ROWS, :] = jnp.concatenate([piece, none], axis=1)
            member = pos_col == lane_row + float(ch * ROWS)
            limit = jnp.sum(jnp.where(member, n_col, 0.0), axis=0, keepdims=True) * PAGE_TOKENS
            limit_ref[u] = jnp.broadcast_to(limit, (8, COLS))
            lengths[u] = jnp.max(limit).astype(jnp.int32)
            rows = f_sorted[ch * ROWS : (ch + 1) * ROWS, :]
            s = nt(rows, qs[u])
            ki = iota((ROWS, COLS), 0)
            ri = lax.rem(iota((ROWS, COLS), 1), ROWS)
            seen = jnp.logical_and(
                lax.div(ki, SCORED_STEPS) == lax.div(ri, SCORED_STEPS), ki <= ri
            )
            s = jnp.where(seen, s, NEGATIVE)
            m0 = jnp.maximum(jnp.max(s, axis=0, keepdims=True), sink_row)
            p = jnp.exp(s - m0).astype(BF16)
            start = nn(values_of(rows), p)
            start = start + jnp.where(
                iota((VROWS, COLS), 0) >= HEAD_WIDTH, jnp.exp(sink_row - m0), 0.0
            )
            m_ref[u] = jnp.broadcast_to(jnp.where(outer_pair, m0, FLOOR), (8, COLS))
            acc[u] = jnp.where(outer_pair, start, 0.0)

    def unit(e, carry):
        def gather(kb, carry):
            p0 = kb * (GK // PAGE_TOKENS)
            ss = lax.div(p0, NPS)
            lane = lax.div(lax.rem(p0, NPS), 2)
            rows = [
                pool[tables[ss, e, i % 2, lane + i // 2] + ss * (N_EP * PAGES)]
                for i in range(GK // PAGE_TOKENS)
            ]
            for i in range(GK // BK):
                part = rows[i * (BK // PAGE_TOKENS) : (i + 1) * (BK // PAGE_TOKENS)]
                found = jnp.concatenate(part, axis=0)
                kv[pl.ds(pl.multiple_of(kb * GK + i * BK, BK), BK), :] = found
                vt[kb * (GK // BK) + i] = values_of(found)
            return carry

        lax.fori_loop(0, lax.div(lengths[e * CHUNKS] + (GK - 1), GK), gather, 0)

        key = iota((BK, COLS), 0).astype(F32)

        def produce(store, u, kb):
            keys = kv[pl.ds(pl.multiple_of(kb * BK, BK), BK), :]
            s = nt(keys, qs[u])
            limit = limit_ref[u][0:1, :] - (kb * BK).astype(F32)
            s = jnp.where(key < limit, s, NEGATIVE)
            store[...] = s
            return jnp.max(s, axis=0, keepdims=True)

        def absorb(store, u, kb, top):
            before = m_ref[u][0:1, :]
            after = jnp.maximum(before, top)
            p = jnp.exp(store[...] - after).astype(BF16)
            acc[u] = acc[u] * jnp.exp(before - after) + nn(vt[kb], p)
            m_ref[u] = jnp.broadcast_to(after, (8, COLS))

        def chunk(ch, top):
            u = e * CHUNKS + ch
            count = lax.div(lengths[u] + (BK - 1), BK)
            after_u = e * CHUNKS + jnp.minimum(ch + 1, CHUNKS - 1)

            def pair(i, top):
                last = 2 * i + 2 >= count
                next_top = produce(s1, u, 2 * i + 1)
                absorb(s0, u, 2 * i, top)
                top = produce(s0, jnp.where(last, after_u, u), jnp.where(last, 0, 2 * i + 2))
                absorb(s1, u, 2 * i + 1, next_top)
                return top

            top = lax.fori_loop(0, lax.div(count, 2), pair, top)

            def odd(top):
                absorb(s0, u, count - 1, top)
                return produce(s0, after_u, jnp.int32(0))

            return lax.cond(lax.rem(count, 2) == 1, odd, lambda top: top, top)

        used = sum([(lengths[e * CHUNKS + ch] > 0).astype(jnp.int32) for ch in range(CHUNKS)])

        @pl.when(used > 0)
        def _():
            top = produce(s0, e * CHUNKS, jnp.int32(0))
            lax.fori_loop(0, used, chunk, top)

        return carry

    lax.fori_loop(0, UNITS, unit, 0)

    for e in range(UNITS):
        pos_col = places[e]
        perm_t = (pos_col == i1.astype(F32)).astype(BF16)
        lse = jnp.zeros((8, 128), F32)
        for ch in range(CHUNKS):
            u = e * CHUNKS + ch
            total = jnp.maximum(acc[u][HEAD_WIDTH : HEAD_WIDTH + 1, :], 1e-30)
            out = acc[u][0:HEAD_WIDTH, :] / total
            padded = jnp.concatenate([out, jnp.zeros_like(out)], axis=0)
            turned = padded.T.astype(BF16)
            for g in range(GROUP):
                sorted_out[e, ch * ROWS : (ch + 1) * ROWS, g * HEAD_WIDTH : (g + 1) * HEAD_WIDTH] = (
                    turned[g * ROWS : (g + 1) * ROWS, 0:HEAD_WIDTH]
                )
            row = m_ref[u][0:1, :] + jnp.log(total)
            mine = lax.div(iota((8, COLS), 1), ROWS) == iota((8, COLS), 0)
            member = (pos_col == lane_row + float(ch * ROWS)).astype(F32)
            lse = lse + nt(jnp.where(mine, row, 0.0), member, HIGHEST)
        lse_ref[e] = lse
        o_ref[e] = nn(perm_t, sorted_out[e]).astype(BF16)


def score(tables, counts, sinks, q_all, f_all, pool):
    vmem = pl.BlockSpec(memory_space=pltpu.VMEM)
    return pl.pallas_call(
        score_kernel,
        out_shape=(
            jax.ShapeDtypeStruct((UNITS, 128, HEAD_COLUMNS), BF16),
            jax.ShapeDtypeStruct((UNITS, 8, 128), F32),
        ),
        in_specs=[pl.BlockSpec(memory_space=pltpu.SMEM)] + [vmem] * 5,
        out_specs=(vmem, vmem),
        scratch_shapes=[
            pltpu.VMEM((KEYS, 128), BF16),
            pltpu.VMEM((KEYS // BK, VROWS, BK), BF16),
            pltpu.VMEM((UNITS * CHUNKS, COLS, 128), BF16),
            pltpu.VMEM((UNITS * CHUNKS, 8, COLS), F32),
            pltpu.VMEM((UNITS * CHUNKS, 8, COLS), F32),
            pltpu.VMEM((UNITS * CHUNKS, VROWS, COLS), F32),
            pltpu.VMEM((UNITS, 128, HEAD_COLUMNS), BF16),
            pltpu.VMEM((BK, COLS), F32),
            pltpu.VMEM((BK, COLS), F32),
            pltpu.VMEM((UNITS, 128, 1), F32),
            pltpu.SMEM((UNITS * CHUNKS,), jnp.int32),
        ],
        compiler_params=pltpu.CompilerParams(vmem_limit_bytes=40 << 20),
        cost_estimate=pl.CostEstimate(
            flops=25_000_000_000, bytes_accessed=8_000_000, transcendentals=20_000_000
        ),
        name="score",
    )(tables, counts, sinks, q_all, f_all, pool)


def merge_kernel(
    o_ref, lse_ref, share_ref, rows_ref, out_ref, mix_ref, o_all, lse_all, o_send, o_recv, l_send, l_recv, local,
):
    y, z, x, c = place()

    def at(dy, dx):
        return device(lax.rem(y + dy, 4), z, lax.rem(x + dx, 4), c)

    plane = [(dy, dx) for dy in range(4) for dx in range(4) if (dy, dx) != (0, 0)]
    barrier = pltpu.get_barrier_semaphore()
    for dy, dx in plane:
        pl.semaphore_signal(barrier, inc=1, device_id=at(dy, dx), device_id_type=MESH)
    pl.semaphore_wait(barrier, len(plane))
    inner_pair = jnp.logical_or(y == 1, y == 2).astype(jnp.int32)
    slot = inner_pair * 8 + head_of(y, x)
    copies = []
    for dy in range(4):
        for dx in range(4):
            n = dy * 4 + dx
            q = lax.rem(y + dy, 4)
            e = lax.rem(x + dx, 4)
            o_source = o_ref.at[e, pl.ds(pl.multiple_of(q * ROWS, ROWS), ROWS)]
            if n == 0:
                pair = [
                    pltpu.make_async_copy(o_source, o_all.at[slot], local.at[0]),
                    pltpu.make_async_copy(lse_ref.at[e], lse_all.at[slot], local.at[1]),
                ]
            else:
                pair = [
                    pltpu.make_async_remote_copy(
                        o_source, o_all.at[slot], o_send.at[n], o_recv.at[n],
                        device_id=at(dy, dx), device_id_type=MESH,
                    ),
                    pltpu.make_async_remote_copy(
                        lse_ref.at[e], lse_all.at[slot], l_send.at[n], l_recv.at[n],
                        device_id=at(dy, dx), device_id_type=MESH,
                    ),
                ]
            for copy in pair:
                copy.start()
            copies.extend(pair)

    share = share_ref[...]
    high = share.astype(BF16)
    low = (share - high.astype(F32)).astype(BF16)
    rows = rows_ref[...].reshape(256, D)
    mix_ref[...] = (nn(high, rows) + nn(low, rows)).astype(BF16)

    for copy in copies:
        copy.wait()
    mine = (iota((ROWS, 128), 1) == iota((ROWS, 128), 0) + y * ROWS).astype(F32)
    logs = nt(mine, lse_all[...].reshape(128, 128), HIGHEST)
    log0, log1 = logs[:, :64], logs[:, 64:]
    top = jnp.maximum(log0, log1)
    w0, w1 = jnp.exp(log0 - top), jnp.exp(log1 - top)
    share0, share1 = w0 / (w0 + w1), w1 / (w0 + w1)
    parts = []
    for share in (share0, share1):
        high = share.astype(BF16)
        parts.append((high, (share - high.astype(F32)).astype(BF16)))
    for h in range(KEY_VALUE_HEADS):
        shape = (64, HEAD_COLUMNS)
        spread = (iota(shape, 0) == lax.div(iota(shape, 1), HEAD_WIDTH) + h * GROUP).astype(BF16)
        wide = [nn(high, spread) + nn(low, spread) for high, low in parts]
        result = wide[0] * o_all[h].astype(F32) + wide[1] * o_all[8 + h].astype(F32)
        out_ref[:, h * HEAD_COLUMNS : (h + 1) * HEAD_COLUMNS] = result.astype(BF16)


def merge(o, lse, share, rows):
    vmem = pl.BlockSpec(memory_space=pltpu.VMEM)
    dma = pltpu.SemaphoreType.DMA
    return pl.pallas_call(
        merge_kernel,
        out_shape=(
            jax.ShapeDtypeStruct((ROWS, QUERY_HEADS * HEAD_WIDTH), BF16),
            jax.ShapeDtypeStruct((ROWS, D), BF16),
        ),
        in_specs=[vmem] * 4,
        out_specs=(vmem, vmem),
        scratch_shapes=[
            pltpu.VMEM((16, ROWS, HEAD_COLUMNS), BF16),
            pltpu.VMEM((16, 8, 128), F32),
            dma((16,)), dma((16,)), dma((16,)), dma((16,)), dma((2,)),
        ],
        compiler_params=pltpu.CompilerParams(
            collective_id=2, has_side_effects=True, vmem_limit_bytes=16 << 20
        ),
        name="merge",
    )(o, lse, share, rows)


def by_prefix(table):
    return table[0].T.reshape(2, N_EP, NPS // 2).transpose(1, 0, 2)


def per_device(
    queries, fresh_key_values, key_value_pages, page_owner, page_slot, page_count, sinks,
    hidden, norm_gain, expert_ids, gate_prob, gate_up, down_proj,
):
    y, z, x, c = place()

    q_all, f_all, pool, tables, counts, result, share = exchange(
        queries.reshape(ROWS, QUERY_HEADS * HEAD_WIDTH),
        fresh_key_values.reshape(ROWS, 2 * KEY_VALUE_HEADS * HEAD_WIDTH),
        key_value_pages.reshape(PAGES * PAGE_TOKENS, 2 * KEY_VALUE_HEADS * HEAD_WIDTH),
        by_prefix(page_owner),
        by_prefix(page_slot),
        page_count,
        hidden.reshape(ROWS, D),
        norm_gain.reshape(1, D),
        expert_ids[0].transpose(1, 2, 0),
        gate_prob[0].transpose(1, 2, 0),
        gate_up,
        down_proj,
    )
    returned = lax.all_to_all(result, ("seq", "ep"), split_axis=0, concat_axis=0, tiled=True)
    head_sinks = lax.dynamic_slice_in_dim(sinks, head_of(y, x) * GROUP, GROUP)
    sink_rows = jnp.broadcast_to(jnp.repeat(head_sinks, ROWS)[None, :], (8, COLS))
    o, lse = score(
        tables, counts, sink_rows, q_all, f_all,
        pool.reshape(2 * N_EP * PAGES, PAGE_TOKENS, 2 * HEAD_WIDTH),
    )
    attention, mixture = merge(o, lse, share, returned)
    return (attention.reshape(queries.shape), mixture.reshape(hidden.shape))


def solution(mesh):
    return jax.shard_map(
        per_device,
        mesh=mesh,
        in_specs=(
            P("seq", "ep", None, None),
            P("seq", "ep", None, None),
            P("seq", "ep", None, None),
            P("seq", None, None),
            P("seq", None, None),
            P(None, "ep"),
            P(),
            P("seq", "ep", None, None),
            P(),
            P("seq", "ep", None, None),
            P("seq", "ep", None, None),
            P(("seq", "ep"), None, None),
            P(("seq", "ep"), None, None),
        ),
        out_specs=(P("seq", "ep", None, None), P("seq", "ep", None, None)),
        check_vma=False,
    )
```

```python
import jax
import jax.numpy as jnp
from jax import lax
from jax.experimental import pallas as pl
from jax.experimental.pallas import tpu as pltpu
from jax.sharding import PartitionSpec as P

D = 2880
QUERY_HEADS = 64
KEY_VALUE_HEADS = 8
GROUP = QUERY_HEADS // KEY_VALUE_HEADS
HEAD_WIDTH = 64
TOPK = 4
HID = 1440
SCORED_STEPS = 4
PAGE_TOKENS = 16
NPS = 256
PAGES = 24
PROMPTS = 8
N_SEQ = 4
N_EP = 32
ROWS = PROMPTS * SCORED_STEPS
HEAD_COLUMNS = GROUP * HEAD_WIDTH
NEGATIVE = -1e30
FLOOR = -1e29
EPSILON = 1e-05
MESH = pl.DeviceIdType.MESH
F32 = jnp.float32
BF16 = jnp.bfloat16
HIGHEST = lax.Precision.HIGHEST


def place():
    y = lax.axis_index("seq")
    ep = lax.axis_index("ep")
    return y, lax.div(ep, 8), lax.rem(lax.div(ep, 2), 4), lax.rem(ep, 2)


def device(y, z, x, c):
    return (y, z * 8 + x * 2 + c)


def head_of(y, x):
    return lax.div(y, 2) * 4 + x


def nt(a, b, precision=None):
    return lax.dot_general(
        a, b, (((1,), (1,)), ((), ())), preferred_element_type=F32, precision=precision
    )


def nn(a, b, precision=None):
    return lax.dot_general(
        a, b, (((1,), (0,)), ((), ())), preferred_element_type=F32, precision=precision
    )


def iota(shape, axis):
    return lax.broadcasted_iota(jnp.int32, shape, axis)


PARTS = ((0, 1024), (1024, 1024), (2048, D - 2048))


def route(id_ref, prob_ref):
    i0 = iota((128, 128), 0)
    i1 = iota((128, 128), 1)
    copies = (iota((8, 128), 0) == lax.rem(iota((8, 128), 1), 8)).astype(F32)
    group = lax.div(iota((TOPK, 128), 1), 8)

    def as_row(ref):
        row = jnp.zeros((1, 128), F32)
        for t in range(SCORED_STEPS):
            wide = nn(ref[t].astype(F32), copies, HIGHEST)
            mine = group == iota((TOPK, 128), 0) + t * TOPK
            row = row + jnp.sum(jnp.where(mine, wide, 0.0), axis=0, keepdims=True)
        return row

    ids = as_row(id_ref)
    column = jnp.sum(jnp.where(i0 == i1, ids, 0.0), axis=1, keepdims=True)
    earlier = jnp.logical_and(column == ids, i0 < i1)
    rank = jnp.sum(jnp.where(earlier, 1.0, 0.0), axis=0, keepdims=True)
    slots = iota((256, 128), 0).astype(F32) == 2.0 * ids + rank

    def token(a):
        return lax.rem(a, 8) * SCORED_STEPS + lax.div(a, 32)

    owner_token = (token(iota((128, ROWS), 0)) == iota((128, ROWS), 1)).astype(BF16)
    mine = token(iota((ROWS, 128), 1)) == iota((ROWS, 128), 0)
    share = nt(jnp.where(mine, as_row(prob_ref), 0.0), slots.astype(F32), HIGHEST)
    return slots.astype(BF16), owner_token, share


def exchange_kernel(
    q_ref, f_ref, page_ref, owner_ref, slot_ref, count_ref, hidden_ref, gain_ref, id_ref, prob_ref,
    up_ref, down_ref,
    q_all, f_all, pool, tables, counts, expert_out, share_ref,
    relay, f_relay, q_rows, table_ref, out0, out1, out2, mid0, mid1, mid2, sorted0, sorted1, sorted2,
    in0, in1, in2, up_w, down_w, projected, active,
    q_send, q_recv, f_send, f_recv, a_send, a_recv, z_send, z_recv, c_send, c_recv,
    i_send, i_recv, d_send, d_recv, e_send, e_recv, local, w_sem,
):
    y, z, x, c = place()
    mate = 3 - y
    rows_out, rows_mid = (out0, out1, out2), (mid0, mid1, mid2)
    rows_sorted, rows_in = (sorted0, sorted1, sorted2), (in0, in1, in2)

    def at(dy, dx):
        return device(lax.rem(y + dy, 4), z, lax.rem(x + dx, 4), c)

    plane = [(dy, dx) for dy in range(4) for dx in range(4) if (dy, dx) != (0, 0)]
    up = device(y, lax.rem(z + 1, 4), x, c)
    down = device(y, lax.rem(z + 3, 4), x, c)
    twin = device(y, z, x, 1 - c)

    def beside(dy, dz):
        return device(lax.rem(y + dy, 4), lax.rem(z + dz, 4), x, c)

    def around(dx, dc):
        return device(y, z, lax.rem(x + dx, 4), lax.rem(c + dc, 2))

    peers = [at(dy, dx) for dy, dx in plane]
    peers += [beside(dy, dz) for dy in range(4) for dz in range(1, 4)]
    peers += [around(dx, 1) for dx in range(4)]
    barrier = pltpu.get_barrier_semaphore()
    for peer in peers:
        pl.semaphore_signal(barrier, inc=1, device_id=peer, device_id_type=MESH)

    weights = []
    for n in range(4):
        part = pl.ds(n * (D // 4), D // 4)
        weights.append(pltpu.make_async_copy(up_ref.at[0, part], up_w.at[part], w_sem.at[n]))
    for n in range(2):
        part = pl.ds(n * (HID // 2), HID // 2)
        weights.append(pltpu.make_async_copy(down_ref.at[0, part], down_w.at[part], w_sem.at[4 + n]))
    for copy in weights:
        copy.start()

    fresh = f_ref[...].reshape(ROWS, f_ref.shape[2])
    for h in range(KEY_VALUE_HEADS):
        low, high = h * HEAD_WIDTH, (h + 1) * HEAD_WIDTH
        split = KEY_VALUE_HEADS * HEAD_WIDTH
        rows = jnp.concatenate(
            [page_ref[:, low:high], page_ref[:, split + low : split + high]], axis=1
        )
        relay[h] = rows.reshape(PAGES, PAGE_TOKENS, 2 * HEAD_WIDTH)
        f_relay[h] = jnp.concatenate(
            [fresh[:, low:high], fresh[:, split + low : split + high]], axis=1
        )
    for xx in range(4):
        e = z * 8 + xx * 2 + c
        table_ref[xx] = owner_ref[e] * PAGES + slot_ref[e]

    pl.semaphore_wait(barrier, len(peers))

    def spot(segment_slot, zz, xx, cc):
        return pool.at[segment_slot, pl.ds((zz * 8 + xx * 2 + cc) * PAGES, PAGES)]

    order = [(0, 0), (0, 1), (0, 3), (1, 0), (1, 1), (1, 3), (0, 2), (1, 2)]
    first = []
    for n, (p, dx) in enumerate(order):
        yy = y if p == 0 else mate
        xx = lax.rem(x + dx, 4)
        target = spot(lax.div(y, 2), z, x, c)
        source = relay.at[head_of(yy, xx)]
        if (p, dx) == (0, 0):
            copy = pltpu.make_async_copy(source, target, local.at[0])
        else:
            copy = pltpu.make_async_remote_copy(
                source, target, a_send.at[n], a_recv.at[n],
                device_id=device(yy, z, xx, c), device_id_type=MESH,
            )
        copy.start()
        first.append(copy)

    small = []
    mine = pltpu.make_async_copy(table_ref, tables.at[lax.div(y, 2)], local.at[1])
    mine.start()
    small.append(mine)
    mine = pltpu.make_async_copy(count_ref, counts.at[x], local.at[2])
    mine.start()
    small.append(mine)
    other = pltpu.make_async_remote_copy(
        table_ref, tables.at[lax.div(y, 2)], i_send.at[0], i_recv.at[0],
        device_id=device(mate, z, x, c), device_id_type=MESH,
    )
    other.start()
    small.append(other)
    for dx in range(1, 4):
        other = pltpu.make_async_remote_copy(
            count_ref, counts.at[x], i_send.at[dx], i_recv.at[dx],
            device_id=at(0, dx), device_id_type=MESH,
        )
        other.start()
        small.append(other)

    h32 = hidden_ref[...].reshape(ROWS, D).astype(F32)
    scale = lax.rsqrt(jnp.mean(h32 * h32, axis=-1, keepdims=True) + EPSILON)
    normed = (h32 * scale * gain_ref[...].reshape(1, D)).astype(BF16)
    slots, owner_token, share = route(id_ref, prob_ref)
    share_ref[...] = share
    spread = nn(slots, owner_token).astype(BF16)
    for k, (first_column, columns) in enumerate(PARTS):
        piece = normed[:, first_column : first_column + columns]
        rows_out[k][...] = nn(spread, piece).astype(BF16).reshape(16, 16, columns)
    routed = []
    for k in range(len(PARTS)):
        for dy in range(4):
            for dz in range(4):
                n = dy * 4 + dz
                source = rows_out[k].at[lax.rem(y + dy, 4) * 4 + lax.rem(z + dz, 4)]
                target = rows_mid[k].at[y * 4 + z]
                if n == 0:
                    copy = pltpu.make_async_copy(source, target, local.at[5 + 2 * k])
                else:
                    copy = pltpu.make_async_remote_copy(
                        source, target, d_send.at[k * 16 + n], d_recv.at[k * 16 + n],
                        device_id=beside(dy, dz), device_id_type=MESH,
                    )
                copy.start()
                routed.append(copy)

    def chunk(n):
        p, dx = order[n]
        yy = y if p == 0 else mate
        return lax.div(yy, 2), lax.rem(x - dx + 4, 4)

    def pass_on(n, zz, way, peer):
        segment_slot, xx = chunk(n)
        block = spot(segment_slot, zz, xx, c)
        sends, recvs = (c_send, c_recv) if way >= 3 else (z_send, z_recv)
        number = (way - 3 if way >= 3 else way) * 8 + n
        copy = pltpu.make_async_remote_copy(
            block, block, sends.at[number], recvs.at[number],
            device_id=peer, device_id_type=MESH,
        )
        copy.start()
        return copy

    upward, downward, further, across = [], [], [], []
    for n in range(8):
        if n == 0:
            first[n].wait()
        else:
            first[n].wait_recv()
        upward.append(pass_on(n, z, 0, up))
        downward.append(pass_on(n, z, 1, down))
        across.append(pass_on(n, z, 3, twin))

    ri = iota((256, 256), 0)
    ci = iota((256, 256), 1)

    def slot_of(i):
        return lax.div(lax.rem(i, 32), 2) * 16 + lax.div(i, 32) * 2 + lax.rem(i, 2)

    regroup = (slot_of(ri) == ci).astype(BF16)
    delivered = [[], [], []]
    for k, (_, columns) in enumerate(PARTS):
        for copy in routed[k * 16 : (k + 1) * 16]:
            copy.wait()
        moved = nn(regroup, rows_mid[k][...].reshape(256, columns)).astype(BF16)
        rows_sorted[k][...] = moved.reshape(8, 32, columns)
        for dx in range(4):
            for dc in range(2):
                n = dx * 2 + dc
                source = rows_sorted[k].at[lax.rem(x + dx, 4) * 2 + lax.rem(c + dc, 2)]
                target = rows_in[k].at[x * 2 + c]
                if n == 0:
                    copy = pltpu.make_async_copy(source, target, local.at[6 + 2 * k])
                else:
                    copy = pltpu.make_async_remote_copy(
                        source, target, e_send.at[k * 8 + n], e_recv.at[k * 8 + n],
                        device_id=around(dx, dc), device_id_type=MESH,
                    )
                copy.start()
                delivered[k].append(copy)


    q_rows[...] = q_ref[...].reshape(ROWS, q_ref.shape[2])
    for dy in range(4):
        for dx in range(4):
            n = dy * 4 + dx
            h = head_of(lax.rem(y + dy, 4), lax.rem(x + dx, 4))
            q_source = q_rows.at[:, pl.ds(pl.multiple_of(h * HEAD_COLUMNS, HEAD_COLUMNS), HEAD_COLUMNS)]
            f_source = f_relay.at[h]
            slot = x * 4 + y
            if n == 0:
                copies = [
                    pltpu.make_async_copy(q_source, q_all.at[slot], local.at[3]),
                    pltpu.make_async_copy(f_source, f_all.at[slot], local.at[4]),
                ]
            else:
                copies = [
                    pltpu.make_async_remote_copy(
                        q_source, q_all.at[slot], q_send.at[n], q_recv.at[n],
                        device_id=at(dy, dx), device_id_type=MESH,
                    ),
                    pltpu.make_async_remote_copy(
                        f_source, f_all.at[slot], f_send.at[n], f_recv.at[n],
                        device_id=at(dy, dx), device_id_type=MESH,
                    ),
                ]
            for copy in copies:
                copy.start()
            small.extend(copies)

    def forward(n):
        upward[n].wait_recv()
        if n % 2 == 0:
            further.append(pass_on(n, lax.rem(z + 3, 4), 2, up))
        across.append(pass_on(n, lax.rem(z + 3, 4), 4, twin))
        downward[n].wait_recv()
        if n % 2 == 1:
            further.append(pass_on(n, lax.rem(z + 1, 4), 2, down))
        across.append(pass_on(n, lax.rem(z + 1, 4), 5, twin))

    for copy in weights:
        copy.wait()

    def tiles(work):
        @pl.loop(0, D // TILE)
        def _(j):
            work(pl.ds(pl.multiple_of(j * TILE, TILE), TILE))

        work(pl.ds(D // TILE * TILE, D % TILE))

    def project(k):
        first_column, columns = PARTS[k]
        for copy in delivered[k]:
            copy.wait()

        def work(part):
            rows = rows_in[k][...].reshape(256, columns)
            term = nn(rows, up_w[first_column : first_column + columns, part])
            projected[:, part] = term if k == 0 else projected[:, part] + term

        tiles(work)

    project(0)
    for n in range(4):
        forward(n)
    project(1)
    for n in range(4, 8):
        forward(n)
    project(2)

    @pl.loop(0, 8)
    def _(j):
        part = pl.ds(pl.multiple_of(j * 32, 32), 32)
        wide = projected[part, :]
        gate, upper = wide[:, :HID], wide[:, HID:]
        active[part, :] = ((upper + 1.0) * gate * jax.nn.sigmoid(1.702 * gate)).astype(BF16)

    back = (slot_of(ci) == ri).astype(BF16)
    active[...] = nn(back, active[...]).astype(BF16)

    def finish(part):
        rows = nn(active[...], down_w[:, part]).astype(BF16)
        expert_out[:, :, part] = rows.reshape(128, 2, rows.shape[1])

    @pl.loop(0, 3)
    def _(j):
        finish(pl.ds(pl.multiple_of(j * TILE, TILE), TILE))

    for n in range(8):
        further[n].wait_recv()
        across.append(pass_on(n, lax.rem(z + 2, 4), 6, twin))

    @pl.loop(3, D // TILE)
    def _(j):
        finish(pl.ds(pl.multiple_of(j * TILE, TILE), TILE))

    finish(pl.ds(D // TILE * TILE, D % TILE))

    for copy in across:
        copy.wait()
    for copy in first[1:] + upward + downward + further:
        copy.wait_send()
    for copy in small:
        copy.wait()


TILE = 512


def exchange(
    queries, fresh, pages, owner, slot, count, hidden, gain, ids, prob, gate_up, down_proj
):
    vmem = pl.BlockSpec(memory_space=pltpu.VMEM)
    anywhere = pl.BlockSpec(memory_space=pl.ANY)
    dma = pltpu.SemaphoreType.DMA
    return pl.pallas_call(
        exchange_kernel,
        out_shape=(
            jax.ShapeDtypeStruct((16, ROWS, HEAD_COLUMNS), BF16),
            jax.ShapeDtypeStruct((16, ROWS, 2 * HEAD_WIDTH), BF16),
            jax.ShapeDtypeStruct((2, N_EP * PAGES, PAGE_TOKENS, 2 * HEAD_WIDTH), BF16),
            jax.ShapeDtypeStruct((2, 4, 2, 128), jnp.int32),
            jax.ShapeDtypeStruct((4, N_SEQ, PROMPTS), jnp.int32),
            jax.ShapeDtypeStruct((128, 2, D), BF16),
            jax.ShapeDtypeStruct((ROWS, 256), F32),
        ),
        in_specs=[vmem] * 10 + [anywhere] * 2,
        out_specs=(anywhere,) * 5 + (vmem, vmem),
        scratch_shapes=[
            pltpu.VMEM((KEY_VALUE_HEADS, PAGES, PAGE_TOKENS, 2 * HEAD_WIDTH), BF16),
            pltpu.VMEM((KEY_VALUE_HEADS, ROWS, 2 * HEAD_WIDTH), BF16),
            pltpu.VMEM((ROWS, QUERY_HEADS * HEAD_WIDTH), BF16),
            pltpu.VMEM((4, 2, 128), jnp.int32),
            *[pltpu.VMEM((16, 16, columns), BF16) for _, columns in PARTS * 2],
            *[pltpu.VMEM((8, 32, columns), BF16) for _, columns in PARTS * 2],
            pltpu.VMEM((D, 2 * HID), BF16),
            pltpu.VMEM((HID, D), BF16),
            pltpu.VMEM((256, 2 * HID), F32),
            pltpu.VMEM((256, HID), BF16),
            dma((16,)), dma((16,)), dma((16,)), dma((16,)), dma((8,)), dma((8,)),
            dma((24,)), dma((24,)), dma((32,)), dma((32,)), dma((4,)), dma((4,)),
            dma((48,)), dma((48,)), dma((24,)), dma((24,)), dma((11,)), dma((6,)),
        ],
        compiler_params=pltpu.CompilerParams(
            collective_id=1, has_side_effects=True, vmem_limit_bytes=56 << 20
        ),
        name="exchange",
    )(queries, fresh, pages, owner, slot, count, hidden, gain, ids, prob, gate_up, down_proj)


BK = 1024
GK = 2048
KEYS = 2 * NPS * PAGE_TOKENS
UNITS = 4
CHUNKS = 4
COLS = 256
VROWS = 80


def values_of(rows):
    pick = (iota((VROWS, 128), 0) + HEAD_WIDTH == iota((VROWS, 128), 1)).astype(BF16)
    moved = nt(pick, rows)
    return jnp.where(iota(moved.shape, 0) >= HEAD_WIDTH, 1.0, moved).astype(BF16)


def score_kernel(
    table_ref, count_ref, sinks, q_ref, f_ref, pool_ref, o_ref, lse_ref,
    tables, counts, q_all, f_all, pool,
    kv, vt, qs, limit_ref, m_ref, acc, sorted_out, s0, s1, places, lengths, sem,
):
    y = lax.axis_index("seq")
    outer_pair = jnp.logical_or(y == 0, y == 3)
    loads = [
        pltpu.make_async_copy(source, target, sem.at[n])
        for n, (source, target) in enumerate(
            [(count_ref, counts), (q_ref, q_all), (f_ref, f_all), (table_ref, tables)]
        )
    ]
    share = pool.shape[0] // 8
    for n in range(8):
        part = pl.ds(n * share, share)
        loads.append(pltpu.make_async_copy(pool_ref.at[part], pool.at[part], sem.at[4 + n]))
    for copy in loads:
        copy.start()
    for copy in loads[:3]:
        copy.wait()
    sink_row = sinks[0:1, :]
    i0 = iota((128, 128), 0)
    i1 = iota((128, 128), 1)
    lane_row = lax.rem(iota((128, COLS), 1), ROWS).astype(F32)

    def ordering(e):
        lane = iota((PROMPTS, 128), 1)
        copies = (iota((PROMPTS, 128), 0) == lax.div(lax.rem(lane, ROWS), SCORED_STEPS)).astype(F32)
        wide = nn(counts[e].astype(F32), copies, HIGHEST)
        mine = lax.div(iota((N_SEQ, 128), 1), ROWS) == iota((N_SEQ, 128), 0)
        c = jnp.sum(jnp.where(mine, wide, 0.0), axis=0, keepdims=True)
        n_row = jnp.where(
            outer_pair,
            jnp.minimum(c, 256.0) + jnp.maximum(c - 768.0, 0.0),
            jnp.clip(c - 256.0, 0.0, 512.0),
        )
        n_col = jnp.sum(jnp.where(i0 == i1, n_row, 0.0), axis=1, keepdims=True)
        behind = jnp.logical_or(n_row > n_col, jnp.logical_and(n_col == n_row, i1 < i0))
        pos_col = jnp.sum(jnp.where(behind, 1.0, 0.0), axis=1, keepdims=True)
        return n_row, n_col, pos_col

    for e in range(UNITS):
        n_row, n_col, pos_col = ordering(e)
        places[e] = pos_col
        ahead = jnp.logical_or(n_col > n_row, jnp.logical_and(n_col == n_row, i0 < i1))
        pos_row = jnp.sum(jnp.where(ahead, 1.0, 0.0), axis=0, keepdims=True)
        perm = (pos_row == i0.astype(F32)).astype(BF16)
        q_sorted = nn(perm, q_all[e * 4 : e * 4 + 4].reshape(128, HEAD_COLUMNS)) * 0.125
        q_sorted = q_sorted.astype(BF16)
        f_sorted = nn(perm, f_all[e * 4 : e * 4 + 4].reshape(128, 128)).astype(BF16)
        none = jnp.zeros((ROWS, HEAD_WIDTH), BF16)
        for ch in range(CHUNKS):
            u = e * CHUNKS + ch
            for g in range(GROUP):
                piece = q_sorted[ch * ROWS : (ch + 1) * ROWS, g * HEAD_WIDTH : (g + 1) * HEAD_WIDTH]
                qs[u, g * ROWS : (g + 1) * ROWS, :] = jnp.concatenate([piece, none], axis=1)
            member = pos_col == lane_row + float(ch * ROWS)
            limit = jnp.sum(jnp.where(member, n_col, 0.0), axis=0, keepdims=True) * PAGE_TOKENS
            limit_ref[u] = jnp.broadcast_to(limit, (8, COLS))
            lengths[u] = jnp.max(limit).astype(jnp.int32)
            rows = f_sorted[ch * ROWS : (ch + 1) * ROWS, :]
            s = nt(rows, qs[u])
            ki = iota((ROWS, COLS), 0)
            ri = lax.rem(iota((ROWS, COLS), 1), ROWS)
            seen = jnp.logical_and(
                lax.div(ki, SCORED_STEPS) == lax.div(ri, SCORED_STEPS), ki <= ri
            )
            s = jnp.where(seen, s, NEGATIVE)
            m0 = jnp.maximum(jnp.max(s, axis=0, keepdims=True), sink_row)
            p = jnp.exp(s - m0).astype(BF16)
            start = nn(values_of(rows), p)
            start = start + jnp.where(
                iota((VROWS, COLS), 0) >= HEAD_WIDTH, jnp.exp(sink_row - m0), 0.0
            )
            m_ref[u] = jnp.broadcast_to(jnp.where(outer_pair, m0, FLOOR), (8, COLS))
            acc[u] = jnp.where(outer_pair, start, 0.0)

    def unit(e, carry):
        def gather(kb, carry):
            p0 = kb * (GK // PAGE_TOKENS)
            ss = lax.div(p0, NPS)
            lane = lax.div(lax.rem(p0, NPS), 2)
            rows = [
                pool[tables[ss, e, i % 2, lane + i // 2] + ss * (N_EP * PAGES)]
                for i in range(GK // PAGE_TOKENS)
            ]
            for i in range(GK // BK):
                part = rows[i * (BK // PAGE_TOKENS) : (i + 1) * (BK // PAGE_TOKENS)]
                found = jnp.concatenate(part, axis=0)
                kv[pl.ds(pl.multiple_of(kb * GK + i * BK, BK), BK), :] = found
                vt[kb * (GK // BK) + i] = values_of(found)
            return carry

        lax.fori_loop(0, lax.div(lengths[e * CHUNKS] + (GK - 1), GK), gather, 0)

        key = iota((BK, COLS), 0).astype(F32)

        def produce(store, u, kb):
            keys = kv[pl.ds(pl.multiple_of(kb * BK, BK), BK), :]
            s = nt(keys, qs[u])
            limit = limit_ref[u][0:1, :] - (kb * BK).astype(F32)
            s = jnp.where(key < limit, s, NEGATIVE)
            store[...] = s
            return jnp.max(s, axis=0, keepdims=True)

        def absorb(store, u, kb, top):
            before = m_ref[u][0:1, :]
            after = jnp.maximum(before, top)
            p = jnp.exp(store[...] - after).astype(BF16)
            acc[u] = acc[u] * jnp.exp(before - after) + nn(vt[kb], p)
            m_ref[u] = jnp.broadcast_to(after, (8, COLS))

        def chunk(ch, top):
            u = e * CHUNKS + ch
            count = lax.div(lengths[u] + (BK - 1), BK)
            after_u = e * CHUNKS + jnp.minimum(ch + 1, CHUNKS - 1)

            def pair(i, top):
                last = 2 * i + 2 >= count
                next_top = produce(s1, u, 2 * i + 1)
                absorb(s0, u, 2 * i, top)
                top = produce(s0, jnp.where(last, after_u, u), jnp.where(last, 0, 2 * i + 2))
                absorb(s1, u, 2 * i + 1, next_top)
                return top

            top = lax.fori_loop(0, lax.div(count, 2), pair, top)

            def odd(top):
                absorb(s0, u, count - 1, top)
                return produce(s0, after_u, jnp.int32(0))

            return lax.cond(lax.rem(count, 2) == 1, odd, lambda top: top, top)

        used = sum([(lengths[e * CHUNKS + ch] > 0).astype(jnp.int32) for ch in range(CHUNKS)])

        @pl.when(used > 0)
        def _():
            top = produce(s0, e * CHUNKS, jnp.int32(0))
            lax.fori_loop(0, used, chunk, top)

        return carry

    for copy in loads[3:]:
        copy.wait()
    lax.fori_loop(0, UNITS, unit, 0)

    for e in range(UNITS):
        pos_col = places[e]
        perm_t = (pos_col == i1.astype(F32)).astype(BF16)
        lse = jnp.zeros((8, 128), F32)
        for ch in range(CHUNKS):
            u = e * CHUNKS + ch
            total = jnp.maximum(acc[u][HEAD_WIDTH : HEAD_WIDTH + 1, :], 1e-30)
            out = acc[u][0:HEAD_WIDTH, :] / total
            padded = jnp.concatenate([out, jnp.zeros_like(out)], axis=0)
            turned = padded.T.astype(BF16)
            for g in range(GROUP):
                sorted_out[e, ch * ROWS : (ch + 1) * ROWS, g * HEAD_WIDTH : (g + 1) * HEAD_WIDTH] = (
                    turned[g * ROWS : (g + 1) * ROWS, 0:HEAD_WIDTH]
                )
            row = m_ref[u][0:1, :] + jnp.log(total)
            mine = lax.div(iota((8, COLS), 1), ROWS) == iota((8, COLS), 0)
            member = (pos_col == lane_row + float(ch * ROWS)).astype(F32)
            lse = lse + nt(jnp.where(mine, row, 0.0), member, HIGHEST)
        lse_ref[e] = lse
        o_ref[e] = nn(perm_t, sorted_out[e]).astype(BF16)


def score(tables, counts, sinks, q_all, f_all, pool):
    vmem = pl.BlockSpec(memory_space=pltpu.VMEM)
    anywhere = pl.BlockSpec(memory_space=pl.ANY)
    return pl.pallas_call(
        score_kernel,
        out_shape=(
            jax.ShapeDtypeStruct((UNITS, 128, HEAD_COLUMNS), BF16),
            jax.ShapeDtypeStruct((UNITS, 8, 128), F32),
        ),
        in_specs=[anywhere, anywhere, vmem, anywhere, anywhere, anywhere],
        out_specs=(vmem, vmem),
        scratch_shapes=[
            pltpu.SMEM((2, UNITS, 2, 128), jnp.int32),
            pltpu.VMEM((UNITS, N_SEQ, PROMPTS), jnp.int32),
            pltpu.VMEM((16, ROWS, HEAD_COLUMNS), BF16),
            pltpu.VMEM((16, ROWS, 2 * HEAD_WIDTH), BF16),
            pltpu.VMEM((2 * N_EP * PAGES, PAGE_TOKENS, 2 * HEAD_WIDTH), BF16),
            pltpu.VMEM((KEYS, 128), BF16),
            pltpu.VMEM((KEYS // BK, VROWS, BK), BF16),
            pltpu.VMEM((UNITS * CHUNKS, COLS, 128), BF16),
            pltpu.VMEM((UNITS * CHUNKS, 8, COLS), F32),
            pltpu.VMEM((UNITS * CHUNKS, 8, COLS), F32),
            pltpu.VMEM((UNITS * CHUNKS, VROWS, COLS), F32),
            pltpu.VMEM((UNITS, 128, HEAD_COLUMNS), BF16),
            pltpu.VMEM((BK, COLS), F32),
            pltpu.VMEM((BK, COLS), F32),
            pltpu.VMEM((UNITS, 128, 1), F32),
            pltpu.SMEM((UNITS * CHUNKS,), jnp.int32),
            pltpu.SemaphoreType.DMA((12,)),
        ],
        compiler_params=pltpu.CompilerParams(vmem_limit_bytes=60 << 20),
        cost_estimate=pl.CostEstimate(
            flops=25_000_000_000, bytes_accessed=8_000_000, transcendentals=20_000_000
        ),
        name="score",
    )(tables, counts, sinks, q_all, f_all, pool)


def merge_kernel(
    o_ref, lse_ref, share_ref, rows_ref, out_ref, mix_ref, o_all, lse_all, o_send, o_recv, l_send, l_recv, local,
):
    y, z, x, c = place()

    def at(dy, dx):
        return device(lax.rem(y + dy, 4), z, lax.rem(x + dx, 4), c)

    plane = [(dy, dx) for dy in range(4) for dx in range(4) if (dy, dx) != (0, 0)]
    barrier = pltpu.get_barrier_semaphore()
    for dy, dx in plane:
        pl.semaphore_signal(barrier, inc=1, device_id=at(dy, dx), device_id_type=MESH)
    pl.semaphore_wait(barrier, len(plane))
    inner_pair = jnp.logical_or(y == 1, y == 2).astype(jnp.int32)
    slot = inner_pair * 8 + head_of(y, x)
    copies = []
    for dy in range(4):
        for dx in range(4):
            n = dy * 4 + dx
            q = lax.rem(y + dy, 4)
            e = lax.rem(x + dx, 4)
            o_source = o_ref.at[e, pl.ds(pl.multiple_of(q * ROWS, ROWS), ROWS)]
            if n == 0:
                pair = [
                    pltpu.make_async_copy(o_source, o_all.at[slot], local.at[0]),
                    pltpu.make_async_copy(lse_ref.at[e], lse_all.at[slot], local.at[1]),
                ]
            else:
                pair = [
                    pltpu.make_async_remote_copy(
                        o_source, o_all.at[slot], o_send.at[n], o_recv.at[n],
                        device_id=at(dy, dx), device_id_type=MESH,
                    ),
                    pltpu.make_async_remote_copy(
                        lse_ref.at[e], lse_all.at[slot], l_send.at[n], l_recv.at[n],
                        device_id=at(dy, dx), device_id_type=MESH,
                    ),
                ]
            for copy in pair:
                copy.start()
            copies.extend(pair)

    share = share_ref[...]
    high = share.astype(BF16)
    low = (share - high.astype(F32)).astype(BF16)
    rows = rows_ref[...].reshape(256, D)
    mix_ref[...] = (nn(high, rows) + nn(low, rows)).astype(BF16)

    for copy in copies:
        copy.wait()
    mine = (iota((ROWS, 128), 1) == iota((ROWS, 128), 0) + y * ROWS).astype(F32)
    logs = nt(mine, lse_all[...].reshape(128, 128), HIGHEST)
    log0, log1 = logs[:, :64], logs[:, 64:]
    top = jnp.maximum(log0, log1)
    w0, w1 = jnp.exp(log0 - top), jnp.exp(log1 - top)
    share0, share1 = w0 / (w0 + w1), w1 / (w0 + w1)
    parts = []
    for share in (share0, share1):
        high = share.astype(BF16)
        parts.append((high, (share - high.astype(F32)).astype(BF16)))
    for h in range(KEY_VALUE_HEADS):
        shape = (64, HEAD_COLUMNS)
        spread = (iota(shape, 0) == lax.div(iota(shape, 1), HEAD_WIDTH) + h * GROUP).astype(BF16)
        wide = [nn(high, spread) + nn(low, spread) for high, low in parts]
        result = wide[0] * o_all[h].astype(F32) + wide[1] * o_all[8 + h].astype(F32)
        out_ref[:, h * HEAD_COLUMNS : (h + 1) * HEAD_COLUMNS] = result.astype(BF16)


def merge(o, lse, share, rows):
    vmem = pl.BlockSpec(memory_space=pltpu.VMEM)
    dma = pltpu.SemaphoreType.DMA
    return pl.pallas_call(
        merge_kernel,
        out_shape=(
            jax.ShapeDtypeStruct((ROWS, QUERY_HEADS * HEAD_WIDTH), BF16),
            jax.ShapeDtypeStruct((ROWS, D), BF16),
        ),
        in_specs=[vmem] * 4,
        out_specs=(vmem, vmem),
        scratch_shapes=[
            pltpu.VMEM((16, ROWS, HEAD_COLUMNS), BF16),
            pltpu.VMEM((16, 8, 128), F32),
            dma((16,)), dma((16,)), dma((16,)), dma((16,)), dma((2,)),
        ],
        compiler_params=pltpu.CompilerParams(
            collective_id=2, has_side_effects=True, vmem_limit_bytes=16 << 20
        ),
        name="merge",
    )(o, lse, share, rows)


def by_prefix(table):
    return table[0].T.reshape(2, N_EP, NPS // 2).transpose(1, 0, 2)


def per_device(
    queries, fresh_key_values, key_value_pages, page_owner, page_slot, page_count, sinks,
    hidden, norm_gain, expert_ids, gate_prob, gate_up, down_proj,
):
    y, z, x, c = place()

    q_all, f_all, pool, tables, counts, result, share = exchange(
        queries[0],
        fresh_key_values[0],
        key_value_pages.reshape(PAGES * PAGE_TOKENS, 2 * KEY_VALUE_HEADS * HEAD_WIDTH),
        by_prefix(page_owner),
        by_prefix(page_slot),
        page_count,
        hidden[0],
        norm_gain,
        expert_ids[0].transpose(1, 2, 0),
        gate_prob[0].transpose(1, 2, 0),
        gate_up,
        down_proj,
    )
    returned = lax.all_to_all(result, ("seq", "ep"), split_axis=0, concat_axis=0, tiled=True)
    head_sinks = lax.dynamic_slice_in_dim(sinks, head_of(y, x) * GROUP, GROUP)
    sink_rows = jnp.broadcast_to(jnp.repeat(head_sinks, ROWS)[None, :], (8, COLS))
    o, lse = score(
        tables, counts, sink_rows, q_all, f_all,
        pool.reshape(2 * N_EP * PAGES, PAGE_TOKENS, 2 * HEAD_WIDTH),
    )
    attention, mixture = merge(o, lse, share, returned)
    return (attention.reshape(queries.shape), mixture.reshape(hidden.shape))


def solution(mesh):
    return jax.shard_map(
        per_device,
        mesh=mesh,
        in_specs=(
            P("seq", "ep", None, None),
            P("seq", "ep", None, None),
            P("seq", "ep", None, None),
            P("seq", None, None),
            P("seq", None, None),
            P(None, "ep"),
            P(),
            P("seq", "ep", None, None),
            P(),
            P("seq", "ep", None, None),
            P("seq", "ep", None, None),
            P(("seq", "ep"), None, None),
            P(("seq", "ep"), None, None),
        ),
        out_specs=(P("seq", "ep", None, None), P("seq", "ep", None, None)),
        check_vma=False,
    )
```

```python
import jax
import jax.numpy as jnp
from jax import lax
from jax.experimental import pallas as pl
from jax.experimental.pallas import tpu as pltpu
from jax.sharding import PartitionSpec as P

D = 2880
QUERY_HEADS = 64
KEY_VALUE_HEADS = 8
GROUP = QUERY_HEADS // KEY_VALUE_HEADS
HEAD_WIDTH = 64
TOPK = 4
HID = 1440
SCORED_STEPS = 4
PAGE_TOKENS = 16
NPS = 256
PAGES = 24
PROMPTS = 8
N_SEQ = 4
N_EP = 32
ROWS = PROMPTS * SCORED_STEPS
HEAD_COLUMNS = GROUP * HEAD_WIDTH
NEGATIVE = -1e30
FLOOR = -1e29
EPSILON = 1e-05
MESH = pl.DeviceIdType.MESH
F32 = jnp.float32
BF16 = jnp.bfloat16
HIGHEST = lax.Precision.HIGHEST


def place():
    y = lax.axis_index("seq")
    ep = lax.axis_index("ep")
    return y, lax.div(ep, 8), lax.rem(lax.div(ep, 2), 4), lax.rem(ep, 2)


def device(y, z, x, c):
    return (y, z * 8 + x * 2 + c)


def head_of(y, x):
    return lax.div(y, 2) * 4 + x


def nt(a, b, precision=None):
    return lax.dot_general(
        a, b, (((1,), (1,)), ((), ())), preferred_element_type=F32, precision=precision
    )


def nn(a, b, precision=None):
    return lax.dot_general(
        a, b, (((1,), (0,)), ((), ())), preferred_element_type=F32, precision=precision
    )


def iota(shape, axis):
    return lax.broadcasted_iota(jnp.int32, shape, axis)


PARTS = ((0, 1024), (1024, 1024), (2048, D - 2048))


def route(id_ref, prob_ref):
    i0 = iota((128, 128), 0)
    i1 = iota((128, 128), 1)
    copies = (iota((8, 128), 0) == lax.rem(iota((8, 128), 1), 8)).astype(F32)
    group = lax.div(iota((TOPK, 128), 1), 8)

    def as_row(ref):
        row = jnp.zeros((1, 128), F32)
        for t in range(SCORED_STEPS):
            wide = nn(ref[t].astype(F32), copies, HIGHEST)
            mine = group == iota((TOPK, 128), 0) + t * TOPK
            row = row + jnp.sum(jnp.where(mine, wide, 0.0), axis=0, keepdims=True)
        return row

    ids = as_row(id_ref)
    column = jnp.sum(jnp.where(i0 == i1, ids, 0.0), axis=1, keepdims=True)
    earlier = jnp.logical_and(column == ids, i0 < i1)
    rank = jnp.sum(jnp.where(earlier, 1.0, 0.0), axis=0, keepdims=True)
    slots = iota((256, 128), 0).astype(F32) == 2.0 * ids + rank

    def token(a):
        return lax.rem(a, 8) * SCORED_STEPS + lax.div(a, 32)

    owner_token = (token(iota((128, ROWS), 0)) == iota((128, ROWS), 1)).astype(BF16)
    mine = token(iota((ROWS, 128), 1)) == iota((ROWS, 128), 0)
    share = nt(jnp.where(mine, as_row(prob_ref), 0.0), slots.astype(F32), HIGHEST)
    return slots.astype(BF16), owner_token, share


def exchange_kernel(
    q_ref, f_ref, page_ref, owner_ref, slot_ref, count_ref, hidden_ref, gain_ref, id_ref, prob_ref,
    up_ref, down_ref,
    q_all, f_all, pool, tables, counts, expert_out, share_ref,
    relay, f_relay, q_rows, table_ref, count_rows, out0, out1, out2, mid0, mid1, mid2, sorted0, sorted1, sorted2,
    in0, in1, in2, up_w, down_w, projected, active,
    q_send, q_recv, f_send, f_recv, a_send, a_recv, z_send, z_recv, c_send, c_recv,
    i_send, i_recv, d_send, d_recv, e_send, e_recv, local, w_sem,
):
    y, z, x, c = place()
    mate = 3 - y
    rows_out, rows_mid = (out0, out1, out2), (mid0, mid1, mid2)
    rows_sorted, rows_in = (sorted0, sorted1, sorted2), (in0, in1, in2)

    def at(dy, dx):
        return device(lax.rem(y + dy, 4), z, lax.rem(x + dx, 4), c)

    plane = [(dy, dx) for dy in range(4) for dx in range(4) if (dy, dx) != (0, 0)]
    up = device(y, lax.rem(z + 1, 4), x, c)
    down = device(y, lax.rem(z + 3, 4), x, c)
    twin = device(y, z, x, 1 - c)

    def beside(dy, dz):
        return device(lax.rem(y + dy, 4), lax.rem(z + dz, 4), x, c)

    def around(dx, dc):
        return device(y, z, lax.rem(x + dx, 4), lax.rem(c + dc, 2))

    peers = [at(dy, dx) for dy, dx in plane]
    peers += [beside(dy, dz) for dy in range(4) for dz in range(1, 4)]
    peers += [around(dx, 1) for dx in range(4)]
    barrier = pltpu.get_barrier_semaphore()
    for peer in peers:
        pl.semaphore_signal(barrier, inc=1, device_id=peer, device_id_type=MESH)

    weights = []
    for n in range(4):
        part = pl.ds(n * (D // 4), D // 4)
        weights.append(pltpu.make_async_copy(up_ref.at[0, part], up_w.at[part], w_sem.at[n]))
    for n in range(2):
        part = pl.ds(n * (HID // 2), HID // 2)
        weights.append(pltpu.make_async_copy(down_ref.at[0, part], down_w.at[part], w_sem.at[4 + n]))
    for copy in weights:
        copy.start()

    fresh = f_ref[...].reshape(ROWS, f_ref.shape[2])
    for h in range(KEY_VALUE_HEADS):
        low, high = h * HEAD_WIDTH, (h + 1) * HEAD_WIDTH
        split = KEY_VALUE_HEADS * HEAD_WIDTH
        rows = jnp.concatenate(
            [page_ref[:, low:high], page_ref[:, split + low : split + high]], axis=1
        )
        relay[h] = rows.reshape(PAGES, PAGE_TOKENS, 2 * HEAD_WIDTH)
        f_relay[h] = jnp.concatenate(
            [fresh[:, low:high], fresh[:, split + low : split + high]], axis=1
        )
    for xx in range(4):
        e = z * 8 + xx * 2 + c
        pages = owner_ref[e] * PAGES + slot_ref[e]
        for half in range(2):
            lanes = slice(half * 64, half * 64 + 64)
            table_ref[xx, half : half + 1, :] = jnp.concatenate(
                [pages[0:1, lanes], pages[1:2, lanes]], axis=1
            )
    lane = iota((PROMPTS, 128), 1)
    copies = (iota((PROMPTS, 128), 0) == lax.div(lax.rem(lane, ROWS), SCORED_STEPS)).astype(F32)
    wide = nn(count_ref[...].astype(F32), copies, HIGHEST)
    mine = lax.div(iota((N_SEQ, 128), 1), ROWS) == iota((N_SEQ, 128), 0)
    wide = jnp.sum(jnp.where(mine, wide, 0.0), axis=0, keepdims=True)
    count_rows[...] = jnp.broadcast_to(wide, (8, 128))

    pl.semaphore_wait(barrier, len(peers))

    def spot(segment_slot, zz, xx, cc):
        return pool.at[segment_slot, pl.ds((zz * 8 + xx * 2 + cc) * PAGES, PAGES)]

    order = [(0, 0), (0, 1), (0, 3), (1, 0), (1, 1), (1, 3), (0, 2), (1, 2)]
    first = []
    for n, (p, dx) in enumerate(order):
        yy = y if p == 0 else mate
        xx = lax.rem(x + dx, 4)
        target = spot(lax.div(y, 2), z, x, c)
        source = relay.at[head_of(yy, xx)]
        if (p, dx) == (0, 0):
            copy = pltpu.make_async_copy(source, target, local.at[0])
        else:
            copy = pltpu.make_async_remote_copy(
                source, target, a_send.at[n], a_recv.at[n],
                device_id=device(yy, z, xx, c), device_id_type=MESH,
            )
        copy.start()
        first.append(copy)

    small = []
    mine = pltpu.make_async_copy(table_ref, tables.at[lax.div(y, 2)], local.at[1])
    mine.start()
    small.append(mine)
    mine = pltpu.make_async_copy(count_rows, counts.at[x], local.at[2])
    mine.start()
    small.append(mine)
    other = pltpu.make_async_remote_copy(
        table_ref, tables.at[lax.div(y, 2)], i_send.at[0], i_recv.at[0],
        device_id=device(mate, z, x, c), device_id_type=MESH,
    )
    other.start()
    small.append(other)
    for dx in range(1, 4):
        other = pltpu.make_async_remote_copy(
            count_rows, counts.at[x], i_send.at[dx], i_recv.at[dx],
            device_id=at(0, dx), device_id_type=MESH,
        )
        other.start()
        small.append(other)

    h32 = hidden_ref[...].reshape(ROWS, D).astype(F32)
    scale = lax.rsqrt(jnp.mean(h32 * h32, axis=-1, keepdims=True) + EPSILON)
    normed = (h32 * scale * gain_ref[...].reshape(1, D)).astype(BF16)
    slots, owner_token, share = route(id_ref, prob_ref)
    share_ref[...] = share
    spread = nn(slots, owner_token).astype(BF16)
    for k, (first_column, columns) in enumerate(PARTS):
        piece = normed[:, first_column : first_column + columns]
        rows_out[k][...] = nn(spread, piece).astype(BF16).reshape(16, 16, columns)
    routed = []
    for k in range(len(PARTS)):
        for dy in range(4):
            for dz in range(4):
                n = dy * 4 + dz
                source = rows_out[k].at[lax.rem(y + dy, 4) * 4 + lax.rem(z + dz, 4)]
                target = rows_mid[k].at[y * 4 + z]
                if n == 0:
                    copy = pltpu.make_async_copy(source, target, local.at[5 + 2 * k])
                else:
                    copy = pltpu.make_async_remote_copy(
                        source, target, d_send.at[k * 16 + n], d_recv.at[k * 16 + n],
                        device_id=beside(dy, dz), device_id_type=MESH,
                    )
                copy.start()
                routed.append(copy)

    def chunk(n):
        p, dx = order[n]
        yy = y if p == 0 else mate
        return lax.div(yy, 2), lax.rem(x - dx + 4, 4)

    def pass_on(n, zz, way, peer):
        segment_slot, xx = chunk(n)
        block = spot(segment_slot, zz, xx, c)
        sends, recvs = (c_send, c_recv) if way >= 3 else (z_send, z_recv)
        number = (way - 3 if way >= 3 else way) * 8 + n
        copy = pltpu.make_async_remote_copy(
            block, block, sends.at[number], recvs.at[number],
            device_id=peer, device_id_type=MESH,
        )
        copy.start()
        return copy

    upward, downward, further, across = [], [], [], []

    def begin(n):
        if n == 0:
            first[n].wait()
        else:
            first[n].wait_recv()
        upward.append(pass_on(n, z, 0, up))
        downward.append(pass_on(n, z, 1, down))
        across.append(pass_on(n, z, 3, twin))

    def forward(n):
        upward[n].wait_recv()
        if n % 2 == 0:
            further.append(pass_on(n, lax.rem(z + 3, 4), 2, up))
        across.append(pass_on(n, lax.rem(z + 3, 4), 4, twin))
        downward[n].wait_recv()
        if n % 2 == 1:
            further.append(pass_on(n, lax.rem(z + 1, 4), 2, down))
        across.append(pass_on(n, lax.rem(z + 1, 4), 5, twin))

    begin(0)
    begin(1)

    ri = iota((256, 256), 0)
    ci = iota((256, 256), 1)

    def slot_of(i):
        return lax.div(lax.rem(i, 32), 2) * 16 + lax.div(i, 32) * 2 + lax.rem(i, 2)

    regroup = (slot_of(ri) == ci).astype(BF16)
    delivered = [[], [], []]
    for k, (_, columns) in enumerate(PARTS):
        for copy in routed[k * 16 : (k + 1) * 16]:
            copy.wait()
        moved = nn(regroup, rows_mid[k][...].reshape(256, columns)).astype(BF16)
        rows_sorted[k][...] = moved.reshape(8, 32, columns)
        for dx in range(4):
            for dc in range(2):
                n = dx * 2 + dc
                source = rows_sorted[k].at[lax.rem(x + dx, 4) * 2 + lax.rem(c + dc, 2)]
                target = rows_in[k].at[x * 2 + c]
                if n == 0:
                    copy = pltpu.make_async_copy(source, target, local.at[6 + 2 * k])
                else:
                    copy = pltpu.make_async_remote_copy(
                        source, target, e_send.at[k * 8 + n], e_recv.at[k * 8 + n],
                        device_id=around(dx, dc), device_id_type=MESH,
                    )
                copy.start()
                delivered[k].append(copy)
        begin(2 + 2 * k)
        begin(3 + 2 * k)
        if k > 0:
            forward(2 * k - 2)
            forward(2 * k - 1)


    q_rows[...] = q_ref[...].reshape(ROWS, q_ref.shape[2])
    for dy in range(4):
        for dx in range(4):
            n = dy * 4 + dx
            h = head_of(lax.rem(y + dy, 4), lax.rem(x + dx, 4))
            q_source = q_rows.at[:, pl.ds(pl.multiple_of(h * HEAD_COLUMNS, HEAD_COLUMNS), HEAD_COLUMNS)]
            f_source = f_relay.at[h]
            slot = x * 4 + y
            if n == 0:
                copies = [
                    pltpu.make_async_copy(q_source, q_all.at[slot], local.at[3]),
                    pltpu.make_async_copy(f_source, f_all.at[slot], local.at[4]),
                ]
            else:
                copies = [
                    pltpu.make_async_remote_copy(
                        q_source, q_all.at[slot], q_send.at[n], q_recv.at[n],
                        device_id=at(dy, dx), device_id_type=MESH,
                    ),
                    pltpu.make_async_remote_copy(
                        f_source, f_all.at[slot], f_send.at[n], f_recv.at[n],
                        device_id=at(dy, dx), device_id_type=MESH,
                    ),
                ]
            for copy in copies:
                copy.start()
            small.extend(copies)

    for copy in weights:
        copy.wait()

    def tiles(work):
        @pl.loop(0, D // TILE)
        def _(j):
            work(pl.ds(pl.multiple_of(j * TILE, TILE), TILE))

        work(pl.ds(D // TILE * TILE, D % TILE))

    def project(k):
        first_column, columns = PARTS[k]
        for copy in delivered[k]:
            copy.wait()

        def work(part):
            rows = rows_in[k][...].reshape(256, columns)
            term = nn(rows, up_w[first_column : first_column + columns, part])
            projected[:, part] = term if k == 0 else projected[:, part] + term

        tiles(work)

    project(0)
    forward(4)
    forward(5)
    project(1)
    forward(6)
    forward(7)
    project(2)

    @pl.loop(0, 8)
    def _(j):
        part = pl.ds(pl.multiple_of(j * 32, 32), 32)
        wide = projected[part, :]
        gate, upper = wide[:, :HID], wide[:, HID:]
        active[part, :] = ((upper + 1.0) * gate * jax.nn.sigmoid(1.702 * gate)).astype(BF16)

    back = (slot_of(ci) == ri).astype(BF16)
    active[...] = nn(back, active[...]).astype(BF16)

    def finish(part):
        rows = nn(active[...], down_w[:, part]).astype(BF16)
        expert_out[:, :, part] = rows.reshape(128, 2, rows.shape[1])

    @pl.loop(0, 3)
    def _(j):
        finish(pl.ds(pl.multiple_of(j * TILE, TILE), TILE))

    for n in range(8):
        further[n].wait_recv()
        across.append(pass_on(n, lax.rem(z + 2, 4), 6, twin))

    @pl.loop(3, D // TILE)
    def _(j):
        finish(pl.ds(pl.multiple_of(j * TILE, TILE), TILE))

    finish(pl.ds(D // TILE * TILE, D % TILE))

    for copy in across:
        copy.wait()
    for copy in first[1:] + upward + downward + further:
        copy.wait_send()
    for copy in small:
        copy.wait()


TILE = 512


def exchange(
    queries, fresh, pages, owner, slot, count, hidden, gain, ids, prob, gate_up, down_proj
):
    vmem = pl.BlockSpec(memory_space=pltpu.VMEM)
    anywhere = pl.BlockSpec(memory_space=pl.ANY)
    dma = pltpu.SemaphoreType.DMA
    return pl.pallas_call(
        exchange_kernel,
        out_shape=(
            jax.ShapeDtypeStruct((16, ROWS, HEAD_COLUMNS), BF16),
            jax.ShapeDtypeStruct((16, ROWS, 2 * HEAD_WIDTH), BF16),
            jax.ShapeDtypeStruct((2, N_EP * PAGES, PAGE_TOKENS, 2 * HEAD_WIDTH), BF16),
            jax.ShapeDtypeStruct((2, 4, 2, 128), jnp.int32),
            jax.ShapeDtypeStruct((4, 8, 128), F32),
            jax.ShapeDtypeStruct((128, 2, D), BF16),
            jax.ShapeDtypeStruct((ROWS, 256), F32),
        ),
        in_specs=[vmem] * 10 + [anywhere] * 2,
        out_specs=(anywhere,) * 5 + (vmem, vmem),
        scratch_shapes=[
            pltpu.VMEM((KEY_VALUE_HEADS, PAGES, PAGE_TOKENS, 2 * HEAD_WIDTH), BF16),
            pltpu.VMEM((KEY_VALUE_HEADS, ROWS, 2 * HEAD_WIDTH), BF16),
            pltpu.VMEM((ROWS, QUERY_HEADS * HEAD_WIDTH), BF16),
            pltpu.VMEM((4, 2, 128), jnp.int32),
            pltpu.VMEM((8, 128), F32),
            *[pltpu.VMEM((16, 16, columns), BF16) for _, columns in PARTS * 2],
            *[pltpu.VMEM((8, 32, columns), BF16) for _, columns in PARTS * 2],
            pltpu.VMEM((D, 2 * HID), BF16),
            pltpu.VMEM((HID, D), BF16),
            pltpu.VMEM((256, 2 * HID), F32),
            pltpu.VMEM((256, HID), BF16),
            dma((16,)), dma((16,)), dma((16,)), dma((16,)), dma((8,)), dma((8,)),
            dma((24,)), dma((24,)), dma((32,)), dma((32,)), dma((4,)), dma((4,)),
            dma((48,)), dma((48,)), dma((24,)), dma((24,)), dma((11,)), dma((6,)),
        ],
        compiler_params=pltpu.CompilerParams(
            collective_id=1, has_side_effects=True, vmem_limit_bytes=56 << 20
        ),
        name="exchange",
    )(queries, fresh, pages, owner, slot, count, hidden, gain, ids, prob, gate_up, down_proj)


BK = 1024
GK = 2048
KEYS = 2 * NPS * PAGE_TOKENS
UNITS = 4
CHUNKS = 4
COLS = 256
VROWS = 80


def values_of(rows):
    pick = (iota((VROWS, 128), 0) + HEAD_WIDTH == iota((VROWS, 128), 1)).astype(BF16)
    moved = nt(pick, rows)
    return jnp.where(iota(moved.shape, 0) >= HEAD_WIDTH, 1.0, moved).astype(BF16)


def score_kernel(
    table_ref, count_ref, sinks, q_ref, f_ref, pool_ref, o_ref, lse_ref,
    tables, counts, q_all, f_all, pool,
    kv, vt, qs, limit_ref, m_ref, acc, sorted_out, s0, s1, places, lengths, sem,
):
    y = lax.axis_index("seq")
    outer_pair = jnp.logical_or(y == 0, y == 3)
    loads = [
        pltpu.make_async_copy(source, target, sem.at[n])
        for n, (source, target) in enumerate(
            [(count_ref, counts), (q_ref, q_all), (f_ref, f_all), (table_ref, tables)]
        )
    ]
    share = pool.shape[0] // 8
    for n in range(8):
        part = pl.ds(n * share, share)
        loads.append(pltpu.make_async_copy(pool_ref.at[part], pool.at[part], sem.at[4 + n]))
    for copy in loads:
        copy.start()
    for copy in loads[:3]:
        copy.wait()
    sink_row = sinks[0:1, :]
    i0 = iota((128, 128), 0)
    i1 = iota((128, 128), 1)
    lane_row = lax.rem(iota((128, COLS), 1), ROWS).astype(F32)

    def ordering(e):
        c = counts[e][0:1, :]
        n_row = jnp.where(
            outer_pair,
            jnp.minimum(c, 256.0) + jnp.maximum(c - 768.0, 0.0),
            jnp.clip(c - 256.0, 0.0, 512.0),
        )
        n_col = jnp.sum(jnp.where(i0 == i1, n_row, 0.0), axis=1, keepdims=True)
        behind = jnp.logical_or(n_row > n_col, jnp.logical_and(n_col == n_row, i1 < i0))
        pos_col = jnp.sum(jnp.where(behind, 1.0, 0.0), axis=1, keepdims=True)
        return n_row, n_col, pos_col

    for e in range(UNITS):
        n_row, n_col, pos_col = ordering(e)
        places[e] = pos_col
        ahead = jnp.logical_or(n_col > n_row, jnp.logical_and(n_col == n_row, i0 < i1))
        pos_row = jnp.sum(jnp.where(ahead, 1.0, 0.0), axis=0, keepdims=True)
        perm = (pos_row == i0.astype(F32)).astype(BF16)
        q_sorted = nn(perm, q_all[e * 4 : e * 4 + 4].reshape(128, HEAD_COLUMNS)) * 0.125
        q_sorted = q_sorted.astype(BF16)
        f_sorted = nn(perm, f_all[e * 4 : e * 4 + 4].reshape(128, 128)).astype(BF16)
        none = jnp.zeros((ROWS, HEAD_WIDTH), BF16)
        for ch in range(CHUNKS):
            u = e * CHUNKS + ch
            for g in range(GROUP):
                piece = q_sorted[ch * ROWS : (ch + 1) * ROWS, g * HEAD_WIDTH : (g + 1) * HEAD_WIDTH]
                qs[u, g * ROWS : (g + 1) * ROWS, :] = jnp.concatenate([piece, none], axis=1)
            member = pos_col == lane_row + float(ch * ROWS)
            limit = jnp.sum(jnp.where(member, n_col, 0.0), axis=0, keepdims=True) * PAGE_TOKENS
            limit_ref[u] = jnp.broadcast_to(limit, (8, COLS))
            lengths[u] = jnp.max(limit).astype(jnp.int32)
            rows = f_sorted[ch * ROWS : (ch + 1) * ROWS, :]
            s = nt(rows, qs[u])
            ki = iota((ROWS, COLS), 0)
            ri = lax.rem(iota((ROWS, COLS), 1), ROWS)
            seen = jnp.logical_and(
                lax.div(ki, SCORED_STEPS) == lax.div(ri, SCORED_STEPS), ki <= ri
            )
            s = jnp.where(seen, s, NEGATIVE)
            m0 = jnp.maximum(jnp.max(s, axis=0, keepdims=True), sink_row)
            p = jnp.exp(s - m0).astype(BF16)
            start = nn(values_of(rows), p)
            start = start + jnp.where(
                iota((VROWS, COLS), 0) >= HEAD_WIDTH, jnp.exp(sink_row - m0), 0.0
            )
            m_ref[u] = jnp.broadcast_to(jnp.where(outer_pair, m0, FLOOR), (8, COLS))
            acc[u] = jnp.where(outer_pair, start, 0.0)

    def unit(e, carry):
        def gather(kb, carry):
            ss = lax.div(kb, 2)
            half = lax.rem(kb, 2)
            rows = [
                pool[tables[ss, e, half, i % 2 * 64 + i // 2] + ss * (N_EP * PAGES)]
                for i in range(GK // PAGE_TOKENS)
            ]
            for i in range(GK // BK):
                part = rows[i * (BK // PAGE_TOKENS) : (i + 1) * (BK // PAGE_TOKENS)]
                found = jnp.concatenate(part, axis=0)
                kv[pl.ds(pl.multiple_of(kb * GK + i * BK, BK), BK), :] = found
                vt[kb * (GK // BK) + i] = values_of(found)
            return carry

        lax.fori_loop(0, lax.div(lengths[e * CHUNKS] + (GK - 1), GK), gather, 0)

        key = iota((BK, COLS), 0).astype(F32)

        def produce(store, u, kb):
            keys = kv[pl.ds(pl.multiple_of(kb * BK, BK), BK), :]
            s = nt(keys, qs[u])
            limit = limit_ref[u][0:1, :] - (kb * BK).astype(F32)
            s = jnp.where(key < limit, s, NEGATIVE)
            store[...] = s
            return jnp.max(s, axis=0, keepdims=True)

        def absorb(store, u, kb, top):
            before = m_ref[u][0:1, :]
            after = jnp.maximum(before, top)
            p = jnp.exp(store[...] - after).astype(BF16)
            acc[u] = acc[u] * jnp.exp(before - after) + nn(vt[kb], p)
            m_ref[u] = jnp.broadcast_to(after, (8, COLS))

        def chunk(ch, top):
            u = e * CHUNKS + ch
            count = lax.div(lengths[u] + (BK - 1), BK)
            after_u = e * CHUNKS + jnp.minimum(ch + 1, CHUNKS - 1)

            def pair(i, top):
                last = 2 * i + 2 >= count
                next_top = produce(s1, u, 2 * i + 1)
                absorb(s0, u, 2 * i, top)
                top = produce(s0, jnp.where(last, after_u, u), jnp.where(last, 0, 2 * i + 2))
                absorb(s1, u, 2 * i + 1, next_top)
                return top

            top = lax.fori_loop(0, lax.div(count, 2), pair, top)

            def odd(top):
                absorb(s0, u, count - 1, top)
                return produce(s0, after_u, jnp.int32(0))

            return lax.cond(lax.rem(count, 2) == 1, odd, lambda top: top, top)

        used = sum([(lengths[e * CHUNKS + ch] > 0).astype(jnp.int32) for ch in range(CHUNKS)])

        @pl.when(used > 0)
        def _():
            top = produce(s0, e * CHUNKS, jnp.int32(0))
            lax.fori_loop(0, used, chunk, top)

        return carry

    for copy in loads[3:]:
        copy.wait()
    lax.fori_loop(0, UNITS, unit, 0)

    for e in range(UNITS):
        pos_col = places[e]
        perm_t = (pos_col == i1.astype(F32)).astype(BF16)
        lse = jnp.zeros((8, 128), F32)
        for ch in range(CHUNKS):
            u = e * CHUNKS + ch
            total = jnp.maximum(acc[u][HEAD_WIDTH : HEAD_WIDTH + 1, :], 1e-30)
            out = acc[u][0:HEAD_WIDTH, :] / total
            padded = jnp.concatenate([out, jnp.zeros_like(out)], axis=0)
            turned = padded.T.astype(BF16)
            for g in range(GROUP):
                sorted_out[e, ch * ROWS : (ch + 1) * ROWS, g * HEAD_WIDTH : (g + 1) * HEAD_WIDTH] = (
                    turned[g * ROWS : (g + 1) * ROWS, 0:HEAD_WIDTH]
                )
            row = m_ref[u][0:1, :] + jnp.log(total)
            mine = lax.div(iota((8, COLS), 1), ROWS) == iota((8, COLS), 0)
            member = (pos_col == lane_row + float(ch * ROWS)).astype(F32)
            lse = lse + nt(jnp.where(mine, row, 0.0), member, HIGHEST)
        lse_ref[e] = lse
        o_ref[e] = nn(perm_t, sorted_out[e]).astype(BF16)


def score(tables, counts, sinks, q_all, f_all, pool):
    vmem = pl.BlockSpec(memory_space=pltpu.VMEM)
    anywhere = pl.BlockSpec(memory_space=pl.ANY)
    return pl.pallas_call(
        score_kernel,
        out_shape=(
            jax.ShapeDtypeStruct((UNITS, 128, HEAD_COLUMNS), BF16),
            jax.ShapeDtypeStruct((UNITS, 8, 128), F32),
        ),
        in_specs=[anywhere, anywhere, vmem, anywhere, anywhere, anywhere],
        out_specs=(vmem, vmem),
        scratch_shapes=[
            pltpu.SMEM((2, UNITS, 2, 128), jnp.int32),
            pltpu.VMEM((UNITS, 8, 128), F32),
            pltpu.VMEM((16, ROWS, HEAD_COLUMNS), BF16),
            pltpu.VMEM((16, ROWS, 2 * HEAD_WIDTH), BF16),
            pltpu.VMEM((2 * N_EP * PAGES, PAGE_TOKENS, 2 * HEAD_WIDTH), BF16),
            pltpu.VMEM((KEYS, 128), BF16),
            pltpu.VMEM((KEYS // BK, VROWS, BK), BF16),
            pltpu.VMEM((UNITS * CHUNKS, COLS, 128), BF16),
            pltpu.VMEM((UNITS * CHUNKS, 8, COLS), F32),
            pltpu.VMEM((UNITS * CHUNKS, 8, COLS), F32),
            pltpu.VMEM((UNITS * CHUNKS, VROWS, COLS), F32),
            pltpu.VMEM((UNITS, 128, HEAD_COLUMNS), BF16),
            pltpu.VMEM((BK, COLS), F32),
            pltpu.VMEM((BK, COLS), F32),
            pltpu.VMEM((UNITS, 128, 1), F32),
            pltpu.SMEM((UNITS * CHUNKS,), jnp.int32),
            pltpu.SemaphoreType.DMA((12,)),
        ],
        compiler_params=pltpu.CompilerParams(vmem_limit_bytes=60 << 20),
        cost_estimate=pl.CostEstimate(
            flops=25_000_000_000, bytes_accessed=8_000_000, transcendentals=20_000_000
        ),
        name="score",
    )(tables, counts, sinks, q_all, f_all, pool)


def merge_kernel(
    o_ref, lse_ref, share_ref, rows_ref, out_ref, mix_ref, rows_here, o_all, lse_all, o_send, o_recv, l_send, l_recv, local,
):
    y, z, x, c = place()

    def at(dy, dx):
        return device(lax.rem(y + dy, 4), z, lax.rem(x + dx, 4), c)

    load = pltpu.make_async_copy(rows_ref, rows_here, local.at[2])
    load.start()
    plane = [(dy, dx) for dy in range(4) for dx in range(4) if (dy, dx) != (0, 0)]
    barrier = pltpu.get_barrier_semaphore()
    for dy, dx in plane:
        pl.semaphore_signal(barrier, inc=1, device_id=at(dy, dx), device_id_type=MESH)
    pl.semaphore_wait(barrier, len(plane))
    inner_pair = jnp.logical_or(y == 1, y == 2).astype(jnp.int32)
    slot = inner_pair * 8 + head_of(y, x)
    copies = []
    for dy in range(4):
        for dx in range(4):
            n = dy * 4 + dx
            q = lax.rem(y + dy, 4)
            e = lax.rem(x + dx, 4)
            o_source = o_ref.at[e, pl.ds(pl.multiple_of(q * ROWS, ROWS), ROWS)]
            if n == 0:
                pair = [
                    pltpu.make_async_copy(o_source, o_all.at[slot], local.at[0]),
                    pltpu.make_async_copy(lse_ref.at[e], lse_all.at[slot], local.at[1]),
                ]
            else:
                pair = [
                    pltpu.make_async_remote_copy(
                        o_source, o_all.at[slot], o_send.at[n], o_recv.at[n],
                        device_id=at(dy, dx), device_id_type=MESH,
                    ),
                    pltpu.make_async_remote_copy(
                        lse_ref.at[e], lse_all.at[slot], l_send.at[n], l_recv.at[n],
                        device_id=at(dy, dx), device_id_type=MESH,
                    ),
                ]
            for copy in pair:
                copy.start()
            copies.extend(pair)

    share = share_ref[...]
    high = share.astype(BF16)
    low = (share - high.astype(F32)).astype(BF16)
    load.wait()
    rows = rows_here[...].reshape(256, D)
    mix_ref[...] = (nn(high, rows) + nn(low, rows)).astype(BF16)

    for copy in copies:
        copy.wait()
    mine = (iota((ROWS, 128), 1) == iota((ROWS, 128), 0) + y * ROWS).astype(F32)
    logs = nt(mine, lse_all[...].reshape(128, 128), HIGHEST)
    log0, log1 = logs[:, :64], logs[:, 64:]
    top = jnp.maximum(log0, log1)
    w0, w1 = jnp.exp(log0 - top), jnp.exp(log1 - top)
    share0, share1 = w0 / (w0 + w1), w1 / (w0 + w1)
    parts = []
    for share in (share0, share1):
        high = share.astype(BF16)
        parts.append((high, (share - high.astype(F32)).astype(BF16)))
    for h in range(KEY_VALUE_HEADS):
        shape = (64, HEAD_COLUMNS)
        spread = (iota(shape, 0) == lax.div(iota(shape, 1), HEAD_WIDTH) + h * GROUP).astype(BF16)
        wide = [nn(high, spread) + nn(low, spread) for high, low in parts]
        result = wide[0] * o_all[h].astype(F32) + wide[1] * o_all[8 + h].astype(F32)
        out_ref[:, h * HEAD_COLUMNS : (h + 1) * HEAD_COLUMNS] = result.astype(BF16)


def merge(o, lse, share, rows):
    vmem = pl.BlockSpec(memory_space=pltpu.VMEM)
    anywhere = pl.BlockSpec(memory_space=pl.ANY)
    dma = pltpu.SemaphoreType.DMA
    return pl.pallas_call(
        merge_kernel,
        out_shape=(
            jax.ShapeDtypeStruct((ROWS, QUERY_HEADS * HEAD_WIDTH), BF16),
            jax.ShapeDtypeStruct((ROWS, D), BF16),
        ),
        in_specs=[anywhere, anywhere, vmem, anywhere],
        out_specs=(vmem, vmem),
        scratch_shapes=[
            pltpu.VMEM((128, 2, D), BF16),
            pltpu.VMEM((16, ROWS, HEAD_COLUMNS), BF16),
            pltpu.VMEM((16, 8, 128), F32),
            dma((16,)), dma((16,)), dma((16,)), dma((16,)), dma((3,)),
        ],
        compiler_params=pltpu.CompilerParams(
            collective_id=2, has_side_effects=True, vmem_limit_bytes=60 << 20
        ),
        name="merge",
    )(o, lse, share, rows)


def by_prefix(table):
    return table[0].T.reshape(2, N_EP, NPS // 2).transpose(1, 0, 2)


def per_device(
    queries, fresh_key_values, key_value_pages, page_owner, page_slot, page_count, sinks,
    hidden, norm_gain, expert_ids, gate_prob, gate_up, down_proj,
):
    y, z, x, c = place()

    q_all, f_all, pool, tables, counts, result, share = exchange(
        queries[0],
        fresh_key_values[0],
        key_value_pages.reshape(PAGES * PAGE_TOKENS, 2 * KEY_VALUE_HEADS * HEAD_WIDTH),
        by_prefix(page_owner),
        by_prefix(page_slot),
        page_count,
        hidden[0],
        norm_gain,
        expert_ids[0].transpose(1, 2, 0),
        gate_prob[0].transpose(1, 2, 0),
        gate_up,
        down_proj,
    )
    returned = lax.all_to_all(result, ("seq", "ep"), split_axis=0, concat_axis=0, tiled=True)
    head_sinks = lax.dynamic_slice_in_dim(sinks, head_of(y, x) * GROUP, GROUP)
    sink_rows = jnp.broadcast_to(jnp.repeat(head_sinks, ROWS)[None, :], (8, COLS))
    o, lse = score(
        tables, counts, sink_rows, q_all, f_all,
        pool.reshape(2 * N_EP * PAGES, PAGE_TOKENS, 2 * HEAD_WIDTH),
    )
    attention, mixture = merge(o, lse, share, returned)
    return (attention.reshape(queries.shape), mixture.reshape(hidden.shape))


def solution(mesh):
    return jax.shard_map(
        per_device,
        mesh=mesh,
        in_specs=(
            P("seq", "ep", None, None),
            P("seq", "ep", None, None),
            P("seq", "ep", None, None),
            P("seq", None, None),
            P("seq", None, None),
            P(None, "ep"),
            P(),
            P("seq", "ep", None, None),
            P(),
            P("seq", "ep", None, None),
            P("seq", "ep", None, None),
            P(("seq", "ep"), None, None),
            P(("seq", "ep"), None, None),
        ),
        out_specs=(P("seq", "ep", None, None), P("seq", "ep", None, None)),
        check_vma=False,
    )
```

```python
import jax
import jax.numpy as jnp
from jax import lax
from jax.experimental import pallas as pl
from jax.experimental.pallas import tpu as pltpu
from jax.sharding import PartitionSpec as P

D = 2880
QUERY_HEADS = 64
KEY_VALUE_HEADS = 8
GROUP = QUERY_HEADS // KEY_VALUE_HEADS
HEAD_WIDTH = 64
TOPK = 4
HID = 1440
SCORED_STEPS = 4
PAGE_TOKENS = 16
NPS = 256
PAGES = 24
PROMPTS = 8
N_SEQ = 4
N_EP = 32
ROWS = PROMPTS * SCORED_STEPS
HEAD_COLUMNS = GROUP * HEAD_WIDTH
NEGATIVE = -1e30
FLOOR = -1e29
EPSILON = 1e-05
MESH = pl.DeviceIdType.MESH
F32 = jnp.float32
BF16 = jnp.bfloat16
HIGHEST = lax.Precision.HIGHEST


def place():
    y = lax.axis_index("seq")
    ep = lax.axis_index("ep")
    return y, lax.div(ep, 8), lax.rem(lax.div(ep, 2), 4), lax.rem(ep, 2)


def device(y, z, x, c):
    return (y, z * 8 + x * 2 + c)


def head_of(y, x):
    return lax.div(y, 2) * 4 + x


def nt(a, b, precision=None):
    return lax.dot_general(
        a, b, (((1,), (1,)), ((), ())), preferred_element_type=F32, precision=precision
    )


def nn(a, b, precision=None):
    return lax.dot_general(
        a, b, (((1,), (0,)), ((), ())), preferred_element_type=F32, precision=precision
    )


def iota(shape, axis):
    return lax.broadcasted_iota(jnp.int32, shape, axis)


PARTS = ((0, 1024), (1024, 1024), (2048, D - 2048))


def route(id_ref, prob_ref):
    i0 = iota((128, 128), 0)
    i1 = iota((128, 128), 1)
    copies = (iota((8, 128), 0) == lax.rem(iota((8, 128), 1), 8)).astype(F32)
    group = lax.div(iota((TOPK, 128), 1), 8)

    def as_row(ref):
        row = jnp.zeros((1, 128), F32)
        for t in range(SCORED_STEPS):
            wide = nn(ref[t].astype(F32), copies, HIGHEST)
            mine = group == iota((TOPK, 128), 0) + t * TOPK
            row = row + jnp.sum(jnp.where(mine, wide, 0.0), axis=0, keepdims=True)
        return row

    ids = as_row(id_ref)
    column = jnp.sum(jnp.where(i0 == i1, ids, 0.0), axis=1, keepdims=True)
    earlier = jnp.logical_and(column == ids, i0 < i1)
    rank = jnp.sum(jnp.where(earlier, 1.0, 0.0), axis=0, keepdims=True)
    slots = iota((256, 128), 0).astype(F32) == 2.0 * ids + rank

    def token(a):
        return lax.rem(a, 8) * SCORED_STEPS + lax.div(a, 32)

    owner_token = (token(iota((128, ROWS), 0)) == iota((128, ROWS), 1)).astype(BF16)
    mine = token(iota((ROWS, 128), 1)) == iota((ROWS, 128), 0)
    share = nt(jnp.where(mine, as_row(prob_ref), 0.0), slots.astype(F32), HIGHEST)
    return slots.astype(BF16), owner_token, share


def exchange_kernel(
    q_ref, f_ref, page_ref, owner_ref, slot_ref, count_ref, hidden_ref, gain_ref, id_ref, prob_ref,
    up_ref, down_ref,
    q_all, f_all, pool, tables, counts, expert_out, share_ref,
    relay, f_relay, q_rows, table_ref, count_rows, out0, out1, out2, mid0, mid1, mid2, sorted0, sorted1, sorted2,
    in0, in1, in2, up_w, down_w, projected, active,
    q_send, q_recv, f_send, f_recv, a_send, a_recv, z_send, z_recv, c_send, c_recv,
    i_send, i_recv, d_send, d_recv, e_send, e_recv, local, w_sem,
):
    y, z, x, c = place()
    mate = 3 - y
    rows_out, rows_mid = (out0, out1, out2), (mid0, mid1, mid2)
    rows_sorted, rows_in = (sorted0, sorted1, sorted2), (in0, in1, in2)

    def at(dy, dx):
        return device(lax.rem(y + dy, 4), z, lax.rem(x + dx, 4), c)

    plane = [(dy, dx) for dy in range(4) for dx in range(4) if (dy, dx) != (0, 0)]
    up = device(y, lax.rem(z + 1, 4), x, c)
    down = device(y, lax.rem(z + 3, 4), x, c)
    twin = device(y, z, x, 1 - c)

    def beside(dy, dz):
        return device(lax.rem(y + dy, 4), lax.rem(z + dz, 4), x, c)

    def around(dx, dc):
        return device(y, z, lax.rem(x + dx, 4), lax.rem(c + dc, 2))

    peers = [at(dy, dx) for dy, dx in plane]
    peers += [beside(dy, dz) for dy in range(4) for dz in range(1, 4)]
    peers += [around(dx, 1) for dx in range(4)]
    barrier = pltpu.get_barrier_semaphore()
    for peer in peers:
        pl.semaphore_signal(barrier, inc=1, device_id=peer, device_id_type=MESH)

    weights = []
    for n in range(4):
        part = pl.ds(n * (D // 4), D // 4)
        weights.append(pltpu.make_async_copy(up_ref.at[0, part], up_w.at[part], w_sem.at[n]))
    for n in range(2):
        part = pl.ds(n * (HID // 2), HID // 2)
        weights.append(pltpu.make_async_copy(down_ref.at[0, part], down_w.at[part], w_sem.at[4 + n]))
    for copy in weights:
        copy.start()

    fresh = f_ref[...].reshape(ROWS, f_ref.shape[2])
    for h in range(KEY_VALUE_HEADS):
        low, high = h * HEAD_WIDTH, (h + 1) * HEAD_WIDTH
        split = KEY_VALUE_HEADS * HEAD_WIDTH
        rows = jnp.concatenate(
            [page_ref[:, low:high], page_ref[:, split + low : split + high]], axis=1
        )
        relay[h] = rows.reshape(PAGES, PAGE_TOKENS, 2 * HEAD_WIDTH)
        f_relay[h] = jnp.concatenate(
            [fresh[:, low:high], fresh[:, split + low : split + high]], axis=1
        )
    for xx in range(4):
        e = z * 8 + xx * 2 + c
        pages = owner_ref[e] * PAGES + slot_ref[e]
        for half in range(2):
            lanes = slice(half * 64, half * 64 + 64)
            table_ref[xx, half : half + 1, :] = jnp.concatenate(
                [pages[0:1, lanes], pages[1:2, lanes]], axis=1
            )
    lane = iota((PROMPTS, 128), 1)
    copies = (iota((PROMPTS, 128), 0) == lax.div(lax.rem(lane, ROWS), SCORED_STEPS)).astype(F32)
    wide = nn(count_ref[...].astype(F32), copies, HIGHEST)
    mine = lax.div(iota((N_SEQ, 128), 1), ROWS) == iota((N_SEQ, 128), 0)
    wide = jnp.sum(jnp.where(mine, wide, 0.0), axis=0, keepdims=True)
    count_rows[...] = jnp.broadcast_to(wide, (8, 128))

    h32 = hidden_ref[...].reshape(ROWS, D).astype(F32)
    scale = lax.rsqrt(jnp.mean(h32 * h32, axis=-1, keepdims=True) + EPSILON)
    normed = (h32 * scale * gain_ref[...].reshape(1, D)).astype(BF16)
    slots, owner_token, share = route(id_ref, prob_ref)
    share_ref[...] = share
    spread = nn(slots, owner_token).astype(BF16)
    for k, (first_column, columns) in enumerate(PARTS):
        piece = normed[:, first_column : first_column + columns]
        rows_out[k][...] = nn(spread, piece).astype(BF16).reshape(16, 16, columns)
    pl.semaphore_wait(barrier, len(peers))

    def spot(segment_slot, zz, xx, cc):
        return pool.at[segment_slot, pl.ds((zz * 8 + xx * 2 + cc) * PAGES, PAGES)]

    order = [(0, 0), (0, 1), (0, 3), (0, 2), (1, 0), (1, 1), (1, 3), (1, 2)]
    first = []

    def hand_out(n):
        p, dx = order[n]
        yy = y if p == 0 else mate
        xx = lax.rem(x + dx, 4)
        target = spot(lax.div(y, 2), z, x, c)
        source = relay.at[head_of(yy, xx)]
        if (p, dx) == (0, 0):
            copy = pltpu.make_async_copy(source, target, local.at[0])
        else:
            copy = pltpu.make_async_remote_copy(
                source, target, a_send.at[n], a_recv.at[n],
                device_id=device(yy, z, xx, c), device_id_type=MESH,
            )
        copy.start()
        first.append(copy)

    for n in range(4):
        hand_out(n)
    routed = []
    for k in range(len(PARTS)):
        for dy in range(4):
            for dz in range(4):
                n = dy * 4 + dz
                source = rows_out[k].at[lax.rem(y + dy, 4) * 4 + lax.rem(z + dz, 4)]
                target = rows_mid[k].at[y * 4 + z]
                if n == 0:
                    copy = pltpu.make_async_copy(source, target, local.at[5 + 2 * k])
                else:
                    copy = pltpu.make_async_remote_copy(
                        source, target, d_send.at[k * 16 + n], d_recv.at[k * 16 + n],
                        device_id=beside(dy, dz), device_id_type=MESH,
                    )
                copy.start()
                routed.append(copy)

    for n in range(4, 8):
        hand_out(n)

    small = []
    mine = pltpu.make_async_copy(table_ref, tables.at[lax.div(y, 2)], local.at[1])
    mine.start()
    small.append(mine)
    mine = pltpu.make_async_copy(count_rows, counts.at[x], local.at[2])
    mine.start()
    small.append(mine)
    other = pltpu.make_async_remote_copy(
        table_ref, tables.at[lax.div(y, 2)], i_send.at[0], i_recv.at[0],
        device_id=device(mate, z, x, c), device_id_type=MESH,
    )
    other.start()
    small.append(other)
    for dx in range(1, 4):
        other = pltpu.make_async_remote_copy(
            count_rows, counts.at[x], i_send.at[dx], i_recv.at[dx],
            device_id=at(0, dx), device_id_type=MESH,
        )
        other.start()
        small.append(other)

    def chunk(n):
        p, dx = order[n]
        yy = y if p == 0 else mate
        return lax.div(yy, 2), lax.rem(x - dx + 4, 4)

    def pass_on(n, zz, way, peer):
        segment_slot, xx = chunk(n)
        block = spot(segment_slot, zz, xx, c)
        sends, recvs = (c_send, c_recv) if way >= 3 else (z_send, z_recv)
        number = (way - 3 if way >= 3 else way) * 8 + n
        copy = pltpu.make_async_remote_copy(
            block, block, sends.at[number], recvs.at[number],
            device_id=peer, device_id_type=MESH,
        )
        copy.start()
        return copy

    upward, downward, further, across = [], [], [], []

    def begin(n):
        if n == 0:
            first[n].wait()
        else:
            first[n].wait_recv()
        upward.append(pass_on(n, z, 0, up))
        downward.append(pass_on(n, z, 1, down))
        across.append(pass_on(n, z, 3, twin))

    def forward(n):
        upward[n].wait_recv()
        if n % 2 == 0:
            further.append(pass_on(n, lax.rem(z + 3, 4), 2, up))
        across.append(pass_on(n, lax.rem(z + 3, 4), 4, twin))
        downward[n].wait_recv()
        if n % 2 == 1:
            further.append(pass_on(n, lax.rem(z + 1, 4), 2, down))
        across.append(pass_on(n, lax.rem(z + 1, 4), 5, twin))

    for n in range(4):
        begin(n)

    ri = iota((256, 256), 0)
    ci = iota((256, 256), 1)

    def slot_of(i):
        return lax.div(lax.rem(i, 32), 2) * 16 + lax.div(i, 32) * 2 + lax.rem(i, 2)

    def arrive(copies):
        copies[0].wait()
        for copy in copies[1:]:
            copy.wait_recv()

    regroup = (slot_of(ri) == ci).astype(BF16)
    delivered = [[], [], []]
    for k, (_, columns) in enumerate(PARTS):
        arrive(routed[k * 16 : (k + 1) * 16])
        moved = nn(regroup, rows_mid[k][...].reshape(256, columns)).astype(BF16)
        rows_sorted[k][...] = moved.reshape(8, 32, columns)
        for dx in range(4):
            for dc in range(2):
                n = dx * 2 + dc
                source = rows_sorted[k].at[lax.rem(x + dx, 4) * 2 + lax.rem(c + dc, 2)]
                target = rows_in[k].at[x * 2 + c]
                if n == 0:
                    copy = pltpu.make_async_copy(source, target, local.at[6 + 2 * k])
                else:
                    copy = pltpu.make_async_remote_copy(
                        source, target, e_send.at[k * 8 + n], e_recv.at[k * 8 + n],
                        device_id=around(dx, dc), device_id_type=MESH,
                    )
                copy.start()
                delivered[k].append(copy)
        if k == 1:
            for n in (0, 1):
                forward(n)
    for n in range(4, 8):
        begin(n)
    for n in (2, 3):
        forward(n)

    q_rows[...] = q_ref[...].reshape(ROWS, q_ref.shape[2])
    for dy in range(4):
        for dx in range(4):
            n = dy * 4 + dx
            h = head_of(lax.rem(y + dy, 4), lax.rem(x + dx, 4))
            q_source = q_rows.at[:, pl.ds(pl.multiple_of(h * HEAD_COLUMNS, HEAD_COLUMNS), HEAD_COLUMNS)]
            f_source = f_relay.at[h]
            slot = x * 4 + y
            if n == 0:
                copies = [
                    pltpu.make_async_copy(q_source, q_all.at[slot], local.at[3]),
                    pltpu.make_async_copy(f_source, f_all.at[slot], local.at[4]),
                ]
            else:
                copies = [
                    pltpu.make_async_remote_copy(
                        q_source, q_all.at[slot], q_send.at[n], q_recv.at[n],
                        device_id=at(dy, dx), device_id_type=MESH,
                    ),
                    pltpu.make_async_remote_copy(
                        f_source, f_all.at[slot], f_send.at[n], f_recv.at[n],
                        device_id=at(dy, dx), device_id_type=MESH,
                    ),
                ]
            for copy in copies:
                copy.start()
            small.extend(copies)

    for copy in weights:
        copy.wait()

    def tiles(work):
        @pl.loop(0, D // TILE)
        def _(j):
            work(pl.ds(pl.multiple_of(j * TILE, TILE), TILE))

        work(pl.ds(D // TILE * TILE, D % TILE))

    def project(k):
        first_column, columns = PARTS[k]
        arrive(delivered[k])

        def work(part):
            rows = rows_in[k][...].reshape(256, columns)
            term = nn(rows, up_w[first_column : first_column + columns, part])
            projected[:, part] = term if k == 0 else projected[:, part] + term

        tiles(work)

    project(0)
    project(1)
    forward(4)
    forward(5)
    project(2)
    forward(6)
    forward(7)

    @pl.loop(0, 8)
    def _(j):
        part = pl.ds(pl.multiple_of(j * 32, 32), 32)
        wide = projected[part, :]
        gate, upper = wide[:, :HID], wide[:, HID:]
        active[part, :] = ((upper + 1.0) * gate * jax.nn.sigmoid(1.702 * gate)).astype(BF16)

    back = (slot_of(ci) == ri).astype(BF16)
    active[...] = nn(back, active[...]).astype(BF16)

    def finish(part):
        rows = nn(active[...], down_w[:, part]).astype(BF16)
        expert_out[:, :, part] = rows.reshape(128, 2, rows.shape[1])

    @pl.loop(0, 3)
    def _(j):
        finish(pl.ds(pl.multiple_of(j * TILE, TILE), TILE))

    for n in range(8):
        further[n].wait_recv()
        across.append(pass_on(n, lax.rem(z + 2, 4), 6, twin))

    @pl.loop(3, D // TILE)
    def _(j):
        finish(pl.ds(pl.multiple_of(j * TILE, TILE), TILE))

    finish(pl.ds(D // TILE * TILE, D % TILE))

    for copy in across:
        copy.wait()
    for copy in first[1:] + upward + downward + further:
        copy.wait_send()
    for n, copy in enumerate(routed):
        if n % 16 > 0:
            copy.wait_send()
    for copy in sum([copies[1:] for copies in delivered], []):
        copy.wait_send()
    for copy in small:
        copy.wait()


TILE = 512


def exchange(
    queries, fresh, pages, owner, slot, count, hidden, gain, ids, prob, gate_up, down_proj
):
    vmem = pl.BlockSpec(memory_space=pltpu.VMEM)
    anywhere = pl.BlockSpec(memory_space=pl.ANY)
    dma = pltpu.SemaphoreType.DMA
    return pl.pallas_call(
        exchange_kernel,
        out_shape=(
            jax.ShapeDtypeStruct((16, ROWS, HEAD_COLUMNS), BF16),
            jax.ShapeDtypeStruct((16, ROWS, 2 * HEAD_WIDTH), BF16),
            jax.ShapeDtypeStruct((2, N_EP * PAGES, PAGE_TOKENS, 2 * HEAD_WIDTH), BF16),
            jax.ShapeDtypeStruct((2, 4, 2, 128), jnp.int32),
            jax.ShapeDtypeStruct((4, 8, 128), F32),
            jax.ShapeDtypeStruct((128, 2, D), BF16),
            jax.ShapeDtypeStruct((ROWS, 256), F32),
        ),
        in_specs=[vmem] * 10 + [anywhere] * 2,
        out_specs=(anywhere,) * 5 + (vmem, vmem),
        scratch_shapes=[
            pltpu.VMEM((KEY_VALUE_HEADS, PAGES, PAGE_TOKENS, 2 * HEAD_WIDTH), BF16),
            pltpu.VMEM((KEY_VALUE_HEADS, ROWS, 2 * HEAD_WIDTH), BF16),
            pltpu.VMEM((ROWS, QUERY_HEADS * HEAD_WIDTH), BF16),
            pltpu.VMEM((4, 2, 128), jnp.int32),
            pltpu.VMEM((8, 128), F32),
            *[pltpu.VMEM((16, 16, columns), BF16) for _, columns in PARTS * 2],
            *[pltpu.VMEM((8, 32, columns), BF16) for _, columns in PARTS * 2],
            pltpu.VMEM((D, 2 * HID), BF16),
            pltpu.VMEM((HID, D), BF16),
            pltpu.VMEM((256, 2 * HID), F32),
            pltpu.VMEM((256, HID), BF16),
            dma((16,)), dma((16,)), dma((16,)), dma((16,)), dma((8,)), dma((8,)),
            dma((24,)), dma((24,)), dma((32,)), dma((32,)), dma((4,)), dma((4,)),
            dma((48,)), dma((48,)), dma((24,)), dma((24,)), dma((11,)), dma((6,)),
        ],
        compiler_params=pltpu.CompilerParams(
            collective_id=1, has_side_effects=True, vmem_limit_bytes=56 << 20
        ),
        name="exchange",
    )(queries, fresh, pages, owner, slot, count, hidden, gain, ids, prob, gate_up, down_proj)


BK = 1024
GK = 2048
KEYS = 2 * NPS * PAGE_TOKENS
UNITS = 4
CHUNKS = 4
COLS = 256
VROWS = 80


def values_of(rows):
    pick = (iota((VROWS, 128), 0) + HEAD_WIDTH == iota((VROWS, 128), 1)).astype(BF16)
    moved = nt(pick, rows)
    return jnp.where(iota(moved.shape, 0) >= HEAD_WIDTH, 1.0, moved).astype(BF16)


def score_kernel(
    table_ref, count_ref, sinks, q_ref, f_ref, pool_ref, o_ref, lse_ref,
    tables, counts, q_all, f_all, pool,
    kv, vt, qs, limit_ref, m_ref, acc, sorted_out, s0, s1, places, lengths, sem,
):
    y = lax.axis_index("seq")
    outer_pair = jnp.logical_or(y == 0, y == 3)
    loads = [
        pltpu.make_async_copy(source, target, sem.at[n])
        for n, (source, target) in enumerate(
            [(count_ref, counts), (q_ref, q_all), (f_ref, f_all), (table_ref, tables)]
        )
    ]
    share = pool.shape[0] // 8
    for n in range(8):
        part = pl.ds(n * share, share)
        loads.append(pltpu.make_async_copy(pool_ref.at[part], pool.at[part], sem.at[4 + n]))
    for copy in loads:
        copy.start()
    for copy in loads[:3]:
        copy.wait()
    sink_row = sinks[0:1, :]
    i0 = iota((128, 128), 0)
    i1 = iota((128, 128), 1)
    lane_row = lax.rem(iota((128, COLS), 1), ROWS).astype(F32)

    def ordering(e):
        c = counts[e][0:1, :]
        n_row = jnp.where(
            outer_pair,
            jnp.minimum(c, 256.0) + jnp.maximum(c - 768.0, 0.0),
            jnp.clip(c - 256.0, 0.0, 512.0),
        )
        n_col = jnp.sum(jnp.where(i0 == i1, n_row, 0.0), axis=1, keepdims=True)
        behind = jnp.logical_or(n_row > n_col, jnp.logical_and(n_col == n_row, i1 < i0))
        pos_col = jnp.sum(jnp.where(behind, 1.0, 0.0), axis=1, keepdims=True)
        return n_row, n_col, pos_col

    for e in range(UNITS):
        n_row, n_col, pos_col = ordering(e)
        places[e] = pos_col
        ahead = jnp.logical_or(n_col > n_row, jnp.logical_and(n_col == n_row, i0 < i1))
        pos_row = jnp.sum(jnp.where(ahead, 1.0, 0.0), axis=0, keepdims=True)
        perm = (pos_row == i0.astype(F32)).astype(BF16)
        q_sorted = nn(perm, q_all[e * 4 : e * 4 + 4].reshape(128, HEAD_COLUMNS)) * 0.125
        q_sorted = q_sorted.astype(BF16)
        f_sorted = nn(perm, f_all[e * 4 : e * 4 + 4].reshape(128, 128)).astype(BF16)
        none = jnp.zeros((ROWS, HEAD_WIDTH), BF16)
        for ch in range(CHUNKS):
            u = e * CHUNKS + ch
            for g in range(GROUP):
                piece = q_sorted[ch * ROWS : (ch + 1) * ROWS, g * HEAD_WIDTH : (g + 1) * HEAD_WIDTH]
                qs[u, g * ROWS : (g + 1) * ROWS, :] = jnp.concatenate([piece, none], axis=1)
            member = pos_col == lane_row + float(ch * ROWS)
            limit = jnp.sum(jnp.where(member, n_col, 0.0), axis=0, keepdims=True) * PAGE_TOKENS
            limit_ref[u] = jnp.broadcast_to(limit, (8, COLS))
            lengths[u] = jnp.max(limit).astype(jnp.int32)
            rows = f_sorted[ch * ROWS : (ch + 1) * ROWS, :]
            s = nt(rows, qs[u])
            ki = iota((ROWS, COLS), 0)
            ri = lax.rem(iota((ROWS, COLS), 1), ROWS)
            seen = jnp.logical_and(
                lax.div(ki, SCORED_STEPS) == lax.div(ri, SCORED_STEPS), ki <= ri
            )
            s = jnp.where(seen, s, NEGATIVE)
            m0 = jnp.maximum(jnp.max(s, axis=0, keepdims=True), sink_row)
            p = jnp.exp(s - m0).astype(BF16)
            start = nn(values_of(rows), p)
            start = start + jnp.where(
                iota((VROWS, COLS), 0) >= HEAD_WIDTH, jnp.exp(sink_row - m0), 0.0
            )
            m_ref[u] = jnp.broadcast_to(jnp.where(outer_pair, m0, FLOOR), (8, COLS))
            acc[u] = jnp.where(outer_pair, start, 0.0)

    def unit(e, carry):
        def gather(kb, carry):
            ss = lax.div(kb, 2)
            half = lax.rem(kb, 2)
            rows = [
                pool[tables[ss, e, half, i % 2 * 64 + i // 2] + ss * (N_EP * PAGES)]
                for i in range(GK // PAGE_TOKENS)
            ]
            for i in range(GK // BK):
                part = rows[i * (BK // PAGE_TOKENS) : (i + 1) * (BK // PAGE_TOKENS)]
                found = jnp.concatenate(part, axis=0)
                kv[pl.ds(pl.multiple_of(kb * GK + i * BK, BK), BK), :] = found
                vt[kb * (GK // BK) + i] = values_of(found)
            return carry

        lax.fori_loop(0, lax.div(lengths[e * CHUNKS] + (GK - 1), GK), gather, 0)

        key = iota((BK, COLS), 0).astype(F32)

        def produce(store, u, kb):
            keys = kv[pl.ds(pl.multiple_of(kb * BK, BK), BK), :]
            s = nt(keys, qs[u])
            limit = limit_ref[u][0:1, :] - (kb * BK).astype(F32)
            s = jnp.where(key < limit, s, NEGATIVE)
            store[...] = s
            return jnp.max(s, axis=0, keepdims=True)

        def absorb(store, u, kb, top):
            before = m_ref[u][0:1, :]
            after = jnp.maximum(before, top)
            p = jnp.exp(store[...] - after).astype(BF16)
            acc[u] = acc[u] * jnp.exp(before - after) + nn(vt[kb], p)
            m_ref[u] = jnp.broadcast_to(after, (8, COLS))

        def chunk(ch, top):
            u = e * CHUNKS + ch
            count = lax.div(lengths[u] + (BK - 1), BK)
            after_u = e * CHUNKS + jnp.minimum(ch + 1, CHUNKS - 1)

            def pair(i, top):
                last = 2 * i + 2 >= count
                next_top = produce(s1, u, 2 * i + 1)
                absorb(s0, u, 2 * i, top)
                top = produce(s0, jnp.where(last, after_u, u), jnp.where(last, 0, 2 * i + 2))
                absorb(s1, u, 2 * i + 1, next_top)
                return top

            top = lax.fori_loop(0, lax.div(count, 2), pair, top)

            def odd(top):
                absorb(s0, u, count - 1, top)
                return produce(s0, after_u, jnp.int32(0))

            return lax.cond(lax.rem(count, 2) == 1, odd, lambda top: top, top)

        used = sum([(lengths[e * CHUNKS + ch] > 0).astype(jnp.int32) for ch in range(CHUNKS)])

        @pl.when(used > 0)
        def _():
            top = produce(s0, e * CHUNKS, jnp.int32(0))
            lax.fori_loop(0, used, chunk, top)

        return carry

    for copy in loads[3:]:
        copy.wait()
    lax.fori_loop(0, UNITS, unit, 0)

    for e in range(UNITS):
        pos_col = places[e]
        perm_t = (pos_col == i1.astype(F32)).astype(BF16)
        lse = jnp.zeros((8, 128), F32)
        for ch in range(CHUNKS):
            u = e * CHUNKS + ch
            total = jnp.maximum(acc[u][HEAD_WIDTH : HEAD_WIDTH + 1, :], 1e-30)
            out = acc[u][0:HEAD_WIDTH, :] / total
            padded = jnp.concatenate([out, jnp.zeros_like(out)], axis=0)
            turned = padded.T.astype(BF16)
            for g in range(GROUP):
                sorted_out[e, ch * ROWS : (ch + 1) * ROWS, g * HEAD_WIDTH : (g + 1) * HEAD_WIDTH] = (
                    turned[g * ROWS : (g + 1) * ROWS, 0:HEAD_WIDTH]
                )
            row = m_ref[u][0:1, :] + jnp.log(total)
            mine = lax.div(iota((8, COLS), 1), ROWS) == iota((8, COLS), 0)
            member = (pos_col == lane_row + float(ch * ROWS)).astype(F32)
            lse = lse + nt(jnp.where(mine, row, 0.0), member, HIGHEST)
        lse_ref[e] = lse
        o_ref[e] = nn(perm_t, sorted_out[e]).astype(BF16)


def score(tables, counts, sinks, q_all, f_all, pool):
    vmem = pl.BlockSpec(memory_space=pltpu.VMEM)
    anywhere = pl.BlockSpec(memory_space=pl.ANY)
    return pl.pallas_call(
        score_kernel,
        out_shape=(
            jax.ShapeDtypeStruct((UNITS, 128, HEAD_COLUMNS), BF16),
            jax.ShapeDtypeStruct((UNITS, 8, 128), F32),
        ),
        in_specs=[anywhere, anywhere, vmem, anywhere, anywhere, anywhere],
        out_specs=(vmem, vmem),
        scratch_shapes=[
            pltpu.SMEM((2, UNITS, 2, 128), jnp.int32),
            pltpu.VMEM((UNITS, 8, 128), F32),
            pltpu.VMEM((16, ROWS, HEAD_COLUMNS), BF16),
            pltpu.VMEM((16, ROWS, 2 * HEAD_WIDTH), BF16),
            pltpu.VMEM((2 * N_EP * PAGES, PAGE_TOKENS, 2 * HEAD_WIDTH), BF16),
            pltpu.VMEM((KEYS, 128), BF16),
            pltpu.VMEM((KEYS // BK, VROWS, BK), BF16),
            pltpu.VMEM((UNITS * CHUNKS, COLS, 128), BF16),
            pltpu.VMEM((UNITS * CHUNKS, 8, COLS), F32),
            pltpu.VMEM((UNITS * CHUNKS, 8, COLS), F32),
            pltpu.VMEM((UNITS * CHUNKS, VROWS, COLS), F32),
            pltpu.VMEM((UNITS, 128, HEAD_COLUMNS), BF16),
            pltpu.VMEM((BK, COLS), F32),
            pltpu.VMEM((BK, COLS), F32),
            pltpu.VMEM((UNITS, 128, 1), F32),
            pltpu.SMEM((UNITS * CHUNKS,), jnp.int32),
            pltpu.SemaphoreType.DMA((12,)),
        ],
        compiler_params=pltpu.CompilerParams(vmem_limit_bytes=60 << 20),
        cost_estimate=pl.CostEstimate(
            flops=25_000_000_000, bytes_accessed=8_000_000, transcendentals=20_000_000
        ),
        name="score",
    )(tables, counts, sinks, q_all, f_all, pool)


def merge_kernel(
    o_ref, lse_ref, share_ref, rows_ref, out_ref, mix_ref, o_all, lse_all, o_send, o_recv, l_send, l_recv, local,
):
    y, z, x, c = place()

    def at(dy, dx):
        return device(lax.rem(y + dy, 4), z, lax.rem(x + dx, 4), c)

    plane = [(dy, dx) for dy in range(4) for dx in range(4) if (dy, dx) != (0, 0)]
    barrier = pltpu.get_barrier_semaphore()
    for dy, dx in plane:
        pl.semaphore_signal(barrier, inc=1, device_id=at(dy, dx), device_id_type=MESH)
    pl.semaphore_wait(barrier, len(plane))
    inner_pair = jnp.logical_or(y == 1, y == 2).astype(jnp.int32)
    slot = inner_pair * 8 + head_of(y, x)
    copies = []
    for dy in range(4):
        for dx in range(4):
            n = dy * 4 + dx
            q = lax.rem(y + dy, 4)
            e = lax.rem(x + dx, 4)
            o_source = o_ref.at[e, pl.ds(pl.multiple_of(q * ROWS, ROWS), ROWS)]
            if n == 0:
                pair = [
                    pltpu.make_async_copy(o_source, o_all.at[slot], local.at[0]),
                    pltpu.make_async_copy(lse_ref.at[e], lse_all.at[slot], local.at[1]),
                ]
            else:
                pair = [
                    pltpu.make_async_remote_copy(
                        o_source, o_all.at[slot], o_send.at[n], o_recv.at[n],
                        device_id=at(dy, dx), device_id_type=MESH,
                    ),
                    pltpu.make_async_remote_copy(
                        lse_ref.at[e], lse_all.at[slot], l_send.at[n], l_recv.at[n],
                        device_id=at(dy, dx), device_id_type=MESH,
                    ),
                ]
            for copy in pair:
                copy.start()
            copies.extend(pair)

    share = share_ref[...]
    high = share.astype(BF16)
    low = (share - high.astype(F32)).astype(BF16)
    rows = rows_ref[...].reshape(256, D)
    mix_ref[...] = (nn(high, rows) + nn(low, rows)).astype(BF16)

    for copy in copies:
        copy.wait()
    mine = (iota((ROWS, 128), 1) == iota((ROWS, 128), 0) + y * ROWS).astype(F32)
    logs = nt(mine, lse_all[...].reshape(128, 128), HIGHEST)
    log0, log1 = logs[:, :64], logs[:, 64:]
    top = jnp.maximum(log0, log1)
    w0, w1 = jnp.exp(log0 - top), jnp.exp(log1 - top)
    share0, share1 = w0 / (w0 + w1), w1 / (w0 + w1)
    parts = []
    for share in (share0, share1):
        high = share.astype(BF16)
        parts.append((high, (share - high.astype(F32)).astype(BF16)))
    for h in range(KEY_VALUE_HEADS):
        shape = (64, HEAD_COLUMNS)
        spread = (iota(shape, 0) == lax.div(iota(shape, 1), HEAD_WIDTH) + h * GROUP).astype(BF16)
        wide = [nn(high, spread) + nn(low, spread) for high, low in parts]
        result = wide[0] * o_all[h].astype(F32) + wide[1] * o_all[8 + h].astype(F32)
        out_ref[:, h * HEAD_COLUMNS : (h + 1) * HEAD_COLUMNS] = result.astype(BF16)


def merge(o, lse, share, rows):
    vmem = pl.BlockSpec(memory_space=pltpu.VMEM)
    anywhere = pl.BlockSpec(memory_space=pl.ANY)
    dma = pltpu.SemaphoreType.DMA
    return pl.pallas_call(
        merge_kernel,
        out_shape=(
            jax.ShapeDtypeStruct((ROWS, QUERY_HEADS * HEAD_WIDTH), BF16),
            jax.ShapeDtypeStruct((ROWS, D), BF16),
        ),
        in_specs=[anywhere, anywhere, vmem, vmem],
        out_specs=(vmem, vmem),
        scratch_shapes=[
            pltpu.VMEM((16, ROWS, HEAD_COLUMNS), BF16),
            pltpu.VMEM((16, 8, 128), F32),
            dma((16,)), dma((16,)), dma((16,)), dma((16,)), dma((2,)),
        ],
        compiler_params=pltpu.CompilerParams(
            collective_id=2, has_side_effects=True, vmem_limit_bytes=16 << 20
        ),
        name="merge",
    )(o, lse, share, rows)


def by_prefix(table):
    return table[0].T.reshape(2, N_EP, NPS // 2).transpose(1, 0, 2)


def per_device(
    queries, fresh_key_values, key_value_pages, page_owner, page_slot, page_count, sinks,
    hidden, norm_gain, expert_ids, gate_prob, gate_up, down_proj,
):
    y, z, x, c = place()

    q_all, f_all, pool, tables, counts, result, share = exchange(
        queries[0],
        fresh_key_values[0],
        key_value_pages.reshape(PAGES * PAGE_TOKENS, 2 * KEY_VALUE_HEADS * HEAD_WIDTH),
        by_prefix(page_owner),
        by_prefix(page_slot),
        page_count,
        hidden[0],
        norm_gain,
        expert_ids[0].transpose(1, 2, 0),
        gate_prob[0].transpose(1, 2, 0),
        gate_up,
        down_proj,
    )
    returned = lax.all_to_all(result, ("seq", "ep"), split_axis=0, concat_axis=0, tiled=True)
    head_sinks = lax.dynamic_slice_in_dim(sinks, head_of(y, x) * GROUP, GROUP)
    sink_rows = jnp.broadcast_to(jnp.repeat(head_sinks, ROWS)[None, :], (8, COLS))
    o, lse = score(
        tables, counts, sink_rows, q_all, f_all,
        pool.reshape(2 * N_EP * PAGES, PAGE_TOKENS, 2 * HEAD_WIDTH),
    )
    attention, mixture = merge(o, lse, share, returned)
    return (attention.reshape(queries.shape), mixture.reshape(hidden.shape))


def solution(mesh):
    return jax.shard_map(
        per_device,
        mesh=mesh,
        in_specs=(
            P("seq", "ep", None, None),
            P("seq", "ep", None, None),
            P("seq", "ep", None, None),
            P("seq", None, None),
            P("seq", None, None),
            P(None, "ep"),
            P(),
            P("seq", "ep", None, None),
            P(),
            P("seq", "ep", None, None),
            P("seq", "ep", None, None),
            P(("seq", "ep"), None, None),
            P(("seq", "ep"), None, None),
        ),
        out_specs=(P("seq", "ep", None, None), P("seq", "ep", None, None)),
        check_vma=False,
    )
```

```python
import jax
import jax.numpy as jnp
from jax import lax
from jax.experimental import pallas as pl
from jax.experimental.pallas import tpu as pltpu
from jax.sharding import PartitionSpec as P

D = 2880
QUERY_HEADS = 64
KEY_VALUE_HEADS = 8
GROUP = QUERY_HEADS // KEY_VALUE_HEADS
HEAD_WIDTH = 64
TOPK = 4
HID = 1440
SCORED_STEPS = 4
PAGE_TOKENS = 16
NPS = 256
PAGES = 24
PROMPTS = 8
N_SEQ = 4
N_EP = 32
ROWS = PROMPTS * SCORED_STEPS
HEAD_COLUMNS = GROUP * HEAD_WIDTH
NEGATIVE = -1e30
FLOOR = -1e29
EPSILON = 1e-05
MESH = pl.DeviceIdType.MESH
F32 = jnp.float32
BF16 = jnp.bfloat16
HIGHEST = lax.Precision.HIGHEST


def place():
    y = lax.axis_index("seq")
    ep = lax.axis_index("ep")
    return y, lax.div(ep, 8), lax.rem(lax.div(ep, 2), 4), lax.rem(ep, 2)


def device(y, z, x, c):
    return (y, z * 8 + x * 2 + c)


def head_of(y, x):
    return lax.div(y, 2) * 4 + x


def nt(a, b, precision=None):
    return lax.dot_general(
        a, b, (((1,), (1,)), ((), ())), preferred_element_type=F32, precision=precision
    )


def nn(a, b, precision=None):
    return lax.dot_general(
        a, b, (((1,), (0,)), ((), ())), preferred_element_type=F32, precision=precision
    )


def iota(shape, axis):
    return lax.broadcasted_iota(jnp.int32, shape, axis)


PARTS = ((0, 1024), (1024, 1024), (2048, D - 2048))


def route(id_ref, prob_ref):
    i0 = iota((128, 128), 0)
    i1 = iota((128, 128), 1)
    copies = (iota((8, 128), 0) == lax.rem(iota((8, 128), 1), 8)).astype(F32)
    group = lax.div(iota((TOPK, 128), 1), 8)

    def as_row(ref):
        row = jnp.zeros((1, 128), F32)
        for t in range(SCORED_STEPS):
            wide = nn(ref[t].astype(F32), copies, HIGHEST)
            mine = group == iota((TOPK, 128), 0) + t * TOPK
            row = row + jnp.sum(jnp.where(mine, wide, 0.0), axis=0, keepdims=True)
        return row

    ids = as_row(id_ref)
    column = jnp.sum(jnp.where(i0 == i1, ids, 0.0), axis=1, keepdims=True)
    earlier = jnp.logical_and(column == ids, i0 < i1)
    rank = jnp.sum(jnp.where(earlier, 1.0, 0.0), axis=0, keepdims=True)
    slots = iota((256, 128), 0).astype(F32) == 2.0 * ids + rank

    def token(a):
        return lax.rem(a, 8) * SCORED_STEPS + lax.div(a, 32)

    owner_token = (token(iota((128, ROWS), 0)) == iota((128, ROWS), 1)).astype(BF16)
    mine = token(iota((ROWS, 128), 1)) == iota((ROWS, 128), 0)
    share = nt(jnp.where(mine, as_row(prob_ref), 0.0), slots.astype(F32), HIGHEST)
    return slots.astype(BF16), owner_token, share


def exchange_kernel(
    q_ref, f_ref, page_ref, owner_ref, slot_ref, count_ref, hidden_ref, gain_ref, id_ref, prob_ref,
    up_ref, down_ref,
    q_all, f_all, pool, tables, counts, expert_out, share_ref,
    relay, f_relay, q_rows, table_ref, count_rows, out0, out1, out2, mid0, mid1, mid2, sorted0, sorted1, sorted2,
    in0, in1, in2, up_w, down_w, projected, active,
    q_send, q_recv, f_send, f_recv, a_send, a_recv, z_send, z_recv, c_send, c_recv,
    i_send, i_recv, d_send, d_recv, e_send, e_recv, local, w_sem,
):
    y, z, x, c = place()
    mate = 3 - y
    rows_out, rows_mid = (out0, out1, out2), (mid0, mid1, mid2)
    rows_sorted, rows_in = (sorted0, sorted1, sorted2), (in0, in1, in2)

    def at(dy, dx):
        return device(lax.rem(y + dy, 4), z, lax.rem(x + dx, 4), c)

    plane = [(dy, dx) for dy in range(4) for dx in range(4) if (dy, dx) != (0, 0)]
    up = device(y, lax.rem(z + 1, 4), x, c)
    down = device(y, lax.rem(z + 3, 4), x, c)
    twin = device(y, z, x, 1 - c)

    def beside(dy, dz):
        return device(lax.rem(y + dy, 4), lax.rem(z + dz, 4), x, c)

    def around(dx, dc):
        return device(y, z, lax.rem(x + dx, 4), lax.rem(c + dc, 2))

    peers = [at(dy, dx) for dy, dx in plane]
    peers += [beside(dy, dz) for dy in range(4) for dz in range(1, 4)]
    peers += [around(dx, 1) for dx in range(4)]
    barrier = pltpu.get_barrier_semaphore()
    for peer in peers:
        pl.semaphore_signal(barrier, inc=1, device_id=peer, device_id_type=MESH)

    weights = []
    for n in range(4):
        part = pl.ds(n * (D // 4), D // 4)
        weights.append(pltpu.make_async_copy(up_ref.at[0, part], up_w.at[part], w_sem.at[n]))
    for n in range(2):
        part = pl.ds(n * (HID // 2), HID // 2)
        weights.append(pltpu.make_async_copy(down_ref.at[0, part], down_w.at[part], w_sem.at[4 + n]))
    for copy in weights:
        copy.start()

    fresh = f_ref[...].reshape(ROWS, f_ref.shape[2])
    for h in range(KEY_VALUE_HEADS):
        low, high = h * HEAD_WIDTH, (h + 1) * HEAD_WIDTH
        split = KEY_VALUE_HEADS * HEAD_WIDTH
        rows = jnp.concatenate(
            [page_ref[:, low:high], page_ref[:, split + low : split + high]], axis=1
        )
        relay[h] = rows.reshape(PAGES, PAGE_TOKENS, 2 * HEAD_WIDTH)
        f_relay[h] = jnp.concatenate(
            [fresh[:, low:high], fresh[:, split + low : split + high]], axis=1
        )
    for xx in range(4):
        e = z * 8 + xx * 2 + c
        pages = owner_ref[e] * PAGES + slot_ref[e]
        for half in range(2):
            lanes = slice(half * 64, half * 64 + 64)
            table_ref[xx, half : half + 1, :] = jnp.concatenate(
                [pages[0:1, lanes], pages[1:2, lanes]], axis=1
            )
    lane = iota((PROMPTS, 128), 1)
    copies = (iota((PROMPTS, 128), 0) == lax.div(lax.rem(lane, ROWS), SCORED_STEPS)).astype(F32)
    wide = nn(count_ref[...].astype(F32), copies, HIGHEST)
    mine = lax.div(iota((N_SEQ, 128), 1), ROWS) == iota((N_SEQ, 128), 0)
    wide = jnp.sum(jnp.where(mine, wide, 0.0), axis=0, keepdims=True)
    count_rows[...] = jnp.broadcast_to(wide, (8, 128))

    h32 = hidden_ref[...].reshape(ROWS, D).astype(F32)
    scale = lax.rsqrt(jnp.mean(h32 * h32, axis=-1, keepdims=True) + EPSILON)
    normed = (h32 * scale * gain_ref[...].reshape(1, D)).astype(BF16)
    slots, owner_token, share = route(id_ref, prob_ref)
    share_ref[...] = share
    spread = nn(slots, owner_token).astype(BF16)
    for k, (first_column, columns) in enumerate(PARTS):
        piece = normed[:, first_column : first_column + columns]
        rows_out[k][...] = nn(spread, piece).astype(BF16).reshape(16, 16, columns)
    pl.semaphore_wait(barrier, len(peers))

    def spot(segment_slot, zz, xx, cc):
        return pool.at[segment_slot, pl.ds((zz * 8 + xx * 2 + cc) * PAGES, PAGES)]

    order = [(0, 0), (0, 1), (0, 3), (0, 2), (1, 0), (1, 1), (1, 3), (1, 2)]
    first = []

    def hand_out(n):
        p, dx = order[n]
        yy = y if p == 0 else mate
        xx = lax.rem(x + dx, 4)
        target = spot(lax.div(y, 2), z, x, c)
        source = relay.at[head_of(yy, xx)]
        if (p, dx) == (0, 0):
            copy = pltpu.make_async_copy(source, target, local.at[0])
        else:
            copy = pltpu.make_async_remote_copy(
                source, target, a_send.at[n], a_recv.at[n],
                device_id=device(yy, z, xx, c), device_id_type=MESH,
            )
        copy.start()
        first.append(copy)

    for n in range(4):
        hand_out(n)
    routed = []
    for k in range(len(PARTS)):
        for dy in range(4):
            for dz in range(4):
                n = dy * 4 + dz
                source = rows_out[k].at[lax.rem(y + dy, 4) * 4 + lax.rem(z + dz, 4)]
                target = rows_mid[k].at[y * 4 + z]
                if n == 0:
                    copy = pltpu.make_async_copy(source, target, local.at[5 + 2 * k])
                else:
                    copy = pltpu.make_async_remote_copy(
                        source, target, d_send.at[k * 16 + n], d_recv.at[k * 16 + n],
                        device_id=beside(dy, dz), device_id_type=MESH,
                    )
                copy.start()
                routed.append(copy)

    for n in range(4, 8):
        hand_out(n)

    small = []
    mine = pltpu.make_async_copy(table_ref, tables.at[lax.div(y, 2)], local.at[1])
    mine.start()
    small.append(mine)
    mine = pltpu.make_async_copy(count_rows, counts.at[x], local.at[2])
    mine.start()
    small.append(mine)
    other = pltpu.make_async_remote_copy(
        table_ref, tables.at[lax.div(y, 2)], i_send.at[0], i_recv.at[0],
        device_id=device(mate, z, x, c), device_id_type=MESH,
    )
    other.start()
    small.append(other)
    for dx in range(1, 4):
        other = pltpu.make_async_remote_copy(
            count_rows, counts.at[x], i_send.at[dx], i_recv.at[dx],
            device_id=at(0, dx), device_id_type=MESH,
        )
        other.start()
        small.append(other)

    def chunk(n):
        p, dx = order[n]
        yy = y if p == 0 else mate
        return lax.div(yy, 2), lax.rem(x - dx + 4, 4)

    def pass_on(n, zz, way, peer):
        segment_slot, xx = chunk(n)
        block = spot(segment_slot, zz, xx, c)
        sends, recvs = (c_send, c_recv) if way >= 3 else (z_send, z_recv)
        number = (way - 3 if way >= 3 else way) * 8 + n
        copy = pltpu.make_async_remote_copy(
            block, block, sends.at[number], recvs.at[number],
            device_id=peer, device_id_type=MESH,
        )
        copy.start()
        return copy

    upward, downward, further, across = [], [], [], []

    def begin(n):
        if n == 0:
            first[n].wait()
        else:
            first[n].wait_recv()
        upward.append(pass_on(n, z, 0, up))
        downward.append(pass_on(n, z, 1, down))
        across.append(pass_on(n, z, 3, twin))

    def forward(n):
        upward[n].wait_recv()
        if n % 2 == 0:
            further.append(pass_on(n, lax.rem(z + 3, 4), 2, up))
        across.append(pass_on(n, lax.rem(z + 3, 4), 4, twin))
        downward[n].wait_recv()
        if n % 2 == 1:
            further.append(pass_on(n, lax.rem(z + 1, 4), 2, down))
        across.append(pass_on(n, lax.rem(z + 1, 4), 5, twin))

    for n in range(4):
        begin(n)

    ri = iota((256, 256), 0)
    ci = iota((256, 256), 1)

    def slot_of(i):
        return lax.div(lax.rem(i, 32), 2) * 16 + lax.div(i, 32) * 2 + lax.rem(i, 2)

    def arrive(copies):
        copies[0].wait()
        for copy in copies[1:]:
            copy.wait_recv()

    regroup = (slot_of(ri) == ci).astype(BF16)
    delivered = [[], [], []]
    for k, (_, columns) in enumerate(PARTS):
        arrive(routed[k * 16 : (k + 1) * 16])
        moved = nn(regroup, rows_mid[k][...].reshape(256, columns)).astype(BF16)
        rows_sorted[k][...] = moved.reshape(8, 32, columns)
        for dx in range(4):
            for dc in range(2):
                n = dx * 2 + dc
                source = rows_sorted[k].at[lax.rem(x + dx, 4) * 2 + lax.rem(c + dc, 2)]
                target = rows_in[k].at[x * 2 + c]
                if n == 0:
                    copy = pltpu.make_async_copy(source, target, local.at[6 + 2 * k])
                else:
                    copy = pltpu.make_async_remote_copy(
                        source, target, e_send.at[k * 8 + n], e_recv.at[k * 8 + n],
                        device_id=around(dx, dc), device_id_type=MESH,
                    )
                copy.start()
                delivered[k].append(copy)
        if k == 1:
            for n in (0, 1):
                forward(n)
    for n in range(4, 8):
        begin(n)
    for n in (2, 3):
        forward(n)

    q_rows[...] = q_ref[...].reshape(ROWS, q_ref.shape[2])
    for dy in range(4):
        for dx in range(4):
            n = dy * 4 + dx
            h = head_of(lax.rem(y + dy, 4), lax.rem(x + dx, 4))
            q_source = q_rows.at[:, pl.ds(pl.multiple_of(h * HEAD_COLUMNS, HEAD_COLUMNS), HEAD_COLUMNS)]
            f_source = f_relay.at[h]
            slot = x * 4 + y
            if n == 0:
                copies = [
                    pltpu.make_async_copy(q_source, q_all.at[slot], local.at[3]),
                    pltpu.make_async_copy(f_source, f_all.at[slot], local.at[4]),
                ]
            else:
                copies = [
                    pltpu.make_async_remote_copy(
                        q_source, q_all.at[slot], q_send.at[n], q_recv.at[n],
                        device_id=at(dy, dx), device_id_type=MESH,
                    ),
                    pltpu.make_async_remote_copy(
                        f_source, f_all.at[slot], f_send.at[n], f_recv.at[n],
                        device_id=at(dy, dx), device_id_type=MESH,
                    ),
                ]
            for copy in copies:
                copy.start()
            small.extend(copies)

    for copy in weights:
        copy.wait()

    def tiles(work):
        @pl.loop(0, D // TILE)
        def _(j):
            work(pl.ds(pl.multiple_of(j * TILE, TILE), TILE))

        work(pl.ds(D // TILE * TILE, D % TILE))

    def project(k):
        first_column, columns = PARTS[k]
        arrive(delivered[k])

        def work(part):
            rows = rows_in[k][...].reshape(256, columns)
            term = nn(rows, up_w[first_column : first_column + columns, part])
            projected[:, part] = term if k == 0 else projected[:, part] + term

        tiles(work)

    project(0)
    project(1)
    forward(4)
    forward(5)
    project(2)
    forward(6)
    forward(7)

    @pl.loop(0, 8)
    def _(j):
        part = pl.ds(pl.multiple_of(j * 32, 32), 32)
        wide = projected[part, :]
        gate, upper = wide[:, :HID], wide[:, HID:]
        active[part, :] = ((upper + 1.0) * gate * jax.nn.sigmoid(1.702 * gate)).astype(BF16)

    back = (slot_of(ci) == ri).astype(BF16)
    active[...] = nn(back, active[...]).astype(BF16)

    def finish(part):
        rows = nn(active[...], down_w[:, part]).astype(BF16)
        expert_out[:, :, part] = rows.reshape(128, 2, rows.shape[1])

    @pl.loop(0, 3)
    def _(j):
        finish(pl.ds(pl.multiple_of(j * TILE, TILE), TILE))

    for n in range(8):
        further[n].wait_recv()
        across.append(pass_on(n, lax.rem(z + 2, 4), 6, twin))

    @pl.loop(3, D // TILE)
    def _(j):
        finish(pl.ds(pl.multiple_of(j * TILE, TILE), TILE))

    finish(pl.ds(D // TILE * TILE, D % TILE))

    for copy in across:
        copy.wait()
    for copy in first[1:] + upward + downward + further:
        copy.wait_send()
    for n, copy in enumerate(routed):
        if n % 16 > 0:
            copy.wait_send()
    for copy in sum([copies[1:] for copies in delivered], []):
        copy.wait_send()
    for copy in small:
        copy.wait()


TILE = 512


def exchange(
    queries, fresh, pages, owner, slot, count, hidden, gain, ids, prob, gate_up, down_proj
):
    vmem = pl.BlockSpec(memory_space=pltpu.VMEM)
    anywhere = pl.BlockSpec(memory_space=pl.ANY)
    dma = pltpu.SemaphoreType.DMA
    return pl.pallas_call(
        exchange_kernel,
        out_shape=(
            jax.ShapeDtypeStruct((16, ROWS, HEAD_COLUMNS), BF16),
            jax.ShapeDtypeStruct((16, ROWS, 2 * HEAD_WIDTH), BF16),
            jax.ShapeDtypeStruct((2, N_EP * PAGES, PAGE_TOKENS, 2 * HEAD_WIDTH), BF16),
            jax.ShapeDtypeStruct((2, 4, 2, 128), jnp.int32),
            jax.ShapeDtypeStruct((4, 8, 128), F32),
            jax.ShapeDtypeStruct((128, 2, D), BF16),
            jax.ShapeDtypeStruct((ROWS, 256), F32),
        ),
        in_specs=[vmem] * 10 + [anywhere] * 2,
        out_specs=(anywhere,) * 5 + (vmem, vmem),
        scratch_shapes=[
            pltpu.VMEM((KEY_VALUE_HEADS, PAGES, PAGE_TOKENS, 2 * HEAD_WIDTH), BF16),
            pltpu.VMEM((KEY_VALUE_HEADS, ROWS, 2 * HEAD_WIDTH), BF16),
            pltpu.VMEM((ROWS, QUERY_HEADS * HEAD_WIDTH), BF16),
            pltpu.VMEM((4, 2, 128), jnp.int32),
            pltpu.VMEM((8, 128), F32),
            *[pltpu.VMEM((16, 16, columns), BF16) for _, columns in PARTS * 2],
            *[pltpu.VMEM((8, 32, columns), BF16) for _, columns in PARTS * 2],
            pltpu.VMEM((D, 2 * HID), BF16),
            pltpu.VMEM((HID, D), BF16),
            pltpu.VMEM((256, 2 * HID), F32),
            pltpu.VMEM((256, HID), BF16),
            dma((16,)), dma((16,)), dma((16,)), dma((16,)), dma((8,)), dma((8,)),
            dma((24,)), dma((24,)), dma((32,)), dma((32,)), dma((4,)), dma((4,)),
            dma((48,)), dma((48,)), dma((24,)), dma((24,)), dma((11,)), dma((6,)),
        ],
        compiler_params=pltpu.CompilerParams(
            collective_id=1, has_side_effects=True, vmem_limit_bytes=56 << 20
        ),
        name="exchange",
    )(queries, fresh, pages, owner, slot, count, hidden, gain, ids, prob, gate_up, down_proj)


BK = 1024
GK = 4096
KEYS = 2 * NPS * PAGE_TOKENS
UNITS = 4
CHUNKS = 4
COLS = 256
VROWS = 80


def values_of(rows):
    pick = (iota((VROWS, 128), 0) + HEAD_WIDTH == iota((VROWS, 128), 1)).astype(BF16)
    moved = nt(pick, rows)
    return jnp.where(iota(moved.shape, 0) >= HEAD_WIDTH, 1.0, moved).astype(BF16)


def score_kernel(
    table_ref, count_ref, sinks, q_ref, f_ref, pool_ref, o_ref, lse_ref,
    tables, counts, q_all, f_all, pool,
    kv, vt, qs, limit_ref, m_ref, acc, sorted_out, s0, s1, places, lengths, sem,
):
    y = lax.axis_index("seq")
    outer_pair = jnp.logical_or(y == 0, y == 3)
    loads = [
        pltpu.make_async_copy(source, target, sem.at[n])
        for n, (source, target) in enumerate(
            [(count_ref, counts), (q_ref, q_all), (f_ref, f_all), (table_ref, tables)]
        )
    ]
    share = pool.shape[0] // 8
    for n in range(8):
        part = pl.ds(n * share, share)
        loads.append(pltpu.make_async_copy(pool_ref.at[part], pool.at[part], sem.at[4 + n]))
    for copy in loads:
        copy.start()
    for copy in loads[:3]:
        copy.wait()
    sink_row = sinks[0:1, :]
    i0 = iota((128, 128), 0)
    i1 = iota((128, 128), 1)
    lane_row = lax.rem(iota((128, COLS), 1), ROWS).astype(F32)

    def ordering(e):
        c = counts[e][0:1, :]
        n_row = jnp.where(
            outer_pair,
            jnp.minimum(c, 256.0) + jnp.maximum(c - 768.0, 0.0),
            jnp.clip(c - 256.0, 0.0, 512.0),
        )
        n_col = jnp.sum(jnp.where(i0 == i1, n_row, 0.0), axis=1, keepdims=True)
        behind = jnp.logical_or(n_row > n_col, jnp.logical_and(n_col == n_row, i1 < i0))
        pos_col = jnp.sum(jnp.where(behind, 1.0, 0.0), axis=1, keepdims=True)
        return n_row, n_col, pos_col

    for e in range(UNITS):
        n_row, n_col, pos_col = ordering(e)
        places[e] = pos_col
        ahead = jnp.logical_or(n_col > n_row, jnp.logical_and(n_col == n_row, i0 < i1))
        pos_row = jnp.sum(jnp.where(ahead, 1.0, 0.0), axis=0, keepdims=True)
        perm = (pos_row == i0.astype(F32)).astype(BF16)
        q_sorted = nn(perm, q_all[e * 4 : e * 4 + 4].reshape(128, HEAD_COLUMNS)) * 0.125
        f_sorted = nn(perm, f_all[e * 4 : e * 4 + 4].reshape(128, 128)).astype(BF16)
        none = jnp.zeros((COLS, HEAD_WIDTH), F32)
        for ch in range(CHUNKS):
            u = e * CHUNKS + ch
            pieces = [
                q_sorted[ch * ROWS : (ch + 1) * ROWS, g * HEAD_WIDTH : (g + 1) * HEAD_WIDTH]
                for g in range(GROUP)
            ]
            stacked = jnp.concatenate([jnp.concatenate(pieces, axis=0), none], axis=1)
            qs[u] = stacked.T.astype(BF16)
            member = pos_col == lane_row + float(ch * ROWS)
            limit = jnp.sum(jnp.where(member, n_col, 0.0), axis=0, keepdims=True) * PAGE_TOKENS
            limit_ref[u] = jnp.broadcast_to(limit, (8, COLS))
            lengths[u] = jnp.max(limit).astype(jnp.int32)
            rows = f_sorted[ch * ROWS : (ch + 1) * ROWS, :]
            s = nn(rows, qs[u])
            ki = iota((ROWS, COLS), 0)
            ri = lax.rem(iota((ROWS, COLS), 1), ROWS)
            seen = jnp.logical_and(
                lax.div(ki, SCORED_STEPS) == lax.div(ri, SCORED_STEPS), ki <= ri
            )
            s = jnp.where(seen, s, NEGATIVE)
            m0 = jnp.maximum(jnp.max(s, axis=0, keepdims=True), sink_row)
            p = jnp.exp(s - m0).astype(BF16)
            start = nn(values_of(rows), p)
            start = start + jnp.where(
                iota((VROWS, COLS), 0) >= HEAD_WIDTH, jnp.exp(sink_row - m0), 0.0
            )
            m_ref[u] = jnp.broadcast_to(jnp.where(outer_pair, m0, FLOOR), (8, COLS))
            acc[u] = jnp.where(outer_pair, start, 0.0)

    def unit(e, carry):
        def gather(kb, carry):
            rows = [
                pool[tables[kb, e, i // 128, i % 2 * 64 + i % 128 // 2] + kb * (N_EP * PAGES)]
                for i in range(GK // PAGE_TOKENS)
            ]
            for i in range(GK // BK):
                part = rows[i * (BK // PAGE_TOKENS) : (i + 1) * (BK // PAGE_TOKENS)]
                found = jnp.concatenate(part, axis=0)
                kv[pl.ds(pl.multiple_of(kb * GK + i * BK, BK), BK), :] = found
                vt[kb * (GK // BK) + i] = values_of(found)
            return carry

        lax.fori_loop(0, lax.div(lengths[e * CHUNKS] + (GK - 1), GK), gather, 0)

        key = iota((BK, COLS), 0).astype(F32)

        def produce(store, u, kb):
            keys = kv[pl.ds(pl.multiple_of(kb * BK, BK), BK), :]
            s = nn(keys, qs[u])
            limit = limit_ref[u][0:1, :] - (kb * BK).astype(F32)
            s = jnp.where(key < limit, s, NEGATIVE)
            store[...] = s
            return jnp.max(s, axis=0, keepdims=True)

        def absorb(store, u, kb, top):
            before = m_ref[u][0:1, :]
            after = jnp.maximum(before, top)
            p = jnp.exp(store[...] - after).astype(BF16)
            acc[u] = acc[u] * jnp.exp(before - after) + nn(vt[kb], p)
            m_ref[u] = jnp.broadcast_to(after, (8, COLS))

        def chunk(ch, top):
            u = e * CHUNKS + ch
            count = lax.div(lengths[u] + (BK - 1), BK)
            after_u = e * CHUNKS + jnp.minimum(ch + 1, CHUNKS - 1)

            def pair(i, top):
                last = 2 * i + 2 >= count
                next_top = produce(s1, u, 2 * i + 1)
                absorb(s0, u, 2 * i, top)
                top = produce(s0, jnp.where(last, after_u, u), jnp.where(last, 0, 2 * i + 2))
                absorb(s1, u, 2 * i + 1, next_top)
                return top

            top = lax.fori_loop(0, lax.div(count, 2), pair, top)

            def odd(top):
                absorb(s0, u, count - 1, top)
                return produce(s0, after_u, jnp.int32(0))

            return lax.cond(lax.rem(count, 2) == 1, odd, lambda top: top, top)

        used = sum([(lengths[e * CHUNKS + ch] > 0).astype(jnp.int32) for ch in range(CHUNKS)])

        @pl.when(used > 0)
        def _():
            top = produce(s0, e * CHUNKS, jnp.int32(0))
            lax.fori_loop(0, used, chunk, top)

        return carry

    for copy in loads[3:]:
        copy.wait()
    lax.fori_loop(0, UNITS, unit, 0)

    for e in range(UNITS):
        pos_col = places[e]
        perm_t = (pos_col == i1.astype(F32)).astype(BF16)
        lse = jnp.zeros((8, 128), F32)
        for ch in range(CHUNKS):
            u = e * CHUNKS + ch
            total = jnp.maximum(acc[u][HEAD_WIDTH : HEAD_WIDTH + 1, :], 1e-30)
            out = acc[u][0:HEAD_WIDTH, :] / total
            padded = jnp.concatenate([out, jnp.zeros_like(out)], axis=0)
            turned = padded.T.astype(BF16)
            for g in range(GROUP):
                sorted_out[e, ch * ROWS : (ch + 1) * ROWS, g * HEAD_WIDTH : (g + 1) * HEAD_WIDTH] = (
                    turned[g * ROWS : (g + 1) * ROWS, 0:HEAD_WIDTH]
                )
            row = m_ref[u][0:1, :] + jnp.log(total)
            mine = lax.div(iota((8, COLS), 1), ROWS) == iota((8, COLS), 0)
            member = (pos_col == lane_row + float(ch * ROWS)).astype(BF16)
            rest = jnp.where(mine, row, 0.0)
            layers = []
            for _ in range(3):
                layers.append(rest.astype(BF16))
                rest = rest - layers[-1].astype(F32)
            moved = nt(jnp.concatenate([layer.astype(F32) for layer in layers], axis=0).astype(BF16), member)
            lse = lse + (moved[0:8] + moved[8:16] + moved[16:24])
        lse_ref[e] = lse
        o_ref[e] = nn(perm_t, sorted_out[e]).astype(BF16)


def score(tables, counts, sinks, q_all, f_all, pool):
    vmem = pl.BlockSpec(memory_space=pltpu.VMEM)
    anywhere = pl.BlockSpec(memory_space=pl.ANY)
    return pl.pallas_call(
        score_kernel,
        out_shape=(
            jax.ShapeDtypeStruct((UNITS, 128, HEAD_COLUMNS), BF16),
            jax.ShapeDtypeStruct((UNITS, 8, 128), F32),
        ),
        in_specs=[anywhere, anywhere, vmem, anywhere, anywhere, anywhere],
        out_specs=(vmem, vmem),
        scratch_shapes=[
            pltpu.SMEM((2, UNITS, 2, 128), jnp.int32),
            pltpu.VMEM((UNITS, 8, 128), F32),
            pltpu.VMEM((16, ROWS, HEAD_COLUMNS), BF16),
            pltpu.VMEM((16, ROWS, 2 * HEAD_WIDTH), BF16),
            pltpu.VMEM((2 * N_EP * PAGES, PAGE_TOKENS, 2 * HEAD_WIDTH), BF16),
            pltpu.VMEM((KEYS, 128), BF16),
            pltpu.VMEM((KEYS // BK, VROWS, BK), BF16),
            pltpu.VMEM((UNITS * CHUNKS, 128, COLS), BF16),
            pltpu.VMEM((UNITS * CHUNKS, 8, COLS), F32),
            pltpu.VMEM((UNITS * CHUNKS, 8, COLS), F32),
            pltpu.VMEM((UNITS * CHUNKS, VROWS, COLS), F32),
            pltpu.VMEM((UNITS, 128, HEAD_COLUMNS), BF16),
            pltpu.VMEM((BK, COLS), F32),
            pltpu.VMEM((BK, COLS), F32),
            pltpu.VMEM((UNITS, 128, 1), F32),
            pltpu.SMEM((UNITS * CHUNKS,), jnp.int32),
            pltpu.SemaphoreType.DMA((12,)),
        ],
        compiler_params=pltpu.CompilerParams(vmem_limit_bytes=60 << 20),
        cost_estimate=pl.CostEstimate(
            flops=25_000_000_000, bytes_accessed=8_000_000, transcendentals=20_000_000
        ),
        name="score",
    )(tables, counts, sinks, q_all, f_all, pool)


def merge_kernel(
    o_ref, lse_ref, share_ref, rows_ref, out_ref, mix_ref, o_all, lse_all, o_send, o_recv, l_send, l_recv, local,
):
    y, z, x, c = place()

    def at(dy, dx):
        return device(lax.rem(y + dy, 4), z, lax.rem(x + dx, 4), c)

    plane = [(dy, dx) for dy in range(4) for dx in range(4) if (dy, dx) != (0, 0)]
    barrier = pltpu.get_barrier_semaphore()
    for dy, dx in plane:
        pl.semaphore_signal(barrier, inc=1, device_id=at(dy, dx), device_id_type=MESH)
    pl.semaphore_wait(barrier, len(plane))
    inner_pair = jnp.logical_or(y == 1, y == 2).astype(jnp.int32)
    slot = inner_pair * 8 + head_of(y, x)
    copies = []
    for dy in range(4):
        for dx in range(4):
            n = dy * 4 + dx
            q = lax.rem(y + dy, 4)
            e = lax.rem(x + dx, 4)
            o_source = o_ref.at[e, pl.ds(pl.multiple_of(q * ROWS, ROWS), ROWS)]
            if n == 0:
                pair = [
                    pltpu.make_async_copy(o_source, o_all.at[slot], local.at[0]),
                    pltpu.make_async_copy(lse_ref.at[e], lse_all.at[slot], local.at[1]),
                ]
            else:
                pair = [
                    pltpu.make_async_remote_copy(
                        o_source, o_all.at[slot], o_send.at[n], o_recv.at[n],
                        device_id=at(dy, dx), device_id_type=MESH,
                    ),
                    pltpu.make_async_remote_copy(
                        lse_ref.at[e], lse_all.at[slot], l_send.at[n], l_recv.at[n],
                        device_id=at(dy, dx), device_id_type=MESH,
                    ),
                ]
            for copy in pair:
                copy.start()
            copies.extend(pair)

    share = share_ref[...]
    high = share.astype(BF16)
    low = (share - high.astype(F32)).astype(BF16)
    rows = rows_ref[...].reshape(256, D)
    mix_ref[...] = (nn(high, rows) + nn(low, rows)).astype(BF16)

    for copy in copies:
        copy.wait()
    mine = (iota((ROWS, 128), 1) == iota((ROWS, 128), 0) + y * ROWS).astype(F32)
    logs = nt(mine, lse_all[...].reshape(128, 128), HIGHEST)
    log0, log1 = logs[:, :64], logs[:, 64:]
    top = jnp.maximum(log0, log1)
    w0, w1 = jnp.exp(log0 - top), jnp.exp(log1 - top)
    share0, share1 = w0 / (w0 + w1), w1 / (w0 + w1)
    shares = jnp.concatenate([share0, share1], axis=0)
    high = shares.astype(BF16)
    low = (shares - high.astype(F32)).astype(BF16)
    both = jnp.concatenate([high, low], axis=1)
    for h in range(KEY_VALUE_HEADS):
        shape = (128, HEAD_COLUMNS)
        head = lax.div(iota(shape, 1), HEAD_WIDTH) + h * GROUP
        spread = (lax.rem(iota(shape, 0), QUERY_HEADS) == head).astype(BF16)
        wide = nn(both, spread)
        result = wide[:ROWS] * o_all[h].astype(F32) + wide[ROWS:] * o_all[8 + h].astype(F32)
        out_ref[:, h * HEAD_COLUMNS : (h + 1) * HEAD_COLUMNS] = result.astype(BF16)


def merge(o, lse, share, rows):
    vmem = pl.BlockSpec(memory_space=pltpu.VMEM)
    anywhere = pl.BlockSpec(memory_space=pl.ANY)
    dma = pltpu.SemaphoreType.DMA
    return pl.pallas_call(
        merge_kernel,
        out_shape=(
            jax.ShapeDtypeStruct((ROWS, QUERY_HEADS * HEAD_WIDTH), BF16),
            jax.ShapeDtypeStruct((ROWS, D), BF16),
        ),
        in_specs=[anywhere, anywhere, vmem, vmem],
        out_specs=(vmem, vmem),
        scratch_shapes=[
            pltpu.VMEM((16, ROWS, HEAD_COLUMNS), BF16),
            pltpu.VMEM((16, 8, 128), F32),
            dma((16,)), dma((16,)), dma((16,)), dma((16,)), dma((2,)),
        ],
        compiler_params=pltpu.CompilerParams(
            collective_id=2, has_side_effects=True, vmem_limit_bytes=16 << 20
        ),
        name="merge",
    )(o, lse, share, rows)


def by_prefix(table):
    return table[0].T.reshape(2, N_EP, NPS // 2).transpose(1, 0, 2)


def per_device(
    queries, fresh_key_values, key_value_pages, page_owner, page_slot, page_count, sinks,
    hidden, norm_gain, expert_ids, gate_prob, gate_up, down_proj,
):
    y, z, x, c = place()

    q_all, f_all, pool, tables, counts, result, share = exchange(
        queries[0],
        fresh_key_values[0],
        key_value_pages.reshape(PAGES * PAGE_TOKENS, 2 * KEY_VALUE_HEADS * HEAD_WIDTH),
        by_prefix(page_owner),
        by_prefix(page_slot),
        page_count,
        hidden[0],
        norm_gain,
        expert_ids[0].transpose(1, 2, 0),
        gate_prob[0].transpose(1, 2, 0),
        gate_up,
        down_proj,
    )
    returned = lax.all_to_all(result, ("seq", "ep"), split_axis=0, concat_axis=0, tiled=True)
    head_sinks = lax.dynamic_slice_in_dim(sinks, head_of(y, x) * GROUP, GROUP)
    sink_rows = jnp.broadcast_to(jnp.repeat(head_sinks, ROWS)[None, :], (8, COLS))
    o, lse = score(
        tables, counts, sink_rows, q_all, f_all,
        pool.reshape(2 * N_EP * PAGES, PAGE_TOKENS, 2 * HEAD_WIDTH),
    )
    attention, mixture = merge(o, lse, share, returned)
    return (attention.reshape(queries.shape), mixture.reshape(hidden.shape))


def solution(mesh):
    return jax.shard_map(
        per_device,
        mesh=mesh,
        in_specs=(
            P("seq", "ep", None, None),
            P("seq", "ep", None, None),
            P("seq", "ep", None, None),
            P("seq", None, None),
            P("seq", None, None),
            P(None, "ep"),
            P(),
            P("seq", "ep", None, None),
            P(),
            P("seq", "ep", None, None),
            P("seq", "ep", None, None),
            P(("seq", "ep"), None, None),
            P(("seq", "ep"), None, None),
        ),
        out_specs=(P("seq", "ep", None, None), P("seq", "ep", None, None)),
        check_vma=False,
    )
```

```python
import jax
import jax.numpy as jnp
from jax import lax
from jax.experimental import pallas as pl
from jax.experimental.pallas import tpu as pltpu
from jax.sharding import PartitionSpec as P

D = 2880
QUERY_HEADS = 64
KEY_VALUE_HEADS = 8
GROUP = QUERY_HEADS // KEY_VALUE_HEADS
HEAD_WIDTH = 64
TOPK = 4
HID = 1440
SCORED_STEPS = 4
PAGE_TOKENS = 16
NPS = 256
PAGES = 24
PROMPTS = 8
N_SEQ = 4
N_EP = 32
ROWS = PROMPTS * SCORED_STEPS
HEAD_COLUMNS = GROUP * HEAD_WIDTH
NEGATIVE = -1e30
FLOOR = -1e29
EPSILON = 1e-05
MESH = pl.DeviceIdType.MESH
F32 = jnp.float32
BF16 = jnp.bfloat16
HIGHEST = lax.Precision.HIGHEST


def place():
    y = lax.axis_index("seq")
    ep = lax.axis_index("ep")
    return y, lax.div(ep, 8), lax.rem(lax.div(ep, 2), 4), lax.rem(ep, 2)


def device(y, z, x, c):
    return (y, z * 8 + x * 2 + c)


def head_of(y, x):
    return lax.div(y, 2) * 4 + x


def nt(a, b, precision=None):
    return lax.dot_general(
        a, b, (((1,), (1,)), ((), ())), preferred_element_type=F32, precision=precision
    )


def nn(a, b, precision=None):
    return lax.dot_general(
        a, b, (((1,), (0,)), ((), ())), preferred_element_type=F32, precision=precision
    )


def iota(shape, axis):
    return lax.broadcasted_iota(jnp.int32, shape, axis)


PARTS = ((0, 1024), (1024, 1024), (2048, D - 2048))


def route(id_ref, prob_ref):
    i0 = iota((128, 128), 0)
    i1 = iota((128, 128), 1)
    copies = (iota((8, 128), 0) == lax.rem(iota((8, 128), 1), 8)).astype(F32)
    group = lax.div(iota((TOPK, 128), 1), 8)

    def as_row(ref):
        row = jnp.zeros((1, 128), F32)
        for t in range(SCORED_STEPS):
            wide = nn(ref[t].astype(F32), copies, HIGHEST)
            mine = group == iota((TOPK, 128), 0) + t * TOPK
            row = row + jnp.sum(jnp.where(mine, wide, 0.0), axis=0, keepdims=True)
        return row

    ids = as_row(id_ref)
    column = jnp.sum(jnp.where(i0 == i1, ids, 0.0), axis=1, keepdims=True)
    earlier = jnp.logical_and(column == ids, i0 < i1)
    rank = jnp.sum(jnp.where(earlier, 1.0, 0.0), axis=0, keepdims=True)
    slots = iota((256, 128), 0).astype(F32) == 2.0 * ids + rank

    def token(a):
        return lax.rem(a, 8) * SCORED_STEPS + lax.div(a, 32)

    owner_token = (token(iota((128, ROWS), 0)) == iota((128, ROWS), 1)).astype(BF16)
    mine = token(iota((ROWS, 128), 1)) == iota((ROWS, 128), 0)
    share = nt(jnp.where(mine, as_row(prob_ref), 0.0), slots.astype(F32), HIGHEST)
    return slots.astype(BF16), owner_token, share


def exchange_kernel(
    q_ref, f_ref, page_ref, owner_ref, slot_ref, count_ref, hidden_ref, gain_ref, id_ref, prob_ref,
    up_ref, down_ref,
    q_all, f_all, pool, tables, counts, expert_out, share_ref,
    relay, f_relay, q_rows, table_ref, count_rows, out0, out1, out2, mid0, mid1, mid2, sorted0, sorted1, sorted2,
    in0, in1, in2, up_w, down_w, projected, active,
    q_send, q_recv, f_send, f_recv, a_send, a_recv, z_send, z_recv, c_send, c_recv,
    i_send, i_recv, d_send, d_recv, e_send, e_recv, local, w_sem,
):
    y, z, x, c = place()
    mate = 3 - y
    rows_out, rows_mid = (out0, out1, out2), (mid0, mid1, mid2)
    rows_sorted, rows_in = (sorted0, sorted1, sorted2), (in0, in1, in2)

    def at(dy, dx):
        return device(lax.rem(y + dy, 4), z, lax.rem(x + dx, 4), c)

    plane = [(dy, dx) for dy in range(4) for dx in range(4) if (dy, dx) != (0, 0)]
    up = device(y, lax.rem(z + 1, 4), x, c)
    down = device(y, lax.rem(z + 3, 4), x, c)
    twin = device(y, z, x, 1 - c)

    def beside(dy, dz):
        return device(lax.rem(y + dy, 4), lax.rem(z + dz, 4), x, c)

    def around(dx, dc):
        return device(y, z, lax.rem(x + dx, 4), lax.rem(c + dc, 2))

    peers = [at(dy, dx) for dy, dx in plane]
    peers += [beside(dy, dz) for dy in range(4) for dz in range(1, 4)]
    peers += [around(dx, 1) for dx in range(4)]
    barrier = pltpu.get_barrier_semaphore()
    for peer in peers:
        pl.semaphore_signal(barrier, inc=1, device_id=peer, device_id_type=MESH)

    weights = []
    for n in range(4):
        part = pl.ds(n * (D // 4), D // 4)
        weights.append(pltpu.make_async_copy(up_ref.at[0, part], up_w.at[part], w_sem.at[n]))
    for n in range(2):
        part = pl.ds(n * (HID // 2), HID // 2)
        weights.append(pltpu.make_async_copy(down_ref.at[0, part], down_w.at[part], w_sem.at[4 + n]))
    for copy in weights:
        copy.start()

    fresh = f_ref[...].reshape(ROWS, f_ref.shape[2])
    for h in range(KEY_VALUE_HEADS):
        low, high = h * HEAD_WIDTH, (h + 1) * HEAD_WIDTH
        split = KEY_VALUE_HEADS * HEAD_WIDTH
        rows = jnp.concatenate(
            [page_ref[:, low:high], page_ref[:, split + low : split + high]], axis=1
        )
        relay[h] = rows.reshape(PAGES, PAGE_TOKENS, 2 * HEAD_WIDTH)
        f_relay[h] = jnp.concatenate(
            [fresh[:, low:high], fresh[:, split + low : split + high]], axis=1
        )
    for xx in range(4):
        e = z * 8 + xx * 2 + c
        pages = owner_ref[e] * PAGES + slot_ref[e]
        for half in range(2):
            lanes = slice(half * 64, half * 64 + 64)
            table_ref[xx, half : half + 1, :] = jnp.concatenate(
                [pages[0:1, lanes], pages[1:2, lanes]], axis=1
            )
    lane = iota((PROMPTS, 128), 1)
    copies = (iota((PROMPTS, 128), 0) == lax.div(lax.rem(lane, ROWS), SCORED_STEPS)).astype(F32)
    wide = nn(count_ref[...].astype(F32), copies, HIGHEST)
    mine = lax.div(iota((N_SEQ, 128), 1), ROWS) == iota((N_SEQ, 128), 0)
    wide = jnp.sum(jnp.where(mine, wide, 0.0), axis=0, keepdims=True)
    count_rows[...] = jnp.broadcast_to(wide, (8, 128))

    h32 = hidden_ref[...].reshape(ROWS, D).astype(F32)
    scale = lax.rsqrt(jnp.mean(h32 * h32, axis=-1, keepdims=True) + EPSILON)
    normed = (h32 * scale * gain_ref[...].reshape(1, D)).astype(BF16)
    slots, owner_token, share = route(id_ref, prob_ref)
    share_ref[...] = share
    spread = nn(slots, owner_token).astype(BF16)
    for k, (first_column, columns) in enumerate(PARTS):
        piece = normed[:, first_column : first_column + columns]
        rows_out[k][...] = nn(spread, piece).astype(BF16).reshape(16, 16, columns)
    pl.semaphore_wait(barrier, len(peers))

    def spot(segment_slot, zz, xx, cc):
        return pool.at[segment_slot, pl.ds((zz * 8 + xx * 2 + cc) * PAGES, PAGES)]

    order = [(0, 0), (0, 1), (0, 3), (0, 2), (1, 0), (1, 1), (1, 3), (1, 2)]
    first = []

    def hand_out(n):
        p, dx = order[n]
        yy = y if p == 0 else mate
        xx = lax.rem(x + dx, 4)
        target = spot(lax.div(y, 2), z, x, c)
        source = relay.at[head_of(yy, xx)]
        if (p, dx) == (0, 0):
            copy = pltpu.make_async_copy(source, target, local.at[0])
        else:
            copy = pltpu.make_async_remote_copy(
                source, target, a_send.at[n], a_recv.at[n],
                device_id=device(yy, z, xx, c), device_id_type=MESH,
            )
        copy.start()
        first.append(copy)

    for n in range(4):
        hand_out(n)
    routed = []
    for k in range(len(PARTS)):
        for dy in range(4):
            for dz in range(4):
                n = dy * 4 + dz
                source = rows_out[k].at[lax.rem(y + dy, 4) * 4 + lax.rem(z + dz, 4)]
                target = rows_mid[k].at[y * 4 + z]
                if n == 0:
                    copy = pltpu.make_async_copy(source, target, local.at[5 + 2 * k])
                else:
                    copy = pltpu.make_async_remote_copy(
                        source, target, d_send.at[k * 16 + n], d_recv.at[k * 16 + n],
                        device_id=beside(dy, dz), device_id_type=MESH,
                    )
                copy.start()
                routed.append(copy)

    for n in range(4, 8):
        hand_out(n)

    small = []
    mine = pltpu.make_async_copy(table_ref, tables.at[lax.div(y, 2)], local.at[1])
    mine.start()
    small.append(mine)
    mine = pltpu.make_async_copy(count_rows, counts.at[x], local.at[2])
    mine.start()
    small.append(mine)
    other = pltpu.make_async_remote_copy(
        table_ref, tables.at[lax.div(y, 2)], i_send.at[0], i_recv.at[0],
        device_id=device(mate, z, x, c), device_id_type=MESH,
    )
    other.start()
    small.append(other)
    for dx in range(1, 4):
        other = pltpu.make_async_remote_copy(
            count_rows, counts.at[x], i_send.at[dx], i_recv.at[dx],
            device_id=at(0, dx), device_id_type=MESH,
        )
        other.start()
        small.append(other)

    def chunk(n):
        p, dx = order[n]
        yy = y if p == 0 else mate
        return lax.div(yy, 2), lax.rem(x - dx + 4, 4)

    def pass_on(n, zz, way, peer):
        segment_slot, xx = chunk(n)
        block = spot(segment_slot, zz, xx, c)
        sends, recvs = (c_send, c_recv) if way >= 3 else (z_send, z_recv)
        number = (way - 3 if way >= 3 else way) * 8 + n
        copy = pltpu.make_async_remote_copy(
            block, block, sends.at[number], recvs.at[number],
            device_id=peer, device_id_type=MESH,
        )
        copy.start()
        return copy

    upward, downward, further, across = [], [], [], []

    def begin(n):
        if n == 0:
            first[n].wait()
        else:
            first[n].wait_recv()
        upward.append(pass_on(n, z, 0, up))
        downward.append(pass_on(n, z, 1, down))
        across.append(pass_on(n, z, 3, twin))

    def forward(n):
        upward[n].wait_recv()
        if n % 2 == 0:
            further.append(pass_on(n, lax.rem(z + 3, 4), 2, up))
        across.append(pass_on(n, lax.rem(z + 3, 4), 4, twin))
        downward[n].wait_recv()
        if n % 2 == 1:
            further.append(pass_on(n, lax.rem(z + 1, 4), 2, down))
        across.append(pass_on(n, lax.rem(z + 1, 4), 5, twin))

    for n in range(4):
        begin(n)

    ri = iota((256, 256), 0)
    ci = iota((256, 256), 1)

    def slot_of(i):
        return lax.div(lax.rem(i, 32), 2) * 16 + lax.div(i, 32) * 2 + lax.rem(i, 2)

    def arrive(copies):
        copies[0].wait()
        for copy in copies[1:]:
            copy.wait_recv()

    regroup = (slot_of(ri) == ci).astype(BF16)
    delivered = [[], [], []]
    for k, (_, columns) in enumerate(PARTS):
        arrive(routed[k * 16 : (k + 1) * 16])
        moved = nn(regroup, rows_mid[k][...].reshape(256, columns)).astype(BF16)
        rows_sorted[k][...] = moved.reshape(8, 32, columns)
        for dx in range(4):
            for dc in range(2):
                n = dx * 2 + dc
                source = rows_sorted[k].at[lax.rem(x + dx, 4) * 2 + lax.rem(c + dc, 2)]
                target = rows_in[k].at[x * 2 + c]
                if n == 0:
                    copy = pltpu.make_async_copy(source, target, local.at[6 + 2 * k])
                else:
                    copy = pltpu.make_async_remote_copy(
                        source, target, e_send.at[k * 8 + n], e_recv.at[k * 8 + n],
                        device_id=around(dx, dc), device_id_type=MESH,
                    )
                copy.start()
                delivered[k].append(copy)
        if k == 1:
            for n in (0, 1):
                forward(n)
    for n in range(4, 8):
        begin(n)
    for n in (2, 3):
        forward(n)

    q_rows[...] = q_ref[...].reshape(ROWS, q_ref.shape[2])
    for dy in range(4):
        for dx in range(4):
            n = dy * 4 + dx
            h = head_of(lax.rem(y + dy, 4), lax.rem(x + dx, 4))
            q_source = q_rows.at[:, pl.ds(pl.multiple_of(h * HEAD_COLUMNS, HEAD_COLUMNS), HEAD_COLUMNS)]
            f_source = f_relay.at[h]
            slot = x * 4 + y
            if n == 0:
                copies = [
                    pltpu.make_async_copy(q_source, q_all.at[slot], local.at[3]),
                    pltpu.make_async_copy(f_source, f_all.at[slot], local.at[4]),
                ]
            else:
                copies = [
                    pltpu.make_async_remote_copy(
                        q_source, q_all.at[slot], q_send.at[n], q_recv.at[n],
                        device_id=at(dy, dx), device_id_type=MESH,
                    ),
                    pltpu.make_async_remote_copy(
                        f_source, f_all.at[slot], f_send.at[n], f_recv.at[n],
                        device_id=at(dy, dx), device_id_type=MESH,
                    ),
                ]
            for copy in copies:
                copy.start()
            small.extend(copies)

    for copy in weights:
        copy.wait()

    def tiles(work):
        @pl.loop(0, D // TILE)
        def _(j):
            work(pl.ds(pl.multiple_of(j * TILE, TILE), TILE))

        work(pl.ds(D // TILE * TILE, D % TILE))

    def project(k):
        first_column, columns = PARTS[k]
        arrive(delivered[k])

        def work(part):
            rows = rows_in[k][...].reshape(256, columns)
            term = nn(rows, up_w[first_column : first_column + columns, part])
            projected[:, part] = term if k == 0 else projected[:, part] + term

        tiles(work)

    project(0)
    project(1)
    forward(4)
    forward(5)
    project(2)
    forward(6)
    forward(7)

    @pl.loop(0, 8)
    def _(j):
        part = pl.ds(pl.multiple_of(j * 32, 32), 32)
        wide = projected[part, :]
        gate, upper = wide[:, :HID], wide[:, HID:]
        active[part, :] = ((upper + 1.0) * gate * jax.nn.sigmoid(1.702 * gate)).astype(BF16)

    back = (slot_of(ci) == ri).astype(BF16)
    active[...] = nn(back, active[...]).astype(BF16)

    def finish(part):
        rows = nn(active[...], down_w[:, part]).astype(BF16)
        expert_out[:, :, part] = rows.reshape(128, 2, rows.shape[1])

    @pl.loop(0, 3)
    def _(j):
        finish(pl.ds(pl.multiple_of(j * TILE, TILE), TILE))

    for n in range(8):
        further[n].wait_recv()
        across.append(pass_on(n, lax.rem(z + 2, 4), 6, twin))

    @pl.loop(3, D // TILE)
    def _(j):
        finish(pl.ds(pl.multiple_of(j * TILE, TILE), TILE))

    finish(pl.ds(D // TILE * TILE, D % TILE))

    for copy in across:
        copy.wait()
    for copy in first[1:] + upward + downward + further:
        copy.wait_send()
    for n, copy in enumerate(routed):
        if n % 16 > 0:
            copy.wait_send()
    for copy in sum([copies[1:] for copies in delivered], []):
        copy.wait_send()
    for copy in small:
        copy.wait()


TILE = 512


def exchange(
    queries, fresh, pages, owner, slot, count, hidden, gain, ids, prob, gate_up, down_proj
):
    vmem = pl.BlockSpec(memory_space=pltpu.VMEM)
    anywhere = pl.BlockSpec(memory_space=pl.ANY)
    dma = pltpu.SemaphoreType.DMA
    return pl.pallas_call(
        exchange_kernel,
        out_shape=(
            jax.ShapeDtypeStruct((16, ROWS, HEAD_COLUMNS), BF16),
            jax.ShapeDtypeStruct((16, ROWS, 2 * HEAD_WIDTH), BF16),
            jax.ShapeDtypeStruct((2, N_EP * PAGES, PAGE_TOKENS, 2 * HEAD_WIDTH), BF16),
            jax.ShapeDtypeStruct((2, 4, 2, 128), jnp.int32),
            jax.ShapeDtypeStruct((4, 8, 128), F32),
            jax.ShapeDtypeStruct((128, 2, D), BF16),
            jax.ShapeDtypeStruct((ROWS, 256), F32),
        ),
        in_specs=[vmem] * 10 + [anywhere] * 2,
        out_specs=(anywhere,) * 5 + (vmem, vmem),
        scratch_shapes=[
            pltpu.VMEM((KEY_VALUE_HEADS, PAGES, PAGE_TOKENS, 2 * HEAD_WIDTH), BF16),
            pltpu.VMEM((KEY_VALUE_HEADS, ROWS, 2 * HEAD_WIDTH), BF16),
            pltpu.VMEM((ROWS, QUERY_HEADS * HEAD_WIDTH), BF16),
            pltpu.VMEM((4, 2, 128), jnp.int32),
            pltpu.VMEM((8, 128), F32),
            *[pltpu.VMEM((16, 16, columns), BF16) for _, columns in PARTS * 2],
            *[pltpu.VMEM((8, 32, columns), BF16) for _, columns in PARTS * 2],
            pltpu.VMEM((D, 2 * HID), BF16),
            pltpu.VMEM((HID, D), BF16),
            pltpu.VMEM((256, 2 * HID), F32),
            pltpu.VMEM((256, HID), BF16),
            dma((16,)), dma((16,)), dma((16,)), dma((16,)), dma((8,)), dma((8,)),
            dma((24,)), dma((24,)), dma((32,)), dma((32,)), dma((4,)), dma((4,)),
            dma((48,)), dma((48,)), dma((24,)), dma((24,)), dma((11,)), dma((6,)),
        ],
        compiler_params=pltpu.CompilerParams(
            collective_id=1, has_side_effects=True, vmem_limit_bytes=56 << 20
        ),
        name="exchange",
    )(queries, fresh, pages, owner, slot, count, hidden, gain, ids, prob, gate_up, down_proj)


BK = 1024
GK = 4096
KEYS = 2 * NPS * PAGE_TOKENS
UNITS = 4
CHUNKS = 4
COLS = 256
VROWS = 80


def values_of(rows):
    pick = (iota((VROWS, 128), 0) + HEAD_WIDTH == iota((VROWS, 128), 1)).astype(BF16)
    moved = nt(pick, rows)
    return jnp.where(iota(moved.shape, 0) >= HEAD_WIDTH, 1.0, moved).astype(BF16)


def score_kernel(
    table_ref, count_ref, sinks, q_ref, f_ref, pool_ref, o_ref, lse_ref,
    tables, counts, q_all, f_all, pool,
    kv, vt, qs, limit_ref, m_ref, acc, sorted_out, s0, s1, places, lengths, sem,
):
    y = lax.axis_index("seq")
    outer_pair = jnp.logical_or(y == 0, y == 3)
    loads = [
        pltpu.make_async_copy(source, target, sem.at[n])
        for n, (source, target) in enumerate(
            [(count_ref, counts), (q_ref, q_all), (f_ref, f_all), (table_ref, tables)]
        )
    ]
    share = pool.shape[0] // 8
    for n in range(8):
        part = pl.ds(n * share, share)
        loads.append(pltpu.make_async_copy(pool_ref.at[part], pool.at[part], sem.at[4 + n]))
    for copy in loads:
        copy.start()
    for copy in loads[:3]:
        copy.wait()
    head = head_of(y, lax.rem(lax.div(lax.axis_index("ep"), 2), 4))
    spread = iota((QUERY_HEADS, COLS), 0) == head * GROUP + lax.div(iota((QUERY_HEADS, COLS), 1), ROWS)
    sink_row = nn(sinks[...].reshape(1, QUERY_HEADS), spread.astype(F32), HIGHEST)
    i0 = iota((128, 128), 0)
    i1 = iota((128, 128), 1)
    lane_row = lax.rem(iota((128, COLS), 1), ROWS).astype(F32)

    def ordering(e):
        c = counts[e][0:1, :]
        n_row = jnp.where(
            outer_pair,
            jnp.minimum(c, 256.0) + jnp.maximum(c - 768.0, 0.0),
            jnp.clip(c - 256.0, 0.0, 512.0),
        )
        n_col = jnp.sum(jnp.where(i0 == i1, n_row, 0.0), axis=1, keepdims=True)
        behind = jnp.logical_or(n_row > n_col, jnp.logical_and(n_col == n_row, i1 < i0))
        pos_col = jnp.sum(jnp.where(behind, 1.0, 0.0), axis=1, keepdims=True)
        return n_row, n_col, pos_col

    for e in range(UNITS):
        n_row, n_col, pos_col = ordering(e)
        places[e] = pos_col
        ahead = jnp.logical_or(n_col > n_row, jnp.logical_and(n_col == n_row, i0 < i1))
        pos_row = jnp.sum(jnp.where(ahead, 1.0, 0.0), axis=0, keepdims=True)
        perm = (pos_row == i0.astype(F32)).astype(BF16)
        q_sorted = nn(perm, q_all[e * 4 : e * 4 + 4].reshape(128, HEAD_COLUMNS)) * 0.125
        f_sorted = nn(perm, f_all[e * 4 : e * 4 + 4].reshape(128, 128)).astype(BF16)
        none = jnp.zeros((COLS, HEAD_WIDTH), F32)
        for ch in range(CHUNKS):
            u = e * CHUNKS + ch
            pieces = [
                q_sorted[ch * ROWS : (ch + 1) * ROWS, g * HEAD_WIDTH : (g + 1) * HEAD_WIDTH]
                for g in range(GROUP)
            ]
            stacked = jnp.concatenate([jnp.concatenate(pieces, axis=0), none], axis=1)
            qs[u] = stacked.T.astype(BF16)
            member = pos_col == lane_row + float(ch * ROWS)
            limit = jnp.sum(jnp.where(member, n_col, 0.0), axis=0, keepdims=True)
            limit_ref[u] = jnp.broadcast_to(limit.astype(jnp.int32), (8, COLS))
            lengths[u] = jnp.max(limit).astype(jnp.int32) * PAGE_TOKENS
            rows = f_sorted[ch * ROWS : (ch + 1) * ROWS, :]
            s = nn(rows, qs[u])
            ki = iota((ROWS, COLS), 0)
            ri = lax.rem(iota((ROWS, COLS), 1), ROWS)
            seen = jnp.logical_and(
                lax.div(ki, SCORED_STEPS) == lax.div(ri, SCORED_STEPS), ki <= ri
            )
            s = jnp.where(seen, s, NEGATIVE)
            m0 = jnp.maximum(jnp.max(s, axis=0, keepdims=True), sink_row)
            p = jnp.exp(s - m0).astype(BF16)
            start = nn(values_of(rows), p)
            start = start + jnp.where(
                iota((VROWS, COLS), 0) >= HEAD_WIDTH, jnp.exp(sink_row - m0), 0.0
            )
            m_ref[u] = jnp.broadcast_to(jnp.where(outer_pair, m0, FLOOR), (8, COLS))
            acc[u] = jnp.where(outer_pair, start, 0.0)

    def unit(e, carry):
        def gather(kb, carry):
            rows = [
                pool[tables[kb, e, i // 128, i % 2 * 64 + i % 128 // 2] + kb * (N_EP * PAGES)]
                for i in range(GK // PAGE_TOKENS)
            ]
            for i in range(GK // BK):
                part = rows[i * (BK // PAGE_TOKENS) : (i + 1) * (BK // PAGE_TOKENS)]
                found = jnp.concatenate(part, axis=0)
                kv[pl.ds(pl.multiple_of(kb * GK + i * BK, BK), BK), :] = found
                vt[kb * (GK // BK) + i] = values_of(found)
            return carry

        lax.fori_loop(0, lax.div(lengths[e * CHUNKS] + (GK - 1), GK), gather, 0)

        page = iota((BK // PAGE_TOKENS, PAGE_TOKENS // 8, 8, COLS), 0)

        def produce(store, u, kb):
            keys = kv[pl.ds(pl.multiple_of(kb * BK, BK), BK), :]
            s = nn(keys, qs[u])
            live = page < (limit_ref[u] - kb * (BK // PAGE_TOKENS))[None, None]
            s = jnp.where(live, s.reshape(page.shape), NEGATIVE).reshape(BK, COLS)
            store[...] = s
            return jnp.max(s, axis=0, keepdims=True)

        def absorb(store, u, kb, top):
            before = m_ref[u][0:1, :]
            after = jnp.maximum(before, top)
            p = jnp.exp(store[...] - after).astype(BF16)
            acc[u] = acc[u] * jnp.exp(before - after) + nn(vt[kb], p)
            m_ref[u] = jnp.broadcast_to(after, (8, COLS))

        def chunk(ch, top):
            u = e * CHUNKS + ch
            count = lax.div(lengths[u] + (BK - 1), BK)
            after_u = e * CHUNKS + jnp.minimum(ch + 1, CHUNKS - 1)

            def pair(i, top):
                last = 2 * i + 2 >= count
                next_top = produce(s1, u, 2 * i + 1)
                absorb(s0, u, 2 * i, top)
                top = produce(s0, jnp.where(last, after_u, u), jnp.where(last, 0, 2 * i + 2))
                absorb(s1, u, 2 * i + 1, next_top)
                return top

            top = lax.fori_loop(0, lax.div(count, 2), pair, top)

            def odd(top):
                absorb(s0, u, count - 1, top)
                return produce(s0, after_u, jnp.int32(0))

            return lax.cond(lax.rem(count, 2) == 1, odd, lambda top: top, top)

        used = sum([(lengths[e * CHUNKS + ch] > 0).astype(jnp.int32) for ch in range(CHUNKS)])

        @pl.when(used > 0)
        def _():
            top = produce(s0, e * CHUNKS, jnp.int32(0))
            lax.fori_loop(0, used, chunk, top)

        return carry

    for copy in loads[3:]:
        copy.wait()
    lax.fori_loop(0, UNITS, unit, 0)

    for e in range(UNITS):
        pos_col = places[e]
        perm_t = (pos_col == i1.astype(F32)).astype(BF16)
        lse = jnp.zeros((8, 128), F32)
        for ch in range(CHUNKS):
            u = e * CHUNKS + ch
            total = jnp.maximum(acc[u][HEAD_WIDTH : HEAD_WIDTH + 1, :], 1e-30)
            out = acc[u][0:HEAD_WIDTH, :] / total
            padded = jnp.concatenate([out, jnp.zeros_like(out)], axis=0)
            turned = padded.T.astype(BF16)
            for g in range(GROUP):
                sorted_out[e, ch * ROWS : (ch + 1) * ROWS, g * HEAD_WIDTH : (g + 1) * HEAD_WIDTH] = (
                    turned[g * ROWS : (g + 1) * ROWS, 0:HEAD_WIDTH]
                )
            row = m_ref[u][0:1, :] + jnp.log(total)
            mine = lax.div(iota((8, COLS), 1), ROWS) == iota((8, COLS), 0)
            member = (pos_col == lane_row + float(ch * ROWS)).astype(BF16)
            rest = jnp.where(mine, row, 0.0)
            layers = []
            for _ in range(3):
                layers.append(rest.astype(BF16))
                rest = rest - layers[-1].astype(F32)
            moved = nt(jnp.concatenate([layer.astype(F32) for layer in layers], axis=0).astype(BF16), member)
            lse = lse + (moved[0:8] + moved[8:16] + moved[16:24])
        lse_ref[e] = lse
        o_ref[e] = nn(perm_t, sorted_out[e]).astype(BF16)


def score(tables, counts, sinks, q_all, f_all, pool):
    vmem = pl.BlockSpec(memory_space=pltpu.VMEM)
    anywhere = pl.BlockSpec(memory_space=pl.ANY)
    return pl.pallas_call(
        score_kernel,
        out_shape=(
            jax.ShapeDtypeStruct((UNITS, 128, HEAD_COLUMNS), BF16),
            jax.ShapeDtypeStruct((UNITS, 8, 128), F32),
        ),
        in_specs=[anywhere, anywhere, vmem, anywhere, anywhere, anywhere],
        out_specs=(vmem, vmem),
        scratch_shapes=[
            pltpu.SMEM((2, UNITS, 2, 128), jnp.int32),
            pltpu.VMEM((UNITS, 8, 128), F32),
            pltpu.VMEM((16, ROWS, HEAD_COLUMNS), BF16),
            pltpu.VMEM((16, ROWS, 2 * HEAD_WIDTH), BF16),
            pltpu.VMEM((2 * N_EP * PAGES, PAGE_TOKENS, 2 * HEAD_WIDTH), BF16),
            pltpu.VMEM((KEYS, 128), BF16),
            pltpu.VMEM((KEYS // BK, VROWS, BK), BF16),
            pltpu.VMEM((UNITS * CHUNKS, 128, COLS), BF16),
            pltpu.VMEM((UNITS * CHUNKS, 8, COLS), jnp.int32),
            pltpu.VMEM((UNITS * CHUNKS, 8, COLS), F32),
            pltpu.VMEM((UNITS * CHUNKS, VROWS, COLS), F32),
            pltpu.VMEM((UNITS, 128, HEAD_COLUMNS), BF16),
            pltpu.VMEM((BK, COLS), F32),
            pltpu.VMEM((BK, COLS), F32),
            pltpu.VMEM((UNITS, 128, 1), F32),
            pltpu.SMEM((UNITS * CHUNKS,), jnp.int32),
            pltpu.SemaphoreType.DMA((12,)),
        ],
        compiler_params=pltpu.CompilerParams(vmem_limit_bytes=60 << 20),
        cost_estimate=pl.CostEstimate(
            flops=25_000_000_000, bytes_accessed=8_000_000, transcendentals=20_000_000
        ),
        name="score",
    )(tables, counts, sinks, q_all, f_all, pool)


def merge_kernel(
    o_ref, lse_ref, share_ref, rows_ref, out_ref, mix_ref, o_all, lse_all, o_send, o_recv, l_send, l_recv, local,
):
    y, z, x, c = place()

    def at(dy, dx):
        return device(lax.rem(y + dy, 4), z, lax.rem(x + dx, 4), c)

    plane = [(dy, dx) for dy in range(4) for dx in range(4) if (dy, dx) != (0, 0)]
    barrier = pltpu.get_barrier_semaphore()
    for dy, dx in plane:
        pl.semaphore_signal(barrier, inc=1, device_id=at(dy, dx), device_id_type=MESH)
    pl.semaphore_wait(barrier, len(plane))
    inner_pair = jnp.logical_or(y == 1, y == 2).astype(jnp.int32)
    slot = inner_pair * 8 + head_of(y, x)
    copies = []
    for dy in range(4):
        for dx in range(4):
            n = dy * 4 + dx
            q = lax.rem(y + dy, 4)
            e = lax.rem(x + dx, 4)
            o_source = o_ref.at[e, pl.ds(pl.multiple_of(q * ROWS, ROWS), ROWS)]
            if n == 0:
                pair = [
                    pltpu.make_async_copy(o_source, o_all.at[slot], local.at[0]),
                    pltpu.make_async_copy(lse_ref.at[e], lse_all.at[slot], local.at[1]),
                ]
            else:
                pair = [
                    pltpu.make_async_remote_copy(
                        o_source, o_all.at[slot], o_send.at[n], o_recv.at[n],
                        device_id=at(dy, dx), device_id_type=MESH,
                    ),
                    pltpu.make_async_remote_copy(
                        lse_ref.at[e], lse_all.at[slot], l_send.at[n], l_recv.at[n],
                        device_id=at(dy, dx), device_id_type=MESH,
                    ),
                ]
            for copy in pair:
                copy.start()
            copies.extend(pair)

    share = share_ref[...]
    high = share.astype(BF16)
    low = (share - high.astype(F32)).astype(BF16)
    rows = rows_ref[...].reshape(256, D)
    mix_ref[...] = (nn(high, rows) + nn(low, rows)).astype(BF16)

    for copy in copies:
        copy.wait()
    mine = (iota((ROWS, 128), 1) == iota((ROWS, 128), 0) + y * ROWS).astype(F32)
    logs = nt(mine, lse_all[...].reshape(128, 128), HIGHEST)
    log0, log1 = logs[:, :64], logs[:, 64:]
    top = jnp.maximum(log0, log1)
    w0, w1 = jnp.exp(log0 - top), jnp.exp(log1 - top)
    share0, share1 = w0 / (w0 + w1), w1 / (w0 + w1)
    shares = jnp.concatenate([share0, share1], axis=0)
    high = shares.astype(BF16)
    low = (shares - high.astype(F32)).astype(BF16)
    both = jnp.concatenate([high, low], axis=1)
    for h in range(KEY_VALUE_HEADS):
        shape = (128, HEAD_COLUMNS)
        head = lax.div(iota(shape, 1), HEAD_WIDTH) + h * GROUP
        spread = (lax.rem(iota(shape, 0), QUERY_HEADS) == head).astype(BF16)
        wide = nn(both, spread)
        result = wide[:ROWS] * o_all[h].astype(F32) + wide[ROWS:] * o_all[8 + h].astype(F32)
        out_ref[:, h * HEAD_COLUMNS : (h + 1) * HEAD_COLUMNS] = result.astype(BF16)


def merge(o, lse, share, rows):
    vmem = pl.BlockSpec(memory_space=pltpu.VMEM)
    anywhere = pl.BlockSpec(memory_space=pl.ANY)
    dma = pltpu.SemaphoreType.DMA
    return pl.pallas_call(
        merge_kernel,
        out_shape=(
            jax.ShapeDtypeStruct((ROWS, QUERY_HEADS * HEAD_WIDTH), BF16),
            jax.ShapeDtypeStruct((ROWS, D), BF16),
        ),
        in_specs=[anywhere, anywhere, vmem, vmem],
        out_specs=(vmem, vmem),
        scratch_shapes=[
            pltpu.VMEM((16, ROWS, HEAD_COLUMNS), BF16),
            pltpu.VMEM((16, 8, 128), F32),
            dma((16,)), dma((16,)), dma((16,)), dma((16,)), dma((2,)),
        ],
        compiler_params=pltpu.CompilerParams(
            collective_id=2, has_side_effects=True, vmem_limit_bytes=16 << 20
        ),
        name="merge",
    )(o, lse, share, rows)


def by_prefix(table):
    return table[0].T.reshape(2, N_EP, NPS // 2).transpose(1, 0, 2)


def per_device(
    queries, fresh_key_values, key_value_pages, page_owner, page_slot, page_count, sinks,
    hidden, norm_gain, expert_ids, gate_prob, gate_up, down_proj,
):
    q_all, f_all, pool, tables, counts, result, share = exchange(
        queries[0],
        fresh_key_values[0],
        key_value_pages.reshape(PAGES * PAGE_TOKENS, 2 * KEY_VALUE_HEADS * HEAD_WIDTH),
        by_prefix(page_owner),
        by_prefix(page_slot),
        page_count,
        hidden[0],
        norm_gain,
        expert_ids[0].transpose(1, 2, 0),
        gate_prob[0].transpose(1, 2, 0),
        gate_up,
        down_proj,
    )
    returned = lax.all_to_all(result, ("seq", "ep"), split_axis=0, concat_axis=0, tiled=True)
    o, lse = score(
        tables, counts, sinks, q_all, f_all,
        pool.reshape(2 * N_EP * PAGES, PAGE_TOKENS, 2 * HEAD_WIDTH),
    )
    attention, mixture = merge(o, lse, share, returned)
    return (attention.reshape(queries.shape), mixture.reshape(hidden.shape))


def solution(mesh):
    return jax.shard_map(
        per_device,
        mesh=mesh,
        in_specs=(
            P("seq", "ep", None, None),
            P("seq", "ep", None, None),
            P("seq", "ep", None, None),
            P("seq", None, None),
            P("seq", None, None),
            P(None, "ep"),
            P(),
            P("seq", "ep", None, None),
            P(),
            P("seq", "ep", None, None),
            P("seq", "ep", None, None),
            P(("seq", "ep"), None, None),
            P(("seq", "ep"), None, None),
        ),
        out_specs=(P("seq", "ep", None, None), P("seq", "ep", None, None)),
        check_vma=False,
    )
```

```python
import jax
import jax.numpy as jnp
from jax import lax
from jax.experimental import pallas as pl
from jax.experimental.pallas import tpu as pltpu
from jax.sharding import PartitionSpec as P

D = 2880
QUERY_HEADS = 64
KEY_VALUE_HEADS = 8
GROUP = QUERY_HEADS // KEY_VALUE_HEADS
HEAD_WIDTH = 64
TOPK = 4
HID = 1440
SCORED_STEPS = 4
PAGE_TOKENS = 16
NPS = 256
PAGES = 24
PROMPTS = 8
N_SEQ = 4
N_EP = 32
ROWS = PROMPTS * SCORED_STEPS
HEAD_COLUMNS = GROUP * HEAD_WIDTH
NEGATIVE = -1e30
FLOOR = -1e29
EPSILON = 1e-05
MESH = pl.DeviceIdType.MESH
F32 = jnp.float32
BF16 = jnp.bfloat16
HIGHEST = lax.Precision.HIGHEST


def place():
    y = lax.axis_index("seq")
    ep = lax.axis_index("ep")
    return y, lax.div(ep, 8), lax.rem(lax.div(ep, 2), 4), lax.rem(ep, 2)


def device(y, z, x, c):
    return (y, z * 8 + x * 2 + c)


def head_of(y, x):
    return lax.div(y, 2) * 4 + x


def nt(a, b, precision=None):
    return lax.dot_general(
        a, b, (((1,), (1,)), ((), ())), preferred_element_type=F32, precision=precision
    )


def nn(a, b, precision=None):
    return lax.dot_general(
        a, b, (((1,), (0,)), ((), ())), preferred_element_type=F32, precision=precision
    )


def iota(shape, axis):
    return lax.broadcasted_iota(jnp.int32, shape, axis)


PARTS = ((0, 1024), (1024, 1024), (2048, D - 2048))


def route(id_ref, prob_ref):
    i0 = iota((128, 128), 0)
    i1 = iota((128, 128), 1)
    copies = (iota((8, 128), 0) == lax.rem(iota((8, 128), 1), 8)).astype(F32)
    group = lax.div(iota((TOPK, 128), 1), 8)

    def as_row(ref):
        row = jnp.zeros((1, 128), F32)
        for t in range(SCORED_STEPS):
            wide = nn(ref[t].astype(F32), copies, HIGHEST)
            mine = group == iota((TOPK, 128), 0) + t * TOPK
            row = row + jnp.sum(jnp.where(mine, wide, 0.0), axis=0, keepdims=True)
        return row

    ids = as_row(id_ref)
    column = jnp.sum(jnp.where(i0 == i1, ids, 0.0), axis=1, keepdims=True)
    earlier = jnp.logical_and(column == ids, i0 < i1)
    rank = jnp.sum(jnp.where(earlier, 1.0, 0.0), axis=0, keepdims=True)
    slots = iota((256, 128), 0).astype(F32) == 2.0 * ids + rank

    def token(a):
        return lax.rem(a, 8) * SCORED_STEPS + lax.div(a, 32)

    owner_token = (token(iota((128, ROWS), 0)) == iota((128, ROWS), 1)).astype(BF16)
    mine = token(iota((ROWS, 128), 1)) == iota((ROWS, 128), 0)
    share = nt(jnp.where(mine, as_row(prob_ref), 0.0), slots.astype(F32), HIGHEST)
    return slots.astype(BF16), owner_token, share


def exchange_kernel(
    q_ref, f_ref, page_ref, owner_ref, slot_ref, count_ref, hidden_ref, gain_ref, id_ref, prob_ref,
    up_ref, down_ref,
    q_all, f_all, pool, tables, counts, expert_out, share_ref,
    relay, f_relay, q_rows, table_ref, count_rows, out0, out1, out2, mid0, mid1, mid2, sorted0, sorted1, sorted2,
    in0, in1, in2, up_w, down_w, projected, active,
    q_send, q_recv, f_send, f_recv, a_send, a_recv, z_send, z_recv, c_send, c_recv,
    i_send, i_recv, d_send, d_recv, e_send, e_recv, local, w_sem,
):
    y, z, x, c = place()
    mate = 3 - y
    rows_out, rows_mid = (out0, out1, out2), (mid0, mid1, mid2)
    rows_sorted, rows_in = (sorted0, sorted1, sorted2), (in0, in1, in2)

    def at(dy, dx):
        return device(lax.rem(y + dy, 4), z, lax.rem(x + dx, 4), c)

    plane = [(dy, dx) for dy in range(4) for dx in range(4) if (dy, dx) != (0, 0)]
    up = device(y, lax.rem(z + 1, 4), x, c)
    down = device(y, lax.rem(z + 3, 4), x, c)
    twin = device(y, z, x, 1 - c)

    def beside(dy, dz):
        return device(lax.rem(y + dy, 4), lax.rem(z + dz, 4), x, c)

    def around(dx, dc):
        return device(y, z, lax.rem(x + dx, 4), lax.rem(c + dc, 2))

    peers = [at(dy, dx) for dy, dx in plane]
    peers += [beside(dy, dz) for dy in range(4) for dz in range(1, 4)]
    peers += [around(dx, 1) for dx in range(4)]
    barrier = pltpu.get_barrier_semaphore()
    for peer in peers:
        pl.semaphore_signal(barrier, inc=1, device_id=peer, device_id_type=MESH)

    weights = []
    for n in range(4):
        part = pl.ds(n * (D // 4), D // 4)
        weights.append(pltpu.make_async_copy(up_ref.at[0, part], up_w.at[part], w_sem.at[n]))
    for n in range(2):
        part = pl.ds(n * (HID // 2), HID // 2)
        weights.append(pltpu.make_async_copy(down_ref.at[0, part], down_w.at[part], w_sem.at[4 + n]))
    for copy in weights:
        copy.start()

    fresh = f_ref[...].reshape(ROWS, f_ref.shape[2])
    for h in range(KEY_VALUE_HEADS):
        low, high = h * HEAD_WIDTH, (h + 1) * HEAD_WIDTH
        split = KEY_VALUE_HEADS * HEAD_WIDTH
        rows = jnp.concatenate(
            [page_ref[:, low:high], page_ref[:, split + low : split + high]], axis=1
        )
        relay[h] = rows.reshape(PAGES, PAGE_TOKENS, 2 * HEAD_WIDTH)
        f_relay[h] = jnp.concatenate(
            [fresh[:, low:high], fresh[:, split + low : split + high]], axis=1
        )
    for xx in range(4):
        e = z * 8 + xx * 2 + c
        pages = owner_ref[e] * PAGES + slot_ref[e]
        for half in range(2):
            lanes = slice(half * 64, half * 64 + 64)
            table_ref[xx, half : half + 1, :] = jnp.concatenate(
                [pages[0:1, lanes], pages[1:2, lanes]], axis=1
            )
    lane = iota((PROMPTS, 128), 1)
    copies = (iota((PROMPTS, 128), 0) == lax.div(lax.rem(lane, ROWS), SCORED_STEPS)).astype(F32)
    wide = nn(count_ref[...].astype(F32), copies, HIGHEST)
    mine = lax.div(iota((N_SEQ, 128), 1), ROWS) == iota((N_SEQ, 128), 0)
    wide = jnp.sum(jnp.where(mine, wide, 0.0), axis=0, keepdims=True)
    count_rows[...] = jnp.broadcast_to(wide, (8, 128))

    h32 = hidden_ref[...].reshape(ROWS, D).astype(F32)
    scale = lax.rsqrt(jnp.mean(h32 * h32, axis=-1, keepdims=True) + EPSILON)
    normed = (h32 * scale * gain_ref[...].reshape(1, D)).astype(BF16)
    slots, owner_token, share = route(id_ref, prob_ref)
    share_ref[...] = share
    spread = nn(slots, owner_token).astype(BF16)
    for k, (first_column, columns) in enumerate(PARTS):
        piece = normed[:, first_column : first_column + columns]
        rows_out[k][...] = nn(spread, piece).astype(BF16).reshape(16, 16, columns)
    pl.semaphore_wait(barrier, len(peers))

    def spot(segment_slot, zz, xx, cc):
        return pool.at[segment_slot, pl.ds((zz * 8 + xx * 2 + cc) * PAGES, PAGES)]

    order = [(0, 0), (0, 1), (0, 3), (0, 2), (1, 0), (1, 1), (1, 3), (1, 2)]
    first = []

    def hand_out(n):
        p, dx = order[n]
        yy = y if p == 0 else mate
        xx = lax.rem(x + dx, 4)
        target = spot(lax.div(y, 2), z, x, c)
        source = relay.at[head_of(yy, xx)]
        if (p, dx) == (0, 0):
            copy = pltpu.make_async_copy(source, target, local.at[0])
        else:
            copy = pltpu.make_async_remote_copy(
                source, target, a_send.at[n], a_recv.at[n],
                device_id=device(yy, z, xx, c), device_id_type=MESH,
            )
        copy.start()
        first.append(copy)

    for n in range(4):
        hand_out(n)
    routed = []
    for k in range(len(PARTS)):
        for dy in range(4):
            for dz in range(4):
                n = dy * 4 + dz
                source = rows_out[k].at[lax.rem(y + dy, 4) * 4 + lax.rem(z + dz, 4)]
                target = rows_mid[k].at[y * 4 + z]
                if n == 0:
                    copy = pltpu.make_async_copy(source, target, local.at[5 + 2 * k])
                else:
                    copy = pltpu.make_async_remote_copy(
                        source, target, d_send.at[k * 16 + n], d_recv.at[k * 16 + n],
                        device_id=beside(dy, dz), device_id_type=MESH,
                    )
                copy.start()
                routed.append(copy)

    for n in range(4, 8):
        hand_out(n)

    small = []
    mine = pltpu.make_async_copy(table_ref, tables.at[lax.div(y, 2)], local.at[1])
    mine.start()
    small.append(mine)
    mine = pltpu.make_async_copy(count_rows, counts.at[x], local.at[2])
    mine.start()
    small.append(mine)
    other = pltpu.make_async_remote_copy(
        table_ref, tables.at[lax.div(y, 2)], i_send.at[0], i_recv.at[0],
        device_id=device(mate, z, x, c), device_id_type=MESH,
    )
    other.start()
    small.append(other)
    for dx in range(1, 4):
        other = pltpu.make_async_remote_copy(
            count_rows, counts.at[x], i_send.at[dx], i_recv.at[dx],
            device_id=at(0, dx), device_id_type=MESH,
        )
        other.start()
        small.append(other)

    def chunk(n):
        p, dx = order[n]
        yy = y if p == 0 else mate
        return lax.div(yy, 2), lax.rem(x - dx + 4, 4)

    def pass_on(n, zz, way, peer):
        segment_slot, xx = chunk(n)
        block = spot(segment_slot, zz, xx, c)
        sends, recvs = (c_send, c_recv) if way >= 3 else (z_send, z_recv)
        number = (way - 3 if way >= 3 else way) * 8 + n
        copy = pltpu.make_async_remote_copy(
            block, block, sends.at[number], recvs.at[number],
            device_id=peer, device_id_type=MESH,
        )
        copy.start()
        return copy

    upward, downward, further, across = [], [], [], []

    def begin(n):
        if n == 0:
            first[n].wait()
        else:
            first[n].wait_recv()
        upward.append(pass_on(n, z, 0, up))
        downward.append(pass_on(n, z, 1, down))
        across.append(pass_on(n, z, 3, twin))

    def forward(n):
        upward[n].wait_recv()
        if n % 2 == 0:
            further.append(pass_on(n, lax.rem(z + 3, 4), 2, up))
        across.append(pass_on(n, lax.rem(z + 3, 4), 4, twin))
        downward[n].wait_recv()
        if n % 2 == 1:
            further.append(pass_on(n, lax.rem(z + 1, 4), 2, down))
        across.append(pass_on(n, lax.rem(z + 1, 4), 5, twin))

    for n in range(4):
        begin(n)

    ri = iota((256, 256), 0)
    ci = iota((256, 256), 1)

    def slot_of(i):
        return lax.div(lax.rem(i, 32), 2) * 16 + lax.div(i, 32) * 2 + lax.rem(i, 2)

    def arrive(copies):
        copies[0].wait()
        for copy in copies[1:]:
            copy.wait_recv()

    regroup = (slot_of(ri) == ci).astype(BF16)
    delivered = [[], [], []]
    for k, (_, columns) in enumerate(PARTS):
        arrive(routed[k * 16 : (k + 1) * 16])
        moved = nn(regroup, rows_mid[k][...].reshape(256, columns)).astype(BF16)
        rows_sorted[k][...] = moved.reshape(8, 32, columns)
        for dx in range(4):
            for dc in range(2):
                n = dx * 2 + dc
                source = rows_sorted[k].at[lax.rem(x + dx, 4) * 2 + lax.rem(c + dc, 2)]
                target = rows_in[k].at[x * 2 + c]
                if n == 0:
                    copy = pltpu.make_async_copy(source, target, local.at[6 + 2 * k])
                else:
                    copy = pltpu.make_async_remote_copy(
                        source, target, e_send.at[k * 8 + n], e_recv.at[k * 8 + n],
                        device_id=around(dx, dc), device_id_type=MESH,
                    )
                copy.start()
                delivered[k].append(copy)
        if k == 1:
            for n in (0, 1):
                forward(n)
    for n in range(4, 8):
        begin(n)
    for n in (2, 3):
        forward(n)

    q_rows[...] = q_ref[...].reshape(ROWS, q_ref.shape[2])
    for dy in range(4):
        for dx in range(4):
            n = dy * 4 + dx
            h = head_of(lax.rem(y + dy, 4), lax.rem(x + dx, 4))
            q_source = q_rows.at[:, pl.ds(pl.multiple_of(h * HEAD_COLUMNS, HEAD_COLUMNS), HEAD_COLUMNS)]
            f_source = f_relay.at[h]
            slot = x * 4 + y
            if n == 0:
                copies = [
                    pltpu.make_async_copy(q_source, q_all.at[slot], local.at[3]),
                    pltpu.make_async_copy(f_source, f_all.at[slot], local.at[4]),
                ]
            else:
                copies = [
                    pltpu.make_async_remote_copy(
                        q_source, q_all.at[slot], q_send.at[n], q_recv.at[n],
                        device_id=at(dy, dx), device_id_type=MESH,
                    ),
                    pltpu.make_async_remote_copy(
                        f_source, f_all.at[slot], f_send.at[n], f_recv.at[n],
                        device_id=at(dy, dx), device_id_type=MESH,
                    ),
                ]
            for copy in copies:
                copy.start()
            small.extend(copies)

    for copy in weights:
        copy.wait()

    def tiles(work):
        @pl.loop(0, D // TILE)
        def _(j):
            work(pl.ds(pl.multiple_of(j * TILE, TILE), TILE))

        work(pl.ds(D // TILE * TILE, D % TILE))

    def project(k):
        first_column, columns = PARTS[k]
        arrive(delivered[k])

        def work(part):
            rows = rows_in[k][...].reshape(256, columns)
            term = nn(rows, up_w[first_column : first_column + columns, part])
            projected[:, part] = term if k == 0 else projected[:, part] + term

        tiles(work)

    project(0)
    project(1)
    forward(4)
    forward(5)
    project(2)
    forward(6)
    forward(7)

    @pl.loop(0, 8)
    def _(j):
        part = pl.ds(pl.multiple_of(j * 32, 32), 32)
        wide = projected[part, :]
        gate, upper = wide[:, :HID], wide[:, HID:]
        active[part, :] = ((upper + 1.0) * gate * jax.nn.sigmoid(1.702 * gate)).astype(BF16)

    back = (slot_of(ci) == ri).astype(BF16)
    active[...] = nn(back, active[...]).astype(BF16)

    def finish(part):
        rows = nn(active[...], down_w[:, part]).astype(BF16)
        expert_out[:, :, part] = rows.reshape(128, 2, rows.shape[1])

    @pl.loop(0, 3)
    def _(j):
        finish(pl.ds(pl.multiple_of(j * TILE, TILE), TILE))

    for n in range(8):
        further[n].wait_recv()
        across.append(pass_on(n, lax.rem(z + 2, 4), 6, twin))

    @pl.loop(3, D // TILE)
    def _(j):
        finish(pl.ds(pl.multiple_of(j * TILE, TILE), TILE))

    finish(pl.ds(D // TILE * TILE, D % TILE))

    for copy in across:
        copy.wait()
    for copy in first[1:] + upward + downward + further:
        copy.wait_send()
    for n, copy in enumerate(routed):
        if n % 16 > 0:
            copy.wait_send()
    for copy in sum([copies[1:] for copies in delivered], []):
        copy.wait_send()
    for copy in small:
        copy.wait()


TILE = 512


def exchange(
    queries, fresh, pages, owner, slot, count, hidden, gain, ids, prob, gate_up, down_proj
):
    vmem = pl.BlockSpec(memory_space=pltpu.VMEM)
    anywhere = pl.BlockSpec(memory_space=pl.ANY)
    dma = pltpu.SemaphoreType.DMA
    return pl.pallas_call(
        exchange_kernel,
        out_shape=(
            jax.ShapeDtypeStruct((16, ROWS, HEAD_COLUMNS), BF16),
            jax.ShapeDtypeStruct((16, ROWS, 2 * HEAD_WIDTH), BF16),
            jax.ShapeDtypeStruct((2, N_EP * PAGES, PAGE_TOKENS, 2 * HEAD_WIDTH), BF16),
            jax.ShapeDtypeStruct((2, 4, 2, 128), jnp.int32),
            jax.ShapeDtypeStruct((4, 8, 128), F32),
            jax.ShapeDtypeStruct((128, 2, D), BF16),
            jax.ShapeDtypeStruct((ROWS, 256), F32),
        ),
        in_specs=[vmem] * 10 + [anywhere] * 2,
        out_specs=(anywhere,) * 5 + (vmem, vmem),
        scratch_shapes=[
            pltpu.VMEM((KEY_VALUE_HEADS, PAGES, PAGE_TOKENS, 2 * HEAD_WIDTH), BF16),
            pltpu.VMEM((KEY_VALUE_HEADS, ROWS, 2 * HEAD_WIDTH), BF16),
            pltpu.VMEM((ROWS, QUERY_HEADS * HEAD_WIDTH), BF16),
            pltpu.VMEM((4, 2, 128), jnp.int32),
            pltpu.VMEM((8, 128), F32),
            *[pltpu.VMEM((16, 16, columns), BF16) for _, columns in PARTS * 2],
            *[pltpu.VMEM((8, 32, columns), BF16) for _, columns in PARTS * 2],
            pltpu.VMEM((D, 2 * HID), BF16),
            pltpu.VMEM((HID, D), BF16),
            pltpu.VMEM((256, 2 * HID), F32),
            pltpu.VMEM((256, HID), BF16),
            dma((16,)), dma((16,)), dma((16,)), dma((16,)), dma((8,)), dma((8,)),
            dma((24,)), dma((24,)), dma((32,)), dma((32,)), dma((4,)), dma((4,)),
            dma((48,)), dma((48,)), dma((24,)), dma((24,)), dma((11,)), dma((6,)),
        ],
        compiler_params=pltpu.CompilerParams(
            collective_id=1, has_side_effects=True, vmem_limit_bytes=56 << 20
        ),
        name="exchange",
    )(queries, fresh, pages, owner, slot, count, hidden, gain, ids, prob, gate_up, down_proj)


BK = 1024
PIECE = 256
GK = 4096
KEYS = 2 * NPS * PAGE_TOKENS
UNITS = 4
CHUNKS = 4
COLS = 256
VROWS = 80


def values_of(rows):
    pick = (iota((VROWS, 128), 0) + HEAD_WIDTH == iota((VROWS, 128), 1)).astype(BF16)
    moved = nt(pick, rows)
    return jnp.where(iota(moved.shape, 0) >= HEAD_WIDTH, 1.0, moved).astype(BF16)


def score_kernel(
    table_ref, count_ref, sinks, q_ref, f_ref, pool_ref, o_ref, lse_ref,
    tables, counts, q_all, f_all, pool,
    kv, vt, qs, limit_ref, m_ref, acc, sorted_out, s0, s1, places, lengths, sem,
):
    y = lax.axis_index("seq")
    outer_pair = jnp.logical_or(y == 0, y == 3)
    loads = [
        pltpu.make_async_copy(source, target, sem.at[n])
        for n, (source, target) in enumerate(
            [(count_ref, counts), (q_ref, q_all), (f_ref, f_all), (table_ref, tables)]
        )
    ]
    share = pool.shape[0] // 8
    for n in range(8):
        part = pl.ds(n * share, share)
        loads.append(pltpu.make_async_copy(pool_ref.at[part], pool.at[part], sem.at[4 + n]))
    for copy in loads:
        copy.start()
    for copy in loads[:3]:
        copy.wait()
    head = head_of(y, lax.rem(lax.div(lax.axis_index("ep"), 2), 4))
    spread = iota((QUERY_HEADS, COLS), 0) == head * GROUP + lax.div(iota((QUERY_HEADS, COLS), 1), ROWS)
    sink_row = nn(sinks[...].reshape(1, QUERY_HEADS), spread.astype(F32), HIGHEST)
    i0 = iota((128, 128), 0)
    i1 = iota((128, 128), 1)
    lane_row = lax.rem(iota((128, COLS), 1), ROWS).astype(F32)

    def ordering(e):
        c = counts[e][0:1, :]
        n_row = jnp.where(
            outer_pair,
            jnp.minimum(c, 256.0) + jnp.maximum(c - 768.0, 0.0),
            jnp.clip(c - 256.0, 0.0, 512.0),
        )
        n_col = jnp.sum(jnp.where(i0 == i1, n_row, 0.0), axis=1, keepdims=True)
        behind = jnp.logical_or(n_row > n_col, jnp.logical_and(n_col == n_row, i1 < i0))
        pos_col = jnp.sum(jnp.where(behind, 1.0, 0.0), axis=1, keepdims=True)
        return n_row, n_col, pos_col

    for e in range(UNITS):
        n_row, n_col, pos_col = ordering(e)
        places[e] = pos_col
        ahead = jnp.logical_or(n_col > n_row, jnp.logical_and(n_col == n_row, i0 < i1))
        pos_row = jnp.sum(jnp.where(ahead, 1.0, 0.0), axis=0, keepdims=True)
        perm = (pos_row == i0.astype(F32)).astype(BF16)
        q_sorted = nn(perm, q_all[e * 4 : e * 4 + 4].reshape(128, HEAD_COLUMNS)) * 0.125
        f_sorted = nn(perm, f_all[e * 4 : e * 4 + 4].reshape(128, 128)).astype(BF16)
        none = jnp.zeros((COLS, HEAD_WIDTH), F32)
        for ch in range(CHUNKS):
            u = e * CHUNKS + ch
            pieces = [
                q_sorted[ch * ROWS : (ch + 1) * ROWS, g * HEAD_WIDTH : (g + 1) * HEAD_WIDTH]
                for g in range(GROUP)
            ]
            stacked = jnp.concatenate([jnp.concatenate(pieces, axis=0), none], axis=1)
            qs[u] = stacked.T.astype(BF16)
            member = pos_col == lane_row + float(ch * ROWS)
            limit = jnp.sum(jnp.where(member, n_col, 0.0), axis=0, keepdims=True)
            limit_ref[u] = jnp.broadcast_to(limit.astype(jnp.int32), (8, COLS))
            lengths[u] = jnp.max(limit).astype(jnp.int32) * PAGE_TOKENS
            rows = f_sorted[ch * ROWS : (ch + 1) * ROWS, :]
            s = nn(rows, qs[u])
            ki = iota((ROWS, COLS), 0)
            ri = lax.rem(iota((ROWS, COLS), 1), ROWS)
            seen = jnp.logical_and(
                lax.div(ki, SCORED_STEPS) == lax.div(ri, SCORED_STEPS), ki <= ri
            )
            s = jnp.where(seen, s, NEGATIVE)
            m0 = jnp.maximum(jnp.max(s, axis=0, keepdims=True), sink_row)
            p = jnp.exp(s - m0).astype(BF16)
            start = nn(values_of(rows), p)
            start = start + jnp.where(
                iota((VROWS, COLS), 0) >= HEAD_WIDTH, jnp.exp(sink_row - m0), 0.0
            )
            m_ref[u] = jnp.broadcast_to(jnp.where(outer_pair, m0, FLOOR), (8, COLS))
            acc[u] = jnp.where(outer_pair, start, 0.0)

    def unit(e, carry):
        def gather(kb, carry):
            rows = [
                pool[tables[kb, e, i // 128, i % 2 * 64 + i % 128 // 2] + kb * (N_EP * PAGES)]
                for i in range(GK // PAGE_TOKENS)
            ]
            for i in range(GK // BK):
                part = rows[i * (BK // PAGE_TOKENS) : (i + 1) * (BK // PAGE_TOKENS)]
                found = jnp.concatenate(part, axis=0)
                kv[pl.ds(pl.multiple_of(kb * GK + i * BK, BK), BK), :] = found
                vt[kb * (GK // BK) + i] = values_of(found)
            return carry

        lax.fori_loop(0, lax.div(lengths[e * CHUNKS] + (GK - 1), GK), gather, 0)

        page = iota((PIECE // PAGE_TOKENS, PAGE_TOKENS // 8, 8, COLS), 0)

        def produce(store, u, kb, i):
            start = pl.multiple_of(kb * BK + i * PIECE, PIECE)
            s = nn(kv[pl.ds(start, PIECE), :], qs[u])
            live = page < (limit_ref[u] - lax.div(start, PAGE_TOKENS))[None, None]
            s = jnp.where(live, s.reshape(page.shape), NEGATIVE).reshape(PIECE, COLS)
            store[i * PIECE : (i + 1) * PIECE, :] = s
            return jnp.max(s, axis=0, keepdims=True)

        def step(store, u, kb, top, next_store, next_u, next_kb):
            before = m_ref[u][0:1, :]
            after = jnp.maximum(before, top)
            total = acc[u] * jnp.exp(before - after)
            next_top = None
            for i in range(BK // PIECE):
                part = slice(i * PIECE, (i + 1) * PIECE)
                p = jnp.exp(store[part, :] - after).astype(BF16)
                found = produce(next_store, next_u, next_kb, i)
                next_top = found if i == 0 else jnp.maximum(next_top, found)
                total = total + nn(vt[kb, :, part], p)
            acc[u] = total
            m_ref[u] = jnp.broadcast_to(after, (8, COLS))
            return next_top

        def chunk(ch, top):
            u = e * CHUNKS + ch
            count = lax.div(lengths[u] + (BK - 1), BK)
            after_u = e * CHUNKS + jnp.minimum(ch + 1, CHUNKS - 1)

            def pair(i, top):
                last = 2 * i + 2 >= count
                top = step(s0, u, 2 * i, top, s1, u, 2 * i + 1)
                next_u = jnp.where(last, after_u, u)
                return step(s1, u, 2 * i + 1, top, s0, next_u, jnp.where(last, 0, 2 * i + 2))

            top = lax.fori_loop(0, lax.div(count, 2), pair, top)

            def odd(top):
                return step(s0, u, count - 1, top, s0, after_u, jnp.int32(0))

            return lax.cond(lax.rem(count, 2) == 1, odd, lambda top: top, top)

        used = sum([(lengths[e * CHUNKS + ch] > 0).astype(jnp.int32) for ch in range(CHUNKS)])

        @pl.when(used > 0)
        def _():
            tops = [produce(s0, e * CHUNKS, jnp.int32(0), i) for i in range(BK // PIECE)]
            top = jnp.max(jnp.concatenate(tops, axis=0), axis=0, keepdims=True)
            lax.fori_loop(0, used, chunk, top)

        return carry

    for copy in loads[3:]:
        copy.wait()
    lax.fori_loop(0, UNITS, unit, 0)

    for e in range(UNITS):
        pos_col = places[e]
        perm_t = (pos_col == i1.astype(F32)).astype(BF16)
        lse = jnp.zeros((8, 128), F32)
        for ch in range(CHUNKS):
            u = e * CHUNKS + ch
            total = jnp.maximum(acc[u][HEAD_WIDTH : HEAD_WIDTH + 1, :], 1e-30)
            out = acc[u][0:HEAD_WIDTH, :] / total
            padded = jnp.concatenate([out, jnp.zeros_like(out)], axis=0)
            turned = padded.T.astype(BF16)
            for g in range(GROUP):
                sorted_out[e, ch * ROWS : (ch + 1) * ROWS, g * HEAD_WIDTH : (g + 1) * HEAD_WIDTH] = (
                    turned[g * ROWS : (g + 1) * ROWS, 0:HEAD_WIDTH]
                )
            row = m_ref[u][0:1, :] + jnp.log(total)
            mine = lax.div(iota((8, COLS), 1), ROWS) == iota((8, COLS), 0)
            member = (pos_col == lane_row + float(ch * ROWS)).astype(BF16)
            rest = jnp.where(mine, row, 0.0)
            layers = []
            for _ in range(3):
                layers.append(rest.astype(BF16))
                rest = rest - layers[-1].astype(F32)
            moved = nt(jnp.concatenate([layer.astype(F32) for layer in layers], axis=0).astype(BF16), member)
            lse = lse + (moved[0:8] + moved[8:16] + moved[16:24])
        lse_ref[e] = lse
        o_ref[e] = nn(perm_t, sorted_out[e]).astype(BF16)


def score(tables, counts, sinks, q_all, f_all, pool):
    vmem = pl.BlockSpec(memory_space=pltpu.VMEM)
    anywhere = pl.BlockSpec(memory_space=pl.ANY)
    return pl.pallas_call(
        score_kernel,
        out_shape=(
            jax.ShapeDtypeStruct((UNITS, 128, HEAD_COLUMNS), BF16),
            jax.ShapeDtypeStruct((UNITS, 8, 128), F32),
        ),
        in_specs=[anywhere, anywhere, vmem, anywhere, anywhere, anywhere],
        out_specs=(vmem, vmem),
        scratch_shapes=[
            pltpu.SMEM((2, UNITS, 2, 128), jnp.int32),
            pltpu.VMEM((UNITS, 8, 128), F32),
            pltpu.VMEM((16, ROWS, HEAD_COLUMNS), BF16),
            pltpu.VMEM((16, ROWS, 2 * HEAD_WIDTH), BF16),
            pltpu.VMEM((2 * N_EP * PAGES, PAGE_TOKENS, 2 * HEAD_WIDTH), BF16),
            pltpu.VMEM((KEYS, 128), BF16),
            pltpu.VMEM((KEYS // BK, VROWS, BK), BF16),
            pltpu.VMEM((UNITS * CHUNKS, 128, COLS), BF16),
            pltpu.VMEM((UNITS * CHUNKS, 8, COLS), jnp.int32),
            pltpu.VMEM((UNITS * CHUNKS, 8, COLS), F32),
            pltpu.VMEM((UNITS * CHUNKS, VROWS, COLS), F32),
            pltpu.VMEM((UNITS, 128, HEAD_COLUMNS), BF16),
            pltpu.VMEM((BK, COLS), F32),
            pltpu.VMEM((BK, COLS), F32),
            pltpu.VMEM((UNITS, 128, 1), F32),
            pltpu.SMEM((UNITS * CHUNKS,), jnp.int32),
            pltpu.SemaphoreType.DMA((12,)),
        ],
        compiler_params=pltpu.CompilerParams(vmem_limit_bytes=60 << 20),
        cost_estimate=pl.CostEstimate(
            flops=25_000_000_000, bytes_accessed=8_000_000, transcendentals=20_000_000
        ),
        name="score",
    )(tables, counts, sinks, q_all, f_all, pool)


def merge_kernel(
    o_ref, lse_ref, share_ref, rows_ref, out_ref, mix_ref, o_all, lse_all, o_send, o_recv, l_send, l_recv, local,
):
    y, z, x, c = place()

    def at(dy, dx):
        return device(lax.rem(y + dy, 4), z, lax.rem(x + dx, 4), c)

    plane = [(dy, dx) for dy in range(4) for dx in range(4) if (dy, dx) != (0, 0)]
    barrier = pltpu.get_barrier_semaphore()
    for dy, dx in plane:
        pl.semaphore_signal(barrier, inc=1, device_id=at(dy, dx), device_id_type=MESH)
    pl.semaphore_wait(barrier, len(plane))
    inner_pair = jnp.logical_or(y == 1, y == 2).astype(jnp.int32)
    slot = inner_pair * 8 + head_of(y, x)
    copies = []
    for dy in range(4):
        for dx in range(4):
            n = dy * 4 + dx
            q = lax.rem(y + dy, 4)
            e = lax.rem(x + dx, 4)
            o_source = o_ref.at[e, pl.ds(pl.multiple_of(q * ROWS, ROWS), ROWS)]
            if n == 0:
                pair = [
                    pltpu.make_async_copy(o_source, o_all.at[slot], local.at[0]),
                    pltpu.make_async_copy(lse_ref.at[e], lse_all.at[slot], local.at[1]),
                ]
            else:
                pair = [
                    pltpu.make_async_remote_copy(
                        o_source, o_all.at[slot], o_send.at[n], o_recv.at[n],
                        device_id=at(dy, dx), device_id_type=MESH,
                    ),
                    pltpu.make_async_remote_copy(
                        lse_ref.at[e], lse_all.at[slot], l_send.at[n], l_recv.at[n],
                        device_id=at(dy, dx), device_id_type=MESH,
                    ),
                ]
            for copy in pair:
                copy.start()
            copies.extend(pair)

    share = share_ref[...]
    high = share.astype(BF16)
    low = (share - high.astype(F32)).astype(BF16)
    rows = rows_ref[...].reshape(256, D)
    mix_ref[...] = (nn(high, rows) + nn(low, rows)).astype(BF16)

    for copy in copies:
        copy.wait()
    mine = (iota((ROWS, 128), 1) == iota((ROWS, 128), 0) + y * ROWS).astype(F32)
    logs = nt(mine, lse_all[...].reshape(128, 128), HIGHEST)
    log0, log1 = logs[:, :64], logs[:, 64:]
    top = jnp.maximum(log0, log1)
    w0, w1 = jnp.exp(log0 - top), jnp.exp(log1 - top)
    share0, share1 = w0 / (w0 + w1), w1 / (w0 + w1)
    shares = jnp.concatenate([share0, share1], axis=0)
    high = shares.astype(BF16)
    low = (shares - high.astype(F32)).astype(BF16)
    both = jnp.concatenate([high, low], axis=1)
    for h in range(KEY_VALUE_HEADS):
        shape = (128, HEAD_COLUMNS)
        head = lax.div(iota(shape, 1), HEAD_WIDTH) + h * GROUP
        spread = (lax.rem(iota(shape, 0), QUERY_HEADS) == head).astype(BF16)
        wide = nn(both, spread)
        result = wide[:ROWS] * o_all[h].astype(F32) + wide[ROWS:] * o_all[8 + h].astype(F32)
        out_ref[:, h * HEAD_COLUMNS : (h + 1) * HEAD_COLUMNS] = result.astype(BF16)


def merge(o, lse, share, rows):
    vmem = pl.BlockSpec(memory_space=pltpu.VMEM)
    anywhere = pl.BlockSpec(memory_space=pl.ANY)
    dma = pltpu.SemaphoreType.DMA
    return pl.pallas_call(
        merge_kernel,
        out_shape=(
            jax.ShapeDtypeStruct((ROWS, QUERY_HEADS * HEAD_WIDTH), BF16),
            jax.ShapeDtypeStruct((ROWS, D), BF16),
        ),
        in_specs=[anywhere, anywhere, vmem, vmem],
        out_specs=(vmem, vmem),
        scratch_shapes=[
            pltpu.VMEM((16, ROWS, HEAD_COLUMNS), BF16),
            pltpu.VMEM((16, 8, 128), F32),
            dma((16,)), dma((16,)), dma((16,)), dma((16,)), dma((2,)),
        ],
        compiler_params=pltpu.CompilerParams(
            collective_id=2, has_side_effects=True, vmem_limit_bytes=16 << 20
        ),
        name="merge",
    )(o, lse, share, rows)


def by_prefix(table):
    return table[0].T.reshape(2, N_EP, NPS // 2).transpose(1, 0, 2)


def per_device(
    queries, fresh_key_values, key_value_pages, page_owner, page_slot, page_count, sinks,
    hidden, norm_gain, expert_ids, gate_prob, gate_up, down_proj,
):
    q_all, f_all, pool, tables, counts, result, share = exchange(
        queries[0],
        fresh_key_values[0],
        key_value_pages.reshape(PAGES * PAGE_TOKENS, 2 * KEY_VALUE_HEADS * HEAD_WIDTH),
        by_prefix(page_owner),
        by_prefix(page_slot),
        page_count,
        hidden[0],
        norm_gain,
        expert_ids[0].transpose(1, 2, 0),
        gate_prob[0].transpose(1, 2, 0),
        gate_up,
        down_proj,
    )
    returned = lax.all_to_all(result, ("seq", "ep"), split_axis=0, concat_axis=0, tiled=True)
    o, lse = score(
        tables, counts, sinks, q_all, f_all,
        pool.reshape(2 * N_EP * PAGES, PAGE_TOKENS, 2 * HEAD_WIDTH),
    )
    attention, mixture = merge(o, lse, share, returned)
    return (attention.reshape(queries.shape), mixture.reshape(hidden.shape))


def solution(mesh):
    return jax.shard_map(
        per_device,
        mesh=mesh,
        in_specs=(
            P("seq", "ep", None, None),
            P("seq", "ep", None, None),
            P("seq", "ep", None, None),
            P("seq", None, None),
            P("seq", None, None),
            P(None, "ep"),
            P(),
            P("seq", "ep", None, None),
            P(),
            P("seq", "ep", None, None),
            P("seq", "ep", None, None),
            P(("seq", "ep"), None, None),
            P(("seq", "ep"), None, None),
        ),
        out_specs=(P("seq", "ep", None, None), P("seq", "ep", None, None)),
        check_vma=False,
    )
```

```python
import jax
import jax.numpy as jnp
from jax import lax
from jax.experimental import pallas as pl
from jax.experimental.pallas import tpu as pltpu
from jax.sharding import PartitionSpec as P

D = 2880
QUERY_HEADS = 64
KEY_VALUE_HEADS = 8
GROUP = QUERY_HEADS // KEY_VALUE_HEADS
HEAD_WIDTH = 64
TOPK = 4
HID = 1440
SCORED_STEPS = 4
PAGE_TOKENS = 16
NPS = 256
PAGES = 24
PROMPTS = 8
N_SEQ = 4
N_EP = 32
ROWS = PROMPTS * SCORED_STEPS
HEAD_COLUMNS = GROUP * HEAD_WIDTH
NEGATIVE = -1e30
FLOOR = -1e29
EPSILON = 1e-05
MESH = pl.DeviceIdType.MESH
F32 = jnp.float32
BF16 = jnp.bfloat16
HIGHEST = lax.Precision.HIGHEST


def place():
    y = lax.axis_index("seq")
    ep = lax.axis_index("ep")
    return y, lax.div(ep, 8), lax.rem(lax.div(ep, 2), 4), lax.rem(ep, 2)


def device(y, z, x, c):
    return (y, z * 8 + x * 2 + c)


def head_of(y, x):
    return lax.div(y, 2) * 4 + x


def nt(a, b, precision=None):
    return lax.dot_general(
        a, b, (((1,), (1,)), ((), ())), preferred_element_type=F32, precision=precision
    )


def nn(a, b, precision=None):
    return lax.dot_general(
        a, b, (((1,), (0,)), ((), ())), preferred_element_type=F32, precision=precision
    )


def iota(shape, axis):
    return lax.broadcasted_iota(jnp.int32, shape, axis)


PARTS = ((0, 1024), (1024, 1024), (2048, D - 2048))


def route(id_ref, prob_ref):
    i0 = iota((128, 128), 0)
    i1 = iota((128, 128), 1)
    copies = (iota((8, 128), 0) == lax.rem(iota((8, 128), 1), 8)).astype(F32)
    group = lax.div(iota((TOPK, 128), 1), 8)

    def as_row(ref):
        row = jnp.zeros((1, 128), F32)
        for t in range(SCORED_STEPS):
            wide = nn(ref[t].astype(F32), copies, HIGHEST)
            mine = group == iota((TOPK, 128), 0) + t * TOPK
            row = row + jnp.sum(jnp.where(mine, wide, 0.0), axis=0, keepdims=True)
        return row

    ids = as_row(id_ref)
    column = jnp.sum(jnp.where(i0 == i1, ids, 0.0), axis=1, keepdims=True)
    earlier = jnp.logical_and(column == ids, i0 < i1)
    rank = jnp.sum(jnp.where(earlier, 1.0, 0.0), axis=0, keepdims=True)
    slots = iota((256, 128), 0).astype(F32) == 2.0 * ids + rank

    def token(a):
        return lax.rem(a, 8) * SCORED_STEPS + lax.div(a, 32)

    owner_token = (token(iota((128, ROWS), 0)) == iota((128, ROWS), 1)).astype(BF16)
    mine = token(iota((ROWS, 128), 1)) == iota((ROWS, 128), 0)
    share = nt(jnp.where(mine, as_row(prob_ref), 0.0), slots.astype(F32), HIGHEST)
    return slots.astype(BF16), owner_token, share


def exchange_kernel(
    q_ref, f_ref, page_ref, owner_ref, slot_ref, count_ref, hidden_ref, gain_ref, id_ref, prob_ref,
    up_ref, down_ref,
    q_all, f_all, pool, tables, counts, expert_out, share_ref,
    relay, f_relay, q_rows, table_ref, count_rows, out0, out1, out2, mid0, mid1, mid2, sorted0, sorted1, sorted2,
    in0, in1, in2, up_w, down_w, projected, active,
    q_send, q_recv, f_send, f_recv, a_send, a_recv, z_send, z_recv, c_send, c_recv,
    i_send, i_recv, d_send, d_recv, e_send, e_recv, local, w_sem,
):
    y, z, x, c = place()
    mate = 3 - y
    rows_out, rows_mid = (out0, out1, out2), (mid0, mid1, mid2)
    rows_sorted, rows_in = (sorted0, sorted1, sorted2), (in0, in1, in2)

    def at(dy, dx):
        return device(lax.rem(y + dy, 4), z, lax.rem(x + dx, 4), c)

    plane = [(dy, dx) for dy in range(4) for dx in range(4) if (dy, dx) != (0, 0)]
    up = device(y, lax.rem(z + 1, 4), x, c)
    down = device(y, lax.rem(z + 3, 4), x, c)
    twin = device(y, z, x, 1 - c)

    def beside(dy, dz):
        return device(lax.rem(y + dy, 4), lax.rem(z + dz, 4), x, c)

    def around(dx, dc):
        return device(y, z, lax.rem(x + dx, 4), lax.rem(c + dc, 2))

    peers = [at(dy, dx) for dy, dx in plane]
    peers += [beside(dy, dz) for dy in range(4) for dz in range(1, 4)]
    peers += [around(dx, 1) for dx in range(4)]
    barrier = pltpu.get_barrier_semaphore()
    for peer in peers:
        pl.semaphore_signal(barrier, inc=1, device_id=peer, device_id_type=MESH)

    weights = []
    for n in range(4):
        part = pl.ds(n * (D // 4), D // 4)
        weights.append(pltpu.make_async_copy(up_ref.at[0, part], up_w.at[part], w_sem.at[n]))
    for n in range(2):
        part = pl.ds(n * (HID // 2), HID // 2)
        weights.append(pltpu.make_async_copy(down_ref.at[0, part], down_w.at[part], w_sem.at[4 + n]))
    for copy in weights:
        copy.start()

    fresh = f_ref[...].reshape(ROWS, f_ref.shape[2])
    for h in range(KEY_VALUE_HEADS):
        low, high = h * HEAD_WIDTH, (h + 1) * HEAD_WIDTH
        split = KEY_VALUE_HEADS * HEAD_WIDTH
        rows = jnp.concatenate(
            [page_ref[:, low:high], page_ref[:, split + low : split + high]], axis=1
        )
        relay[h] = rows.reshape(PAGES, PAGE_TOKENS, 2 * HEAD_WIDTH)
        f_relay[h] = jnp.concatenate(
            [fresh[:, low:high], fresh[:, split + low : split + high]], axis=1
        )
    for xx in range(4):
        e = z * 8 + xx * 2 + c
        pages = owner_ref[e] * PAGES + slot_ref[e]
        for half in range(2):
            lanes = slice(half * 64, half * 64 + 64)
            table_ref[xx, half : half + 1, :] = jnp.concatenate(
                [pages[0:1, lanes], pages[1:2, lanes]], axis=1
            )
    lane = iota((PROMPTS, 128), 1)
    copies = (iota((PROMPTS, 128), 0) == lax.div(lax.rem(lane, ROWS), SCORED_STEPS)).astype(F32)
    wide = nn(count_ref[...].astype(F32), copies, HIGHEST)
    mine = lax.div(iota((N_SEQ, 128), 1), ROWS) == iota((N_SEQ, 128), 0)
    wide = jnp.sum(jnp.where(mine, wide, 0.0), axis=0, keepdims=True)
    count_rows[...] = jnp.broadcast_to(wide, (8, 128))

    h32 = hidden_ref[...].reshape(ROWS, D).astype(F32)
    scale = lax.rsqrt(jnp.mean(h32 * h32, axis=-1, keepdims=True) + EPSILON)
    normed = (h32 * scale * gain_ref[...].reshape(1, D)).astype(BF16)
    slots, owner_token, share = route(id_ref, prob_ref)
    share_ref[...] = share
    spread = nn(slots, owner_token).astype(BF16)
    for k, (first_column, columns) in enumerate(PARTS):
        piece = normed[:, first_column : first_column + columns]
        rows_out[k][...] = nn(spread, piece).astype(BF16).reshape(16, 16, columns)
    pl.semaphore_wait(barrier, len(peers))

    def spot(segment_slot, zz, xx, cc):
        return pool.at[segment_slot, pl.ds((zz * 8 + xx * 2 + cc) * PAGES, PAGES)]

    order = [(0, 0), (0, 1), (0, 3), (0, 2), (1, 0), (1, 1), (1, 3), (1, 2)]
    first = []

    def hand_out(n):
        p, dx = order[n]
        yy = y if p == 0 else mate
        xx = lax.rem(x + dx, 4)
        target = spot(lax.div(y, 2), z, x, c)
        source = relay.at[head_of(yy, xx)]
        if (p, dx) == (0, 0):
            copy = pltpu.make_async_copy(source, target, local.at[0])
        else:
            copy = pltpu.make_async_remote_copy(
                source, target, a_send.at[n], a_recv.at[n],
                device_id=device(yy, z, xx, c), device_id_type=MESH,
            )
        copy.start()
        first.append(copy)

    for n in range(4):
        hand_out(n)
    routed = []
    for k in range(len(PARTS)):
        for dy in range(4):
            for dz in range(4):
                n = dy * 4 + dz
                source = rows_out[k].at[lax.rem(y + dy, 4) * 4 + lax.rem(z + dz, 4)]
                target = rows_mid[k].at[y * 4 + z]
                if n == 0:
                    copy = pltpu.make_async_copy(source, target, local.at[5 + 2 * k])
                else:
                    copy = pltpu.make_async_remote_copy(
                        source, target, d_send.at[k * 16 + n], d_recv.at[k * 16 + n],
                        device_id=beside(dy, dz), device_id_type=MESH,
                    )
                copy.start()
                routed.append(copy)

    for n in range(4, 8):
        hand_out(n)

    small = []
    mine = pltpu.make_async_copy(table_ref, tables.at[lax.div(y, 2)], local.at[1])
    mine.start()
    small.append(mine)
    mine = pltpu.make_async_copy(count_rows, counts.at[x], local.at[2])
    mine.start()
    small.append(mine)
    other = pltpu.make_async_remote_copy(
        table_ref, tables.at[lax.div(y, 2)], i_send.at[0], i_recv.at[0],
        device_id=device(mate, z, x, c), device_id_type=MESH,
    )
    other.start()
    small.append(other)
    for dx in range(1, 4):
        other = pltpu.make_async_remote_copy(
            count_rows, counts.at[x], i_send.at[dx], i_recv.at[dx],
            device_id=at(0, dx), device_id_type=MESH,
        )
        other.start()
        small.append(other)

    def chunk(n):
        p, dx = order[n]
        yy = y if p == 0 else mate
        return lax.div(yy, 2), lax.rem(x - dx + 4, 4)

    def pass_on(n, zz, way, peer):
        segment_slot, xx = chunk(n)
        block = spot(segment_slot, zz, xx, c)
        sends, recvs = (c_send, c_recv) if way >= 3 else (z_send, z_recv)
        number = (way - 3 if way >= 3 else way) * 8 + n
        copy = pltpu.make_async_remote_copy(
            block, block, sends.at[number], recvs.at[number],
            device_id=peer, device_id_type=MESH,
        )
        copy.start()
        return copy

    upward, downward, further, across = [], [], [], []

    def begin(n):
        if n == 0:
            first[n].wait()
        else:
            first[n].wait_recv()
        upward.append(pass_on(n, z, 0, up))
        downward.append(pass_on(n, z, 1, down))
        across.append(pass_on(n, z, 3, twin))

    def forward(n):
        upward[n].wait_recv()
        if n % 2 == 0:
            further.append(pass_on(n, lax.rem(z + 3, 4), 2, up))
        across.append(pass_on(n, lax.rem(z + 3, 4), 4, twin))
        downward[n].wait_recv()
        if n % 2 == 1:
            further.append(pass_on(n, lax.rem(z + 1, 4), 2, down))
        across.append(pass_on(n, lax.rem(z + 1, 4), 5, twin))

    for n in range(4):
        begin(n)

    ri = iota((256, 256), 0)
    ci = iota((256, 256), 1)

    def slot_of(i):
        return lax.div(lax.rem(i, 32), 2) * 16 + lax.div(i, 32) * 2 + lax.rem(i, 2)

    def arrive(copies):
        copies[0].wait()
        for copy in copies[1:]:
            copy.wait_recv()

    regroup = (slot_of(ri) == ci).astype(BF16)
    delivered = [[], [], []]
    for k, (_, columns) in enumerate(PARTS):
        arrive(routed[k * 16 : (k + 1) * 16])
        moved = nn(regroup, rows_mid[k][...].reshape(256, columns)).astype(BF16)
        rows_sorted[k][...] = moved.reshape(8, 32, columns)
        for dx in range(4):
            for dc in range(2):
                n = dx * 2 + dc
                source = rows_sorted[k].at[lax.rem(x + dx, 4) * 2 + lax.rem(c + dc, 2)]
                target = rows_in[k].at[x * 2 + c]
                if n == 0:
                    copy = pltpu.make_async_copy(source, target, local.at[6 + 2 * k])
                else:
                    copy = pltpu.make_async_remote_copy(
                        source, target, e_send.at[k * 8 + n], e_recv.at[k * 8 + n],
                        device_id=around(dx, dc), device_id_type=MESH,
                    )
                copy.start()
                delivered[k].append(copy)
        if k == 1:
            for n in (0, 1):
                forward(n)
    for n in range(4, 8):
        begin(n)
    for n in (2, 3):
        forward(n)

    q_rows[...] = q_ref[...].reshape(ROWS, q_ref.shape[2])
    for dy in range(4):
        for dx in range(4):
            n = dy * 4 + dx
            h = head_of(lax.rem(y + dy, 4), lax.rem(x + dx, 4))
            q_source = q_rows.at[:, pl.ds(pl.multiple_of(h * HEAD_COLUMNS, HEAD_COLUMNS), HEAD_COLUMNS)]
            f_source = f_relay.at[h]
            slot = x * 4 + y
            if n == 0:
                copies = [
                    pltpu.make_async_copy(q_source, q_all.at[slot], local.at[3]),
                    pltpu.make_async_copy(f_source, f_all.at[slot], local.at[4]),
                ]
            else:
                copies = [
                    pltpu.make_async_remote_copy(
                        q_source, q_all.at[slot], q_send.at[n], q_recv.at[n],
                        device_id=at(dy, dx), device_id_type=MESH,
                    ),
                    pltpu.make_async_remote_copy(
                        f_source, f_all.at[slot], f_send.at[n], f_recv.at[n],
                        device_id=at(dy, dx), device_id_type=MESH,
                    ),
                ]
            for copy in copies:
                copy.start()
            small.extend(copies)

    for copy in weights:
        copy.wait()

    def tiles(work):
        @pl.loop(0, D // TILE)
        def _(j):
            work(pl.ds(pl.multiple_of(j * TILE, TILE), TILE))

        work(pl.ds(D // TILE * TILE, D % TILE))

    def project(k):
        first_column, columns = PARTS[k]
        arrive(delivered[k])

        def work(part):
            rows = rows_in[k][...].reshape(256, columns)
            term = nn(rows, up_w[first_column : first_column + columns, part])
            projected[:, part] = term if k == 0 else projected[:, part] + term

        tiles(work)

    project(0)
    project(1)
    forward(4)
    forward(5)
    project(2)
    forward(6)
    forward(7)

    @pl.loop(0, 8)
    def _(j):
        part = pl.ds(pl.multiple_of(j * 32, 32), 32)
        wide = projected[part, :]
        gate, upper = wide[:, :HID], wide[:, HID:]
        active[part, :] = ((upper + 1.0) * gate * jax.nn.sigmoid(1.702 * gate)).astype(BF16)

    back = (slot_of(ci) == ri).astype(BF16)
    active[...] = nn(back, active[...]).astype(BF16)

    def finish(part):
        rows = nn(active[...], down_w[:, part]).astype(BF16)
        expert_out[:, :, part] = rows.reshape(128, 2, rows.shape[1])

    @pl.loop(0, 3)
    def _(j):
        finish(pl.ds(pl.multiple_of(j * TILE, TILE), TILE))

    for n in range(8):
        further[n].wait_recv()
        across.append(pass_on(n, lax.rem(z + 2, 4), 6, twin))

    @pl.loop(3, D // TILE)
    def _(j):
        finish(pl.ds(pl.multiple_of(j * TILE, TILE), TILE))

    finish(pl.ds(D // TILE * TILE, D % TILE))

    for copy in across:
        copy.wait()
    for copy in first[1:] + upward + downward + further:
        copy.wait_send()
    for n, copy in enumerate(routed):
        if n % 16 > 0:
            copy.wait_send()
    for copy in sum([copies[1:] for copies in delivered], []):
        copy.wait_send()
    for copy in small:
        copy.wait()


TILE = 512


def exchange(
    queries, fresh, pages, owner, slot, count, hidden, gain, ids, prob, gate_up, down_proj
):
    vmem = pl.BlockSpec(memory_space=pltpu.VMEM)
    anywhere = pl.BlockSpec(memory_space=pl.ANY)
    dma = pltpu.SemaphoreType.DMA
    return pl.pallas_call(
        exchange_kernel,
        out_shape=(
            jax.ShapeDtypeStruct((16, ROWS, HEAD_COLUMNS), BF16),
            jax.ShapeDtypeStruct((16, ROWS, 2 * HEAD_WIDTH), BF16),
            jax.ShapeDtypeStruct((2, N_EP * PAGES, PAGE_TOKENS, 2 * HEAD_WIDTH), BF16),
            jax.ShapeDtypeStruct((2, 4, 2, 128), jnp.int32),
            jax.ShapeDtypeStruct((4, 8, 128), F32),
            jax.ShapeDtypeStruct((128, 2, D), BF16),
            jax.ShapeDtypeStruct((ROWS, 256), F32),
        ),
        in_specs=[vmem] * 10 + [anywhere] * 2,
        out_specs=(anywhere,) * 5 + (vmem, vmem),
        scratch_shapes=[
            pltpu.VMEM((KEY_VALUE_HEADS, PAGES, PAGE_TOKENS, 2 * HEAD_WIDTH), BF16),
            pltpu.VMEM((KEY_VALUE_HEADS, ROWS, 2 * HEAD_WIDTH), BF16),
            pltpu.VMEM((ROWS, QUERY_HEADS * HEAD_WIDTH), BF16),
            pltpu.VMEM((4, 2, 128), jnp.int32),
            pltpu.VMEM((8, 128), F32),
            *[pltpu.VMEM((16, 16, columns), BF16) for _, columns in PARTS * 2],
            *[pltpu.VMEM((8, 32, columns), BF16) for _, columns in PARTS * 2],
            pltpu.VMEM((D, 2 * HID), BF16),
            pltpu.VMEM((HID, D), BF16),
            pltpu.VMEM((256, 2 * HID), F32),
            pltpu.VMEM((256, HID), BF16),
            dma((16,)), dma((16,)), dma((16,)), dma((16,)), dma((8,)), dma((8,)),
            dma((24,)), dma((24,)), dma((32,)), dma((32,)), dma((4,)), dma((4,)),
            dma((48,)), dma((48,)), dma((24,)), dma((24,)), dma((11,)), dma((6,)),
        ],
        compiler_params=pltpu.CompilerParams(
            collective_id=1, has_side_effects=True, vmem_limit_bytes=56 << 20
        ),
        name="exchange",
    )(queries, fresh, pages, owner, slot, count, hidden, gain, ids, prob, gate_up, down_proj)


BK = 2048
PIECE = 256
GK = 4096
KEYS = 2 * NPS * PAGE_TOKENS
UNITS = 4
CHUNKS = 4
COLS = 256
VROWS = 80


def values_of(rows):
    pick = (iota((VROWS, 128), 0) + HEAD_WIDTH == iota((VROWS, 128), 1)).astype(BF16)
    moved = nt(pick, rows)
    return jnp.where(iota(moved.shape, 0) >= HEAD_WIDTH, 1.0, moved).astype(BF16)


def score_kernel(
    table_ref, count_ref, sinks, q_ref, f_ref, pool_ref, o_ref, lse_ref,
    tables, counts, q_all, f_all, pool,
    kv, vt, qs, limit_ref, m_ref, acc, sorted_out, s0, s1, places, lengths, sem,
):
    y = lax.axis_index("seq")
    outer_pair = jnp.logical_or(y == 0, y == 3)
    loads = [
        pltpu.make_async_copy(source, target, sem.at[n])
        for n, (source, target) in enumerate(
            [(count_ref, counts), (q_ref, q_all), (f_ref, f_all), (table_ref, tables)]
        )
    ]
    share = pool.shape[0] // 8
    for n in range(8):
        part = pl.ds(n * share, share)
        loads.append(pltpu.make_async_copy(pool_ref.at[part], pool.at[part], sem.at[4 + n]))
    for copy in loads:
        copy.start()
    loads[0].wait()
    head = head_of(y, lax.rem(lax.div(lax.axis_index("ep"), 2), 4))
    spread = iota((QUERY_HEADS, COLS), 0) == head * GROUP + lax.div(iota((QUERY_HEADS, COLS), 1), ROWS)
    sink_row = nn(sinks[...].reshape(1, QUERY_HEADS), spread.astype(F32), HIGHEST)
    i0 = iota((128, 128), 0)
    i1 = iota((128, 128), 1)
    lane_row = lax.rem(iota((128, COLS), 1), ROWS).astype(F32)

    def ordering(e):
        c = counts[e][0:1, :]
        n_row = jnp.where(
            outer_pair,
            jnp.minimum(c, 256.0) + jnp.maximum(c - 768.0, 0.0),
            jnp.clip(c - 256.0, 0.0, 512.0),
        )
        n_col = jnp.sum(jnp.where(i0 == i1, n_row, 0.0), axis=1, keepdims=True)
        behind = jnp.logical_or(n_row > n_col, jnp.logical_and(n_col == n_row, i1 < i0))
        pos_col = jnp.sum(jnp.where(behind, 1.0, 0.0), axis=1, keepdims=True)
        return n_row, n_col, pos_col

    orders = [ordering(e) for e in range(UNITS)]
    for copy in loads[1:3]:
        copy.wait()
    for e in range(UNITS):
        n_row, n_col, pos_col = orders[e]
        places[e] = pos_col
        ahead = jnp.logical_or(n_col > n_row, jnp.logical_and(n_col == n_row, i0 < i1))
        pos_row = jnp.sum(jnp.where(ahead, 1.0, 0.0), axis=0, keepdims=True)
        perm = (pos_row == i0.astype(F32)).astype(BF16)
        q_sorted = nn(perm, q_all[e * 4 : e * 4 + 4].reshape(128, HEAD_COLUMNS)) * 0.125
        f_sorted = nn(perm, f_all[e * 4 : e * 4 + 4].reshape(128, 128)).astype(BF16)
        none = jnp.zeros((COLS, HEAD_WIDTH), F32)
        for ch in range(CHUNKS):
            u = e * CHUNKS + ch
            pieces = [
                q_sorted[ch * ROWS : (ch + 1) * ROWS, g * HEAD_WIDTH : (g + 1) * HEAD_WIDTH]
                for g in range(GROUP)
            ]
            stacked = jnp.concatenate([jnp.concatenate(pieces, axis=0), none], axis=1)
            qs[u] = stacked.T.astype(BF16)
            member = pos_col == lane_row + float(ch * ROWS)
            limit = jnp.sum(jnp.where(member, n_col, 0.0), axis=0, keepdims=True)
            limit_ref[u] = jnp.broadcast_to(limit.astype(jnp.int32), (8, COLS))
            lengths[u] = jnp.max(limit).astype(jnp.int32) * PAGE_TOKENS
            rows = f_sorted[ch * ROWS : (ch + 1) * ROWS, :]
            s = nn(rows, qs[u])
            ki = iota((ROWS, COLS), 0)
            ri = lax.rem(iota((ROWS, COLS), 1), ROWS)
            seen = jnp.logical_and(
                lax.div(ki, SCORED_STEPS) == lax.div(ri, SCORED_STEPS), ki <= ri
            )
            s = jnp.where(seen, s, NEGATIVE)
            m0 = jnp.maximum(jnp.max(s, axis=0, keepdims=True), sink_row)
            p = jnp.exp(s - m0).astype(BF16)
            start = nn(values_of(rows), p)
            start = start + jnp.where(
                iota((VROWS, COLS), 0) >= HEAD_WIDTH, jnp.exp(sink_row - m0), 0.0
            )
            m_ref[u] = jnp.broadcast_to(jnp.where(outer_pair, m0, FLOOR), (8, COLS))
            acc[u] = jnp.where(outer_pair, start, 0.0)

    def unit(e, carry):
        def gather(kb, carry):
            rows = [
                pool[tables[kb, e, i // 128, i % 2 * 64 + i % 128 // 2] + kb * (N_EP * PAGES)]
                for i in range(GK // PAGE_TOKENS)
            ]
            for i in range(GK // BK):
                part = rows[i * (BK // PAGE_TOKENS) : (i + 1) * (BK // PAGE_TOKENS)]
                found = jnp.concatenate(part, axis=0)
                kv[pl.ds(pl.multiple_of(kb * GK + i * BK, BK), BK), :] = found
                vt[kb * (GK // BK) + i] = values_of(found)
            return carry

        lax.fori_loop(0, lax.div(lengths[e * CHUNKS] + (GK - 1), GK), gather, 0)

        page = iota((PIECE // PAGE_TOKENS, PAGE_TOKENS // 8, 8, COLS), 0)

        def produce(store, u, kb, i):
            start = pl.multiple_of(kb * BK + i * PIECE, PIECE)
            s = nn(kv[pl.ds(start, PIECE), :], qs[u])
            live = page < (limit_ref[u] - lax.div(start, PAGE_TOKENS))[None, None]
            s = jnp.where(live, s.reshape(page.shape), NEGATIVE).reshape(PIECE, COLS)
            store[i * PIECE : (i + 1) * PIECE, :] = s
            return jnp.max(s, axis=0, keepdims=True)

        def step(store, u, kb, top, next_store, next_u, next_kb):
            before = m_ref[u][0:1, :]
            after = jnp.maximum(before, top)
            total = acc[u] * jnp.exp(before - after)
            next_top = None
            for i in range(BK // PIECE):
                part = slice(i * PIECE, (i + 1) * PIECE)
                p = jnp.exp(store[part, :] - after).astype(BF16)
                found = produce(next_store, next_u, next_kb, i)
                next_top = found if i == 0 else jnp.maximum(next_top, found)
                total = total + nn(vt[kb, :, part], p)
            acc[u] = total
            m_ref[u] = jnp.broadcast_to(after, (8, COLS))
            return next_top

        def chunk(ch, top):
            u = e * CHUNKS + ch
            count = lax.div(lengths[u] + (BK - 1), BK)
            after_u = e * CHUNKS + jnp.minimum(ch + 1, CHUNKS - 1)

            def pair(i, top):
                last = 2 * i + 2 >= count
                top = step(s0, u, 2 * i, top, s1, u, 2 * i + 1)
                next_u = jnp.where(last, after_u, u)
                return step(s1, u, 2 * i + 1, top, s0, next_u, jnp.where(last, 0, 2 * i + 2))

            top = lax.fori_loop(0, lax.div(count, 2), pair, top)

            def odd(top):
                return step(s0, u, count - 1, top, s0, after_u, jnp.int32(0))

            return lax.cond(lax.rem(count, 2) == 1, odd, lambda top: top, top)

        used = sum([(lengths[e * CHUNKS + ch] > 0).astype(jnp.int32) for ch in range(CHUNKS)])

        @pl.when(used > 0)
        def _():
            tops = [produce(s0, e * CHUNKS, jnp.int32(0), i) for i in range(BK // PIECE)]
            top = jnp.max(jnp.concatenate(tops, axis=0), axis=0, keepdims=True)
            lax.fori_loop(0, used, chunk, top)

        return carry

    for copy in loads[3:]:
        copy.wait()
    lax.fori_loop(0, UNITS, unit, 0)

    for e in range(UNITS):
        pos_col = places[e]
        perm_t = (pos_col == i1.astype(F32)).astype(BF16)
        lse = jnp.zeros((8, 128), F32)
        for ch in range(CHUNKS):
            u = e * CHUNKS + ch
            total = jnp.maximum(acc[u][HEAD_WIDTH : HEAD_WIDTH + 1, :], 1e-30)
            out = acc[u][0:HEAD_WIDTH, :] / total
            padded = jnp.concatenate([out, jnp.zeros_like(out)], axis=0)
            turned = padded.T.astype(BF16)
            for g in range(GROUP):
                sorted_out[e, ch * ROWS : (ch + 1) * ROWS, g * HEAD_WIDTH : (g + 1) * HEAD_WIDTH] = (
                    turned[g * ROWS : (g + 1) * ROWS, 0:HEAD_WIDTH]
                )
            row = m_ref[u][0:1, :] + jnp.log(total)
            mine = lax.div(iota((8, COLS), 1), ROWS) == iota((8, COLS), 0)
            member = (pos_col == lane_row + float(ch * ROWS)).astype(BF16)
            rest = jnp.where(mine, row, 0.0)
            layers = []
            for _ in range(3):
                layers.append(rest.astype(BF16))
                rest = rest - layers[-1].astype(F32)
            moved = nt(jnp.concatenate([layer.astype(F32) for layer in layers], axis=0).astype(BF16), member)
            lse = lse + (moved[0:8] + moved[8:16] + moved[16:24])
        lse_ref[e] = lse
        o_ref[e] = nn(perm_t, sorted_out[e]).astype(BF16)


def score(tables, counts, sinks, q_all, f_all, pool):
    vmem = pl.BlockSpec(memory_space=pltpu.VMEM)
    anywhere = pl.BlockSpec(memory_space=pl.ANY)
    return pl.pallas_call(
        score_kernel,
        out_shape=(
            jax.ShapeDtypeStruct((UNITS, 128, HEAD_COLUMNS), BF16),
            jax.ShapeDtypeStruct((UNITS, 8, 128), F32),
        ),
        in_specs=[anywhere, anywhere, vmem, anywhere, anywhere, anywhere],
        out_specs=(vmem, vmem),
        scratch_shapes=[
            pltpu.SMEM((2, UNITS, 2, 128), jnp.int32),
            pltpu.VMEM((UNITS, 8, 128), F32),
            pltpu.VMEM((16, ROWS, HEAD_COLUMNS), BF16),
            pltpu.VMEM((16, ROWS, 2 * HEAD_WIDTH), BF16),
            pltpu.VMEM((2 * N_EP * PAGES, PAGE_TOKENS, 2 * HEAD_WIDTH), BF16),
            pltpu.VMEM((KEYS, 128), BF16),
            pltpu.VMEM((KEYS // BK, VROWS, BK), BF16),
            pltpu.VMEM((UNITS * CHUNKS, 128, COLS), BF16),
            pltpu.VMEM((UNITS * CHUNKS, 8, COLS), jnp.int32),
            pltpu.VMEM((UNITS * CHUNKS, 8, COLS), F32),
            pltpu.VMEM((UNITS * CHUNKS, VROWS, COLS), F32),
            pltpu.VMEM((UNITS, 128, HEAD_COLUMNS), BF16),
            pltpu.VMEM((BK, COLS), F32),
            pltpu.VMEM((BK, COLS), F32),
            pltpu.VMEM((UNITS, 128, 1), F32),
            pltpu.SMEM((UNITS * CHUNKS,), jnp.int32),
            pltpu.SemaphoreType.DMA((12,)),
        ],
        compiler_params=pltpu.CompilerParams(vmem_limit_bytes=60 << 20),
        cost_estimate=pl.CostEstimate(
            flops=25_000_000_000, bytes_accessed=8_000_000, transcendentals=20_000_000
        ),
        name="score",
    )(tables, counts, sinks, q_all, f_all, pool)


def merge_kernel(
    o_ref, lse_ref, share_ref, rows_ref, out_ref, mix_ref, o_all, lse_all, o_send, o_recv, l_send, l_recv, local,
):
    y, z, x, c = place()

    def at(dy, dx):
        return device(lax.rem(y + dy, 4), z, lax.rem(x + dx, 4), c)

    plane = [(dy, dx) for dy in range(4) for dx in range(4) if (dy, dx) != (0, 0)]
    barrier = pltpu.get_barrier_semaphore()
    for dy, dx in plane:
        pl.semaphore_signal(barrier, inc=1, device_id=at(dy, dx), device_id_type=MESH)
    pl.semaphore_wait(barrier, len(plane))
    inner_pair = jnp.logical_or(y == 1, y == 2).astype(jnp.int32)
    slot = inner_pair * 8 + head_of(y, x)
    copies = []
    for dy in range(4):
        for dx in range(4):
            n = dy * 4 + dx
            q = lax.rem(y + dy, 4)
            e = lax.rem(x + dx, 4)
            o_source = o_ref.at[e, pl.ds(pl.multiple_of(q * ROWS, ROWS), ROWS)]
            if n == 0:
                pair = [
                    pltpu.make_async_copy(o_source, o_all.at[slot], local.at[0]),
                    pltpu.make_async_copy(lse_ref.at[e], lse_all.at[slot], local.at[1]),
                ]
            else:
                pair = [
                    pltpu.make_async_remote_copy(
                        o_source, o_all.at[slot], o_send.at[n], o_recv.at[n],
                        device_id=at(dy, dx), device_id_type=MESH,
                    ),
                    pltpu.make_async_remote_copy(
                        lse_ref.at[e], lse_all.at[slot], l_send.at[n], l_recv.at[n],
                        device_id=at(dy, dx), device_id_type=MESH,
                    ),
                ]
            for copy in pair:
                copy.start()
            copies.extend(pair)

    share = share_ref[...]
    high = share.astype(BF16)
    low = (share - high.astype(F32)).astype(BF16)
    rows = rows_ref[...].reshape(256, D)
    mix_ref[...] = (nn(high, rows) + nn(low, rows)).astype(BF16)

    for copy in copies:
        copy.wait()
    mine = (iota((ROWS, 128), 1) == iota((ROWS, 128), 0) + y * ROWS).astype(F32)
    logs = nt(mine, lse_all[...].reshape(128, 128), HIGHEST)
    log0, log1 = logs[:, :64], logs[:, 64:]
    top = jnp.maximum(log0, log1)
    w0, w1 = jnp.exp(log0 - top), jnp.exp(log1 - top)
    share0, share1 = w0 / (w0 + w1), w1 / (w0 + w1)
    shares = jnp.concatenate([share0, share1], axis=0)
    high = shares.astype(BF16)
    low = (shares - high.astype(F32)).astype(BF16)
    both = jnp.concatenate([high, low], axis=1)
    for h in range(KEY_VALUE_HEADS):
        shape = (128, HEAD_COLUMNS)
        head = lax.div(iota(shape, 1), HEAD_WIDTH) + h * GROUP
        spread = (lax.rem(iota(shape, 0), QUERY_HEADS) == head).astype(BF16)
        wide = nn(both, spread)
        result = wide[:ROWS] * o_all[h].astype(F32) + wide[ROWS:] * o_all[8 + h].astype(F32)
        out_ref[:, h * HEAD_COLUMNS : (h + 1) * HEAD_COLUMNS] = result.astype(BF16)


def merge(o, lse, share, rows):
    vmem = pl.BlockSpec(memory_space=pltpu.VMEM)
    anywhere = pl.BlockSpec(memory_space=pl.ANY)
    dma = pltpu.SemaphoreType.DMA
    return pl.pallas_call(
        merge_kernel,
        out_shape=(
            jax.ShapeDtypeStruct((ROWS, QUERY_HEADS * HEAD_WIDTH), BF16),
            jax.ShapeDtypeStruct((ROWS, D), BF16),
        ),
        in_specs=[anywhere, anywhere, vmem, vmem],
        out_specs=(vmem, vmem),
        scratch_shapes=[
            pltpu.VMEM((16, ROWS, HEAD_COLUMNS), BF16),
            pltpu.VMEM((16, 8, 128), F32),
            dma((16,)), dma((16,)), dma((16,)), dma((16,)), dma((2,)),
        ],
        compiler_params=pltpu.CompilerParams(
            collective_id=2, has_side_effects=True, vmem_limit_bytes=16 << 20
        ),
        name="merge",
    )(o, lse, share, rows)


def by_prefix(table):
    return table[0].T.reshape(2, N_EP, NPS // 2).transpose(1, 0, 2)


def per_device(
    queries, fresh_key_values, key_value_pages, page_owner, page_slot, page_count, sinks,
    hidden, norm_gain, expert_ids, gate_prob, gate_up, down_proj,
):
    q_all, f_all, pool, tables, counts, result, share = exchange(
        queries[0],
        fresh_key_values[0],
        key_value_pages.reshape(PAGES * PAGE_TOKENS, 2 * KEY_VALUE_HEADS * HEAD_WIDTH),
        by_prefix(page_owner),
        by_prefix(page_slot),
        page_count,
        hidden[0],
        norm_gain,
        expert_ids[0].transpose(1, 2, 0),
        gate_prob[0].transpose(1, 2, 0),
        gate_up,
        down_proj,
    )
    returned = lax.all_to_all(result, ("seq", "ep"), split_axis=0, concat_axis=0, tiled=True)
    o, lse = score(
        tables, counts, sinks, q_all, f_all,
        pool.reshape(2 * N_EP * PAGES, PAGE_TOKENS, 2 * HEAD_WIDTH),
    )
    attention, mixture = merge(o, lse, share, returned)
    return (attention.reshape(queries.shape), mixture.reshape(hidden.shape))


def solution(mesh):
    return jax.shard_map(
        per_device,
        mesh=mesh,
        in_specs=(
            P("seq", "ep", None, None),
            P("seq", "ep", None, None),
            P("seq", "ep", None, None),
            P("seq", None, None),
            P("seq", None, None),
            P(None, "ep"),
            P(),
            P("seq", "ep", None, None),
            P(),
            P("seq", "ep", None, None),
            P("seq", "ep", None, None),
            P(("seq", "ep"), None, None),
            P(("seq", "ep"), None, None),
        ),
        out_specs=(P("seq", "ep", None, None), P("seq", "ep", None, None)),
        check_vma=False,
    )
```
